32 devices in a mesh: wide: 8 (over z, y), narrow: 4 (over x, core).
Axes of the slice: x: 2, y: 2, z: 4, core: 2. Of those that a mesh axis runs over, the one named last changes fastest.
Arguments:
- hidden: bfloat16 [40, 4096], P('wide', 'narrow'), may hold values from -18 to 18
- w_query: bfloat16 [4096, 4096], P('narrow', 'wide'), may hold values from -0.09375 to 0.09375
- w_keyval: bfloat16 [4096, 1024], P('narrow', 'wide'), may hold values from -0.09375 to 0.09375
- w_out: bfloat16 [4096, 4096], P('narrow', 'wide'), may hold values from -0.09375 to 0.09375
- pool: bfloat16 [4096, 16, 1024], P(('wide', 'narrow')), may hold values from -144 to 144
- page_req: int32 [4096], P(('wide', 'narrow')), may hold values from -1 to 7, as said below
- page_idx: int32 [4096], P(('wide', 'narrow')), may hold values from -1 to 511, as said below
- lengths: int32 [8], replicated, may hold values from 128 to 8192, as said below
- moves: int32 [4096, 1], P(('wide', 'narrow')), may hold values from 0 to 7; in each aligned block of 128 rows (0 to 127, 128 to 255, ...) at most 16 rows name the same one
- accepted: int32 [8], replicated, may hold values from 1 to 5
Outputs:
- attended: bfloat16 [40, 4096], P('narrow', 'wide')
- new_entries: bfloat16 [8, 5, 1024], P('wide')
- moved_pool: bfloat16 [4096, 16, 1024], P(('wide', 'narrow'))
- moved_req: int32 [4096], P(('wide', 'narrow'))
- moved_idx: int32 [4096], P(('wide', 'narrow'))
The draws below stay inside these ranges and needn't reach their ends.
Inputs may be any that keep to these rules, and one draw needn't show every extreme that they name: Request r holds exactly ceil(lengths[r] / 16) slots, whose page numbers are 0 up to that count minus 1, each once; every other slot is free, with page_req and page_idx -1. `page_idx`: see page_req. `lengths`: each length lies either in 128 to 256 or in 6144 to 8192; exactly 4 lie in the second range. `moves`: each device sends exactly 16 of its slots to each index of wide.
All inputs are finite; a program needn't handle non-finite values.
Results may differ from the reference program's by a relative error of at most 0.03.
Values may be sent and summed in bfloat16 or wider, within the bound.
No kernel may reach another device: no remote copies, remote signals or barrier semaphores. Data moves between devices by JAX's collectives and lax.ppermute only.
A program may use at most 128 MiB of HBM per device.

```python
import math
import jax
import jax.numpy as jnp
import numpy as np
from jax import lax

D = 4096
HEADS = 32
KVH = 4
HD = 128
KVW = 1024
STEPS = 5
PAGE = 16
MAXP = 512
REQ = 8
ROWS = 40
SLOTS = 4096
POOL = 128
CAP = 16
N_WIDE = 8
N_NARROW = 4


def request_lengths(key):
    first, second, third = jax.random.split(jax.random.fold_in(key, 11), 3)
    shuffled = jax.random.permutation(first, REQ)
    longflag = shuffled < REQ // 2
    long_len = jax.random.randint(second, (REQ,), 3 * MAXP * PAGE // 4, MAXP * PAGE + 1)
    short_len = jax.random.randint(third, (REQ,), 8 * PAGE, 16 * PAGE + 1)
    result = jnp.where(longflag, long_len, short_len)
    inverse = jnp.argsort(shuffled, stable=True)
    result = result.at[inverse[0]].set(MAXP * PAGE)
    result = result.at[inverse[REQ - 1]].set(8 * PAGE)
    return result.astype(jnp.int32)


def page_layout(key):
    slot_ids = jax.random.permutation(jax.random.fold_in(key, 7), SLOTS)
    owners = slot_ids // MAXP
    numbers = slot_ids % MAXP
    pages_held = (request_lengths(key) + PAGE - 1) // PAGE
    live_mask = numbers < jnp.take(pages_held, owners)
    return (jnp.where(live_mask, owners, -1), jnp.where(live_mask, numbers, -1))


def draw_lengths(key, part):
    return request_lengths(key)


def draw_page_req(key, part):
    return page_layout(key)[0].astype(jnp.int32)


def draw_page_idx(key, part):
    return page_layout(key)[1].astype(jnp.int32)


def draw_hidden(key, part):
    values = jnp.clip(jax.random.normal(jax.random.fold_in(key, 3), (ROWS, D), jnp.float32), -6.0, 6.0)
    return values.astype(jnp.bfloat16)


def draw_pool(key, part):
    values = jnp.clip(jax.random.normal(jax.random.fold_in(key, 13), (SLOTS, PAGE, KVW), jnp.float32), -6.0, 6.0)
    return values.astype(jnp.bfloat16)


def place_ends(array, key, least, top_value):
    longest = array.shape.index(max(array.shape))
    spots = []
    for shift in (0, 1):
        where = [jax.random.randint(jax.random.fold_in(key, axis), (), 0, length) for axis, length in enumerate(array.shape)]
        where[longest] = (where[longest] + shift) % array.shape[longest]
        spots.append(tuple(where))
    return array.at[spots[0]].set(least).at[spots[1]].set(top_value)


def steps_of(key, shape, cuts, smallest, top_value):
    loudness = 1.0
    for position, shards_of in cuts:
        heights = jax.random.uniform(jax.random.fold_in(jax.random.fold_in(key, 6), position), (shards_of,), jnp.float32, smallest / len(cuts), top_value / len(cuts))
        loudness = loudness * jnp.repeat(jnp.exp(heights), shape[position] // shards_of).reshape((-1,) + (1,) * (len(shape) - 1 - position))
    return loudness


def assign_block(own_key, own, number, rows, number_of, top, most, slope):
    order = jax.random.permutation(own_key, number_of)
    packed, usual = portions_of(number_of, rows * top, most, slope, True), portions_of(number_of, rows * top, most, slope, False)
    places = jnp.arange(number_of)

    def named(tallies, rotation):
        used = int((tallies > 0).sum())
        fixed = max(1, used // 4)
        shifted = fixed + (places - fixed + rotation * (used - fixed)) % max(1, number_of - fixed)
        return jnp.zeros((number_of,), jnp.int32).at[order[jnp.where(places < fixed, places, shifted)]].set(jnp.asarray(tallies, jnp.int32))

    tallies = jnp.where(number % 4 == 0, named(packed, number // 4), named(usual, number - number // 4 - 1))
    mixed = jax.random.permutation(jax.random.fold_in(own, 3), number_of)
    giver, taker = mixed[0:number_of // 2 * 2:2], mixed[1:number_of // 2 * 2:2]
    slack = jnp.minimum(tallies[giver] - 1, most - tallies[taker]) // 2
    slack = jnp.where((giver == order[0]) | (taker == order[0]) | (tallies[taker] == 0), 0, jnp.maximum(slack, 0))
    shifted = jax.random.randint(jax.random.fold_in(own, 4), (number_of // 2,), 0, 1 << 20) % (slack + 1)
    tallies = tallies.at[giver].add(-shifted).at[taker].add(shifted)
    items = jnp.searchsorted(jnp.cumsum(tallies), jnp.arange(rows * top), side="right").astype(jnp.int32)
    table = items.reshape(top, rows).T
    table = table[jax.random.permutation(jax.random.fold_in(own, 1), rows)]
    rotation = jax.random.randint(jax.random.fold_in(own, 2), (rows, 1), 0, top)
    return jnp.take_along_axis(table, (jnp.arange(top)[None, :] + rotation) % top, axis=1)


def portions_of(count, total, limit, lean, full):
    weights = [(1 << 20) // math.isqrt(grade ** lean) + 1 for grade in range(1, count + 1)]
    largest = limit if full else min(limit, max(-(-total // count), total * weights[0] // sum(weights)))
    least = 1 if total - largest >= count - 1 else 0
    given, rest = [largest] + [least] * (count - 1), total - largest - least * (count - 1)
    while rest > 0:
        free = [i for i in range(1, count) if given[i] < largest] or [i for i in range(1, count) if given[i] < limit]
        whole, budget = sum([weights[i] for i in free]), rest
        for i in free:
            extra = min(limit - given[i], max(1, budget * weights[i] // whole), rest)
            given[i] = given[i] + extra
            rest = rest - extra
    return np.array(given)


def bell_draw(own_key, dims, width, limit, pieces=(), kind=jnp.bfloat16):
    values = jax.random.normal(own_key, dims, jnp.float32) * width
    if len(pieces) > 0:
        values = steps_of(own_key, dims, pieces, -0.22, 0.18) * values
    return jnp.clip(values, min=-limit, max=limit).astype(kind)


def setup_inputs(seed: int = 0) -> dict:
    splits = jax.random.split(jax.random.key(seed), 11)
    hidden = draw_hidden(jax.random.fold_in(splits[10], 71), 0)
    w_query = bell_draw(splits[1], (D, D), D ** -0.5, 0.09375, ((0, 4), (1, 8)))
    w_keyval = bell_draw(splits[2], (D, KVW), D ** -0.5, 0.09375, ((0, 4), (1, 8)))
    w_out = bell_draw(splits[3], (D, D), D ** -0.5, 0.09375, ((0, 4), (1, 8)))
    pool = draw_pool(jax.random.fold_in(splits[10], 71), 0)
    page_req = draw_page_req(jax.random.fold_in(splits[10], 71), 0)
    page_idx = draw_page_idx(jax.random.fold_in(splits[10], 71), 0)
    lengths = draw_lengths(jax.random.fold_in(splits[10], 71), 0)
    moves_keys = jax.random.split(jax.random.fold_in(splits[8], 1), SLOTS // POOL)
    moves_turns = jax.random.permutation(jax.random.fold_in(splits[8], 3), SLOTS // POOL)
    moves = jax.vmap(lambda own, number: assign_block(jax.random.fold_in(splits[8], 2), own, number, POOL, N_WIDE, 1, CAP, 0))(moves_keys, moves_turns).reshape((SLOTS, 1))
    accepted = place_ends(jax.random.randint(splits[9], (REQ,), 1, STEPS + 1), jax.random.fold_in(splits[9], 1), 1, STEPS).astype(jnp.int32)
    return {"hidden": hidden, "w_query": w_query, "w_keyval": w_keyval, "w_out": w_out, "pool": pool, "page_req": page_req, "page_idx": page_idx, "lengths": lengths, "moves": moves, "accepted": accepted}


NEG_FILL = -1e+30

def reference(hidden, w_query, w_keyval, w_out, pool, page_req, page_idx, lengths, moves, accepted):
    groups = HEADS // KVH
    scale = 1.0 / math.sqrt(HD)
    query = jnp.dot(hidden, w_query, preferred_element_type=jnp.float32).astype(jnp.bfloat16)
    keyval = jnp.dot(hidden, w_keyval, preferred_element_type=jnp.float32).astype(jnp.bfloat16)
    query_r = query.reshape(REQ, STEPS, KVH, groups, HD)
    keyval_r = keyval.reshape(REQ, STEPS, 2, KVH, HD)
    live_key = jnp.where(page_req >= 0, page_req * MAXP + page_idx, REQ * MAXP).astype(jnp.int32)
    slot_of = jnp.zeros((REQ * MAXP,), jnp.int32).at[live_key].set(jnp.arange(SLOTS, dtype=jnp.int32), mode='drop')
    causal = jnp.arange(STEPS)[None, :] <= jnp.arange(STEPS)[:, None]
    positions = jnp.arange(MAXP * PAGE, dtype=jnp.int32)

    def one_request(index):
        slots = lax.dynamic_slice_in_dim(slot_of, index * MAXP, MAXP)
        cache = pool[slots].reshape(MAXP * PAGE, 2, KVH, HD)
        fresh = lax.dynamic_index_in_dim(keyval_r, index, 0, False)
        keys = jnp.concatenate([cache[:, 0], fresh[:, 0]], axis=0).astype(jnp.float32)
        values = jnp.concatenate([cache[:, 1], fresh[:, 1]], axis=0).astype(jnp.float32)
        queries = lax.dynamic_index_in_dim(query_r, index, 0, False).astype(jnp.float32)
        length = lax.dynamic_index_in_dim(lengths, index, 0, False)
        cache_ok = jnp.broadcast_to(positions[None, :] < length, (STEPS, MAXP * PAGE))
        allowed = jnp.concatenate([cache_ok, causal], axis=1)
        scores = jnp.einsum('skgd,tkd->kgst', queries, keys) * scale
        scores = jnp.where(allowed, scores, NEG_FILL)
        top = lax.optimization_barrier(jnp.max(scores, axis=-1, keepdims=True))
        weights = jnp.where(allowed, jnp.exp(scores - top), 0.0)
        total = lax.optimization_barrier(jnp.sum(weights, axis=-1))
        rounded = lax.optimization_barrier(weights.astype(jnp.bfloat16)).astype(jnp.float32)
        mixed = jnp.einsum('kgst,tkd->skgd', rounded, values)
        mixed = mixed / jnp.transpose(total, (2, 0, 1))[..., None]
        return mixed.astype(jnp.bfloat16)
    attn = lax.map(one_request, jnp.arange(REQ, dtype=jnp.int32)).reshape(ROWS, HEADS * HD)
    attended = jnp.dot(attn, w_out, preferred_element_type=jnp.float32).astype(jnp.bfloat16)
    step_ids = jnp.arange(STEPS, dtype=jnp.int32)
    new_entries = jnp.where(step_ids[None, :, None] < accepted[:, None, None], keyval.reshape(REQ, STEPS, KVW), jnp.zeros((), keyval.dtype))
    blocks = SLOTS // POOL
    dest = moves[:, 0].reshape(blocks, POOL)
    order = jnp.arange(POOL, dtype=jnp.int32)
    earlier = order[None, :] < order[:, None]
    rank = lax.optimization_barrier(jnp.sum((dest[:, :, None] == dest[:, None, :]) & earlier[None], axis=2)).astype(jnp.int32)
    block_ids = jnp.arange(blocks, dtype=jnp.int32)
    source_wide = block_ids // N_NARROW
    narrow_ids = block_ids % N_NARROW
    target = ((dest * N_NARROW + narrow_ids[:, None]) * POOL + source_wide[:, None] * CAP + rank).reshape(SLOTS)
    moved_pool = jnp.zeros_like(pool).at[target].set(pool)
    moved_req = jnp.zeros_like(page_req).at[target].set(page_req)
    moved_idx = jnp.zeros_like(page_idx).at[target].set(page_idx)
    return (attended, new_entries, moved_pool, moved_req, moved_idx)
```

```python
import functools
import math

import jax
import jax.numpy as jnp
import numpy as np
from jax import lax
from jax.experimental import pallas as pl
from jax.experimental.pallas import tpu as pltpu
from jax.sharding import PartitionSpec as P

HEADS = 32
KVH = 4
HD = 128
STEPS = 5
PAGE = 16
GROUPS = HEADS // KVH
NEG_FILL = -1e30
SCALE2 = math.log2(math.e) / math.sqrt(HD)
STAT = 16
VMEM = 56 * 1024 * 1024
NT = (((1,), (1,)), ((), ()))


def up(value, unit):
    return -(-value // unit) * unit


def permute_kernel(source_ref, pool_ref, out_ref, sem):
    def start(j, carry):
        pltpu.make_async_copy(pool_ref.at[source_ref[j]], out_ref.at[j], sem).start()
        return carry

    lax.fori_loop(0, pool_ref.shape[0], start, 0)
    pltpu.make_async_copy(pool_ref, out_ref, sem).wait()


def permute_pages(source_of, pool):
    return pl.pallas_call(
        permute_kernel,
        out_shape=jax.ShapeDtypeStruct(pool.shape, pool.dtype),
        in_specs=[
            pl.BlockSpec(memory_space=pltpu.SMEM),
            pl.BlockSpec(memory_space=pl.ANY),
        ],
        out_specs=pl.BlockSpec(memory_space=pl.ANY),
        scratch_shapes=[pltpu.SemaphoreType.DMA],
        cost_estimate=pl.CostEstimate(
            flops=0, bytes_accessed=2 * pool.size * 2, transcendentals=0
        ),
    )(source_of, pool)


def attend_kernel(
    rows,
    piece,
    query_ref,
    key_ref,
    value_ref,
    new_key_ref,
    new_value_ref,
    req_ref,
    pos_ref,
    row_ref,
    new_bias_ref,
    out_ref,
    bias_ref,
    score_ref,
    weight_ref,
):
    tokens = key_ref.shape[0]
    per_block = GROUPS // query_ref.shape[0]

    @pl.when(pl.program_id(0) == 0)
    def _():
        seen = (req_ref[...] == row_ref[:, 0:1]) & (pos_ref[...] < row_ref[:, 1:2])
        bias_ref[...] = jnp.where(seen, 0.0, NEG_FILL)

    query = jnp.concatenate(
        [
            query_ref[g // per_block, :rows, pl.ds((g % per_block) * HD, HD)].astype(jnp.float32)
            for g in range(GROUPS)
        ],
        axis=0,
    ).astype(jnp.bfloat16)
    score_ref[:, :tokens] = lax.dot_general(
        query, key_ref[...], NT, preferred_element_type=jnp.float32
    )
    score_ref[:, tokens:] = lax.dot_general(
        query, new_key_ref[...], NT, preferred_element_type=jnp.float32
    )
    together = 1 if rows % 16 == 0 else 2
    span = together * rows
    peaks, totals = [], []
    for c in range(GROUPS // together):
        block = pl.ds(c * span, span)
        old = score_ref[block, :tokens].reshape(together, rows, tokens) * SCALE2 + bias_ref[...]
        new = score_ref[block, tokens:].reshape(together, rows, -1) * SCALE2 + new_bias_ref[...]
        peak = jnp.maximum(
            jnp.max(old, axis=-1, keepdims=True), jnp.max(new, axis=-1, keepdims=True)
        )
        old = jnp.exp2(old - peak)
        new = jnp.exp2(new - peak)
        totals.append(
            (jnp.sum(old, axis=-1, keepdims=True) + jnp.sum(new, axis=-1, keepdims=True)).reshape(
                span, 1
            )
        )
        peaks.append(peak.reshape(span, 1))
        weight_ref[block, :tokens] = old.reshape(span, tokens).astype(jnp.bfloat16)
        weight_ref[block, tokens:] = new.reshape(span, -1).astype(jnp.bfloat16)
    mixed = jnp.dot(
        weight_ref[:, :tokens], value_ref[...], preferred_element_type=jnp.float32
    ) + jnp.dot(weight_ref[:, tokens:], new_value_ref[...], preferred_element_type=jnp.float32)
    peak = jnp.concatenate(peaks, axis=0)
    total = jnp.concatenate(totals, axis=0)

    def cut(value):
        return value.astype(jnp.bfloat16).astype(jnp.float32)

    peak_high = cut(peak)
    peak_mid = cut(peak - peak_high)
    peak_low = peak - peak_high - peak_mid
    total_high = cut(total)
    total_low = total - total_high
    lane = lax.broadcasted_iota(jnp.int32, (GROUPS * rows, HD), 1)
    stats = jnp.zeros((GROUPS * rows, HD), jnp.float32)
    for i, part in enumerate((peak_high, peak_mid, peak_low, total_high, total_low)):
        stats = jnp.where(lane == i, part, stats)
    pick = (
        lax.broadcasted_iota(jnp.int32, (STAT, HD), 0)
        == lax.broadcasted_iota(jnp.int32, (STAT, HD), 1)
    ).astype(jnp.bfloat16)
    fill = out_ref.shape[1] - STAT - piece
    for c in range(GROUPS * rows // piece):
        part = slice(c * piece, (c + 1) * piece)
        turned = lax.dot_general(
            pick,
            jnp.concatenate(
                [stats[part], jnp.zeros((HD - piece, HD), jnp.float32)], axis=0
            ).astype(jnp.bfloat16),
            NT,
            preferred_element_type=jnp.float32,
        )
        out_ref[c] = jnp.concatenate(
            [turned, mixed[part], jnp.zeros((fill, HD), jnp.float32)], axis=0
        ).astype(jnp.bfloat16)


def attend(queries, keyval, pool, req_tok, pos_tok, row_info, new_bias, rows, piece):
    tokens = pool.shape[0]
    extra = keyval.shape[0]
    blocks = queries.shape[0] // KVH
    pieces = GROUPS * rows // piece
    height = STAT + up(piece, 16)
    whole = lambda shape: pl.BlockSpec(shape, lambda k: (0,) * len(shape))
    return pl.pallas_call(
        functools.partial(attend_kernel, rows, piece),
        grid=(KVH,),
        out_shape=jax.ShapeDtypeStruct((KVH * pieces, height, HD), jnp.bfloat16),
        in_specs=[
            pl.BlockSpec((blocks,) + queries.shape[1:], lambda k: (k, 0, 0)),
            pl.BlockSpec((tokens, HD), lambda k: (0, k)),
            pl.BlockSpec((tokens, HD), lambda k: (0, KVH + k)),
            pl.BlockSpec((extra, HD), lambda k: (0, k)),
            pl.BlockSpec((extra, HD), lambda k: (0, KVH + k)),
            whole(req_tok.shape),
            whole(pos_tok.shape),
            whole(row_info.shape),
            whole(new_bias.shape),
        ],
        out_specs=pl.BlockSpec((pieces, height, HD), lambda k: (k, 0, 0)),
        scratch_shapes=[
            pltpu.VMEM((rows, tokens), jnp.float32),
            pltpu.VMEM((GROUPS * rows, tokens + extra), jnp.float32),
            pltpu.VMEM((GROUPS * rows, tokens + extra), jnp.bfloat16),
        ],
        compiler_params=pltpu.CompilerParams(vmem_limit_bytes=VMEM),
        cost_estimate=pl.CostEstimate(
            flops=4 * HEADS * rows * (tokens + extra) * HD,
            bytes_accessed=pool.size * 2,
            transcendentals=HEADS * rows * (tokens + extra),
        ),
    )(queries, pool, pool, keyval, keyval, req_tok, pos_tok, row_info, new_bias)


def combine_kernel(piece, parts_ref, out_ref):
    count = parts_ref.shape[0]
    peaks, totals = [], []
    for i in range(count):
        stat = parts_ref[i, :STAT, :].astype(jnp.float32)
        peaks.append(stat[0:1] + stat[1:2] + stat[2:3])
        totals.append(stat[3:4] + stat[4:5])
    peak = jnp.concatenate(peaks, axis=0)
    total = jnp.concatenate(totals, axis=0)
    lead = jnp.exp2(peak - jnp.max(peak, axis=0, keepdims=True))
    whole = jnp.sum(lead * total, axis=0, keepdims=True)
    lane = lax.broadcasted_iota(jnp.int32, whole.shape, 1)
    share = lead / jnp.where(lane < piece, whole, 1.0)
    if count % HD:
        share = jnp.concatenate(
            [share, jnp.zeros((up(count, HD) - count, HD), jnp.float32)], axis=0
        )
    share = jnp.transpose(share)
    height = parts_ref.shape[1] - STAT
    result = jnp.zeros((height, HD), jnp.float32)
    for i in range(count):
        result = result + share[:height, i : i + 1] * parts_ref[i, STAT:, :].astype(jnp.float32)
    out_ref[...] = result[:piece].astype(jnp.bfloat16)


def combine(parts, piece):
    return pl.pallas_call(
        functools.partial(combine_kernel, piece),
        out_shape=jax.ShapeDtypeStruct((piece, HD), jnp.bfloat16),
        in_specs=[pl.BlockSpec(memory_space=pltpu.VMEM)],
        out_specs=pl.BlockSpec(memory_space=pltpu.VMEM),
        compiler_params=pltpu.CompilerParams(vmem_limit_bytes=VMEM),
        cost_estimate=pl.CostEstimate(
            flops=2 * parts.size, bytes_accessed=parts.size * 2, transcendentals=0
        ),
    )(parts)


def spread(block, axis):
    count = lax.axis_size(axis)
    return lax.all_to_all(
        jnp.broadcast_to(block[None], (count,) + block.shape),
        axis,
        split_axis=0,
        concat_axis=0,
        tiled=True,
    )


def on_device(hidden, w_query, w_keyval, w_out, pool, page_req, page_idx, lengths, moves, accepted):
    wide = lax.axis_size("wide")
    narrow = lax.axis_size("narrow")
    local_rows = hidden.shape[0]
    rows = local_rows * wide
    requests = rows // STEPS
    slots = pool.shape[0]
    capacity = slots // wide
    query_cols = w_query.shape[1]

    gathered = spread(hidden, "wide").reshape(rows, -1)

    dest = moves[:, 0]
    order = jnp.arange(slots, dtype=jnp.int32)
    rank = jnp.sum((dest[:, None] == dest[None, :]) & (order[None, :] < order[:, None]), axis=1)
    target = dest * capacity + rank
    chosen = target[None, :] == order[:, None]
    source_of = jnp.sum(jnp.where(chosen, order[None, :], 0), axis=1)
    sent_req = jnp.sum(jnp.where(chosen, page_req[None, :], 0), axis=1)
    sent_idx = jnp.sum(jnp.where(chosen, page_idx[None, :], 0), axis=1)
    ordered = permute_pages(source_of, pool)

    partial = jnp.concatenate(
        [
            jnp.dot(gathered, w_query, preferred_element_type=jnp.float32),
            jnp.dot(gathered, w_keyval, preferred_element_type=jnp.float32),
        ],
        axis=1,
    )
    projected = jnp.sum(spread(partial, "narrow"), axis=0).astype(jnp.bfloat16)
    shifted = sent_idx + 1
    tags = jnp.concatenate(
        [
            sent_req.reshape(wide, 1, capacity),
            (shifted // 32).reshape(wide, 1, capacity),
            (shifted % 32).reshape(wide, 1, capacity),
        ],
        axis=2,
    ).astype(jnp.bfloat16)
    height = up(rows + 1, 16)
    packed = jnp.concatenate(
        [
            jnp.broadcast_to(projected[None], (wide,) + projected.shape),
            jnp.pad(
                tags, ((0, 0), (0, height - rows - 1), (0, projected.shape[1] - 3 * capacity))
            ),
        ],
        axis=1,
    )
    received = lax.all_to_all(packed, "wide", split_axis=0, concat_axis=0, tiled=True)

    ordered, received = lax.optimization_barrier((ordered, received))
    moved_pool = lax.all_to_all(ordered, "wide", split_axis=0, concat_axis=0, tiled=True)
    tags_in = received[:, rows, : 3 * capacity].astype(jnp.int32)
    moved_req = tags_in[:, :capacity].reshape(slots)
    moved_idx = (
        tags_in[:, capacity : 2 * capacity] * 32 + tags_in[:, 2 * capacity :] - 1
    ).reshape(slots)

    keyval = jnp.transpose(received[:, :rows, query_cols:], (1, 0, 2)).reshape(rows, -1)
    extra = up(rows, HD)
    here = (lax.axis_index("wide") == 0) & (lax.axis_index("narrow") == 0)
    row_ids = np.arange(rows)[:, None]
    col_ids = np.arange(extra)[None, :]
    causal = (row_ids // STEPS == col_ids // STEPS) & (col_ids <= row_ids) & (col_ids < rows)
    new_bias = jnp.where(jnp.asarray(causal) & here, 0.0, NEG_FILL).astype(jnp.float32)
    req_tok = jnp.broadcast_to(page_req[:, None], (slots, PAGE)).reshape(1, -1)
    pos_tok = (page_idx[:, None] * PAGE + jnp.arange(PAGE, dtype=jnp.int32)[None, :]).reshape(1, -1)
    row_info = jnp.stack(
        [
            jnp.asarray(np.arange(rows) // STEPS, jnp.int32),
            jnp.broadcast_to(lengths[:, None], (requests, STEPS)).reshape(rows),
        ],
        axis=1,
    )
    piece = HEADS * rows // (wide * narrow)
    parts = attend(
        received,
        jnp.pad(keyval, ((0, extra - rows), (0, 0))),
        pool.reshape(slots * PAGE, -1),
        req_tok,
        pos_tok,
        row_info,
        new_bias,
        rows,
        piece,
    )
    parts = lax.all_to_all(parts, ("narrow", "wide"), split_axis=0, concat_axis=0, tiled=True)
    attn = spread(combine(parts, piece), "wide").reshape(-1, rows, HD)
    attn = jnp.transpose(attn, (1, 0, 2)).reshape(rows, -1)
    sums = jnp.dot(attn, w_out, preferred_element_type=jnp.float32)
    sums = sums.reshape(narrow, rows // narrow, -1)
    attended = jnp.sum(
        lax.all_to_all(sums, "narrow", split_axis=0, concat_axis=0, tiled=True), axis=0
    ).astype(jnp.bfloat16)

    local_req = local_rows // STEPS
    first_req = lax.axis_index("wide") * local_req
    fresh = lax.dynamic_slice_in_dim(keyval.reshape(requests, STEPS, -1), first_req, local_req, 0)
    kept = lax.dynamic_slice_in_dim(accepted, first_req, local_req, 0)
    new_entries = jnp.where(
        jnp.arange(STEPS)[None, :, None] < kept[:, None, None], fresh, jnp.zeros((), jnp.bfloat16)
    )
    return (attended, new_entries, moved_pool, moved_req, moved_idx)


def solution(mesh):
    in_specs = (
        P("wide", "narrow"),
        P("narrow", "wide"),
        P("narrow", "wide"),
        P("narrow", "wide"),
        P(("wide", "narrow"), None, None),
        P(("wide", "narrow")),
        P(("wide", "narrow")),
        P(),
        P(("wide", "narrow"), None),
        P(),
    )
    out_specs = (
        P("narrow", "wide"),
        P("wide", None, None),
        P(("wide", "narrow"), None, None),
        P(("wide", "narrow")),
        P(("wide", "narrow")),
    )
    return jax.shard_map(
        on_device, mesh=mesh, in_specs=in_specs, out_specs=out_specs, check_vma=False
    )
```

```python
import functools
import math

import jax
import jax.numpy as jnp
import numpy as np
from jax import lax
from jax.experimental import pallas as pl
from jax.experimental.pallas import tpu as pltpu
from jax.sharding import PartitionSpec as P

HEADS = 32
KVH = 4
HD = 128
STEPS = 5
PAGE = 16
GROUPS = HEADS // KVH
NEG_FILL = -1e30
SCALE2 = math.log2(math.e) / math.sqrt(HD)
STAT = 16
VMEM = 56 * 1024 * 1024
NT = (((1,), (1,)), ((), ()))


def up(value, unit):
    return -(-value // unit) * unit


def permute_kernel(source_ref, place_ref, pool_ref, out_ref, *refs):
    chunk_refs, (pages_ref, in_sem, out_sem) = refs[:-3], refs[-3:]
    count = chunk_refs[0].shape[0]

    def start(j, carry):
        pltpu.make_async_copy(pool_ref.at[source_ref[j]], pages_ref.at[j], in_sem).start()
        return carry

    lax.fori_loop(0, pool_ref.shape[0], start, 0)
    pltpu.make_async_copy(pool_ref, pages_ref, in_sem).wait()
    targets = [out_ref.at[pl.ds(place_ref[0] * count, count)], *chunk_refs]
    copies = [
        pltpu.make_async_copy(pages_ref.at[pl.ds(c * count, count)], target, out_sem.at[c])
        for c, target in enumerate(targets)
    ]
    for copy in copies:
        copy.start()
    for copy in copies:
        copy.wait()


def permute_pages(source_of, place, pool, chunks):
    part = jax.ShapeDtypeStruct((pool.shape[0] // chunks,) + pool.shape[1:], pool.dtype)
    return pl.pallas_call(
        permute_kernel,
        out_shape=[jax.ShapeDtypeStruct(pool.shape, pool.dtype)] + [part] * (chunks - 1),
        in_specs=[
            pl.BlockSpec(memory_space=pltpu.SMEM),
            pl.BlockSpec(memory_space=pltpu.SMEM),
            pl.BlockSpec(memory_space=pl.ANY),
        ],
        out_specs=[pl.BlockSpec(memory_space=pl.ANY)] * chunks,
        scratch_shapes=[
            pltpu.VMEM(pool.shape, pool.dtype),
            pltpu.SemaphoreType.DMA,
            pltpu.SemaphoreType.DMA((chunks,)),
        ],
        compiler_params=pltpu.CompilerParams(vmem_limit_bytes=VMEM),
        cost_estimate=pl.CostEstimate(
            flops=0, bytes_accessed=2 * pool.size * 2, transcendentals=0
        ),
    )(source_of, place, pool)


def place_kernel(place_ref, *refs):
    in_refs, (out_ref, sem) = refs[:-3], refs[-2:]
    copies = []
    for i, chunk in enumerate(in_refs):
        depth = chunk.shape[0]
        copies.append(
            pltpu.make_async_copy(
                chunk, out_ref.at[pl.ds(place_ref[i] * depth, depth)], sem.at[i]
            )
        )
    for copy in copies:
        copy.start()
    for copy in copies:
        copy.wait()


def place_pages(place, chunks, pages):
    count = len(chunks)
    return pl.pallas_call(
        place_kernel,
        out_shape=jax.ShapeDtypeStruct(pages.shape, pages.dtype),
        in_specs=[pl.BlockSpec(memory_space=pltpu.SMEM)]
        + [pl.BlockSpec(memory_space=pltpu.VMEM)] * count
        + [pl.BlockSpec(memory_space=pl.ANY)],
        out_specs=pl.BlockSpec(memory_space=pl.ANY),
        scratch_shapes=[pltpu.SemaphoreType.DMA((count,))],
        input_output_aliases={count + 1: 0},
        compiler_params=pltpu.CompilerParams(vmem_limit_bytes=VMEM),
        cost_estimate=pl.CostEstimate(
            flops=0, bytes_accessed=4 * count * chunks[0].size, transcendentals=0
        ),
    )(place, *chunks, pages)


def attend_kernel(
    rows,
    piece,
    query_ref,
    key_ref,
    value_ref,
    new_key_ref,
    new_value_ref,
    req_ref,
    pos_ref,
    row_ref,
    new_bias_ref,
    out_ref,
    bias_ref,
    score_ref,
    weight_ref,
):
    tokens = key_ref.shape[0]
    per_block = GROUPS // query_ref.shape[0]

    @pl.when(pl.program_id(0) == 0)
    def _():
        seen = (req_ref[...] == row_ref[:, 0:1]) & (pos_ref[...] < row_ref[:, 1:2])
        bias_ref[...] = jnp.where(seen, 0.0, NEG_FILL)

    query = jnp.concatenate(
        [
            query_ref[g // per_block, :rows, pl.ds((g % per_block) * HD, HD)].astype(jnp.float32)
            for g in range(GROUPS)
        ],
        axis=0,
    ).astype(jnp.bfloat16)
    score_ref[:, :tokens] = lax.dot_general(
        query, key_ref[...], NT, preferred_element_type=jnp.float32
    )
    score_ref[:, tokens:] = lax.dot_general(
        query, new_key_ref[...], NT, preferred_element_type=jnp.float32
    )
    together = 1 if rows % 16 == 0 else 2
    span = together * rows
    peaks, totals = [], []
    for c in range(GROUPS // together):
        block = pl.ds(c * span, span)
        old = score_ref[block, :tokens].reshape(together, rows, tokens) * SCALE2 + bias_ref[...]
        new = score_ref[block, tokens:].reshape(together, rows, -1) * SCALE2 + new_bias_ref[...]
        peak = jnp.maximum(
            jnp.max(old, axis=-1, keepdims=True), jnp.max(new, axis=-1, keepdims=True)
        )
        old = jnp.exp2(old - peak)
        new = jnp.exp2(new - peak)
        totals.append(
            (jnp.sum(old, axis=-1, keepdims=True) + jnp.sum(new, axis=-1, keepdims=True)).reshape(
                span, 1
            )
        )
        peaks.append(peak.reshape(span, 1))
        weight_ref[block, :tokens] = old.reshape(span, tokens).astype(jnp.bfloat16)
        weight_ref[block, tokens:] = new.reshape(span, -1).astype(jnp.bfloat16)
    mixed = jnp.dot(
        weight_ref[:, :tokens], value_ref[...], preferred_element_type=jnp.float32
    ) + jnp.dot(weight_ref[:, tokens:], new_value_ref[...], preferred_element_type=jnp.float32)
    peak = jnp.concatenate(peaks, axis=0)
    total = jnp.concatenate(totals, axis=0)

    def cut(value):
        return value.astype(jnp.bfloat16).astype(jnp.float32)

    peak_high = cut(peak)
    peak_mid = cut(peak - peak_high)
    peak_low = peak - peak_high - peak_mid
    total_high = cut(total)
    total_low = total - total_high
    lane = lax.broadcasted_iota(jnp.int32, (GROUPS * rows, HD), 1)
    stats = jnp.zeros((GROUPS * rows, HD), jnp.float32)
    for i, part in enumerate((peak_high, peak_mid, peak_low, total_high, total_low)):
        stats = jnp.where(lane == i, part, stats)
    pick = (
        lax.broadcasted_iota(jnp.int32, (STAT, HD), 0)
        == lax.broadcasted_iota(jnp.int32, (STAT, HD), 1)
    ).astype(jnp.bfloat16)
    fill = out_ref.shape[1] - STAT - piece
    for c in range(GROUPS * rows // piece):
        part = slice(c * piece, (c + 1) * piece)
        turned = lax.dot_general(
            pick,
            jnp.concatenate(
                [stats[part], jnp.zeros((HD - piece, HD), jnp.float32)], axis=0
            ).astype(jnp.bfloat16),
            NT,
            preferred_element_type=jnp.float32,
        )
        out_ref[c] = jnp.concatenate(
            [turned, mixed[part], jnp.zeros((fill, HD), jnp.float32)], axis=0
        ).astype(jnp.bfloat16)


def attend(queries, keyval, pool, req_tok, pos_tok, row_info, new_bias, rows, piece):
    tokens = pool.shape[0]
    extra = keyval.shape[0]
    blocks = queries.shape[0] // KVH
    pieces = GROUPS * rows // piece
    height = STAT + up(piece, 16)
    whole = lambda shape: pl.BlockSpec(shape, lambda k: (0,) * len(shape))
    return pl.pallas_call(
        functools.partial(attend_kernel, rows, piece),
        grid=(KVH,),
        out_shape=jax.ShapeDtypeStruct((KVH * pieces, height, HD), jnp.bfloat16),
        in_specs=[
            pl.BlockSpec((blocks,) + queries.shape[1:], lambda k: (k, 0, 0)),
            pl.BlockSpec((tokens, HD), lambda k: (0, k)),
            pl.BlockSpec((tokens, HD), lambda k: (0, KVH + k)),
            pl.BlockSpec((extra, HD), lambda k: (0, k)),
            pl.BlockSpec((extra, HD), lambda k: (0, KVH + k)),
            whole(req_tok.shape),
            whole(pos_tok.shape),
            whole(row_info.shape),
            whole(new_bias.shape),
        ],
        out_specs=pl.BlockSpec((pieces, height, HD), lambda k: (k, 0, 0)),
        scratch_shapes=[
            pltpu.VMEM((rows, tokens), jnp.float32),
            pltpu.VMEM((GROUPS * rows, tokens + extra), jnp.float32),
            pltpu.VMEM((GROUPS * rows, tokens + extra), jnp.bfloat16),
        ],
        compiler_params=pltpu.CompilerParams(vmem_limit_bytes=VMEM),
        cost_estimate=pl.CostEstimate(
            flops=4 * HEADS * rows * (tokens + extra) * HD,
            bytes_accessed=pool.size * 2,
            transcendentals=HEADS * rows * (tokens + extra),
        ),
    )(queries, pool, pool, keyval, keyval, req_tok, pos_tok, row_info, new_bias)


def combine_kernel(piece, parts_ref, out_ref):
    count = parts_ref.shape[0]
    peaks, totals = [], []
    for i in range(count):
        stat = parts_ref[i, :STAT, :].astype(jnp.float32)
        peaks.append(stat[0:1] + stat[1:2] + stat[2:3])
        totals.append(stat[3:4] + stat[4:5])
    peak = jnp.concatenate(peaks, axis=0)
    total = jnp.concatenate(totals, axis=0)
    lead = jnp.exp2(peak - jnp.max(peak, axis=0, keepdims=True))
    whole = jnp.sum(lead * total, axis=0, keepdims=True)
    lane = lax.broadcasted_iota(jnp.int32, whole.shape, 1)
    share = lead / jnp.where(lane < piece, whole, 1.0)
    if count % HD:
        share = jnp.concatenate(
            [share, jnp.zeros((up(count, HD) - count, HD), jnp.float32)], axis=0
        )
    share = jnp.transpose(share)
    height = parts_ref.shape[1] - STAT
    result = jnp.zeros((height, HD), jnp.float32)
    for i in range(count):
        result = result + share[:height, i : i + 1] * parts_ref[i, STAT:, :].astype(jnp.float32)
    out_ref[...] = result[:piece].astype(jnp.bfloat16)


def combine(parts, piece):
    return pl.pallas_call(
        functools.partial(combine_kernel, piece),
        out_shape=jax.ShapeDtypeStruct((piece, HD), jnp.bfloat16),
        in_specs=[pl.BlockSpec(memory_space=pltpu.VMEM)],
        out_specs=pl.BlockSpec(memory_space=pltpu.VMEM),
        compiler_params=pltpu.CompilerParams(vmem_limit_bytes=VMEM),
        cost_estimate=pl.CostEstimate(
            flops=2 * parts.size, bytes_accessed=parts.size * 2, transcendentals=0
        ),
    )(parts)


def group_of(d, wide):
    return d if wide <= 8 else 1 + (d - 1) * 7 // (wide - 1)


def spread(block, axis):
    count = lax.axis_size(axis)
    return lax.all_to_all(
        jnp.broadcast_to(block[None], (count,) + block.shape),
        axis,
        split_axis=0,
        concat_axis=0,
        tiled=True,
    )


def on_device(hidden, w_query, w_keyval, w_out, pool, page_req, page_idx, lengths, moves, accepted):
    wide = lax.axis_size("wide")
    narrow = lax.axis_size("narrow")
    local_rows = hidden.shape[0]
    rows = local_rows * wide
    requests = rows // STEPS
    slots = pool.shape[0]
    capacity = slots // wide
    query_cols = w_query.shape[1]

    gathered = spread(hidden, "wide").reshape(rows, -1)

    dest = moves[:, 0]
    order = jnp.arange(slots, dtype=jnp.int32)
    rank = jnp.sum((dest[:, None] == dest[None, :]) & (order[None, :] < order[:, None]), axis=1)
    target = dest * capacity + rank
    chosen = target[None, :] == order[:, None]
    me = lax.axis_index("wide")
    moved_to = (dest ^ me) * capacity + rank
    source_of = jnp.sum(
        jnp.where(moved_to[None, :] == order[:, None], order[None, :], 0), axis=1
    )
    sent_req = jnp.sum(jnp.where(chosen, page_req[None, :], 0), axis=1)
    sent_idx = jnp.sum(jnp.where(chosen, page_idx[None, :], 0), axis=1)
    moved_pool, *chunks = permute_pages(source_of, me.reshape(1), pool, wide)
    arrived = {}

    def beside(step, value, groups):
        taken = [d for group in groups for d in range(1, wide) if group_of(d, wide) == group]
        value, *sent = lax.optimization_barrier((value, *[chunks[d - 1] for d in taken]))
        result = step(value)
        got = [
            lax.ppermute(chunk, "wide", [(w, w ^ d) for w in range(wide)])
            for chunk, d in zip(sent, taken)
        ]
        result, *got = lax.optimization_barrier((result, *got))
        arrived.update(zip(taken, got))
        return result

    def placed(pages):
        taken = sorted(arrived)
        place = jnp.stack([me ^ d for d in taken])
        pages = place_pages(place, [arrived[d] for d in taken], pages)
        arrived.clear()
        return pages

    partial = jnp.concatenate(
        [
            jnp.dot(gathered, w_query, preferred_element_type=jnp.float32),
            jnp.dot(gathered, w_keyval, preferred_element_type=jnp.float32),
        ],
        axis=1,
    )
    partial = beside(lambda value: spread(value, "narrow"), partial, (1,))
    projected = jnp.sum(partial, axis=0).astype(jnp.bfloat16)
    shifted = sent_idx + 1
    tags = jnp.concatenate(
        [
            sent_req.reshape(wide, 1, capacity),
            (shifted // 32).reshape(wide, 1, capacity),
            (shifted % 32).reshape(wide, 1, capacity),
        ],
        axis=2,
    ).astype(jnp.bfloat16)
    height = up(rows + 1, 16)
    packed = jnp.concatenate(
        [
            jnp.broadcast_to(projected[None], (wide,) + projected.shape),
            jnp.pad(
                tags, ((0, 0), (0, height - rows - 1), (0, projected.shape[1] - 3 * capacity))
            ),
        ],
        axis=1,
    )
    exchange = functools.partial(lax.all_to_all, split_axis=0, concat_axis=0, tiled=True)
    received = beside(lambda value: exchange(value, "wide"), packed, (4,))

    tags_in = received[:, rows, : 3 * capacity].astype(jnp.int32)
    moved_req = tags_in[:, :capacity].reshape(slots)
    moved_idx = (
        tags_in[:, capacity : 2 * capacity] * 32 + tags_in[:, 2 * capacity :] - 1
    ).reshape(slots)

    keyval = jnp.transpose(received[:, :rows, query_cols:], (1, 0, 2)).reshape(rows, -1)
    extra = up(rows, HD)
    here = (lax.axis_index("wide") == 0) & (lax.axis_index("narrow") == 0)
    row_ids = np.arange(rows)[:, None]
    col_ids = np.arange(extra)[None, :]
    causal = (row_ids // STEPS == col_ids // STEPS) & (col_ids <= row_ids) & (col_ids < rows)
    new_bias = jnp.where(jnp.asarray(causal) & here, 0.0, NEG_FILL).astype(jnp.float32)
    req_tok = jnp.broadcast_to(page_req[:, None], (slots, PAGE)).reshape(1, -1)
    pos_tok = (page_idx[:, None] * PAGE + jnp.arange(PAGE, dtype=jnp.int32)[None, :]).reshape(1, -1)
    row_info = jnp.stack(
        [
            jnp.asarray(np.arange(rows) // STEPS, jnp.int32),
            jnp.broadcast_to(lengths[:, None], (requests, STEPS)).reshape(rows),
        ],
        axis=1,
    )
    piece = HEADS * rows // (wide * narrow)
    new_keyval = jnp.pad(keyval, ((0, extra - rows), (0, 0)))
    tokens = pool.reshape(slots * PAGE, -1)
    parts = beside(
        lambda value: attend(
            value, new_keyval, tokens, req_tok, pos_tok, row_info, new_bias, rows, piece
        ),
        received,
        (2,),
    )
    parts = beside(lambda value: exchange(value, ("narrow", "wide")), parts, (3, 5))
    moved_pool = placed(moved_pool)
    attn = beside(lambda value: spread(value, "wide"), combine(parts, piece), (6,))
    attn = attn.reshape(-1, rows, HD)
    attn = jnp.transpose(attn, (1, 0, 2)).reshape(rows, -1)
    sums = jnp.dot(attn, w_out, preferred_element_type=jnp.float32)
    sums = sums.reshape(narrow, rows // narrow, -1)
    sums = beside(lambda value: exchange(value, "narrow"), sums, (7,))
    attended = jnp.sum(sums, axis=0).astype(jnp.bfloat16)

    moved_pool = placed(moved_pool)

    local_req = local_rows // STEPS
    first_req = lax.axis_index("wide") * local_req
    fresh = lax.dynamic_slice_in_dim(keyval.reshape(requests, STEPS, -1), first_req, local_req, 0)
    kept = lax.dynamic_slice_in_dim(accepted, first_req, local_req, 0)
    new_entries = jnp.where(
        jnp.arange(STEPS)[None, :, None] < kept[:, None, None], fresh, jnp.zeros((), jnp.bfloat16)
    )
    return (attended, new_entries, moved_pool, moved_req, moved_idx)


def solution(mesh):
    in_specs = (
        P("wide", "narrow"),
        P("narrow", "wide"),
        P("narrow", "wide"),
        P("narrow", "wide"),
        P(("wide", "narrow"), None, None),
        P(("wide", "narrow")),
        P(("wide", "narrow")),
        P(),
        P(("wide", "narrow"), None),
        P(),
    )
    out_specs = (
        P("narrow", "wide"),
        P("wide", None, None),
        P(("wide", "narrow"), None, None),
        P(("wide", "narrow")),
        P(("wide", "narrow")),
    )
    return jax.shard_map(
        on_device, mesh=mesh, in_specs=in_specs, out_specs=out_specs, check_vma=False
    )
```

```python
import functools
import math

import jax
import jax.numpy as jnp
import numpy as np
from jax import lax
from jax.experimental import pallas as pl
from jax.experimental.pallas import tpu as pltpu
from jax.sharding import PartitionSpec as P

HEADS = 32
KVH = 4
HD = 128
STEPS = 5
PAGE = 16
GROUPS = HEADS // KVH
NEG_FILL = -1e30
SCALE2 = math.log2(math.e) / math.sqrt(HD)
STAT = 16
MIB = 1024 * 1024
NT = (((1,), (1,)), ((), ()))


def up(value, unit):
    return -(-value // unit) * unit


def permute_kernel(source_ref, place_ref, pool_ref, out_ref, *refs):
    chunk_refs, (pages_ref, in_sem, out_sem) = refs[:-3], refs[-3:]
    count = chunk_refs[0].shape[0]

    def start(j, carry):
        pltpu.make_async_copy(pool_ref.at[source_ref[j]], pages_ref.at[j], in_sem).start()
        return carry

    lax.fori_loop(0, pool_ref.shape[0], start, 0)
    pltpu.make_async_copy(pool_ref, pages_ref, in_sem).wait()
    targets = [out_ref.at[pl.ds(place_ref[0] * count, count)], *chunk_refs]
    copies = [
        pltpu.make_async_copy(pages_ref.at[pl.ds(c * count, count)], target, out_sem.at[c])
        for c, target in enumerate(targets)
    ]
    for copy in copies:
        copy.start()
    for copy in copies:
        copy.wait()


def permute_pages(source_of, place, pool, chunks):
    part = jax.ShapeDtypeStruct((pool.shape[0] // chunks,) + pool.shape[1:], pool.dtype)
    return pl.pallas_call(
        permute_kernel,
        out_shape=[jax.ShapeDtypeStruct(pool.shape, pool.dtype)] + [part] * (chunks - 1),
        in_specs=[
            pl.BlockSpec(memory_space=pltpu.SMEM),
            pl.BlockSpec(memory_space=pltpu.SMEM),
            pl.BlockSpec(memory_space=pl.ANY),
        ],
        out_specs=[pl.BlockSpec(memory_space=pl.ANY)] * chunks,
        scratch_shapes=[
            pltpu.VMEM(pool.shape, pool.dtype),
            pltpu.SemaphoreType.DMA,
            pltpu.SemaphoreType.DMA((chunks,)),
        ],
        compiler_params=pltpu.CompilerParams(vmem_limit_bytes=2 * pool.size + 2 * MIB),
        cost_estimate=pl.CostEstimate(
            flops=0, bytes_accessed=2 * pool.size * 2, transcendentals=0
        ),
    )(source_of, place, pool)


def place_kernel(place_ref, *refs):
    in_refs, (out_ref, sem) = refs[:-3], refs[-2:]
    copies = []
    for i, chunk in enumerate(in_refs):
        depth = chunk.shape[0]
        copies.append(
            pltpu.make_async_copy(
                chunk, out_ref.at[pl.ds(place_ref[i] * depth, depth)], sem.at[i]
            )
        )
    for copy in copies:
        copy.start()
    for copy in copies:
        copy.wait()


def place_pages(place, chunks, pages):
    count = len(chunks)
    return pl.pallas_call(
        place_kernel,
        out_shape=jax.ShapeDtypeStruct(pages.shape, pages.dtype),
        in_specs=[pl.BlockSpec(memory_space=pltpu.SMEM)]
        + [pl.BlockSpec(memory_space=pltpu.VMEM)] * count
        + [pl.BlockSpec(memory_space=pl.ANY)],
        out_specs=pl.BlockSpec(memory_space=pl.ANY),
        scratch_shapes=[pltpu.SemaphoreType.DMA((count,))],
        input_output_aliases={count + 1: 0},
        compiler_params=pltpu.CompilerParams(vmem_limit_bytes=2 * count * chunks[0].size + 2 * MIB),
        cost_estimate=pl.CostEstimate(
            flops=0, bytes_accessed=4 * count * chunks[0].size, transcendentals=0
        ),
    )(place, *chunks, pages)


def cut(value):
    return value.astype(jnp.bfloat16).astype(jnp.float32)


def split_stats(peak, total):
    high = cut(peak)
    mid = cut(peak - high)
    return high, mid, peak - high - mid, cut(total), total - cut(total)


def attend_kernel(
    rows,
    piece,
    query_ref,
    key_ref,
    value_ref,
    new_key_ref,
    new_value_ref,
    req_ref,
    pos_ref,
    row_ref,
    new_bias_ref,
    out_ref,
    bias_ref,
    score_ref,
    weight_ref,
):
    tokens = key_ref.shape[0]

    @pl.when(pl.program_id(0) == 0)
    def _():
        seen = (req_ref[...] == row_ref[:, 0:1]) & (pos_ref[...] < row_ref[:, 1:2])
        bias_ref[...] = jnp.where(seen, 0.0, NEG_FILL)

    query = query_ref[0]
    score_ref[:, :tokens] = lax.dot_general(
        query, key_ref[...], NT, preferred_element_type=jnp.float32
    )
    score_ref[:, tokens:] = lax.dot_general(
        query, new_key_ref[...], NT, preferred_element_type=jnp.float32
    )
    together = 1 if rows % 16 == 0 else 2
    span = together * rows
    peaks, totals = [], []
    for c in range(GROUPS // together):
        block = pl.ds(c * span, span)
        old = score_ref[block, :tokens].reshape(together, rows, tokens) * SCALE2 + bias_ref[...]
        new = score_ref[block, tokens:].reshape(together, rows, -1) * SCALE2 + new_bias_ref[...]
        peak = jnp.maximum(
            jnp.max(old, axis=-1, keepdims=True), jnp.max(new, axis=-1, keepdims=True)
        )
        old = jnp.exp2(old - peak)
        new = jnp.exp2(new - peak)
        totals.append(
            (jnp.sum(old, axis=-1, keepdims=True) + jnp.sum(new, axis=-1, keepdims=True)).reshape(
                span, 1
            )
        )
        peaks.append(peak.reshape(span, 1))
        weight_ref[block, :tokens] = old.reshape(span, tokens).astype(jnp.bfloat16)
        weight_ref[block, tokens:] = new.reshape(span, -1).astype(jnp.bfloat16)
    mixed = jnp.dot(
        weight_ref[:, :tokens], value_ref[...], preferred_element_type=jnp.float32
    ) + jnp.dot(weight_ref[:, tokens:], new_value_ref[...], preferred_element_type=jnp.float32)
    peak = jnp.concatenate(peaks, axis=0)
    total = jnp.concatenate(totals, axis=0)

    lane = lax.broadcasted_iota(jnp.int32, (GROUPS * rows, HD), 1)
    stats = jnp.zeros((GROUPS * rows, HD), jnp.float32)
    for i, part in enumerate(split_stats(peak, total)):
        stats = jnp.where(lane == i, part, stats)
    pick = (
        lax.broadcasted_iota(jnp.int32, (STAT, HD), 0)
        == lax.broadcasted_iota(jnp.int32, (STAT, HD), 1)
    ).astype(jnp.bfloat16)
    fill = out_ref.shape[1] - STAT - piece
    for c in range(GROUPS * rows // piece):
        part = slice(c * piece, (c + 1) * piece)
        turned = lax.dot_general(
            pick,
            jnp.concatenate(
                [stats[part], jnp.zeros((HD - piece, HD), jnp.float32)], axis=0
            ).astype(jnp.bfloat16),
            NT,
            preferred_element_type=jnp.float32,
        )
        out_ref[c] = jnp.concatenate(
            [turned, mixed[part], jnp.zeros((fill, HD), jnp.float32)], axis=0
        ).astype(jnp.bfloat16)


def attend(queries, keyval, pool, req_tok, pos_tok, row_info, new_bias, rows, piece):
    tokens = pool.shape[0]
    extra = keyval.shape[0]
    pieces = GROUPS * rows // piece
    height = STAT + up(piece, 16)
    whole = lambda shape: pl.BlockSpec(shape, lambda k: (0,) * len(shape))
    return pl.pallas_call(
        functools.partial(attend_kernel, rows, piece),
        grid=(KVH,),
        out_shape=jax.ShapeDtypeStruct((KVH * pieces, height, HD), jnp.bfloat16),
        in_specs=[
            pl.BlockSpec((1,) + queries.shape[1:], lambda k: (k, 0, 0)),
            pl.BlockSpec((tokens, HD), lambda k: (0, k)),
            pl.BlockSpec((tokens, HD), lambda k: (0, KVH + k)),
            pl.BlockSpec((extra, HD), lambda k: (0, k)),
            pl.BlockSpec((extra, HD), lambda k: (0, KVH + k)),
            whole(req_tok.shape),
            whole(pos_tok.shape),
            whole(row_info.shape),
            whole(new_bias.shape),
        ],
        out_specs=pl.BlockSpec((pieces, height, HD), lambda k: (k, 0, 0)),
        scratch_shapes=[
            pltpu.VMEM((rows, tokens), jnp.float32),
            pltpu.VMEM((GROUPS * rows, tokens + extra), jnp.float32),
            pltpu.VMEM((GROUPS * rows, tokens + extra), jnp.bfloat16),
        ],
        compiler_params=pltpu.CompilerParams(vmem_limit_bytes=32 * MIB),
        cost_estimate=pl.CostEstimate(
            flops=4 * HEADS * rows * (tokens + extra) * HD,
            bytes_accessed=pool.size * 2,
            transcendentals=HEADS * rows * (tokens + extra),
        ),
    )(queries, pool, pool, keyval, keyval, req_tok, pos_tok, row_info, new_bias)


def combine_kernel(piece, last, parts_ref, out_ref):
    count, groups, height = parts_ref.shape[:3]
    peaks, totals = [], []
    for i in range(count):
        for j in range(groups):
            stat = parts_ref[i, j, :STAT, :].astype(jnp.float32)
            peaks.append(stat[0:1] + stat[1:2] + stat[2:3])
            totals.append(stat[3:4] + stat[4:5])
    peak = jnp.concatenate(peaks, axis=0).reshape(count, groups, HD)
    total = jnp.concatenate(totals, axis=0).reshape(count, groups, HD)
    top = jnp.max(peak, axis=0)
    lead = jnp.exp2(peak - top[None])
    whole = jnp.sum(lead * total, axis=0)
    if last:
        lane = lax.broadcasted_iota(jnp.int32, whole.shape, 1)
        lead = lead / jnp.where(lane < piece, whole, 1.0)[None]
    lead = lead.reshape(count * groups, HD)
    if (count * groups) % HD:
        fill = up(count * groups, HD) - count * groups
        lead = jnp.concatenate([lead, jnp.zeros((fill, HD), jnp.float32)], axis=0)
    lead = jnp.transpose(lead)
    rows = height - STAT
    for j in range(groups):
        result = jnp.zeros((rows, HD), jnp.float32)
        for i in range(count):
            c = i * groups + j
            result = result + lead[:rows, c : c + 1] * parts_ref[i, j, STAT:, :].astype(jnp.float32)
        if last:
            out_ref[...] = result[:piece].astype(jnp.bfloat16)
        else:
            stats = split_stats(top[j : j + 1], whole[j : j + 1])
            rest = jnp.zeros((STAT - len(stats), HD), jnp.float32)
            out_ref[j] = jnp.concatenate([*stats, rest, result], axis=0).astype(jnp.bfloat16)


def combine(parts, piece, last):
    groups, height = parts.shape[1:3]
    shape = (piece, HD) if last else (groups, height, HD)
    return pl.pallas_call(
        functools.partial(combine_kernel, piece, last),
        out_shape=jax.ShapeDtypeStruct(shape, jnp.bfloat16),
        in_specs=[pl.BlockSpec(memory_space=pltpu.VMEM)],
        out_specs=pl.BlockSpec(memory_space=pltpu.VMEM),
        compiler_params=pltpu.CompilerParams(vmem_limit_bytes=8 * MIB),
        cost_estimate=pl.CostEstimate(
            flops=2 * parts.size, bytes_accessed=parts.size * 2, transcendentals=0
        ),
    )(parts)


def group_of(d, wide):
    return d if wide <= 8 else 1 + (d - 1) * 7 // (wide - 1)


def spread(block, axis):
    count = lax.axis_size(axis)
    return lax.all_to_all(
        jnp.broadcast_to(block[None], (count,) + block.shape),
        axis,
        split_axis=0,
        concat_axis=0,
        tiled=True,
    )


def on_device(hidden, w_query, w_keyval, w_out, pool, page_req, page_idx, lengths, moves, accepted):
    wide = lax.axis_size("wide")
    narrow = lax.axis_size("narrow")
    local_rows = hidden.shape[0]
    rows = local_rows * wide
    requests = rows // STEPS
    slots = pool.shape[0]
    capacity = slots // wide

    gathered = spread(hidden, "wide").reshape(rows, -1)

    dest = moves[:, 0]
    order = jnp.arange(slots, dtype=jnp.int32)
    rank = jnp.sum((dest[:, None] == dest[None, :]) & (order[None, :] < order[:, None]), axis=1)
    target = dest * capacity + rank
    chosen = target[None, :] == order[:, None]
    me = lax.axis_index("wide")
    moved_to = (dest ^ me) * capacity + rank
    source_of = jnp.sum(
        jnp.where(moved_to[None, :] == order[:, None], order[None, :], 0), axis=1
    )
    sent_req = jnp.sum(jnp.where(chosen, page_req[None, :], 0), axis=1)
    sent_idx = jnp.sum(jnp.where(chosen, page_idx[None, :], 0), axis=1)
    moved_pool, *chunks = permute_pages(source_of, me.reshape(1), pool, wide)
    arrived = {}

    exchange = functools.partial(lax.all_to_all, split_axis=0, concat_axis=0, tiled=True)
    flying = {}

    def beside(step, value, begin=(), end=()):
        taken = [d for d in range(1, wide) if group_of(d, wide) in begin]
        value, *sent = lax.optimization_barrier((value, *[chunks[d - 1] for d in taken]))
        result = step(value)
        for d, chunk in zip(taken, sent):
            flying[d] = lax.ppermute(chunk, "wide", [(w, w ^ d) for w in range(wide)])
        taken = [d for d in range(1, wide) if group_of(d, wide) in end]
        result, *got = lax.optimization_barrier((result, *[flying[d] for d in taken]))
        arrived.update(zip(taken, got))
        return result

    def placed(pages):
        taken = sorted(arrived)
        place = jnp.stack([me ^ d for d in taken])
        pages = place_pages(place, [arrived[d] for d in taken], pages)
        arrived.clear()
        return pages

    query_part = jnp.dot(gathered, w_query, preferred_element_type=jnp.float32)
    keyval_part = jnp.dot(gathered, w_keyval, preferred_element_type=jnp.float32)
    own_cols = query_part.shape[1] // narrow
    query_part = jnp.transpose(query_part.reshape(rows, narrow, own_cols), (1, 0, 2))
    partial = jnp.concatenate(
        [query_part, jnp.broadcast_to(keyval_part[None], (narrow,) + keyval_part.shape)], axis=2
    )
    partial = beside(lambda value: exchange(value, "narrow"), partial, (2, 6), (2, 6))
    projected = jnp.sum(partial, axis=0).astype(jnp.bfloat16)
    shifted = sent_idx + 1
    tags = jnp.concatenate(
        [
            sent_req.reshape(wide, 1, capacity),
            (shifted // 32).reshape(wide, 1, capacity),
            (shifted % 32).reshape(wide, 1, capacity),
        ],
        axis=2,
    ).astype(jnp.bfloat16)
    height = up(rows + 1, 8)
    packed = jnp.concatenate(
        [
            jnp.broadcast_to(projected[None], (wide,) + projected.shape),
            jnp.pad(
                tags, ((0, 0), (0, height - rows - 1), (0, projected.shape[1] - 3 * capacity))
            ),
        ],
        axis=1,
    )
    received = beside(lambda value: exchange(value, "wide"), packed, (1,), (1,))
    queries = beside(
        lambda value: spread(value, "narrow"), received[:, :rows, :own_cols], (3, 7), (3, 7)
    )
    if own_cols == HD:
        queries = jnp.transpose(queries, (1, 0, 2, 3))
    else:
        queries = jnp.transpose(queries, (2, 1, 0, 3)).reshape(rows, HEADS, HD)
        queries = jnp.transpose(queries, (1, 0, 2))
    queries = queries.reshape(KVH, GROUPS * rows, HD)
    tags_in = received[:, rows, : 3 * capacity].astype(jnp.int32)
    moved_req = tags_in[:, :capacity].reshape(slots)
    moved_idx = (
        tags_in[:, capacity : 2 * capacity] * 32 + tags_in[:, 2 * capacity :] - 1
    ).reshape(slots)

    keyval = jnp.transpose(received[:, :rows, own_cols:], (1, 0, 2)).reshape(rows, -1)
    extra = up(rows, HD)
    here = (lax.axis_index("wide") == 0) & (lax.axis_index("narrow") == 0)
    row_ids = np.arange(rows)[:, None]
    col_ids = np.arange(extra)[None, :]
    causal = (row_ids // STEPS == col_ids // STEPS) & (col_ids <= row_ids) & (col_ids < rows)
    new_bias = jnp.where(jnp.asarray(causal) & here, 0.0, NEG_FILL).astype(jnp.float32)
    req_tok = jnp.broadcast_to(page_req[:, None], (slots, PAGE)).reshape(1, -1)
    pos_tok = (page_idx[:, None] * PAGE + jnp.arange(PAGE, dtype=jnp.int32)[None, :]).reshape(1, -1)
    row_info = jnp.stack(
        [
            jnp.asarray(np.arange(rows) // STEPS, jnp.int32),
            jnp.broadcast_to(lengths[:, None], (requests, STEPS)).reshape(rows),
        ],
        axis=1,
    )
    piece = HEADS * rows // (wide * narrow)
    new_keyval = jnp.pad(keyval, ((0, extra - rows), (0, 0)))
    tokens = pool.reshape(slots * PAGE, -1)
    parts = beside(
        lambda value: attend(
            value, new_keyval, tokens, req_tok, pos_tok, row_info, new_bias, rows, piece
        ),
        queries,
        (4,),
    )
    moved_pool = placed(moved_pool)
    parts = beside(lambda value: exchange(value, "narrow"), parts, (), (4,))
    parts = combine(parts.reshape((narrow, wide) + parts.shape[1:]), piece, False)
    parts = beside(lambda value: exchange(value, "wide"), parts, (5,))
    attn = combine(parts[:, None], piece, True)
    attn = beside(lambda value: spread(value, "wide"), attn, (), (5,))
    attn = jnp.transpose(attn.reshape(-1, rows, HD), (1, 0, 2)).reshape(rows, -1)
    sums = jnp.dot(attn, w_out, preferred_element_type=jnp.float32)
    sums = sums.reshape(narrow, rows // narrow, -1)
    sums = exchange(sums, "narrow")
    attended = jnp.sum(sums, axis=0).astype(jnp.bfloat16)

    moved_pool = placed(moved_pool)

    local_req = local_rows // STEPS
    first_req = lax.axis_index("wide") * local_req
    fresh = lax.dynamic_slice_in_dim(keyval.reshape(requests, STEPS, -1), first_req, local_req, 0)
    kept = lax.dynamic_slice_in_dim(accepted, first_req, local_req, 0)
    new_entries = jnp.where(
        jnp.arange(STEPS)[None, :, None] < kept[:, None, None], fresh, jnp.zeros((), jnp.bfloat16)
    )
    return (attended, new_entries, moved_pool, moved_req, moved_idx)


def solution(mesh):
    in_specs = (
        P("wide", "narrow"),
        P("narrow", "wide"),
        P("narrow", "wide"),
        P("narrow", "wide"),
        P(("wide", "narrow"), None, None),
        P(("wide", "narrow")),
        P(("wide", "narrow")),
        P(),
        P(("wide", "narrow"), None),
        P(),
    )
    out_specs = (
        P("narrow", "wide"),
        P("wide", None, None),
        P(("wide", "narrow"), None, None),
        P(("wide", "narrow")),
        P(("wide", "narrow")),
    )
    return jax.shard_map(
        on_device, mesh=mesh, in_specs=in_specs, out_specs=out_specs, check_vma=False
    )
```

```python
import functools
import math

import jax
import jax.numpy as jnp
import numpy as np
from jax import lax
from jax.experimental import pallas as pl
from jax.experimental.pallas import tpu as pltpu
from jax.sharding import PartitionSpec as P

HEADS = 32
KVH = 4
HD = 128
STEPS = 5
PAGE = 16
GROUPS = HEADS // KVH
NEG_FILL = -1e30
SCALE2 = math.log2(math.e) / math.sqrt(HD)
STAT = 16
MIB = 1024 * 1024
NT = (((1,), (1,)), ((), ()))


def up(value, unit):
    return -(-value // unit) * unit


def permute_kernel(source_ref, place_ref, pool_ref, out_ref, *refs):
    chunk_refs, (pages_ref, in_sem, out_sem) = refs[:-3], refs[-3:]
    count = chunk_refs[0].shape[0]

    def start(j, carry):
        pltpu.make_async_copy(pool_ref.at[source_ref[j]], pages_ref.at[j], in_sem.at[j // count]).start()
        return carry

    lax.fori_loop(0, pool_ref.shape[0], start, 0)
    targets = [out_ref.at[pl.ds(place_ref[0] * count, count)], *chunk_refs]
    copies = []
    for c, target in enumerate(targets):
        held = pages_ref.at[pl.ds(c * count, count)]
        pltpu.make_async_copy(pool_ref.at[pl.ds(0, count)], held, in_sem.at[c]).wait()
        copies.append(pltpu.make_async_copy(held, target, out_sem.at[c]))
        copies[-1].start()
    for copy in copies:
        copy.wait()


def permute_pages(source_of, place, pool, chunks):
    part = jax.ShapeDtypeStruct((pool.shape[0] // chunks,) + pool.shape[1:], pool.dtype)
    return pl.pallas_call(
        permute_kernel,
        out_shape=[jax.ShapeDtypeStruct(pool.shape, pool.dtype)] + [part] * (chunks - 1),
        in_specs=[
            pl.BlockSpec(memory_space=pltpu.SMEM),
            pl.BlockSpec(memory_space=pltpu.SMEM),
            pl.BlockSpec(memory_space=pltpu.HBM),
        ],
        out_specs=[pl.BlockSpec(memory_space=pltpu.HBM)] * chunks,
        scratch_shapes=[
            pltpu.VMEM(pool.shape, pool.dtype),
            pltpu.SemaphoreType.DMA((chunks,)),
            pltpu.SemaphoreType.DMA((chunks,)),
        ],
        compiler_params=pltpu.CompilerParams(vmem_limit_bytes=2 * pool.size + 2 * MIB),
        cost_estimate=pl.CostEstimate(
            flops=0, bytes_accessed=2 * pool.size * 2, transcendentals=0
        ),
    )(source_of, place, pool)


def place_kernel(place_ref, *refs):
    in_refs, (out_ref, sem) = refs[:-3], refs[-2:]
    copies = []
    for i, chunk in enumerate(in_refs):
        depth = chunk.shape[0]
        copies.append(
            pltpu.make_async_copy(
                chunk, out_ref.at[pl.ds(place_ref[i] * depth, depth)], sem.at[i]
            )
        )
    for copy in copies:
        copy.start()
    for copy in copies:
        copy.wait()


def place_pages(place, chunks, pages):
    count = len(chunks)
    return pl.pallas_call(
        place_kernel,
        out_shape=jax.ShapeDtypeStruct(pages.shape, pages.dtype),
        in_specs=[pl.BlockSpec(memory_space=pltpu.SMEM)]
        + [pl.BlockSpec(memory_space=pltpu.VMEM)] * count
        + [pl.BlockSpec(memory_space=pl.ANY)],
        out_specs=pl.BlockSpec(memory_space=pl.ANY),
        scratch_shapes=[pltpu.SemaphoreType.DMA((count,))],
        input_output_aliases={count + 1: 0},
        compiler_params=pltpu.CompilerParams(vmem_limit_bytes=2 * count * chunks[0].size + 2 * MIB),
        cost_estimate=pl.CostEstimate(
            flops=0, bytes_accessed=4 * count * chunks[0].size, transcendentals=0
        ),
    )(place, *chunks, pages)


def cut(value):
    return value.astype(jnp.bfloat16).astype(jnp.float32)


def split_stats(peak, total):
    high = cut(peak)
    mid = cut(peak - high)
    return high, mid, peak - high - mid, cut(total), total - cut(total)


def attend_kernel(
    rows,
    piece,
    query_ref,
    key_ref,
    value_ref,
    new_key_ref,
    new_value_ref,
    req_ref,
    pos_ref,
    row_ref,
    new_bias_ref,
    out_ref,
    bias_ref,
    score_ref,
    weight_ref,
):
    tokens = key_ref.shape[0]

    @pl.when(pl.program_id(0) == 0)
    def _():
        seen = (req_ref[...] == row_ref[:, 0:1]) & (pos_ref[...] < row_ref[:, 1:2])
        bias_ref[...] = jnp.where(seen, 0.0, NEG_FILL)

    query = query_ref[0]
    score_ref[:, :tokens] = lax.dot_general(
        query, key_ref[...], NT, preferred_element_type=jnp.float32
    )
    score_ref[:, tokens:] = lax.dot_general(
        query, new_key_ref[...], NT, preferred_element_type=jnp.float32
    )
    together = 1 if rows % 16 == 0 else 2
    span = together * rows
    peaks, totals = [], []
    for c in range(GROUPS // together):
        block = pl.ds(c * span, span)
        old = score_ref[block, :tokens].reshape(together, rows, tokens) * SCALE2 + bias_ref[...]
        new = score_ref[block, tokens:].reshape(together, rows, -1) * SCALE2 + new_bias_ref[...]
        peak = jnp.maximum(
            jnp.max(old, axis=-1, keepdims=True), jnp.max(new, axis=-1, keepdims=True)
        )
        old = jnp.exp2(old - peak)
        new = jnp.exp2(new - peak)
        totals.append(
            (jnp.sum(old, axis=-1, keepdims=True) + jnp.sum(new, axis=-1, keepdims=True)).reshape(
                span, 1
            )
        )
        peaks.append(peak.reshape(span, 1))
        weight_ref[block, :tokens] = old.reshape(span, tokens).astype(jnp.bfloat16)
        weight_ref[block, tokens:] = new.reshape(span, -1).astype(jnp.bfloat16)
    mixed = jnp.dot(
        weight_ref[:, :tokens], value_ref[...], preferred_element_type=jnp.float32
    ) + jnp.dot(weight_ref[:, tokens:], new_value_ref[...], preferred_element_type=jnp.float32)
    peak = jnp.concatenate(peaks, axis=0)
    total = jnp.concatenate(totals, axis=0)

    lane = lax.broadcasted_iota(jnp.int32, (GROUPS * rows, HD), 1)
    stats = jnp.zeros((GROUPS * rows, HD), jnp.float32)
    for i, part in enumerate(split_stats(peak, total)):
        stats = jnp.where(lane == i, part, stats)
    pick = (
        lax.broadcasted_iota(jnp.int32, (STAT, HD), 0)
        == lax.broadcasted_iota(jnp.int32, (STAT, HD), 1)
    ).astype(jnp.bfloat16)
    fill = out_ref.shape[1] - STAT - piece
    for c in range(GROUPS * rows // piece):
        part = slice(c * piece, (c + 1) * piece)
        turned = lax.dot_general(
            pick,
            jnp.concatenate(
                [stats[part], jnp.zeros((HD - piece, HD), jnp.float32)], axis=0
            ).astype(jnp.bfloat16),
            NT,
            preferred_element_type=jnp.float32,
        )
        out_ref[c] = jnp.concatenate(
            [turned, mixed[part], jnp.zeros((fill, HD), jnp.float32)], axis=0
        ).astype(jnp.bfloat16)


def attend(queries, keyval, pool, req_tok, pos_tok, row_info, new_bias, rows, piece):
    tokens = pool.shape[0]
    extra = keyval.shape[0]
    pieces = GROUPS * rows // piece
    height = STAT + up(piece, 16)
    whole = lambda shape: pl.BlockSpec(shape, lambda k: (0,) * len(shape))
    return pl.pallas_call(
        functools.partial(attend_kernel, rows, piece),
        grid=(KVH,),
        out_shape=jax.ShapeDtypeStruct((KVH * pieces, height, HD), jnp.bfloat16),
        in_specs=[
            pl.BlockSpec((1,) + queries.shape[1:], lambda k: (k, 0, 0)),
            pl.BlockSpec((tokens, HD), lambda k: (0, k)),
            pl.BlockSpec((tokens, HD), lambda k: (0, KVH + k)),
            pl.BlockSpec((extra, HD), lambda k: (0, k)),
            pl.BlockSpec((extra, HD), lambda k: (0, KVH + k)),
            whole(req_tok.shape),
            whole(pos_tok.shape),
            whole(row_info.shape),
            whole(new_bias.shape),
        ],
        out_specs=pl.BlockSpec((pieces, height, HD), lambda k: (k, 0, 0)),
        scratch_shapes=[
            pltpu.VMEM((rows, tokens), jnp.float32),
            pltpu.VMEM((GROUPS * rows, tokens + extra), jnp.float32),
            pltpu.VMEM((GROUPS * rows, tokens + extra), jnp.bfloat16),
        ],
        compiler_params=pltpu.CompilerParams(vmem_limit_bytes=32 * MIB),
        cost_estimate=pl.CostEstimate(
            flops=4 * HEADS * rows * (tokens + extra) * HD,
            bytes_accessed=pool.size * 2,
            transcendentals=HEADS * rows * (tokens + extra),
        ),
    )(queries, pool, pool, keyval, keyval, req_tok, pos_tok, row_info, new_bias)


def combine_kernel(piece, last, parts_ref, out_ref):
    count, groups, height = parts_ref.shape[:3]
    peaks, totals = [], []
    for i in range(count):
        for j in range(groups):
            stat = parts_ref[i, j, :STAT, :].astype(jnp.float32)
            peaks.append(stat[0:1] + stat[1:2] + stat[2:3])
            totals.append(stat[3:4] + stat[4:5])
    peak = jnp.concatenate(peaks, axis=0).reshape(count, groups, HD)
    total = jnp.concatenate(totals, axis=0).reshape(count, groups, HD)
    top = jnp.max(peak, axis=0)
    lead = jnp.exp2(peak - top[None])
    whole = jnp.sum(lead * total, axis=0)
    if last:
        lane = lax.broadcasted_iota(jnp.int32, whole.shape, 1)
        lead = lead / jnp.where(lane < piece, whole, 1.0)[None]
    lead = lead.reshape(count * groups, HD)
    if (count * groups) % HD:
        fill = up(count * groups, HD) - count * groups
        lead = jnp.concatenate([lead, jnp.zeros((fill, HD), jnp.float32)], axis=0)
    lead = jnp.transpose(lead)
    rows = height - STAT
    for j in range(groups):
        result = jnp.zeros((rows, HD), jnp.float32)
        for i in range(count):
            c = i * groups + j
            result = result + lead[:rows, c : c + 1] * parts_ref[i, j, STAT:, :].astype(jnp.float32)
        if last:
            out_ref[...] = result[:piece].astype(jnp.bfloat16)
        else:
            stats = split_stats(top[j : j + 1], whole[j : j + 1])
            rest = jnp.zeros((STAT - len(stats), HD), jnp.float32)
            out_ref[j] = jnp.concatenate([*stats, rest, result], axis=0).astype(jnp.bfloat16)


def combine(parts, piece, last):
    groups, height = parts.shape[1:3]
    shape = (piece, HD) if last else (groups, height, HD)
    return pl.pallas_call(
        functools.partial(combine_kernel, piece, last),
        out_shape=jax.ShapeDtypeStruct(shape, jnp.bfloat16),
        in_specs=[pl.BlockSpec(memory_space=pltpu.VMEM)],
        out_specs=pl.BlockSpec(memory_space=pltpu.VMEM),
        compiler_params=pltpu.CompilerParams(vmem_limit_bytes=8 * MIB),
        cost_estimate=pl.CostEstimate(
            flops=2 * parts.size, bytes_accessed=parts.size * 2, transcendentals=0
        ),
    )(parts)


def group_of(d, wide):
    return d if wide <= 8 else 1 + (d - 1) * 7 // (wide - 1)


def spread(block, axis):
    count = lax.axis_size(axis)
    return lax.all_to_all(
        jnp.broadcast_to(block[None], (count,) + block.shape),
        axis,
        split_axis=0,
        concat_axis=0,
        tiled=True,
    )


def on_device(hidden, w_query, w_keyval, w_out, pool, page_req, page_idx, lengths, moves, accepted):
    wide = lax.axis_size("wide")
    narrow = lax.axis_size("narrow")
    local_rows = hidden.shape[0]
    rows = local_rows * wide
    requests = rows // STEPS
    slots = pool.shape[0]
    capacity = slots // wide

    gathered = spread(hidden, "wide").reshape(rows, -1)

    dest = moves[:, 0]
    order = jnp.arange(slots, dtype=jnp.int32)
    rank = jnp.sum((dest[:, None] == dest[None, :]) & (order[None, :] < order[:, None]), axis=1)
    target = dest * capacity + rank
    chosen = target[None, :] == order[:, None]
    me = lax.axis_index("wide")
    moved_to = (dest ^ me) * capacity + rank
    source_of = jnp.sum(
        jnp.where(moved_to[None, :] == order[:, None], order[None, :], 0), axis=1
    )
    sent_req = jnp.sum(jnp.where(chosen, page_req[None, :], 0), axis=1)
    sent_idx = jnp.sum(jnp.where(chosen, page_idx[None, :], 0), axis=1)
    moved_pool, *chunks = permute_pages(source_of, me.reshape(1), pool, wide)
    arrived = {}

    exchange = functools.partial(lax.all_to_all, split_axis=0, concat_axis=0, tiled=True)
    flying = {}

    def members(groups):
        return [d for group in groups for d in range(1, wide) if group_of(d, wide) == group]

    def launch(values, *groups):
        taken = members(groups)
        values, sent = lax.optimization_barrier((values, [chunks[d - 1] for d in taken]))
        for d, chunk in zip(taken, sent):
            flying[d] = lax.ppermute(chunk, "wide", [(w, w ^ d) for w in range(wide)])
        return values

    def land(values, *groups):
        taken = members(groups)
        values, got = lax.optimization_barrier((values, [flying[d] for d in taken]))
        arrived.update(zip(taken, got))
        return values

    def placed(pages):
        taken = sorted(arrived)
        place = jnp.stack([me ^ d for d in taken])
        pages = place_pages(place, [arrived[d] for d in taken], pages)
        arrived.clear()
        return pages

    query_part = jnp.dot(gathered, w_query, preferred_element_type=jnp.float32)
    keyval_part = jnp.dot(gathered, w_keyval, preferred_element_type=jnp.float32)
    own_cols = query_part.shape[1] // narrow
    query_part = jnp.transpose(query_part.reshape(rows, narrow, own_cols), (1, 0, 2))
    partial = jnp.concatenate(
        [query_part, jnp.broadcast_to(keyval_part[None], (narrow,) + keyval_part.shape)], axis=2
    )
    partial = exchange(launch(partial, 6), "narrow")
    projected = jnp.sum(partial, axis=0).astype(jnp.bfloat16)
    shifted = sent_idx + 1
    tags = jnp.concatenate(
        [
            sent_req.reshape(wide, 1, capacity),
            (shifted // 32).reshape(wide, 1, capacity),
            (shifted % 32).reshape(wide, 1, capacity),
        ],
        axis=2,
    ).astype(jnp.bfloat16)
    height = up(rows + 1, 8)
    packed = jnp.concatenate(
        [
            jnp.broadcast_to(projected[None], (wide,) + projected.shape),
            jnp.pad(
                tags, ((0, 0), (0, height - rows - 1), (0, projected.shape[1] - 3 * capacity))
            ),
        ],
        axis=1,
    )
    packed, page_req, page_idx, lengths = lax.optimization_barrier(
        (packed, page_req, page_idx, lengths)
    )
    received = exchange(packed, "wide")
    req_tok = jnp.broadcast_to(page_req[:, None], (slots, PAGE)).reshape(1, -1)
    pos_tok = (page_idx[:, None] * PAGE + jnp.arange(PAGE, dtype=jnp.int32)[None, :]).reshape(1, -1)
    row_info = jnp.stack(
        [
            jnp.asarray(np.arange(rows) // STEPS, jnp.int32),
            jnp.broadcast_to(lengths[:, None], (requests, STEPS)).reshape(rows),
        ],
        axis=1,
    )
    req_tok, pos_tok, row_info = launch((req_tok, pos_tok, row_info), 7, 4, 2, 3, 1)
    queries = spread(received[:, :rows, :own_cols], "narrow")
    if own_cols == HD:
        queries = jnp.transpose(queries, (1, 0, 2, 3))
    else:
        queries = jnp.transpose(queries, (2, 1, 0, 3)).reshape(rows, HEADS, HD)
        queries = jnp.transpose(queries, (1, 0, 2))
    queries = queries.reshape(KVH, GROUPS * rows, HD)
    tags_in = received[:, rows, : 3 * capacity].astype(jnp.int32)
    moved_req = tags_in[:, :capacity].reshape(slots)
    moved_idx = (
        tags_in[:, capacity : 2 * capacity] * 32 + tags_in[:, 2 * capacity :] - 1
    ).reshape(slots)

    keyval = jnp.transpose(received[:, :rows, own_cols:], (1, 0, 2)).reshape(rows, -1)
    extra = up(rows, HD)
    here = (lax.axis_index("wide") == 0) & (lax.axis_index("narrow") == 0)
    row_ids = np.arange(rows)[:, None]
    col_ids = np.arange(extra)[None, :]
    causal = (row_ids // STEPS == col_ids // STEPS) & (col_ids <= row_ids) & (col_ids < rows)
    new_bias = jnp.where(jnp.asarray(causal) & here, 0.0, NEG_FILL).astype(jnp.float32)
    piece = HEADS * rows // (wide * narrow)
    new_keyval = jnp.pad(keyval, ((0, extra - rows), (0, 0)))
    tokens = pool.reshape(slots * PAGE, -1)
    parts = attend(
        queries, new_keyval, tokens, req_tok, pos_tok, row_info, new_bias, rows, piece
    )
    parts = exchange(parts, "narrow")
    parts = combine(parts.reshape((narrow, wide) + parts.shape[1:]), piece, False)
    attn = combine(exchange(parts, "wide")[:, None], piece, True)
    attn = land(attn, 6, 7, 4, 2, 3, 1)
    moved_pool = launch(placed(moved_pool), 5)
    attn = spread(attn, "wide")
    attn = jnp.transpose(attn.reshape(-1, rows, HD), (1, 0, 2)).reshape(rows, -1)
    sums = jnp.dot(attn, w_out, preferred_element_type=jnp.float32)
    sums = sums.reshape(narrow, rows // narrow, -1)
    sums = exchange(sums, "narrow")
    attended = jnp.sum(sums, axis=0).astype(jnp.bfloat16)

    attended = land(attended, 5)
    moved_pool = placed(moved_pool)

    local_req = local_rows // STEPS
    first_req = lax.axis_index("wide") * local_req
    fresh = lax.dynamic_slice_in_dim(keyval.reshape(requests, STEPS, -1), first_req, local_req, 0)
    kept = lax.dynamic_slice_in_dim(accepted, first_req, local_req, 0)
    new_entries = jnp.where(
        jnp.arange(STEPS)[None, :, None] < kept[:, None, None], fresh, jnp.zeros((), jnp.bfloat16)
    )
    return (attended, new_entries, moved_pool, moved_req, moved_idx)


def solution(mesh):
    in_specs = (
        P("wide", "narrow"),
        P("narrow", "wide"),
        P("narrow", "wide"),
        P("narrow", "wide"),
        P(("wide", "narrow"), None, None),
        P(("wide", "narrow")),
        P(("wide", "narrow")),
        P(),
        P(("wide", "narrow"), None),
        P(),
    )
    out_specs = (
        P("narrow", "wide"),
        P("wide", None, None),
        P(("wide", "narrow"), None, None),
        P(("wide", "narrow")),
        P(("wide", "narrow")),
    )
    return jax.shard_map(
        on_device, mesh=mesh, in_specs=in_specs, out_specs=out_specs, check_vma=False
    )
```

```python
import functools
import math

import jax
import jax.numpy as jnp
import numpy as np
from jax import lax
from jax.experimental import pallas as pl
from jax.experimental.pallas import tpu as pltpu
from jax.sharding import PartitionSpec as P

HEADS = 32
KVH = 4
HD = 128
STEPS = 5
PAGE = 16
GROUPS = HEADS // KVH
NEG_FILL = -1e30
SCALE2 = math.log2(math.e) / math.sqrt(HD)
STAT = 16
MIB = 1024 * 1024
PARTS = 2
NT = (((1,), (1,)), ((), ()))


def up(value, unit):
    return -(-value // unit) * unit


def permute_kernel(source_ref, place_ref, pool_ref, out_ref, *refs):
    chunk_refs, (pages_ref, in_sem, out_sem) = refs[:-3], refs[-3:]
    count = chunk_refs[0].shape[0]
    own = out_ref.at[pl.ds(place_ref[0] * (PARTS * count), PARTS * count)]
    targets = [own.at[pl.ds(i * count, count)] for i in range(PARTS)] + list(chunk_refs)

    def start(j, carry):
        pltpu.make_async_copy(
            pool_ref.at[source_ref[j]], pages_ref.at[j], in_sem.at[j // count]
        ).start()
        return carry

    lax.fori_loop(0, pool_ref.shape[0], start, 0)
    copies = []
    for c, target in enumerate(targets):
        held = pages_ref.at[pl.ds(c * count, count)]
        pltpu.make_async_copy(pool_ref.at[pl.ds(0, count)], held, in_sem.at[c]).wait()
        copies.append(pltpu.make_async_copy(held, target, out_sem.at[c]))
        copies[-1].start()
    for copy in copies:
        copy.wait()


def permute_pages(source_of, place, pool, chunks):
    part = jax.ShapeDtypeStruct((pool.shape[0] // chunks,) + pool.shape[1:], pool.dtype)
    return pl.pallas_call(
        permute_kernel,
        out_shape=[jax.ShapeDtypeStruct(pool.shape, pool.dtype)] + [part] * (chunks - PARTS),
        in_specs=[
            pl.BlockSpec(memory_space=pltpu.SMEM),
            pl.BlockSpec(memory_space=pltpu.SMEM),
            pl.BlockSpec(memory_space=pltpu.HBM),
        ],
        out_specs=[pl.BlockSpec(memory_space=pltpu.HBM)] * (1 + chunks - PARTS),
        scratch_shapes=[
            pltpu.VMEM(pool.shape, pool.dtype),
            pltpu.SemaphoreType.DMA((chunks,)),
            pltpu.SemaphoreType.DMA((chunks,)),
        ],
        compiler_params=pltpu.CompilerParams(vmem_limit_bytes=56 * MIB),
        cost_estimate=pl.CostEstimate(
            flops=0, bytes_accessed=2 * pool.size * 2, transcendentals=0
        ),
    )(source_of, place, pool)


def place_kernel(place_ref, *refs):
    in_refs, (out_ref, sem) = refs[:-3], refs[-2:]
    copies = []
    for i, chunk in enumerate(in_refs):
        depth = chunk.shape[0]
        copies.append(
            pltpu.make_async_copy(
                chunk, out_ref.at[pl.ds(place_ref[i] * depth, depth)], sem.at[i]
            )
        )
    for copy in copies:
        copy.start()
    for copy in copies:
        copy.wait()


def place_pages(place, chunks, pages):
    count = len(chunks)
    return pl.pallas_call(
        place_kernel,
        out_shape=jax.ShapeDtypeStruct(pages.shape, pages.dtype),
        in_specs=[pl.BlockSpec(memory_space=pltpu.SMEM)]
        + [pl.BlockSpec(memory_space=pltpu.VMEM)] * count
        + [pl.BlockSpec(memory_space=pl.ANY)],
        out_specs=pl.BlockSpec(memory_space=pl.ANY),
        scratch_shapes=[pltpu.SemaphoreType.DMA((count,))],
        input_output_aliases={count + 1: 0},
        compiler_params=pltpu.CompilerParams(vmem_limit_bytes=2 * count * chunks[0].size + 2 * MIB),
        cost_estimate=pl.CostEstimate(
            flops=0, bytes_accessed=4 * count * chunks[0].size, transcendentals=0
        ),
    )(place, *chunks, pages)


def cut(value):
    return value.astype(jnp.bfloat16).astype(jnp.float32)


def split_stats(peak, total):
    high = cut(peak)
    mid = cut(peak - high)
    return high, mid, peak - high - mid, cut(total), total - cut(total)


def attend_kernel(
    rows,
    piece,
    query_ref,
    key_ref,
    value_ref,
    new_key_ref,
    new_value_ref,
    req_ref,
    pos_ref,
    row_ref,
    new_bias_ref,
    out_ref,
    bias_ref,
    score_ref,
    weight_ref,
):
    tokens = key_ref.shape[0]

    @pl.when(pl.program_id(0) == 0)
    def _():
        seen = (req_ref[...] == row_ref[:, 0:1]) & (pos_ref[...] < row_ref[:, 1:2])
        bias_ref[...] = jnp.where(seen, 0.0, NEG_FILL)

    query = query_ref[0]
    score_ref[:, :tokens] = lax.dot_general(
        query, key_ref[...], NT, preferred_element_type=jnp.float32
    )
    score_ref[:, tokens:] = lax.dot_general(
        query, new_key_ref[...], NT, preferred_element_type=jnp.float32
    )
    together = 1 if rows % 16 == 0 else 2
    span = together * rows
    peaks, totals = [], []
    for c in range(GROUPS // together):
        block = pl.ds(c * span, span)
        old = score_ref[block, :tokens].reshape(together, rows, tokens) * SCALE2 + bias_ref[...]
        new = score_ref[block, tokens:].reshape(together, rows, -1) * SCALE2 + new_bias_ref[...]
        peak = jnp.maximum(
            jnp.max(old, axis=-1, keepdims=True), jnp.max(new, axis=-1, keepdims=True)
        )
        old = jnp.exp2(old - peak)
        new = jnp.exp2(new - peak)
        totals.append(
            (jnp.sum(old, axis=-1, keepdims=True) + jnp.sum(new, axis=-1, keepdims=True)).reshape(
                span, 1
            )
        )
        peaks.append(peak.reshape(span, 1))
        weight_ref[block, :tokens] = old.reshape(span, tokens).astype(jnp.bfloat16)
        weight_ref[block, tokens:] = new.reshape(span, -1).astype(jnp.bfloat16)
    mixed = jnp.dot(
        weight_ref[:, :tokens], value_ref[...], preferred_element_type=jnp.float32
    ) + jnp.dot(weight_ref[:, tokens:], new_value_ref[...], preferred_element_type=jnp.float32)
    peak = jnp.concatenate(peaks, axis=0)
    total = jnp.concatenate(totals, axis=0)

    lane = lax.broadcasted_iota(jnp.int32, (GROUPS * rows, HD), 1)
    stats = jnp.zeros((GROUPS * rows, HD), jnp.float32)
    for i, part in enumerate(split_stats(peak, total)):
        stats = jnp.where(lane == i, part, stats)
    pick = (
        lax.broadcasted_iota(jnp.int32, (STAT, HD), 0)
        == lax.broadcasted_iota(jnp.int32, (STAT, HD), 1)
    ).astype(jnp.bfloat16)
    fill = out_ref.shape[1] - STAT - piece
    for c in range(GROUPS * rows // piece):
        part = slice(c * piece, (c + 1) * piece)
        turned = lax.dot_general(
            pick,
            jnp.concatenate(
                [stats[part], jnp.zeros((HD - piece, HD), jnp.float32)], axis=0
            ).astype(jnp.bfloat16),
            NT,
            preferred_element_type=jnp.float32,
        )
        out_ref[c] = jnp.concatenate(
            [turned, mixed[part], jnp.zeros((fill, HD), jnp.float32)], axis=0
        ).astype(jnp.bfloat16)


def attend(queries, keyval, pool, req_tok, pos_tok, row_info, new_bias, rows, piece):
    tokens = pool.shape[0]
    extra = keyval.shape[0]
    pieces = GROUPS * rows // piece
    height = STAT + up(piece, 16)
    whole = lambda shape: pl.BlockSpec(shape, lambda k: (0,) * len(shape))
    return pl.pallas_call(
        functools.partial(attend_kernel, rows, piece),
        grid=(KVH,),
        out_shape=jax.ShapeDtypeStruct((KVH * pieces, height, HD), jnp.bfloat16),
        in_specs=[
            pl.BlockSpec((1,) + queries.shape[1:], lambda k: (k, 0, 0)),
            pl.BlockSpec((tokens, HD), lambda k: (0, k)),
            pl.BlockSpec((tokens, HD), lambda k: (0, KVH + k)),
            pl.BlockSpec((extra, HD), lambda k: (0, k)),
            pl.BlockSpec((extra, HD), lambda k: (0, KVH + k)),
            whole(req_tok.shape),
            whole(pos_tok.shape),
            whole(row_info.shape),
            whole(new_bias.shape),
        ],
        out_specs=pl.BlockSpec((pieces, height, HD), lambda k: (k, 0, 0)),
        scratch_shapes=[
            pltpu.VMEM((rows, tokens), jnp.float32),
            pltpu.VMEM((GROUPS * rows, tokens + extra), jnp.float32),
            pltpu.VMEM((GROUPS * rows, tokens + extra), jnp.bfloat16),
        ],
        compiler_params=pltpu.CompilerParams(vmem_limit_bytes=32 * MIB),
        cost_estimate=pl.CostEstimate(
            flops=4 * HEADS * rows * (tokens + extra) * HD,
            bytes_accessed=pool.size * 2,
            transcendentals=HEADS * rows * (tokens + extra),
        ),
    )(queries, pool, pool, keyval, keyval, req_tok, pos_tok, row_info, new_bias)


def combine_kernel(piece, last, parts_ref, out_ref):
    count, groups, height = parts_ref.shape[:3]
    peaks, totals = [], []
    for i in range(count):
        for j in range(groups):
            stat = parts_ref[i, j, :STAT, :].astype(jnp.float32)
            peaks.append(stat[0:1] + stat[1:2] + stat[2:3])
            totals.append(stat[3:4] + stat[4:5])
    peak = jnp.concatenate(peaks, axis=0).reshape(count, groups, HD)
    total = jnp.concatenate(totals, axis=0).reshape(count, groups, HD)
    top = jnp.max(peak, axis=0)
    lead = jnp.exp2(peak - top[None])
    whole = jnp.sum(lead * total, axis=0)
    if last:
        lane = lax.broadcasted_iota(jnp.int32, whole.shape, 1)
        lead = lead / jnp.where(lane < piece, whole, 1.0)[None]
    lead = lead.reshape(count * groups, HD)
    if (count * groups) % HD:
        fill = up(count * groups, HD) - count * groups
        lead = jnp.concatenate([lead, jnp.zeros((fill, HD), jnp.float32)], axis=0)
    lead = jnp.transpose(lead)
    rows = height - STAT
    for j in range(groups):
        result = jnp.zeros((rows, HD), jnp.float32)
        for i in range(count):
            c = i * groups + j
            result = result + lead[:rows, c : c + 1] * parts_ref[i, j, STAT:, :].astype(jnp.float32)
        if last:
            out_ref[...] = result[:piece].astype(jnp.bfloat16)
        else:
            stats = split_stats(top[j : j + 1], whole[j : j + 1])
            rest = jnp.zeros((STAT - len(stats), HD), jnp.float32)
            out_ref[j] = jnp.concatenate([*stats, rest, result], axis=0).astype(jnp.bfloat16)


def combine(parts, piece, last):
    groups, height = parts.shape[1:3]
    shape = (piece, HD) if last else (groups, height, HD)
    return pl.pallas_call(
        functools.partial(combine_kernel, piece, last),
        out_shape=jax.ShapeDtypeStruct(shape, jnp.bfloat16),
        in_specs=[pl.BlockSpec(memory_space=pltpu.VMEM)],
        out_specs=pl.BlockSpec(memory_space=pltpu.VMEM),
        compiler_params=pltpu.CompilerParams(vmem_limit_bytes=8 * MIB),
        cost_estimate=pl.CostEstimate(
            flops=2 * parts.size, bytes_accessed=parts.size * 2, transcendentals=0
        ),
    )(parts)


def group_of(d, wide):
    return d if wide <= 8 else 1 + (d - 1) * 7 // (wide - 1)


def spread(block, axis):
    count = lax.axis_size(axis)
    return lax.all_to_all(
        jnp.broadcast_to(block[None], (count,) + block.shape),
        axis,
        split_axis=0,
        concat_axis=0,
        tiled=True,
    )


def on_device(hidden, w_query, w_keyval, w_out, pool, page_req, page_idx, lengths, moves, accepted):
    wide = lax.axis_size("wide")
    narrow = lax.axis_size("narrow")
    local_rows = hidden.shape[0]
    rows = local_rows * wide
    requests = rows // STEPS
    slots = pool.shape[0]
    capacity = slots // wide

    gathered = spread(hidden, "wide").reshape(rows, -1)

    dest = moves[:, 0]
    order = jnp.arange(slots, dtype=jnp.int32)
    rank = jnp.sum((dest[:, None] == dest[None, :]) & (order[None, :] < order[:, None]), axis=1)
    target = dest * capacity + rank
    chosen = target[None, :] == order[:, None]
    me = lax.axis_index("wide")
    moved_to = (dest ^ me) * capacity + rank
    source_of = jnp.sum(
        jnp.where(moved_to[None, :] == order[:, None], order[None, :], 0), axis=1
    )
    sent_req = jnp.sum(jnp.where(chosen, page_req[None, :], 0), axis=1)
    sent_idx = jnp.sum(jnp.where(chosen, page_idx[None, :], 0), axis=1)
    moved_pool, *chunks = permute_pages(source_of, me.reshape(1), pool, wide * PARTS)
    arrived = {}

    exchange = functools.partial(lax.all_to_all, split_axis=0, concat_axis=0, tiled=True)
    flying = {}

    def members(groups):
        return [
            (d - 1) * PARTS + part
            for group, part in groups
            for d in range(1, wide)
            if group_of(d, wide) == group
        ]

    def launch(values, *groups):
        taken = members(groups)
        values, sent = lax.optimization_barrier((values, [chunks[c] for c in taken]))
        for c, chunk in zip(taken, sent):
            peer = 1 + c // PARTS
            flying[c] = lax.ppermute(chunk, "wide", [(w, w ^ peer) for w in range(wide)])
        return values

    def land(values, *groups):
        taken = members(groups)
        values, got = lax.optimization_barrier((values, [flying[c] for c in taken]))
        arrived.update(zip(taken, got))
        return values

    def beside(step, value, *groups):
        return land(step(launch(value, *groups)), *groups)

    def placed(pages):
        taken = sorted(arrived)
        place = jnp.stack([(me ^ (1 + c // PARTS)) * PARTS + c % PARTS for c in taken])
        pages = place_pages(place, [arrived[c] for c in taken], pages)
        arrived.clear()
        return pages

    query_part = jnp.dot(gathered, w_query, preferred_element_type=jnp.float32)
    keyval_part = jnp.dot(gathered, w_keyval, preferred_element_type=jnp.float32)
    own_cols = query_part.shape[1] // narrow
    query_part = jnp.transpose(query_part.reshape(rows, narrow, own_cols), (1, 0, 2))
    partial = jnp.concatenate(
        [query_part, jnp.broadcast_to(keyval_part[None], (narrow,) + keyval_part.shape)], axis=2
    )
    partial = beside(lambda value: exchange(value, "narrow"), partial, (6, 0), (1, 0))
    projected = jnp.sum(partial, axis=0).astype(jnp.bfloat16)
    shifted = sent_idx + 1
    tags = jnp.concatenate(
        [
            sent_req.reshape(wide, 1, capacity),
            (shifted // 32).reshape(wide, 1, capacity),
            (shifted % 32).reshape(wide, 1, capacity),
        ],
        axis=2,
    ).astype(jnp.bfloat16)
    height = up(rows + 1, 8)
    packed = jnp.concatenate(
        [
            jnp.broadcast_to(projected[None], (wide,) + projected.shape),
            jnp.pad(
                tags, ((0, 0), (0, height - rows - 1), (0, projected.shape[1] - 3 * capacity))
            ),
        ],
        axis=1,
    )
    received = beside(lambda value: exchange(value, "wide"), packed, (6, 1))
    req_tok = jnp.broadcast_to(page_req[:, None], (slots, PAGE)).reshape(1, -1)
    pos_tok = (page_idx[:, None] * PAGE + jnp.arange(PAGE, dtype=jnp.int32)[None, :]).reshape(1, -1)
    row_info = jnp.stack(
        [
            jnp.asarray(np.arange(rows) // STEPS, jnp.int32),
            jnp.broadcast_to(lengths[:, None], (requests, STEPS)).reshape(rows),
        ],
        axis=1,
    )
    queries = beside(
        lambda value: spread(value, "narrow"), received[:, :rows, :own_cols], (7, 0), (2, 0)
    )
    if own_cols == HD:
        queries = jnp.transpose(queries, (1, 0, 2, 3))
    else:
        queries = jnp.transpose(queries, (2, 1, 0, 3)).reshape(rows, HEADS, HD)
        queries = jnp.transpose(queries, (1, 0, 2))
    queries = queries.reshape(KVH, GROUPS * rows, HD)
    tags_in = received[:, rows, : 3 * capacity].astype(jnp.int32)
    moved_req = tags_in[:, :capacity].reshape(slots)
    moved_idx = (
        tags_in[:, capacity : 2 * capacity] * 32 + tags_in[:, 2 * capacity :] - 1
    ).reshape(slots)

    keyval = jnp.transpose(received[:, :rows, own_cols:], (1, 0, 2)).reshape(rows, -1)
    extra = up(rows, HD)
    here = (lax.axis_index("wide") == 0) & (lax.axis_index("narrow") == 0)
    row_ids = np.arange(rows)[:, None]
    col_ids = np.arange(extra)[None, :]
    causal = (row_ids // STEPS == col_ids // STEPS) & (col_ids <= row_ids) & (col_ids < rows)
    new_bias = jnp.where(jnp.asarray(causal) & here, 0.0, NEG_FILL).astype(jnp.float32)
    piece = HEADS * rows // (wide * narrow)
    new_keyval = jnp.pad(keyval, ((0, extra - rows), (0, 0)))
    tokens = pool.reshape(slots * PAGE, -1)
    parts = beside(
        lambda value: attend(
            value, new_keyval, tokens, req_tok, pos_tok, row_info, new_bias, rows, piece
        ),
        queries,
        (7, 1),
        (2, 1),
        (1, 1),
    )
    parts = beside(lambda value: exchange(value, "narrow"), parts, (4, 0), (3, 0))
    parts = combine(parts.reshape((narrow, wide) + parts.shape[1:]), piece, False)
    parts = beside(lambda value: exchange(value, "wide"), parts, (4, 1))
    attn = combine(parts[:, None], piece, True)
    attn = beside(lambda value: spread(value, "wide"), attn, (5, 0))
    moved_pool = placed(moved_pool)
    attn = jnp.transpose(attn.reshape(-1, rows, HD), (1, 0, 2)).reshape(rows, -1)
    sums = jnp.dot(attn, w_out, preferred_element_type=jnp.float32)
    sums = sums.reshape(narrow, rows // narrow, -1)
    sums = beside(lambda value: exchange(value, "narrow"), sums, (5, 1), (3, 1))
    attended = jnp.sum(sums, axis=0).astype(jnp.bfloat16)

    moved_pool = placed(moved_pool)

    local_req = local_rows // STEPS
    first_req = lax.axis_index("wide") * local_req
    fresh = lax.dynamic_slice_in_dim(keyval.reshape(requests, STEPS, -1), first_req, local_req, 0)
    kept = lax.dynamic_slice_in_dim(accepted, first_req, local_req, 0)
    new_entries = jnp.where(
        jnp.arange(STEPS)[None, :, None] < kept[:, None, None], fresh, jnp.zeros((), jnp.bfloat16)
    )
    return (attended, new_entries, moved_pool, moved_req, moved_idx)


def solution(mesh):
    in_specs = (
        P("wide", "narrow"),
        P("narrow", "wide"),
        P("narrow", "wide"),
        P("narrow", "wide"),
        P(("wide", "narrow"), None, None),
        P(("wide", "narrow")),
        P(("wide", "narrow")),
        P(),
        P(("wide", "narrow"), None),
        P(),
    )
    out_specs = (
        P("narrow", "wide"),
        P("wide", None, None),
        P(("wide", "narrow"), None, None),
        P(("wide", "narrow")),
        P(("wide", "narrow")),
    )
    return jax.shard_map(
        on_device, mesh=mesh, in_specs=in_specs, out_specs=out_specs, check_vma=False
    )
```

```python
import functools
import math

import jax
import jax.numpy as jnp
import numpy as np
from jax import lax
from jax.experimental import pallas as pl
from jax.experimental.pallas import tpu as pltpu
from jax.sharding import PartitionSpec as P

HEADS = 32
KVH = 4
HD = 128
STEPS = 5
PAGE = 16
GROUPS = HEADS // KVH
NEG_FILL = -1e30
SCALE2 = math.log2(math.e) / math.sqrt(HD)
STAT = 16
MIB = 1024 * 1024
PARTS = 2
NT = (((1,), (1,)), ((), ()))


def up(value, unit):
    return -(-value // unit) * unit


def permute_kernel(source_ref, place_ref, pool_ref, out_ref, *refs):
    chunk_refs, (pages_ref, in_sem, out_sem) = refs[:-3], refs[-3:]
    count = chunk_refs[0].shape[0]
    own = out_ref.at[pl.ds(place_ref[0] * (PARTS * count), PARTS * count)]
    targets = [own.at[pl.ds(i * count, count)] for i in range(PARTS)] + list(chunk_refs)

    def start(j, carry):
        pltpu.make_async_copy(
            pool_ref.at[source_ref[j]], pages_ref.at[j], in_sem.at[j // count]
        ).start()
        return carry

    lax.fori_loop(0, pool_ref.shape[0], start, 0)
    copies = []
    for c, target in enumerate(targets):
        held = pages_ref.at[pl.ds(c * count, count)]
        pltpu.make_async_copy(pool_ref.at[pl.ds(0, count)], held, in_sem.at[c]).wait()
        copies.append(pltpu.make_async_copy(held, target, out_sem.at[c]))
        copies[-1].start()
    for copy in copies:
        copy.wait()


def permute_pages(source_of, place, pool, chunks):
    part = jax.ShapeDtypeStruct((pool.shape[0] // chunks,) + pool.shape[1:], pool.dtype)
    return pl.pallas_call(
        permute_kernel,
        out_shape=[jax.ShapeDtypeStruct(pool.shape, pool.dtype)] + [part] * (chunks - PARTS),
        in_specs=[
            pl.BlockSpec(memory_space=pltpu.SMEM),
            pl.BlockSpec(memory_space=pltpu.SMEM),
            pl.BlockSpec(memory_space=pltpu.HBM),
        ],
        out_specs=[pl.BlockSpec(memory_space=pltpu.HBM)] * (1 + chunks - PARTS),
        scratch_shapes=[
            pltpu.VMEM(pool.shape, pool.dtype),
            pltpu.SemaphoreType.DMA((chunks,)),
            pltpu.SemaphoreType.DMA((chunks,)),
        ],
        compiler_params=pltpu.CompilerParams(vmem_limit_bytes=56 * MIB),
        cost_estimate=pl.CostEstimate(
            flops=0, bytes_accessed=2 * pool.size * 2, transcendentals=0
        ),
    )(source_of, place, pool)


def place_kernel(place_ref, *refs):
    in_refs, (out_ref, sem) = refs[:-3], refs[-2:]
    copies = []
    for i, chunk in enumerate(in_refs):
        depth = chunk.shape[0]
        copies.append(
            pltpu.make_async_copy(
                chunk, out_ref.at[pl.ds(place_ref[i] * depth, depth)], sem.at[i]
            )
        )
    for copy in copies:
        copy.start()
    for copy in copies:
        copy.wait()


def place_pages(place, chunks, pages):
    count = len(chunks)
    return pl.pallas_call(
        place_kernel,
        out_shape=jax.ShapeDtypeStruct(pages.shape, pages.dtype),
        in_specs=[pl.BlockSpec(memory_space=pltpu.SMEM)]
        + [pl.BlockSpec(memory_space=pltpu.VMEM)] * count
        + [pl.BlockSpec(memory_space=pl.ANY)],
        out_specs=pl.BlockSpec(memory_space=pl.ANY),
        scratch_shapes=[pltpu.SemaphoreType.DMA((count,))],
        input_output_aliases={count + 1: 0},
        compiler_params=pltpu.CompilerParams(vmem_limit_bytes=2 * count * chunks[0].size + 2 * MIB),
        cost_estimate=pl.CostEstimate(
            flops=0, bytes_accessed=4 * count * chunks[0].size, transcendentals=0
        ),
    )(place, *chunks, pages)


def cut(value):
    return value.astype(jnp.bfloat16).astype(jnp.float32)


def split_stats(peak, total):
    high = cut(peak)
    mid = cut(peak - high)
    return high, mid, peak - high - mid, cut(total), total - cut(total)


def attend_kernel(rows, piece, peers, me_ref, *refs):
    query_refs, refs = refs[:peers], refs[peers:]
    key_ref, value_ref, new_key_ref, new_value_ref, req_ref, pos_ref, row_ref, new_bias_ref = refs[:8]
    out_refs = refs[8 : 8 + peers]
    bias_ref, score_ref, weight_ref, query_ref, result_ref = refs[8 + peers :]
    tokens = key_ref.shape[0]
    step = pl.program_id(0)

    @pl.when(step == 0)
    def _():
        seen = (req_ref[...] == row_ref[:, 0:1]) & (pos_ref[...] < row_ref[:, 1:2])
        bias_ref[...] = jnp.where(seen, 0.0, NEG_FILL)
        if peers > 1:
            for d in range(peers):
                query_ref[me_ref[1] ^ d] = query_refs[d][...]

    if peers > 1:
        per_step = query_refs[0].shape[0] // KVH
        query = jnp.concatenate(
            [
                query_ref[n, step * per_step + i].astype(jnp.float32)
                for i in range(per_step)
                for n in range(peers)
            ],
            axis=0,
        ).astype(jnp.bfloat16)
    else:
        query = query_refs[0][0]
    score_ref[:, :tokens] = lax.dot_general(
        query, key_ref[...], NT, preferred_element_type=jnp.float32
    )
    score_ref[:, tokens:] = lax.dot_general(
        query, new_key_ref[...], NT, preferred_element_type=jnp.float32
    )
    together = 1 if rows % 16 == 0 else 2
    span = together * rows
    peaks, totals = [], []
    for c in range(GROUPS // together):
        block = pl.ds(c * span, span)
        old = score_ref[block, :tokens].reshape(together, rows, tokens) * SCALE2 + bias_ref[...]
        new = score_ref[block, tokens:].reshape(together, rows, -1) * SCALE2 + new_bias_ref[...]
        peak = jnp.maximum(
            jnp.max(old, axis=-1, keepdims=True), jnp.max(new, axis=-1, keepdims=True)
        )
        old = jnp.exp2(old - peak)
        new = jnp.exp2(new - peak)
        totals.append(
            (jnp.sum(old, axis=-1, keepdims=True) + jnp.sum(new, axis=-1, keepdims=True)).reshape(
                span, 1
            )
        )
        peaks.append(peak.reshape(span, 1))
        weight_ref[block, :tokens] = old.reshape(span, tokens).astype(jnp.bfloat16)
        weight_ref[block, tokens:] = new.reshape(span, -1).astype(jnp.bfloat16)
    mixed = jnp.dot(
        weight_ref[:, :tokens], value_ref[...], preferred_element_type=jnp.float32
    ) + jnp.dot(weight_ref[:, tokens:], new_value_ref[...], preferred_element_type=jnp.float32)
    peak = jnp.concatenate(peaks, axis=0)
    total = jnp.concatenate(totals, axis=0)
    lane = lax.broadcasted_iota(jnp.int32, (GROUPS * rows, HD), 1)
    stats = jnp.zeros((GROUPS * rows, HD), jnp.float32)
    for i, part in enumerate(split_stats(peak, total)):
        stats = jnp.where(lane == i, part, stats)
    pick = (
        lax.broadcasted_iota(jnp.int32, (STAT, HD), 0)
        == lax.broadcasted_iota(jnp.int32, (STAT, HD), 1)
    ).astype(jnp.bfloat16)
    fill = result_ref.shape[1] - STAT - piece
    for c in range(GROUPS * rows // piece):
        part = slice(c * piece, (c + 1) * piece)
        turned = lax.dot_general(
            pick,
            jnp.concatenate(
                [stats[part], jnp.zeros((HD - piece, HD), jnp.float32)], axis=0
            ).astype(jnp.bfloat16),
            NT,
            preferred_element_type=jnp.float32,
        )
        result_ref[c] = jnp.concatenate(
            [turned, mixed[part], jnp.zeros((fill, HD), jnp.float32)], axis=0
        ).astype(jnp.bfloat16)
    if peers > 1:
        for d, out_ref in enumerate(out_refs):

            @pl.when((step ^ me_ref[1]) == d)
            def _():
                out_ref[...] = result_ref[...]
    else:
        out_refs[0][...] = result_ref[...]


def attend(me, queries, keyval, pool, req_tok, pos_tok, row_info, new_bias, rows, piece):
    tokens = pool.shape[0]
    extra = keyval.shape[0]
    peers = len(queries)
    pieces = GROUPS * rows // piece
    height = STAT + up(piece, 16)
    whole = lambda shape: pl.BlockSpec(shape, lambda k: (0,) * len(shape))
    if peers > 1:
        query_spec = whole(queries[0].shape)
        out_spec = whole((pieces, height, HD))
        out_shape = jax.ShapeDtypeStruct((pieces, height, HD), jnp.bfloat16)
    else:
        query_spec = pl.BlockSpec((1,) + queries[0].shape[1:], lambda k: (k, 0, 0))
        out_spec = pl.BlockSpec((pieces, height, HD), lambda k: (k, 0, 0))
        out_shape = jax.ShapeDtypeStruct((KVH * pieces, height, HD), jnp.bfloat16)
    return pl.pallas_call(
        functools.partial(attend_kernel, rows, piece, peers),
        grid=(KVH,),
        out_shape=[out_shape] * peers,
        in_specs=[pl.BlockSpec(memory_space=pltpu.SMEM)]
        + [query_spec] * peers
        + [
            pl.BlockSpec((tokens, HD), lambda k: (0, k)),
            pl.BlockSpec((tokens, HD), lambda k: (0, KVH + k)),
            pl.BlockSpec((extra, HD), lambda k: (0, k)),
            pl.BlockSpec((extra, HD), lambda k: (0, KVH + k)),
            whole(req_tok.shape),
            whole(pos_tok.shape),
            whole(row_info.shape),
            whole(new_bias.shape),
        ],
        out_specs=[out_spec] * peers,
        scratch_shapes=[
            pltpu.VMEM((rows, tokens), jnp.float32),
            pltpu.VMEM((GROUPS * rows, tokens + extra), jnp.float32),
            pltpu.VMEM((GROUPS * rows, tokens + extra), jnp.bfloat16),
            pltpu.VMEM((peers,) + queries[0].shape, jnp.bfloat16),
            pltpu.VMEM((pieces, height, HD), jnp.bfloat16),
        ],
        compiler_params=pltpu.CompilerParams(vmem_limit_bytes=32 * MIB),
        cost_estimate=pl.CostEstimate(
            flops=4 * HEADS * rows * (tokens + extra) * HD,
            bytes_accessed=pool.size * 2,
            transcendentals=HEADS * rows * (tokens + extra),
        ),
    )(me, *queries, pool, pool, keyval, keyval, req_tok, pos_tok, row_info, new_bias)


def combine_kernel(piece, last, count, me_ref, *refs):
    part_refs, refs = refs[:count], refs[count:]
    groups, height = part_refs[0].shape[:2]
    peaks, totals = [], []
    for i in range(count):
        for j in range(groups):
            stat = part_refs[i][j, :STAT, :].astype(jnp.float32)
            peaks.append(stat[0:1] + stat[1:2] + stat[2:3])
            totals.append(stat[3:4] + stat[4:5])
    peak = jnp.concatenate(peaks, axis=0).reshape(count, groups, HD)
    total = jnp.concatenate(totals, axis=0).reshape(count, groups, HD)
    top = jnp.max(peak, axis=0)
    lead = jnp.exp2(peak - top[None])
    whole = jnp.sum(lead * total, axis=0)
    if last:
        lane = lax.broadcasted_iota(jnp.int32, whole.shape, 1)
        lead = lead / jnp.where(lane < piece, whole, 1.0)[None]
    lead = lead.reshape(count * groups, HD)
    if (count * groups) % HD:
        fill = up(count * groups, HD) - count * groups
        lead = jnp.concatenate([lead, jnp.zeros((fill, HD), jnp.float32)], axis=0)
    lead = jnp.transpose(lead)
    rows = height - STAT
    for j in range(groups):
        result = jnp.zeros((rows, HD), jnp.float32)
        for i in range(count):
            c = i * groups + j
            result = result + lead[:rows, c : c + 1] * part_refs[i][j, STAT:, :].astype(jnp.float32)
        if last:
            refs[0][...] = result[:piece].astype(jnp.bfloat16)
        else:
            stats = split_stats(top[j : j + 1], whole[j : j + 1])
            rest = jnp.zeros((STAT - len(stats), HD), jnp.float32)
            refs[-1][j] = jnp.concatenate([*stats, rest, result], axis=0).astype(jnp.bfloat16)
    for d, out_ref in enumerate(refs[:-1]):
        out_ref[...] = refs[-1][me_ref[0] ^ d]


def combine(me, parts, piece, last, apart):
    groups, height = parts[0].shape[:2]
    if last:
        out_shape = [jax.ShapeDtypeStruct((piece, HD), jnp.bfloat16)]
    elif apart:
        out_shape = [jax.ShapeDtypeStruct((height, HD), jnp.bfloat16)] * groups
    else:
        out_shape = [jax.ShapeDtypeStruct((groups, height, HD), jnp.bfloat16)]
    scratch = [pltpu.VMEM((groups, height, HD), jnp.bfloat16)] if apart and not last else []
    return pl.pallas_call(
        functools.partial(combine_kernel, piece, last, len(parts)),
        out_shape=out_shape,
        in_specs=[pl.BlockSpec(memory_space=pltpu.SMEM)]
        + [pl.BlockSpec(memory_space=pltpu.VMEM)] * len(parts),
        out_specs=[pl.BlockSpec(memory_space=pltpu.VMEM)] * len(out_shape),
        scratch_shapes=scratch,
        compiler_params=pltpu.CompilerParams(vmem_limit_bytes=8 * MIB),
        cost_estimate=pl.CostEstimate(
            flops=2 * len(parts) * parts[0].size,
            bytes_accessed=len(parts) * parts[0].size * 2,
            transcendentals=0,
        ),
    )(me, *parts)


def reorder(shape, unit, valid, own, column):
    first, second = (0, 1) if column else (1, 0)
    block = lax.broadcasted_iota(jnp.int32, shape, second) // unit
    place = lax.broadcasted_iota(jnp.int32, shape, second) % unit
    target = (block ^ own) * valid + place
    match = (lax.broadcasted_iota(jnp.int32, shape, first) == target) & (place < valid)
    return match.astype(jnp.bfloat16)


def project_kernel(count, peers, me_ref, *refs):
    hidden_refs, (query_ref, keyval_ref), refs = refs[:count], refs[count : count + 2], refs[count + 2 :]
    out_refs, (full_ref,) = refs[:peers], refs[peers:]
    local, depth = hidden_refs[0].shape
    unit = up(local, 8)
    blocks = []
    for ref in hidden_refs:
        blocks.append(ref[...].astype(jnp.float32))
        if unit > local:
            blocks.append(jnp.zeros((unit - local, depth), jnp.float32))
    hidden = jnp.concatenate(blocks, axis=0).astype(jnp.bfloat16)
    order = reorder((count * local, count * unit), unit, local, me_ref[0], True)
    hidden = jnp.dot(order, hidden, preferred_element_type=jnp.float32).astype(jnp.bfloat16)
    full_ref[...] = jnp.dot(hidden, query_ref[...], preferred_element_type=jnp.float32)
    keyval = jnp.dot(hidden, keyval_ref[...], preferred_element_type=jnp.float32)
    for d, out_ref in enumerate(out_refs):
        start = pl.multiple_of((me_ref[1] ^ d) * HD, HD)
        out_ref[:, :HD] = full_ref[:, pl.ds(start, HD)]
        out_ref[:, HD:] = keyval


def pack_kernel(peers, *refs):
    own = refs[:peers]
    total = (own[0][...] + own[1][...]) + (own[2][...] + own[3][...])
    refs[-1][...] = jnp.concatenate([total, refs[peers][...]], axis=0).astype(jnp.bfloat16)


def unpack_kernel(count, rows, me_ref, *refs):
    part_refs, (query_ref, keyval_ref, tag_ref) = refs[:count], refs[count:]
    line = lax.broadcasted_iota(jnp.int32, (count, HD), 0)
    tags = jnp.zeros((count, HD), jnp.float32)
    for d, ref in enumerate(part_refs):
        source = me_ref[0] ^ d
        part = ref[...].astype(jnp.float32)
        query_ref[source] = part[:rows, :HD].astype(jnp.bfloat16)
        fill = jnp.zeros((keyval_ref.shape[0] - rows, HD), jnp.float32)
        block = jnp.concatenate([part[:rows, HD:], fill], axis=0).astype(jnp.bfloat16)
        keyval_ref[:, pl.ds(pl.multiple_of(source * HD, HD), HD)] = block
        tag = jnp.sum(jnp.where(line == me_ref[0], part[rows:, :HD], 0.0), axis=0, keepdims=True)
        tags = tags + jnp.where(line == source, tag, 0.0)
    tag_ref[...] = tags


def finish_kernel(count, peers, me_ref, *refs):
    part_refs, weight_ref, refs = refs[:count], refs[count], refs[count + 1 :]
    out_refs, (whole_ref,) = refs[:peers], refs[peers:]
    rows = whole_ref.shape[0]
    local = rows // peers
    unit = up(local, 16)
    for d, ref in enumerate(part_refs):
        start = pl.multiple_of((me_ref[0] ^ d) * HD, HD)
        whole_ref[:, pl.ds(start, HD)] = ref[...]
    order = reorder((peers * unit, rows), unit, local, me_ref[1], False)
    mixed = jnp.dot(order, whole_ref[...], preferred_element_type=jnp.float32)
    mixed = jnp.dot(mixed.astype(jnp.bfloat16), weight_ref[...], preferred_element_type=jnp.float32)
    for d, out_ref in enumerate(out_refs):
        out_ref[...] = mixed[d * unit : d * unit + local]


def in_vmem(kernel, out_shape, me, *args, scratch=()):
    head = [] if me is None else [me]
    return pl.pallas_call(
        kernel,
        out_shape=out_shape,
        in_specs=[pl.BlockSpec(memory_space=pltpu.SMEM)] * len(head)
        + [pl.BlockSpec(memory_space=pltpu.VMEM)] * len(args),
        out_specs=jax.tree.map(lambda _: pl.BlockSpec(memory_space=pltpu.VMEM), out_shape),
        scratch_shapes=scratch,
        compiler_params=pltpu.CompilerParams(vmem_limit_bytes=16 * MIB),
        cost_estimate=pl.CostEstimate(
            flops=0, bytes_accessed=sum(2 * arg.size for arg in args), transcendentals=0
        ),
    )(*head, *args)


def group_of(d, wide):
    return d if wide <= 8 else 1 + (d - 1) * 7 // (wide - 1)


def spread(block, axis):
    count = lax.axis_size(axis)
    return lax.all_to_all(
        jnp.broadcast_to(block[None], (count,) + block.shape),
        axis,
        split_axis=0,
        concat_axis=0,
        tiled=True,
    )


def on_device(hidden, w_query, w_keyval, w_out, pool, page_req, page_idx, lengths, moves, accepted):
    wide = lax.axis_size("wide")
    narrow = lax.axis_size("narrow")
    local_rows = hidden.shape[0]
    rows = local_rows * wide
    requests = rows // STEPS
    slots = pool.shape[0]
    capacity = slots // wide
    own_cols = w_query.shape[1] // narrow
    piece = HEADS * rows // (wide * narrow)
    extra = up(rows, HD)
    direct = piece == rows and own_cols == HD and wide == 8 and narrow == 4
    me = lax.axis_index("wide")
    both = jnp.stack([me, lax.axis_index("narrow")])
    exchange = functools.partial(lax.all_to_all, split_axis=0, concat_axis=0, tiled=True)

    def send(block, axis, d):
        return lax.ppermute(block, axis, [(i, i ^ d) for i in range(lax.axis_size(axis))])

    def share(block, axis):
        return [block] + [send(block, axis, d) for d in range(1, lax.axis_size(axis))]

    def deal(blocks, axis):
        return [blocks[0]] + [send(block, axis, d) for d, block in enumerate(blocks) if d]

    if direct:
        gathered = share(hidden, "wide")
    else:
        gathered = spread(hidden, "wide").reshape(rows, -1)

    dest = moves[:, 0]
    order = jnp.arange(slots, dtype=jnp.int32)
    rank = jnp.sum((dest[:, None] == dest[None, :]) & (order[None, :] < order[:, None]), axis=1)
    target = dest * capacity + rank
    chosen = target[None, :] == order[:, None]
    moved_to = (dest ^ me) * capacity + rank
    source_of = jnp.sum(
        jnp.where(moved_to[None, :] == order[:, None], order[None, :], 0), axis=1
    )
    sent_req = jnp.sum(jnp.where(chosen, page_req[None, :], 0), axis=1)
    sent_idx = jnp.sum(jnp.where(chosen, page_idx[None, :], 0), axis=1)
    moved_pool, *chunks = permute_pages(source_of, me.reshape(1), pool, wide * PARTS)
    arrived = {}
    flying = {}

    def members(groups):
        return [
            (d - 1) * PARTS + part
            for group, part in groups
            for d in range(1, wide)
            if group_of(d, wide) == group
        ]

    def launch(values, *groups):
        taken = members(groups)
        values, sent = lax.optimization_barrier((values, [chunks[c] for c in taken]))
        for c, chunk in zip(taken, sent):
            flying[c] = send(chunk, "wide", 1 + c // PARTS)
        return values

    def land(values, *groups):
        taken = members(groups)
        values, got = lax.optimization_barrier((values, [flying[c] for c in taken]))
        arrived.update(zip(taken, got))
        return values

    def beside(step, value, *groups):
        return land(step(launch(value, *groups)), *groups)

    def placed(pages):
        taken = sorted(arrived)
        place = jnp.stack([(me ^ (1 + c // PARTS)) * PARTS + c % PARTS for c in taken])
        pages = place_pages(place, [arrived[c] for c in taken], pages)
        arrived.clear()
        return pages

    shifted = sent_idx + 1
    tags = jnp.concatenate(
        [
            sent_req.reshape(wide, capacity),
            (shifted // 32).reshape(wide, capacity),
            (shifted % 32).reshape(wide, capacity),
        ],
        axis=1,
    )
    req_tok = jnp.broadcast_to(page_req[:, None], (slots, PAGE)).reshape(1, -1)
    pos_tok = (page_idx[:, None] * PAGE + jnp.arange(PAGE, dtype=jnp.int32)[None, :]).reshape(1, -1)
    row_info = jnp.stack(
        [
            jnp.asarray(np.arange(rows) // STEPS, jnp.int32),
            jnp.broadcast_to(lengths[:, None], (requests, STEPS)).reshape(rows),
        ],
        axis=1,
    )
    here = (me == 0) & (lax.axis_index("narrow") == 0)
    row_ids = np.arange(rows)[:, None]
    col_ids = np.arange(extra)[None, :]
    causal = (row_ids // STEPS == col_ids // STEPS) & (col_ids <= row_ids) & (col_ids < rows)
    new_bias = jnp.where(jnp.asarray(causal) & here, 0.0, NEG_FILL).astype(jnp.float32)
    tokens = pool.reshape(slots * PAGE, -1)
    window = {
        "project": ((6, 0),),
        "gather": ((6, 1),),
        "queries": ((7, 0), (2, 0)),
        "attend": ((7, 1), (2, 1), (1, 1)),
        "narrow": ((4, 0), (3, 0)),
        "wide": ((4, 1), (1, 0)),
        "attn": ((5, 0),),
        "finish": ((5, 1), (3, 1)),
    }

    if direct:
        block = jax.ShapeDtypeStruct((rows, 2 * HD), jnp.float32)
        partial = in_vmem(
            functools.partial(project_kernel, wide, narrow),
            [block] * narrow,
            both,
            *gathered,
            w_query,
            w_keyval,
            scratch=[pltpu.VMEM((rows, narrow * HD), jnp.float32)],
        )
        partial = beside(lambda value: deal(value, "narrow"), partial, *window["project"])
        tags = jnp.pad(tags.astype(jnp.float32), ((0, 0), (0, 2 * HD - tags.shape[1])))
        packed = in_vmem(
            functools.partial(pack_kernel, narrow),
            jax.ShapeDtypeStruct((rows + wide, 2 * HD), jnp.bfloat16),
            None,
            *partial,
            tags,
        )
        received = beside(lambda value: share(value, "wide"), packed, *window["gather"])
        queries, keyval, tags_in = in_vmem(
            functools.partial(unpack_kernel, wide, rows),
            [
                jax.ShapeDtypeStruct((wide, rows, HD), jnp.bfloat16),
                jax.ShapeDtypeStruct((extra, wide * HD), jnp.bfloat16),
                jax.ShapeDtypeStruct((wide, HD), jnp.float32),
            ],
            both,
            *received,
        )
        queries = beside(lambda value: share(value, "narrow"), queries, *window["queries"])
    else:
        query_part = jnp.dot(gathered, w_query, preferred_element_type=jnp.float32)
        keyval_part = jnp.dot(gathered, w_keyval, preferred_element_type=jnp.float32)
        query_part = jnp.transpose(query_part.reshape(rows, narrow, own_cols), (1, 0, 2))
        partial = jnp.concatenate(
            [query_part, jnp.broadcast_to(keyval_part[None], (narrow,) + keyval_part.shape)], axis=2
        )
        partial = beside(lambda value: exchange(value, "narrow"), partial, *window["project"])
        projected = jnp.sum(partial, axis=0).astype(jnp.bfloat16)
        tags = tags.astype(jnp.bfloat16)[:, None]
        tags = jnp.pad(tags, ((0, 0), (0, 7), (0, projected.shape[1] - tags.shape[2])))
        packed = jnp.broadcast_to(projected[None], (wide,) + projected.shape)
        packed = jnp.concatenate([packed, tags], axis=1)
        received = beside(lambda value: exchange(value, "wide"), packed, *window["gather"])
        tags_in = received[:, rows]
        queries = beside(
            lambda value: spread(value, "narrow"),
            received[:, :rows, :own_cols],
            *window["queries"],
        )
        queries = jnp.transpose(queries, (2, 1, 0, 3)).reshape(rows, HEADS, HD)
        queries = [jnp.transpose(queries, (1, 0, 2)).reshape(KVH, GROUPS * rows, HD)]
        keyval = jnp.transpose(received[:, :rows, own_cols:], (1, 0, 2)).reshape(rows, -1)
        keyval = jnp.pad(keyval, ((0, extra - rows), (0, 0)))

    parts = beside(
        lambda value: attend(
            both, value, keyval, tokens, req_tok, pos_tok, row_info, new_bias, rows, piece
        ),
        queries,
        *window["attend"],
    )
    if direct:
        parts = beside(lambda value: deal(value, "narrow"), parts, *window["narrow"])
        parts = combine(both, parts, piece, False, True)
        parts = beside(lambda value: deal(value, "wide"), parts, *window["wide"])
        (attn,) = combine(both, [part[None] for part in parts], piece, True, True)
        attn = beside(lambda value: share(value, "wide"), attn, *window["attn"])
        moved_pool = placed(moved_pool)
        sums = in_vmem(
            functools.partial(finish_kernel, wide, narrow),
            [jax.ShapeDtypeStruct((rows // narrow, w_out.shape[1]), jnp.float32)] * narrow,
            both,
            *attn,
            w_out,
            scratch=[pltpu.VMEM((rows, wide * HD), jnp.bfloat16)],
        )
        sums = beside(lambda value: deal(value, "narrow"), sums, *window["finish"])
        attended = ((sums[0] + sums[1]) + (sums[2] + sums[3])).astype(jnp.bfloat16)
    else:
        parts = beside(lambda value: exchange(value, "narrow"), parts[0], *window["narrow"])
        parts = parts.reshape((narrow, wide) + parts.shape[1:])
        (parts,) = combine(both, [parts[i] for i in range(narrow)], piece, False, False)
        parts = beside(lambda value: exchange(value, "wide"), parts, *window["wide"])
        (attn,) = combine(both, [parts[i][None] for i in range(wide)], piece, True, False)
        attn = beside(lambda value: spread(value, "wide"), attn, *window["attn"])
        moved_pool = placed(moved_pool)
        attn = jnp.transpose(attn.reshape(-1, rows, HD), (1, 0, 2)).reshape(rows, -1)
        sums = jnp.dot(attn, w_out, preferred_element_type=jnp.float32)
        sums = sums.reshape(narrow, rows // narrow, -1)
        sums = beside(lambda value: exchange(value, "narrow"), sums, *window["finish"])
        attended = jnp.sum(sums, axis=0).astype(jnp.bfloat16)
    moved_pool = placed(moved_pool)

    tags_in = tags_in.astype(jnp.int32)
    moved_req = tags_in[:, :capacity].reshape(slots)
    moved_idx = tags_in[:, capacity : 2 * capacity] * 32
    moved_idx = (moved_idx + tags_in[:, 2 * capacity : 3 * capacity] - 1).reshape(slots)
    local_req = local_rows // STEPS
    first_row = me * local_rows
    fresh = lax.dynamic_slice_in_dim(keyval, first_row, local_rows, 0)
    fresh = fresh.reshape(local_req, STEPS, -1)
    kept = lax.dynamic_slice_in_dim(accepted, me * local_req, local_req, 0)
    new_entries = jnp.where(
        jnp.arange(STEPS)[None, :, None] < kept[:, None, None], fresh, jnp.zeros((), jnp.bfloat16)
    )
    return (attended, new_entries, moved_pool, moved_req, moved_idx)


def solution(mesh):
    in_specs = (
        P("wide", "narrow"),
        P("narrow", "wide"),
        P("narrow", "wide"),
        P("narrow", "wide"),
        P(("wide", "narrow"), None, None),
        P(("wide", "narrow")),
        P(("wide", "narrow")),
        P(),
        P(("wide", "narrow"), None),
        P(),
    )
    out_specs = (
        P("narrow", "wide"),
        P("wide", None, None),
        P(("wide", "narrow"), None, None),
        P(("wide", "narrow")),
        P(("wide", "narrow")),
    )
    return jax.shard_map(
        on_device, mesh=mesh, in_specs=in_specs, out_specs=out_specs, check_vma=False
    )
```

```python
import functools
import math

import jax
import jax.numpy as jnp
import numpy as np
from jax import lax
from jax.experimental import pallas as pl
from jax.experimental.pallas import tpu as pltpu
from jax.sharding import PartitionSpec as P

HEADS = 32
KVH = 4
HD = 128
STEPS = 5
PAGE = 16
GROUPS = HEADS // KVH
NEG_FILL = -1e30
SCALE2 = math.log2(math.e) / math.sqrt(HD)
STAT = 16
MIB = 1024 * 1024
CUTS = {1: (0, 16), 2: (0, 8, 16), 3: (0, 8, 16), 4: (0, 6, 16), 5: (0, 10, 16), 6: (0, 6, 16), 7: (0, 6, 16)}
NT = (((1,), (1,)), ((), ()))


def up(value, unit):
    return -(-value // unit) * unit


def column(row):
    return jnp.transpose(jnp.broadcast_to(row, (row.shape[1], row.shape[1])))


def order_kernel(
    wide, parts, me_ref, dest_ref, req_ref, idx_ref, pool_ref, out_ref, tag_ref, *refs
):
    chunk_refs, refs = refs[: len(parts)], refs[len(parts) :]
    pages_ref, line_ref, source_ref, in_sem, out_sem, line_sem = refs
    slots = pool_ref.shape[0]
    capacity = slots // wide
    shape = (slots, slots)
    high = lax.broadcasted_iota(jnp.int32, shape, 0)
    low = lax.broadcasted_iota(jnp.int32, shape, 1)
    dest = dest_ref[...]
    same = column(dest.astype(jnp.float32)) == dest.astype(jnp.float32)
    rank = jnp.sum(jnp.where(same & (high < low), 1.0, 0.0), axis=0, keepdims=True)
    moved_to = ((dest ^ me_ref[0]) * capacity).astype(jnp.float32) + rank
    match = column(moved_to) == low.astype(jnp.float32)
    source = jnp.sum(jnp.where(match, high.astype(jnp.float32), 0.0), axis=0, keepdims=True)
    line_ref[...] = source.astype(jnp.int32)
    copy = pltpu.make_async_copy(line_ref, source_ref, line_sem)
    copy.start()
    copy.wait()

    blocks = [(0, capacity, out_ref.at[pl.ds(me_ref[0] * capacity, capacity)])]
    for (d, first, last), chunk in zip(parts, chunk_refs):
        blocks.append((d * capacity + first, last - first, chunk))
    for c, (first, count, _) in enumerate(blocks):

        def start(j, carry, c=c):
            page = source_ref[0, j]
            pltpu.make_async_copy(pool_ref.at[page], pages_ref.at[j], in_sem.at[c]).start()
            return carry

        lax.fori_loop(first, first + count, start, 0)

    shifted = idx_ref[...] + 1
    fields = (req_ref[...], shifted // 32, shifted % 32)
    rank_col = column(rank)
    lane = low.astype(jnp.float32)
    spread_out = jnp.zeros(shape, jnp.float32)
    for i, field in enumerate(fields):
        picked = lane == rank_col + float(i * capacity)
        spread_out = spread_out + jnp.where(picked, column(field.astype(jnp.float32)), 0.0)
    line = lax.broadcasted_iota(jnp.int32, (wide, slots), 0)
    chosen = jnp.where(line == dest, 1.0, 0.0).astype(jnp.bfloat16)
    tag_ref[...] = jnp.dot(
        chosen, spread_out.astype(jnp.bfloat16), preferred_element_type=jnp.float32
    )

    copies = []
    for c, (first, count, target) in enumerate(blocks):
        held = pages_ref.at[pl.ds(first, count)]
        pltpu.make_async_copy(pool_ref.at[pl.ds(0, count)], held, in_sem.at[c]).wait()
        copies.append(pltpu.make_async_copy(held, target, out_sem.at[c]))
        copies[-1].start()
    for copy in copies:
        copy.wait()


def order_pages(me, dest, page_req, page_idx, pool, wide, parts):
    slots = pool.shape[0]
    part = lambda count: jax.ShapeDtypeStruct((count,) + pool.shape[1:], pool.dtype)
    out_shape = [part(slots), jax.ShapeDtypeStruct((wide, slots), jnp.float32)]
    out_shape += [part(last - first) for _, first, last in parts]
    vmem = pl.BlockSpec(memory_space=pltpu.VMEM)
    hbm = pl.BlockSpec(memory_space=pltpu.HBM)
    return pl.pallas_call(
        functools.partial(order_kernel, wide, parts),
        out_shape=out_shape,
        in_specs=[pl.BlockSpec(memory_space=pltpu.SMEM), vmem, vmem, vmem, hbm],
        out_specs=[hbm, vmem] + [hbm] * len(parts),
        scratch_shapes=[
            pltpu.VMEM(pool.shape, pool.dtype),
            pltpu.VMEM((1, slots), jnp.int32),
            pltpu.SMEM((1, slots), jnp.int32),
            pltpu.SemaphoreType.DMA((1 + len(parts),)),
            pltpu.SemaphoreType.DMA((1 + len(parts),)),
            pltpu.SemaphoreType.DMA,
        ],
        compiler_params=pltpu.CompilerParams(vmem_limit_bytes=56 * MIB),
        cost_estimate=pl.CostEstimate(
            flops=0, bytes_accessed=2 * pool.size * 2, transcendentals=0
        ),
    )(me, dest.reshape(1, -1), page_req.reshape(1, -1), page_idx.reshape(1, -1), pool)


def place_kernel(place_ref, *refs):
    in_refs, (out_ref, sem) = refs[:-3], refs[-2:]
    copies = []
    for i, chunk in enumerate(in_refs):
        depth = chunk.shape[0]
        copies.append(
            pltpu.make_async_copy(
                chunk, out_ref.at[pl.ds(place_ref[i], depth)], sem.at[i]
            )
        )
    for copy in copies:
        copy.start()
    for copy in copies:
        copy.wait()


def place_pages(place, chunks, pages):
    count = len(chunks)
    return pl.pallas_call(
        place_kernel,
        out_shape=jax.ShapeDtypeStruct(pages.shape, pages.dtype),
        in_specs=[pl.BlockSpec(memory_space=pltpu.SMEM)]
        + [pl.BlockSpec(memory_space=pltpu.VMEM)] * count
        + [pl.BlockSpec(memory_space=pl.ANY)],
        out_specs=pl.BlockSpec(memory_space=pl.ANY),
        scratch_shapes=[pltpu.SemaphoreType.DMA((count,))],
        input_output_aliases={count + 1: 0},
        compiler_params=pltpu.CompilerParams(vmem_limit_bytes=2 * count * chunks[0].size + 2 * MIB),
        cost_estimate=pl.CostEstimate(
            flops=0, bytes_accessed=4 * count * chunks[0].size, transcendentals=0
        ),
    )(place, *chunks, pages)


def cut(value):
    return value.astype(jnp.bfloat16).astype(jnp.float32)


def split_stats(peak, total):
    high = cut(peak)
    mid = cut(peak - high)
    return high, mid, peak - high - mid, cut(total), total - cut(total)


def attend_kernel(rows, piece, peers, me_ref, *refs):
    query_refs, refs = refs[:peers], refs[peers:]
    key_ref, value_ref, new_key_ref, new_value_ref, req_ref, pos_ref, row_ref, new_bias_ref = refs[:8]
    out_refs = refs[8 : 8 + peers]
    bias_ref, score_ref, weight_ref, query_ref, result_ref = refs[8 + peers :]
    tokens = key_ref.shape[0]
    step = pl.program_id(0)

    @pl.when(step == 0)
    def _():
        seen = (req_ref[...] == row_ref[:, 0:1]) & (pos_ref[...] < row_ref[:, 1:2])
        bias_ref[...] = jnp.where(seen, 0.0, NEG_FILL)
        if peers > 1:
            for d in range(peers):
                query_ref[me_ref[1] ^ d] = query_refs[d][...]

    if peers > 1:
        per_step = query_refs[0].shape[0] // KVH
        query = jnp.concatenate(
            [
                query_ref[n, step * per_step + i].astype(jnp.float32)
                for i in range(per_step)
                for n in range(peers)
            ],
            axis=0,
        ).astype(jnp.bfloat16)
    else:
        query = query_refs[0][0]
    score_ref[:, :tokens] = lax.dot_general(
        query, key_ref[...], NT, preferred_element_type=jnp.float32
    )
    score_ref[:, tokens:] = lax.dot_general(
        query, new_key_ref[...], NT, preferred_element_type=jnp.float32
    )
    together = 1 if rows % 16 == 0 else 2
    span = together * rows
    peaks, totals = [], []
    for c in range(GROUPS // together):
        block = pl.ds(c * span, span)
        old = score_ref[block, :tokens].reshape(together, rows, tokens) * SCALE2 + bias_ref[...]
        new = score_ref[block, tokens:].reshape(together, rows, -1) * SCALE2 + new_bias_ref[...]
        peak = jnp.maximum(
            jnp.max(old, axis=-1, keepdims=True), jnp.max(new, axis=-1, keepdims=True)
        )
        old = jnp.exp2(old - peak)
        new = jnp.exp2(new - peak)
        totals.append(
            (jnp.sum(old, axis=-1, keepdims=True) + jnp.sum(new, axis=-1, keepdims=True)).reshape(
                span, 1
            )
        )
        peaks.append(peak.reshape(span, 1))
        weight_ref[block, :tokens] = old.reshape(span, tokens).astype(jnp.bfloat16)
        weight_ref[block, tokens:] = new.reshape(span, -1).astype(jnp.bfloat16)
    mixed = jnp.dot(
        weight_ref[:, :tokens], value_ref[...], preferred_element_type=jnp.float32
    ) + jnp.dot(weight_ref[:, tokens:], new_value_ref[...], preferred_element_type=jnp.float32)
    peak = jnp.concatenate(peaks, axis=0)
    total = jnp.concatenate(totals, axis=0)
    lane = lax.broadcasted_iota(jnp.int32, (GROUPS * rows, HD), 1)
    stats = jnp.zeros((GROUPS * rows, HD), jnp.float32)
    for i, part in enumerate(split_stats(peak, total)):
        stats = jnp.where(lane == i, part, stats)
    pick = (
        lax.broadcasted_iota(jnp.int32, (STAT, HD), 0)
        == lax.broadcasted_iota(jnp.int32, (STAT, HD), 1)
    ).astype(jnp.bfloat16)
    fill = result_ref.shape[1] - STAT - piece
    for c in range(GROUPS * rows // piece):
        part = slice(c * piece, (c + 1) * piece)
        turned = lax.dot_general(
            pick,
            jnp.concatenate(
                [stats[part], jnp.zeros((HD - piece, HD), jnp.float32)], axis=0
            ).astype(jnp.bfloat16),
            NT,
            preferred_element_type=jnp.float32,
        )
        result_ref[c] = jnp.concatenate(
            [turned, mixed[part], jnp.zeros((fill, HD), jnp.float32)], axis=0
        ).astype(jnp.bfloat16)
    if peers > 1:
        for d, out_ref in enumerate(out_refs):

            @pl.when((step ^ me_ref[1]) == d)
            def _():
                out_ref[...] = result_ref[...]
    else:
        out_refs[0][...] = result_ref[...]


def attend(me, queries, keyval, pool, req_tok, pos_tok, row_info, new_bias, rows, piece):
    tokens = pool.shape[0]
    extra = keyval.shape[0]
    peers = len(queries)
    pieces = GROUPS * rows // piece
    height = STAT + up(piece, 16)
    whole = lambda shape: pl.BlockSpec(shape, lambda k: (0,) * len(shape))
    if peers > 1:
        query_spec = whole(queries[0].shape)
        out_spec = whole((pieces, height, HD))
        out_shape = jax.ShapeDtypeStruct((pieces, height, HD), jnp.bfloat16)
    else:
        query_spec = pl.BlockSpec((1,) + queries[0].shape[1:], lambda k: (k, 0, 0))
        out_spec = pl.BlockSpec((pieces, height, HD), lambda k: (k, 0, 0))
        out_shape = jax.ShapeDtypeStruct((KVH * pieces, height, HD), jnp.bfloat16)
    return pl.pallas_call(
        functools.partial(attend_kernel, rows, piece, peers),
        grid=(KVH,),
        out_shape=[out_shape] * peers,
        in_specs=[pl.BlockSpec(memory_space=pltpu.SMEM)]
        + [query_spec] * peers
        + [
            pl.BlockSpec((tokens, HD), lambda k: (0, k)),
            pl.BlockSpec((tokens, HD), lambda k: (0, KVH + k)),
            pl.BlockSpec((extra, HD), lambda k: (0, k)),
            pl.BlockSpec((extra, HD), lambda k: (0, KVH + k)),
            whole(req_tok.shape),
            whole(pos_tok.shape),
            whole(row_info.shape),
            whole(new_bias.shape),
        ],
        out_specs=[out_spec] * peers,
        scratch_shapes=[
            pltpu.VMEM((rows, tokens), jnp.float32),
            pltpu.VMEM((GROUPS * rows, tokens + extra), jnp.float32),
            pltpu.VMEM((GROUPS * rows, tokens + extra), jnp.bfloat16),
            pltpu.VMEM((peers,) + queries[0].shape, jnp.bfloat16),
            pltpu.VMEM((pieces, height, HD), jnp.bfloat16),
        ],
        compiler_params=pltpu.CompilerParams(vmem_limit_bytes=56 * MIB),
        cost_estimate=pl.CostEstimate(
            flops=4 * HEADS * rows * (tokens + extra) * HD,
            bytes_accessed=pool.size * 2,
            transcendentals=HEADS * rows * (tokens + extra),
        ),
    )(me, *queries, pool, pool, keyval, keyval, req_tok, pos_tok, row_info, new_bias)


def combine_kernel(piece, last, count, *refs):
    part_refs, out_ref = refs[:count], refs[count]
    groups, height = part_refs[0].shape[:2]
    peaks, totals = [], []
    for i in range(count):
        for j in range(groups):
            stat = part_refs[i][j, :STAT, :].astype(jnp.float32)
            peaks.append(stat[0:1] + stat[1:2] + stat[2:3])
            totals.append(stat[3:4] + stat[4:5])
    peak = jnp.concatenate(peaks, axis=0).reshape(count, groups, HD)
    total = jnp.concatenate(totals, axis=0).reshape(count, groups, HD)
    top = jnp.max(peak, axis=0)
    lead = jnp.exp2(peak - top[None])
    whole = jnp.sum(lead * total, axis=0)
    if last:
        lane = lax.broadcasted_iota(jnp.int32, whole.shape, 1)
        lead = lead / jnp.where(lane < piece, whole, 1.0)[None]
    lead = lead.reshape(count * groups, HD)
    if (count * groups) % HD:
        fill = up(count * groups, HD) - count * groups
        lead = jnp.concatenate([lead, jnp.zeros((fill, HD), jnp.float32)], axis=0)
    lead = jnp.transpose(lead)
    rows = height - STAT
    for j in range(groups):
        result = jnp.zeros((rows, HD), jnp.float32)
        for i in range(count):
            c = i * groups + j
            result = result + lead[:rows, c : c + 1] * part_refs[i][j, STAT:, :].astype(jnp.float32)
        if last:
            for i in range(out_ref.shape[0]):
                out_ref[i] = result[:piece].astype(jnp.bfloat16)
        else:
            stats = split_stats(top[j : j + 1], whole[j : j + 1])
            rest = jnp.zeros((STAT - len(stats), HD), jnp.float32)
            out_ref[j] = jnp.concatenate([*stats, rest, result], axis=0).astype(jnp.bfloat16)


def combine(parts, piece, repeats=0):
    groups, height = parts[0].shape[:2]
    shape = (repeats, piece, HD) if repeats else (groups, height, HD)
    return pl.pallas_call(
        functools.partial(combine_kernel, piece, repeats > 0, len(parts)),
        out_shape=jax.ShapeDtypeStruct(shape, jnp.bfloat16),
        in_specs=[pl.BlockSpec(memory_space=pltpu.VMEM)] * len(parts),
        out_specs=pl.BlockSpec(memory_space=pltpu.VMEM),
        compiler_params=pltpu.CompilerParams(vmem_limit_bytes=8 * MIB),
        cost_estimate=pl.CostEstimate(
            flops=2 * len(parts) * parts[0].size,
            bytes_accessed=len(parts) * parts[0].size * 2,
            transcendentals=0,
        ),
    )(*parts)


def reorder(shape, unit, valid, own, column):
    first, second = (0, 1) if column else (1, 0)
    block = lax.broadcasted_iota(jnp.int32, shape, second) // unit
    place = lax.broadcasted_iota(jnp.int32, shape, second) % unit
    target = (block ^ own) * valid + place
    match = (lax.broadcasted_iota(jnp.int32, shape, first) == target) & (place < valid)
    return match.astype(jnp.bfloat16)


def project_kernel(peers, me_ref, hidden_ref, query_ref, keyval_ref, *refs):
    out_refs, (full_ref,) = refs[:peers], refs[peers:]
    count, local, depth = hidden_ref.shape
    unit = up(local, 8)
    blocks = []
    for i in range(count):
        blocks.append(hidden_ref[i].astype(jnp.float32))
        if unit > local:
            blocks.append(jnp.zeros((unit - local, depth), jnp.float32))
    hidden = jnp.concatenate(blocks, axis=0).astype(jnp.bfloat16)
    order = reorder((count * local, count * unit), unit, local, 0, True)
    hidden = jnp.dot(order, hidden, preferred_element_type=jnp.float32).astype(jnp.bfloat16)
    full_ref[...] = jnp.dot(hidden, query_ref[...], preferred_element_type=jnp.float32)
    keyval = jnp.dot(hidden, keyval_ref[...], preferred_element_type=jnp.float32)
    for d, out_ref in enumerate(out_refs):
        start = pl.multiple_of((me_ref[1] ^ d) * HD, HD)
        out_ref[:, :HD] = full_ref[:, pl.ds(start, HD)]
        out_ref[:, HD:] = keyval


def pack_kernel(peers, *refs):
    own, tag_ref, out_ref = refs[:peers], refs[peers], refs[peers + 1]
    total = (own[0][...] + own[1][...]) + (own[2][...] + own[3][...])
    tags = jnp.concatenate([tag_ref[...], jnp.zeros_like(tag_ref[...])], axis=1)
    packed = jnp.concatenate([total, tags], axis=0).astype(jnp.bfloat16)
    for i in range(out_ref.shape[0]):
        out_ref[i] = packed


def unpack_kernel(rows, me_ref, part_ref, query_ref, keyval_ref, tag_ref):
    count = part_ref.shape[0]
    line = lax.broadcasted_iota(jnp.int32, (count, HD), 0)
    tags = jnp.zeros((count, HD), jnp.float32)
    fill = jnp.zeros((keyval_ref.shape[0] - rows, HD), jnp.float32)
    for i in range(count):
        part = part_ref[i].astype(jnp.float32)
        query_ref[i] = part[:rows, :HD].astype(jnp.bfloat16)
        block = jnp.concatenate([part[:rows, HD:], fill], axis=0).astype(jnp.bfloat16)
        keyval_ref[:, i * HD : (i + 1) * HD] = block
        mine = jnp.where(line == me_ref[0], part[rows : rows + count, :HD], 0.0)
        tags = tags + jnp.where(line == i, jnp.sum(mine, axis=0, keepdims=True), 0.0)
    tag_ref[...] = tags


def finish_kernel(peers, me_ref, part_ref, weight_ref, *refs):
    count, rows = part_ref.shape[:2]
    local = rows // peers
    unit = up(local, 16)
    whole = jnp.concatenate([part_ref[i] for i in range(count)], axis=1)
    order = reorder((peers * unit, rows), unit, local, me_ref[1], False)
    mixed = jnp.dot(order, whole, preferred_element_type=jnp.float32)
    mixed = jnp.dot(mixed.astype(jnp.bfloat16), weight_ref[...], preferred_element_type=jnp.float32)
    for d, out_ref in enumerate(refs):
        out_ref[...] = mixed[d * unit : d * unit + local]


def in_vmem(kernel, out_shape, me, *args, scratch=()):
    head = [] if me is None else [me]
    return pl.pallas_call(
        kernel,
        out_shape=out_shape,
        in_specs=[pl.BlockSpec(memory_space=pltpu.SMEM)] * len(head)
        + [pl.BlockSpec(memory_space=pltpu.VMEM)] * len(args),
        out_specs=jax.tree.map(lambda _: pl.BlockSpec(memory_space=pltpu.VMEM), out_shape),
        scratch_shapes=scratch,
        compiler_params=pltpu.CompilerParams(vmem_limit_bytes=16 * MIB),
        cost_estimate=pl.CostEstimate(
            flops=0, bytes_accessed=sum(2 * arg.size for arg in args), transcendentals=0
        ),
    )(*head, *args)


def group_of(d, wide):
    return d if wide <= 8 else 1 + (d - 1) * 7 // (wide - 1)


def spread(block, axis):
    count = lax.axis_size(axis)
    return lax.all_to_all(
        jnp.broadcast_to(block[None], (count,) + block.shape),
        axis,
        split_axis=0,
        concat_axis=0,
        tiled=True,
    )


def on_device(hidden, w_query, w_keyval, w_out, pool, page_req, page_idx, lengths, moves, accepted):
    wide = lax.axis_size("wide")
    narrow = lax.axis_size("narrow")
    local_rows = hidden.shape[0]
    rows = local_rows * wide
    requests = rows // STEPS
    slots = pool.shape[0]
    capacity = slots // wide
    own_cols = w_query.shape[1] // narrow
    piece = HEADS * rows // (wide * narrow)
    extra = up(rows, HD)
    direct = piece == rows and own_cols == HD and wide == 8 and narrow == 4
    me = lax.axis_index("wide")
    both = jnp.stack([me, lax.axis_index("narrow")])
    exchange = functools.partial(lax.all_to_all, split_axis=0, concat_axis=0, tiled=True)

    def send(block, axis, d):
        return lax.ppermute(block, axis, [(i, i ^ d) for i in range(lax.axis_size(axis))])

    def share(block, axis):
        return [block] + [send(block, axis, d) for d in range(1, lax.axis_size(axis))]

    def deal(blocks, axis):
        return [blocks[0]] + [send(block, axis, d) for d, block in enumerate(blocks) if d]

    gathered = spread(hidden, "wide")

    parts = []
    for d in range(1, wide):
        cuts = [cut * capacity // 16 for cut in CUTS[group_of(d, wide)]]
        parts += [(d, a, b) for a, b in zip(cuts[:-1], cuts[1:]) if b > a]
    moved_pool, tags, *chunks = order_pages(
        both, moves, page_req, page_idx, pool, wide, parts
    )
    arrived = {}
    flying = {}

    def members(names):
        taken = []
        for group, which in names:
            cut = CUTS[group][which] * capacity // 16
            end = CUTS[group][which + 1] * capacity // 16
            taken += [
                c
                for c, (d, first, last) in enumerate(parts)
                if group_of(d, wide) == group and (first, last) == (cut, end)
            ]
        return taken

    def launch(values, *names):
        taken = members(names)
        values, sent = lax.optimization_barrier((values, [chunks[c] for c in taken]))
        for c, chunk in zip(taken, sent):
            flying[c] = send(chunk, "wide", parts[c][0])
        return values

    def land(values, *names):
        taken = members(names)
        values, got = lax.optimization_barrier((values, [flying[c] for c in taken]))
        arrived.update(zip(taken, got))
        return values

    def beside(step, value, *names):
        return land(step(launch(value, *names)), *names)

    def placed(pages):
        taken = sorted(arrived)
        place = jnp.stack([(me ^ parts[c][0]) * capacity + parts[c][1] for c in taken])
        pages = place_pages(place, [arrived[c] for c in taken], pages)
        arrived.clear()
        return pages

    req_tok = jnp.broadcast_to(page_req[:, None], (slots, PAGE)).reshape(1, -1)
    pos_tok = (page_idx[:, None] * PAGE + jnp.arange(PAGE, dtype=jnp.int32)[None, :]).reshape(1, -1)
    row_info = jnp.stack(
        [
            jnp.asarray(np.arange(rows) // STEPS, jnp.int32),
            jnp.broadcast_to(lengths[:, None], (requests, STEPS)).reshape(rows),
        ],
        axis=1,
    )
    here = (me == 0) & (lax.axis_index("narrow") == 0)
    row_ids = np.arange(rows)[:, None]
    col_ids = np.arange(extra)[None, :]
    causal = (row_ids // STEPS == col_ids // STEPS) & (col_ids <= row_ids) & (col_ids < rows)
    new_bias = jnp.where(jnp.asarray(causal) & here, 0.0, NEG_FILL).astype(jnp.float32)
    tokens = pool.reshape(slots * PAGE, -1)
    window = {
        "project": ((6, 0), (3, 0)),
        "gather": ((6, 1),),
        "queries": ((7, 0), (2, 0)),
        "attend": ((7, 1), (2, 1)),
        "narrow": ((4, 0), (1, 0)),
        "wide": ((4, 1),),
        "attn": ((5, 0),),
        "finish": ((5, 1), (3, 1)),
    }

    if direct:
        block = jax.ShapeDtypeStruct((rows, 2 * HD), jnp.float32)
        partial = in_vmem(
            functools.partial(project_kernel, narrow),
            [block] * narrow,
            both,
            gathered,
            w_query,
            w_keyval,
            scratch=[pltpu.VMEM((rows, narrow * HD), jnp.float32)],
        )
        partial = beside(lambda value: deal(value, "narrow"), partial, *window["project"])
        packed = in_vmem(
            functools.partial(pack_kernel, narrow),
            jax.ShapeDtypeStruct((wide, rows + wide, 2 * HD), jnp.bfloat16),
            None,
            *partial,
            tags,
        )
        received = beside(lambda value: exchange(value, "wide"), packed, *window["gather"])
        queries, keyval, tags_in = in_vmem(
            functools.partial(unpack_kernel, rows),
            [
                jax.ShapeDtypeStruct((wide, rows, HD), jnp.bfloat16),
                jax.ShapeDtypeStruct((extra, wide * HD), jnp.bfloat16),
                jax.ShapeDtypeStruct((wide, HD), jnp.float32),
            ],
            both,
            received,
        )
        queries = beside(lambda value: share(value, "narrow"), queries, *window["queries"])
    else:
        gathered = gathered.reshape(rows, -1)
        query_part = jnp.dot(gathered, w_query, preferred_element_type=jnp.float32)
        keyval_part = jnp.dot(gathered, w_keyval, preferred_element_type=jnp.float32)
        query_part = jnp.transpose(query_part.reshape(rows, narrow, own_cols), (1, 0, 2))
        partial = jnp.concatenate(
            [query_part, jnp.broadcast_to(keyval_part[None], (narrow,) + keyval_part.shape)], axis=2
        )
        partial = beside(lambda value: exchange(value, "narrow"), partial, *window["project"])
        projected = jnp.sum(partial, axis=0).astype(jnp.bfloat16)
        tags = tags[:, : 3 * capacity].astype(jnp.bfloat16)[:, None]
        tags = jnp.pad(tags, ((0, 0), (0, 7), (0, projected.shape[1] - tags.shape[2])))
        packed = jnp.broadcast_to(projected[None], (wide,) + projected.shape)
        packed = jnp.concatenate([packed, tags], axis=1)
        received = beside(lambda value: exchange(value, "wide"), packed, *window["gather"])
        tags_in = received[:, rows]
        queries = beside(
            lambda value: spread(value, "narrow"),
            received[:, :rows, :own_cols],
            *window["queries"],
        )
        queries = jnp.transpose(queries, (2, 1, 0, 3)).reshape(rows, HEADS, HD)
        queries = [jnp.transpose(queries, (1, 0, 2)).reshape(KVH, GROUPS * rows, HD)]
        keyval = jnp.transpose(received[:, :rows, own_cols:], (1, 0, 2)).reshape(rows, -1)
        keyval = jnp.pad(keyval, ((0, extra - rows), (0, 0)))

    tags_in = tags_in.astype(jnp.int32)
    moved_req = tags_in[:, :capacity].reshape(slots)
    moved_idx = tags_in[:, capacity : 2 * capacity] * 32
    moved_idx = (moved_idx + tags_in[:, 2 * capacity : 3 * capacity] - 1).reshape(slots)
    local_req = local_rows // STEPS
    first_row = me * local_rows
    fresh = lax.dynamic_slice_in_dim(keyval, first_row, local_rows, 0)
    fresh = fresh.reshape(local_req, STEPS, -1)
    kept = lax.dynamic_slice_in_dim(accepted, me * local_req, local_req, 0)
    new_entries = jnp.where(
        jnp.arange(STEPS)[None, :, None] < kept[:, None, None], fresh, jnp.zeros((), jnp.bfloat16)
    )
    mixed = beside(
        lambda value: attend(
            both, value, keyval, tokens, req_tok, pos_tok, row_info, new_bias, rows, piece
        ),
        queries,
        *window["attend"],
    )
    if direct:
        mixed = beside(lambda value: deal(value, "narrow"), mixed, *window["narrow"])
    else:
        mixed = beside(lambda value: exchange(value, "narrow"), mixed[0], *window["narrow"])
        mixed = mixed.reshape((narrow, wide) + mixed.shape[1:])
        mixed = [mixed[i] for i in range(narrow)]
    mixed = combine(mixed, piece)
    mixed, pages = lax.optimization_barrier((mixed, moved_pool))
    pages = placed(pages)
    mixed = beside(lambda value: exchange(value, "wide"), mixed, *window["wide"])
    mixed, moved_pool = lax.optimization_barrier((mixed, pages))
    attn = combine([mixed[i][None] for i in range(wide)], piece, wide)
    attn = beside(lambda value: exchange(value, "wide"), attn, *window["attn"])
    attn, new_entries, moved_req, moved_idx = lax.optimization_barrier(
        (attn, new_entries, moved_req, moved_idx)
    )
    if direct:
        sums = in_vmem(
            functools.partial(finish_kernel, narrow),
            [jax.ShapeDtypeStruct((rows // narrow, w_out.shape[1]), jnp.float32)] * narrow,
            both,
            attn,
            w_out,
        )
        sums = beside(lambda value: deal(value, "narrow"), sums, *window["finish"])
        attended = ((sums[0] + sums[1]) + (sums[2] + sums[3])).astype(jnp.bfloat16)
    else:
        attn = jnp.transpose(attn.reshape(-1, rows, HD), (1, 0, 2)).reshape(rows, -1)
        sums = jnp.dot(attn, w_out, preferred_element_type=jnp.float32)
        sums = sums.reshape(narrow, rows // narrow, -1)
        sums = beside(lambda value: exchange(value, "narrow"), sums, *window["finish"])
        attended = jnp.sum(sums, axis=0).astype(jnp.bfloat16)
    moved_pool = placed(moved_pool)
    return (attended, new_entries, moved_pool, moved_req, moved_idx)


def solution(mesh):
    in_specs = (
        P("wide", "narrow"),
        P("narrow", "wide"),
        P("narrow", "wide"),
        P("narrow", "wide"),
        P(("wide", "narrow"), None, None),
        P(("wide", "narrow")),
        P(("wide", "narrow")),
        P(),
        P(("wide", "narrow"), None),
        P(),
    )
    out_specs = (
        P("narrow", "wide"),
        P("wide", None, None),
        P(("wide", "narrow"), None, None),
        P(("wide", "narrow")),
        P(("wide", "narrow")),
    )
    return jax.shard_map(
        on_device, mesh=mesh, in_specs=in_specs, out_specs=out_specs, check_vma=False
    )
```

```python
import functools
import math

import jax
import jax.numpy as jnp
import numpy as np
from jax import lax
from jax.experimental import pallas as pl
from jax.experimental.pallas import tpu as pltpu
from jax.sharding import PartitionSpec as P

HEADS = 32
KVH = 4
HD = 128
STEPS = 5
PAGE = 16
GROUPS = HEADS // KVH
NEG_FILL = -1e30
SCALE2 = math.log2(math.e) / math.sqrt(HD)
STAT = 16
MIB = 1024 * 1024
CUTS = {1: (0, 8, 16), 2: (0, 16), 3: (0, 8, 16), 4: (0, 12, 16), 5: (0, 8, 16), 6: (0, 6, 16), 7: (0, 8, 16)}
NT = (((1,), (1,)), ((), ()))


def up(value, unit):
    return -(-value // unit) * unit


def column(row):
    return jnp.transpose(jnp.broadcast_to(row, (row.shape[1], row.shape[1])))


def order_kernel(
    wide, parts, me_ref, dest_ref, req_ref, idx_ref, pool_ref, out_ref, tag_ref, *refs
):
    chunk_refs, refs = refs[: len(parts)], refs[len(parts) :]
    pages_ref, line_ref, source_ref, in_sem, out_sem, line_sem = refs
    slots = pool_ref.shape[0]
    capacity = slots // wide
    shape = (slots, slots)
    high = lax.broadcasted_iota(jnp.int32, shape, 0)
    low = lax.broadcasted_iota(jnp.int32, shape, 1)
    dest = dest_ref[...]
    same = column(dest.astype(jnp.float32)) == dest.astype(jnp.float32)
    rank = jnp.sum(jnp.where(same & (high < low), 1.0, 0.0), axis=0, keepdims=True)
    moved_to = ((dest ^ me_ref[0]) * capacity).astype(jnp.float32) + rank
    match = column(moved_to) == low.astype(jnp.float32)
    source = jnp.sum(jnp.where(match, high.astype(jnp.float32), 0.0), axis=0, keepdims=True)
    line_ref[...] = source.astype(jnp.int32)
    copy = pltpu.make_async_copy(line_ref, source_ref, line_sem)
    copy.start()
    copy.wait()

    blocks = [(0, capacity, out_ref.at[pl.ds(me_ref[0] * capacity, capacity)])]
    for (d, first, last), chunk in zip(parts, chunk_refs):
        blocks.append((d * capacity + first, last - first, chunk))
    for c, (first, count, _) in enumerate(blocks):

        def start(j, carry, c=c):
            page = source_ref[0, j]
            pltpu.make_async_copy(pool_ref.at[page], pages_ref.at[j], in_sem.at[c]).start()
            return carry

        lax.fori_loop(first, first + count, start, 0)

    shifted = idx_ref[...] + 1
    fields = (req_ref[...], shifted // 32, shifted % 32)
    rank_col = column(rank)
    lane = low.astype(jnp.float32)
    spread_out = jnp.zeros(shape, jnp.float32)
    for i, field in enumerate(fields):
        picked = lane == rank_col + float(i * capacity)
        spread_out = spread_out + jnp.where(picked, column(field.astype(jnp.float32)), 0.0)
    line = lax.broadcasted_iota(jnp.int32, (wide, slots), 0)
    chosen = jnp.where(line == dest, 1.0, 0.0).astype(jnp.bfloat16)
    tag_ref[...] = jnp.dot(
        chosen, spread_out.astype(jnp.bfloat16), preferred_element_type=jnp.float32
    )

    copies = []
    for c, (first, count, target) in enumerate(blocks):
        held = pages_ref.at[pl.ds(first, count)]
        pltpu.make_async_copy(pool_ref.at[pl.ds(0, count)], held, in_sem.at[c]).wait()
        copies.append(pltpu.make_async_copy(held, target, out_sem.at[c]))
        copies[-1].start()
    for copy in copies:
        copy.wait()


def order_pages(me, dest, page_req, page_idx, pool, wide, parts):
    slots = pool.shape[0]
    part = lambda count: jax.ShapeDtypeStruct((count,) + pool.shape[1:], pool.dtype)
    out_shape = [part(slots), jax.ShapeDtypeStruct((wide, slots), jnp.float32)]
    out_shape += [part(last - first) for _, first, last in parts]
    vmem = pl.BlockSpec(memory_space=pltpu.VMEM)
    hbm = pl.BlockSpec(memory_space=pltpu.HBM)
    return pl.pallas_call(
        functools.partial(order_kernel, wide, parts),
        out_shape=out_shape,
        in_specs=[pl.BlockSpec(memory_space=pltpu.SMEM), vmem, vmem, vmem, hbm],
        out_specs=[hbm, vmem] + [hbm] * len(parts),
        scratch_shapes=[
            pltpu.VMEM(pool.shape, pool.dtype),
            pltpu.VMEM((1, slots), jnp.int32),
            pltpu.SMEM((1, slots), jnp.int32),
            pltpu.SemaphoreType.DMA((1 + len(parts),)),
            pltpu.SemaphoreType.DMA((1 + len(parts),)),
            pltpu.SemaphoreType.DMA,
        ],
        compiler_params=pltpu.CompilerParams(vmem_limit_bytes=56 * MIB),
        cost_estimate=pl.CostEstimate(
            flops=0, bytes_accessed=2 * pool.size * 2, transcendentals=0
        ),
    )(me, dest.reshape(1, -1), page_req.reshape(1, -1), page_idx.reshape(1, -1), pool)


def place_kernel(place_ref, *refs):
    in_refs, (out_ref, sem) = refs[:-3], refs[-2:]
    copies = []
    for i, chunk in enumerate(in_refs):
        depth = chunk.shape[0]
        copies.append(
            pltpu.make_async_copy(
                chunk, out_ref.at[pl.ds(place_ref[i], depth)], sem.at[i]
            )
        )
    for copy in copies:
        copy.start()
    for copy in copies:
        copy.wait()


def place_pages(place, chunks, pages):
    count = len(chunks)
    return pl.pallas_call(
        place_kernel,
        out_shape=jax.ShapeDtypeStruct(pages.shape, pages.dtype),
        in_specs=[pl.BlockSpec(memory_space=pltpu.SMEM)]
        + [pl.BlockSpec(memory_space=pltpu.VMEM)] * count
        + [pl.BlockSpec(memory_space=pl.ANY)],
        out_specs=pl.BlockSpec(memory_space=pl.ANY),
        scratch_shapes=[pltpu.SemaphoreType.DMA((count,))],
        input_output_aliases={count + 1: 0},
        compiler_params=pltpu.CompilerParams(vmem_limit_bytes=2 * count * chunks[0].size + 2 * MIB),
        cost_estimate=pl.CostEstimate(
            flops=0, bytes_accessed=4 * count * chunks[0].size, transcendentals=0
        ),
    )(place, *chunks, pages)


def cut(value):
    return value.astype(jnp.bfloat16).astype(jnp.float32)


def split_stats(peak, total):
    high = cut(peak)
    mid = cut(peak - high)
    return high, mid, peak - high - mid, cut(total), total - cut(total)


def attend_kernel(rows, piece, peers, me_ref, *refs):
    query_refs, refs = refs[:peers], refs[peers:]
    key_ref, value_ref, new_key_ref, new_value_ref, req_ref, pos_ref, row_ref, new_bias_ref = refs[:8]
    out_refs = refs[8 : 8 + peers]
    bias_ref, score_ref, weight_ref, query_ref, result_ref = refs[8 + peers :]
    tokens = key_ref.shape[0]
    step = pl.program_id(0)

    @pl.when(step == 0)
    def _():
        seen = (req_ref[...] == row_ref[:, 0:1]) & (pos_ref[...] < row_ref[:, 1:2])
        bias_ref[...] = jnp.where(seen, 0.0, NEG_FILL)
        if peers > 1:
            for d in range(peers):
                query_ref[me_ref[1] ^ d] = query_refs[d][...]

    if peers > 1:
        per_step = query_refs[0].shape[0] // KVH
        query = jnp.concatenate(
            [
                query_ref[n, step * per_step + i].astype(jnp.float32)
                for i in range(per_step)
                for n in range(peers)
            ],
            axis=0,
        ).astype(jnp.bfloat16)
    else:
        query = query_refs[0][0]
    score_ref[:, :tokens] = lax.dot_general(
        query, key_ref[...], NT, preferred_element_type=jnp.float32
    )
    score_ref[:, tokens:] = lax.dot_general(
        query, new_key_ref[...], NT, preferred_element_type=jnp.float32
    )
    together = 1 if rows % 16 == 0 else 2
    span = together * rows
    peaks, totals = [], []
    for c in range(GROUPS // together):
        block = pl.ds(c * span, span)
        old = score_ref[block, :tokens].reshape(together, rows, tokens) * SCALE2 + bias_ref[...]
        new = score_ref[block, tokens:].reshape(together, rows, -1) * SCALE2 + new_bias_ref[...]
        peak = jnp.maximum(
            jnp.max(old, axis=-1, keepdims=True), jnp.max(new, axis=-1, keepdims=True)
        )
        old = jnp.exp2(old - peak)
        new = jnp.exp2(new - peak)
        totals.append(
            (jnp.sum(old, axis=-1, keepdims=True) + jnp.sum(new, axis=-1, keepdims=True)).reshape(
                span, 1
            )
        )
        peaks.append(peak.reshape(span, 1))
        weight_ref[block, :tokens] = old.reshape(span, tokens).astype(jnp.bfloat16)
        weight_ref[block, tokens:] = new.reshape(span, -1).astype(jnp.bfloat16)
    mixed = jnp.dot(
        weight_ref[:, :tokens], value_ref[...], preferred_element_type=jnp.float32
    ) + jnp.dot(weight_ref[:, tokens:], new_value_ref[...], preferred_element_type=jnp.float32)
    peak = jnp.concatenate(peaks, axis=0)
    total = jnp.concatenate(totals, axis=0)
    lane = lax.broadcasted_iota(jnp.int32, (GROUPS * rows, HD), 1)
    stats = jnp.zeros((GROUPS * rows, HD), jnp.float32)
    for i, part in enumerate(split_stats(peak, total)):
        stats = jnp.where(lane == i, part, stats)
    pick = (
        lax.broadcasted_iota(jnp.int32, (STAT, HD), 0)
        == lax.broadcasted_iota(jnp.int32, (STAT, HD), 1)
    ).astype(jnp.bfloat16)
    fill = result_ref.shape[1] - STAT - piece
    for c in range(GROUPS * rows // piece):
        part = slice(c * piece, (c + 1) * piece)
        turned = lax.dot_general(
            pick,
            jnp.concatenate(
                [stats[part], jnp.zeros((HD - piece, HD), jnp.float32)], axis=0
            ).astype(jnp.bfloat16),
            NT,
            preferred_element_type=jnp.float32,
        )
        result_ref[c] = jnp.concatenate(
            [turned, mixed[part], jnp.zeros((fill, HD), jnp.float32)], axis=0
        ).astype(jnp.bfloat16)
    if peers > 1:
        for d, out_ref in enumerate(out_refs):

            @pl.when((step ^ me_ref[1]) == d)
            def _():
                out_ref[...] = result_ref[...]
    else:
        out_refs[0][...] = result_ref[...]


def attend(me, queries, keyval, pool, req_tok, pos_tok, row_info, new_bias, rows, piece):
    tokens = pool.shape[0]
    extra = keyval.shape[0]
    peers = len(queries)
    pieces = GROUPS * rows // piece
    height = STAT + up(piece, 16)
    whole = lambda shape: pl.BlockSpec(shape, lambda k: (0,) * len(shape))
    if peers > 1:
        query_spec = whole(queries[0].shape)
        out_spec = whole((pieces, height, HD))
        out_shape = jax.ShapeDtypeStruct((pieces, height, HD), jnp.bfloat16)
    else:
        query_spec = pl.BlockSpec((1,) + queries[0].shape[1:], lambda k: (k, 0, 0))
        out_spec = pl.BlockSpec((pieces, height, HD), lambda k: (k, 0, 0))
        out_shape = jax.ShapeDtypeStruct((KVH * pieces, height, HD), jnp.bfloat16)
    return pl.pallas_call(
        functools.partial(attend_kernel, rows, piece, peers),
        grid=(KVH,),
        out_shape=[out_shape] * peers,
        in_specs=[pl.BlockSpec(memory_space=pltpu.SMEM)]
        + [query_spec] * peers
        + [
            pl.BlockSpec((tokens, HD), lambda k: (0, k)),
            pl.BlockSpec((tokens, HD), lambda k: (0, KVH + k)),
            pl.BlockSpec((extra, HD), lambda k: (0, k)),
            pl.BlockSpec((extra, HD), lambda k: (0, KVH + k)),
            whole(req_tok.shape),
            whole(pos_tok.shape),
            whole(row_info.shape),
            whole(new_bias.shape),
        ],
        out_specs=[out_spec] * peers,
        scratch_shapes=[
            pltpu.VMEM((rows, tokens), jnp.float32),
            pltpu.VMEM((GROUPS * rows, tokens + extra), jnp.float32),
            pltpu.VMEM((GROUPS * rows, tokens + extra), jnp.bfloat16),
            pltpu.VMEM((peers,) + queries[0].shape, jnp.bfloat16),
            pltpu.VMEM((pieces, height, HD), jnp.bfloat16),
        ],
        compiler_params=pltpu.CompilerParams(vmem_limit_bytes=56 * MIB),
        cost_estimate=pl.CostEstimate(flops=0, bytes_accessed=0, transcendentals=0),
    )(me, *queries, pool, pool, keyval, keyval, req_tok, pos_tok, row_info, new_bias)


def combine_kernel(piece, last, count, *refs):
    part_refs, out_ref = refs[:count], refs[count]
    groups, height = part_refs[0].shape[:2]
    peaks, totals = [], []
    for i in range(count):
        for j in range(groups):
            stat = part_refs[i][j, :STAT, :].astype(jnp.float32)
            peaks.append(stat[0:1] + stat[1:2] + stat[2:3])
            totals.append(stat[3:4] + stat[4:5])
    peak = jnp.concatenate(peaks, axis=0).reshape(count, groups, HD)
    total = jnp.concatenate(totals, axis=0).reshape(count, groups, HD)
    top = jnp.max(peak, axis=0)
    lead = jnp.exp2(peak - top[None])
    whole = jnp.sum(lead * total, axis=0)
    if last:
        lane = lax.broadcasted_iota(jnp.int32, whole.shape, 1)
        lead = lead / jnp.where(lane < piece, whole, 1.0)[None]
    lead = lead.reshape(count * groups, HD)
    if (count * groups) % HD:
        fill = up(count * groups, HD) - count * groups
        lead = jnp.concatenate([lead, jnp.zeros((fill, HD), jnp.float32)], axis=0)
    lead = jnp.transpose(lead)
    rows = height - STAT
    for j in range(groups):
        result = jnp.zeros((rows, HD), jnp.float32)
        for i in range(count):
            c = i * groups + j
            result = result + lead[:rows, c : c + 1] * part_refs[i][j, STAT:, :].astype(jnp.float32)
        if last:
            for i in range(out_ref.shape[0]):
                out_ref[i] = result[:piece].astype(jnp.bfloat16)
        else:
            stats = split_stats(top[j : j + 1], whole[j : j + 1])
            rest = jnp.zeros((STAT - len(stats), HD), jnp.float32)
            out_ref[j] = jnp.concatenate([*stats, rest, result], axis=0).astype(jnp.bfloat16)


def combine(parts, piece, repeats=0):
    groups, height = parts[0].shape[:2]
    shape = (repeats, piece, HD) if repeats else (groups, height, HD)
    return pl.pallas_call(
        functools.partial(combine_kernel, piece, repeats > 0, len(parts)),
        out_shape=jax.ShapeDtypeStruct(shape, jnp.bfloat16),
        in_specs=[pl.BlockSpec(memory_space=pltpu.VMEM)] * len(parts),
        out_specs=pl.BlockSpec(memory_space=pltpu.VMEM),
        compiler_params=pltpu.CompilerParams(vmem_limit_bytes=8 * MIB),
        cost_estimate=pl.CostEstimate(
            flops=2 * len(parts) * parts[0].size,
            bytes_accessed=len(parts) * parts[0].size * 2,
            transcendentals=0,
        ),
    )(*parts)


def reorder(shape, unit, valid, own, column):
    first, second = (0, 1) if column else (1, 0)
    block = lax.broadcasted_iota(jnp.int32, shape, second) // unit
    place = lax.broadcasted_iota(jnp.int32, shape, second) % unit
    target = (block ^ own) * valid + place
    match = (lax.broadcasted_iota(jnp.int32, shape, first) == target) & (place < valid)
    return match.astype(jnp.bfloat16)


def project_kernel(peers, me_ref, hidden_ref, query_ref, keyval_ref, *refs):
    out_refs, (full_ref,) = refs[:peers], refs[peers:]
    count, local, depth = hidden_ref.shape
    unit = up(local, 8)
    blocks = []
    for i in range(count):
        blocks.append(hidden_ref[i].astype(jnp.float32))
        if unit > local:
            blocks.append(jnp.zeros((unit - local, depth), jnp.float32))
    hidden = jnp.concatenate(blocks, axis=0).astype(jnp.bfloat16)
    order = reorder((count * local, count * unit), unit, local, 0, True)
    hidden = jnp.dot(order, hidden, preferred_element_type=jnp.float32).astype(jnp.bfloat16)
    full_ref[...] = jnp.dot(hidden, query_ref[...], preferred_element_type=jnp.float32)
    keyval = jnp.dot(hidden, keyval_ref[...], preferred_element_type=jnp.float32)
    for d, out_ref in enumerate(out_refs):
        start = pl.multiple_of((me_ref[1] ^ d) * HD, HD)
        out_ref[:, :HD] = full_ref[:, pl.ds(start, HD)]
        out_ref[:, HD:] = keyval


def pack_kernel(peers, *refs):
    own, tag_ref, out_ref = refs[:peers], refs[peers], refs[peers + 1]
    total = (own[0][...] + own[1][...]) + (own[2][...] + own[3][...])
    tags = jnp.concatenate([tag_ref[...], jnp.zeros_like(tag_ref[...])], axis=1)
    packed = jnp.concatenate([total, tags], axis=0).astype(jnp.bfloat16)
    for i in range(out_ref.shape[0]):
        out_ref[i] = packed


def unpack_kernel(rows, me_ref, part_ref, query_ref, keyval_ref, tag_ref):
    count = part_ref.shape[0]
    line = lax.broadcasted_iota(jnp.int32, (count, HD), 0)
    tags = jnp.zeros((count, HD), jnp.float32)
    fill = jnp.zeros((keyval_ref.shape[0] - rows, HD), jnp.float32)
    for i in range(count):
        part = part_ref[i].astype(jnp.float32)
        query_ref[i] = part[:rows, :HD].astype(jnp.bfloat16)
        block = jnp.concatenate([part[:rows, HD:], fill], axis=0).astype(jnp.bfloat16)
        keyval_ref[:, i * HD : (i + 1) * HD] = block
        mine = jnp.where(line == me_ref[0], part[rows : rows + count, :HD], 0.0)
        tags = tags + jnp.where(line == i, jnp.sum(mine, axis=0, keepdims=True), 0.0)
    tag_ref[...] = tags


def finish_kernel(peers, me_ref, part_ref, weight_ref, *refs):
    count, rows = part_ref.shape[:2]
    local = rows // peers
    unit = up(local, 16)
    whole = jnp.concatenate([part_ref[i] for i in range(count)], axis=1)
    order = reorder((peers * unit, rows), unit, local, me_ref[1], False)
    mixed = jnp.dot(order, whole, preferred_element_type=jnp.float32)
    mixed = jnp.dot(mixed.astype(jnp.bfloat16), weight_ref[...], preferred_element_type=jnp.float32)
    for d, out_ref in enumerate(refs):
        out_ref[...] = mixed[d * unit : d * unit + local]


def in_vmem(kernel, out_shape, me, *args, scratch=()):
    head = [] if me is None else [me]
    return pl.pallas_call(
        kernel,
        out_shape=out_shape,
        in_specs=[pl.BlockSpec(memory_space=pltpu.SMEM)] * len(head)
        + [pl.BlockSpec(memory_space=pltpu.VMEM)] * len(args),
        out_specs=jax.tree.map(lambda _: pl.BlockSpec(memory_space=pltpu.VMEM), out_shape),
        scratch_shapes=scratch,
        compiler_params=pltpu.CompilerParams(vmem_limit_bytes=16 * MIB),
        cost_estimate=pl.CostEstimate(
            flops=0, bytes_accessed=sum(2 * arg.size for arg in args), transcendentals=0
        ),
    )(*head, *args)


def group_of(d, wide):
    return d if wide <= 8 else 1 + (d - 1) * 7 // (wide - 1)


def spread(block, axis):
    count = lax.axis_size(axis)
    return lax.all_to_all(
        jnp.broadcast_to(block[None], (count,) + block.shape),
        axis,
        split_axis=0,
        concat_axis=0,
        tiled=True,
    )


def on_device(hidden, w_query, w_keyval, w_out, pool, page_req, page_idx, lengths, moves, accepted):
    wide = lax.axis_size("wide")
    narrow = lax.axis_size("narrow")
    local_rows = hidden.shape[0]
    rows = local_rows * wide
    requests = rows // STEPS
    slots = pool.shape[0]
    capacity = slots // wide
    own_cols = w_query.shape[1] // narrow
    piece = HEADS * rows // (wide * narrow)
    extra = up(rows, HD)
    direct = piece == rows and own_cols == HD and wide == 8 and narrow == 4
    me = lax.axis_index("wide")
    both = jnp.stack([me, lax.axis_index("narrow")])
    exchange = functools.partial(lax.all_to_all, split_axis=0, concat_axis=0, tiled=True)

    def send(block, axis, d):
        return lax.ppermute(block, axis, [(i, i ^ d) for i in range(lax.axis_size(axis))])

    def share(block, axis):
        return [block] + [send(block, axis, d) for d in range(1, lax.axis_size(axis))]

    def deal(blocks, axis):
        return [blocks[0]] + [send(block, axis, d) for d, block in enumerate(blocks) if d]

    gathered = spread(hidden, "wide")

    parts = []
    for d in range(1, wide):
        cuts = [cut * capacity // 16 for cut in CUTS[group_of(d, wide)]]
        parts += [(d, a, b) for a, b in zip(cuts[:-1], cuts[1:]) if b > a]
    moved_pool, tags, *chunks = order_pages(
        both, moves, page_req, page_idx, pool, wide, parts
    )
    arrived = {}
    flying = {}

    def members(names):
        taken = []
        for group, which in names:
            cut = CUTS[group][which] * capacity // 16
            end = CUTS[group][which + 1] * capacity // 16
            taken += [
                c
                for c, (d, first, last) in enumerate(parts)
                if group_of(d, wide) == group and (first, last) == (cut, end)
            ]
        return taken

    def launch(values, *names):
        taken = members(names)
        values, sent = lax.optimization_barrier((values, [chunks[c] for c in taken]))
        for c, chunk in zip(taken, sent):
            flying[c] = send(chunk, "wide", parts[c][0])
        return values

    def land(values, *names):
        taken = members(names)
        values, got = lax.optimization_barrier((values, [flying[c] for c in taken]))
        arrived.update(zip(taken, got))
        return values

    def beside(step, value, *names):
        return land(step(launch(value, *names)), *names)

    def placed(pages):
        taken = sorted(arrived)
        place = jnp.stack([(me ^ parts[c][0]) * capacity + parts[c][1] for c in taken])
        pages = place_pages(place, [arrived[c] for c in taken], pages)
        arrived.clear()
        return pages

    def prepare(page_req, page_idx, lengths):
        req_tok = jnp.broadcast_to(page_req[:, None], (slots, PAGE)).reshape(1, -1)
        pos_tok = page_idx[:, None] * PAGE + jnp.arange(PAGE, dtype=jnp.int32)[None, :]
        row_info = jnp.stack(
            [
                jnp.asarray(np.arange(rows) // STEPS, jnp.int32),
                jnp.broadcast_to(lengths[:, None], (requests, STEPS)).reshape(rows),
            ],
            axis=1,
        )
        return req_tok, pos_tok.reshape(1, -1), row_info

    here = (me == 0) & (lax.axis_index("narrow") == 0)
    row_ids = np.arange(rows)[:, None]
    col_ids = np.arange(extra)[None, :]
    causal = (row_ids // STEPS == col_ids // STEPS) & (col_ids <= row_ids) & (col_ids < rows)
    new_bias = jnp.where(jnp.asarray(causal) & here, 0.0, NEG_FILL).astype(jnp.float32)
    tokens = pool.reshape(slots * PAGE, -1)
    if direct:
        block = jax.ShapeDtypeStruct((rows, 2 * HD), jnp.float32)
        partial = in_vmem(
            functools.partial(project_kernel, narrow),
            [block] * narrow,
            both,
            gathered,
            w_query,
            w_keyval,
            scratch=[pltpu.VMEM((rows, narrow * HD), jnp.float32)],
        )
        partial = beside(lambda value: deal(value, "narrow"), partial, (6, 0), (3, 0))
        packed = in_vmem(
            functools.partial(pack_kernel, narrow),
            jax.ShapeDtypeStruct((wide, rows + wide, 2 * HD), jnp.bfloat16),
            None,
            *partial,
            tags,
        )
        packed, raw = lax.optimization_barrier((packed, (page_req, page_idx, lengths)))
        received = exchange(packed, "wide")
        info = launch(prepare(*raw), (6, 1))
        queries, keyval, tags_in = in_vmem(
            functools.partial(unpack_kernel, rows),
            [
                jax.ShapeDtypeStruct((wide, rows, HD), jnp.bfloat16),
                jax.ShapeDtypeStruct((extra, wide * HD), jnp.bfloat16),
                jax.ShapeDtypeStruct((wide, HD), jnp.float32),
            ],
            both,
            received,
        )
        queries = share(launch(queries, (7, 0)), "narrow")
    else:
        gathered = gathered.reshape(rows, -1)
        query_part = jnp.dot(gathered, w_query, preferred_element_type=jnp.float32)
        keyval_part = jnp.dot(gathered, w_keyval, preferred_element_type=jnp.float32)
        query_part = jnp.transpose(query_part.reshape(rows, narrow, own_cols), (1, 0, 2))
        partial = jnp.concatenate(
            [query_part, jnp.broadcast_to(keyval_part[None], (narrow,) + keyval_part.shape)], axis=2
        )
        partial = beside(lambda value: exchange(value, "narrow"), partial, (6, 0), (3, 0))
        projected = jnp.sum(partial, axis=0).astype(jnp.bfloat16)
        tags = tags[:, : 3 * capacity].astype(jnp.bfloat16)[:, None]
        tags = jnp.pad(tags, ((0, 0), (0, 7), (0, projected.shape[1] - tags.shape[2])))
        packed = jnp.broadcast_to(projected[None], (wide,) + projected.shape)
        packed = jnp.concatenate([packed, tags], axis=1)
        packed, raw = lax.optimization_barrier((packed, (page_req, page_idx, lengths)))
        received = exchange(packed, "wide")
        info = launch(prepare(*raw), (6, 1))
        tags_in = received[:, rows]
        queries = spread(launch(received[:, :rows, :own_cols], (7, 0)), "narrow")
        queries = jnp.transpose(queries, (2, 1, 0, 3)).reshape(rows, HEADS, HD)
        queries = [jnp.transpose(queries, (1, 0, 2)).reshape(KVH, GROUPS * rows, HD)]
        keyval = jnp.transpose(received[:, :rows, own_cols:], (1, 0, 2)).reshape(rows, -1)
        keyval = jnp.pad(keyval, ((0, extra - rows), (0, 0)))

    def small_outputs(keyval, tags):
        tags = tags.astype(jnp.int32)
        moved_req = tags[:, :capacity].reshape(slots)
        moved_idx = tags[:, capacity : 2 * capacity] * 32
        moved_idx = (moved_idx + tags[:, 2 * capacity : 3 * capacity] - 1).reshape(slots)
        local_req = local_rows // STEPS
        fresh = lax.dynamic_slice_in_dim(keyval, me * local_rows, local_rows, 0)
        fresh = fresh.reshape(local_req, STEPS, -1)
        kept = lax.dynamic_slice_in_dim(accepted, me * local_req, local_req, 0)
        step_ids = jnp.arange(STEPS)[None, :, None]
        entries = jnp.where(step_ids < kept[:, None, None], fresh, jnp.zeros((), jnp.bfloat16))
        return entries, moved_req, moved_idx

    queries = launch(land(queries, (6, 1)), (2, 0))
    mixed = attend(both, queries, keyval, tokens, *info, new_bias, rows, piece)
    mixed = launch(land(mixed, (7, 0), (2, 0)), (7, 1), (3, 1))
    if direct:
        mixed = deal(mixed, "narrow")
    else:
        mixed = exchange(mixed[0], "narrow").reshape((narrow, wide) + mixed[0].shape[1:])
        mixed = [mixed[i] for i in range(narrow)]
    mixed = combine(land(mixed, (7, 1), (3, 1)), piece)
    mixed, moved_pool = lax.optimization_barrier((mixed, moved_pool))
    moved_pool = launch(placed(moved_pool), (4, 0), (1, 0))
    mixed = land(exchange(mixed, "wide"), (4, 0), (1, 0))
    attn = combine([mixed[i][None] for i in range(wide)], piece, wide)
    attn, raw = lax.optimization_barrier((attn, (keyval, tags_in)))
    attn = exchange(attn, "wide")
    small = launch(small_outputs(*raw), (5, 0), (4, 1), (1, 1))
    new_entries, moved_req, moved_idx = small
    attn = launch(land(attn, (5, 0), (4, 1), (1, 1)), (5, 1))
    if direct:
        sums = in_vmem(
            functools.partial(finish_kernel, narrow),
            [jax.ShapeDtypeStruct((rows // narrow, w_out.shape[1]), jnp.float32)] * narrow,
            both,
            attn,
            w_out,
        )
        sums = deal(sums, "narrow")
        attended = ((sums[0] + sums[1]) + (sums[2] + sums[3])).astype(jnp.bfloat16)
    else:
        attn = jnp.transpose(attn.reshape(-1, rows, HD), (1, 0, 2)).reshape(rows, -1)
        sums = jnp.dot(attn, w_out, preferred_element_type=jnp.float32)
        sums = sums.reshape(narrow, rows // narrow, -1)
        sums = exchange(sums, "narrow")
        attended = jnp.sum(sums, axis=0).astype(jnp.bfloat16)
    attended = land(attended, (5, 1))
    moved_pool = placed(moved_pool)
    return (attended, new_entries, moved_pool, moved_req, moved_idx)


def solution(mesh):
    in_specs = (
        P("wide", "narrow"),
        P("narrow", "wide"),
        P("narrow", "wide"),
        P("narrow", "wide"),
        P(("wide", "narrow"), None, None),
        P(("wide", "narrow")),
        P(("wide", "narrow")),
        P(),
        P(("wide", "narrow"), None),
        P(),
    )
    out_specs = (
        P("narrow", "wide"),
        P("wide", None, None),
        P(("wide", "narrow"), None, None),
        P(("wide", "narrow")),
        P(("wide", "narrow")),
    )
    return jax.shard_map(
        on_device, mesh=mesh, in_specs=in_specs, out_specs=out_specs, check_vma=False
    )
```

```python
import functools
import math

import jax
import jax.numpy as jnp
from jax import lax
from jax.experimental import pallas as pl
from jax.experimental.pallas import tpu as pltpu
from jax.sharding import PartitionSpec as P

HEADS = 32
KVH = 4
HD = 128
STEPS = 5
PAGE = 16
GROUPS = HEADS // KVH
NEG_FILL = -1e30
SCALE2 = math.log2(math.e) / math.sqrt(HD)
STAT = 16
MIB = 1024 * 1024
CUTS = {1: (0, 8, 16), 2: (0, 16), 3: (0, 8, 16), 4: (0, 16), 5: (0, 10, 16), 6: (0, 4, 16), 7: (0, 4, 11, 16)}
NT = (((1,), (1,)), ((), ()))


def up(value, unit):
    return -(-value // unit) * unit


def column(row):
    return jnp.transpose(jnp.broadcast_to(row, (row.shape[1], row.shape[1])))


def order_kernel(
    wide, parts, me_ref, dest_ref, req_ref, idx_ref, pool_ref, out_ref, tag_ref, token_ref, *refs
):
    chunk_refs, refs = refs[: len(parts)], refs[len(parts) :]
    pages_ref, line_ref, source_ref, in_sem, out_sem, line_sem = refs
    slots = pool_ref.shape[0]
    capacity = slots // wide
    shape = (slots, slots)
    high = lax.broadcasted_iota(jnp.int32, shape, 0)
    low = lax.broadcasted_iota(jnp.int32, shape, 1)
    dest = dest_ref[...]
    same = column(dest.astype(jnp.float32)) == dest.astype(jnp.float32)
    rank = jnp.sum(jnp.where(same & (high < low), 1.0, 0.0), axis=0, keepdims=True)
    moved_to = ((dest ^ me_ref[0]) * capacity).astype(jnp.float32) + rank
    match = column(moved_to) == low.astype(jnp.float32)
    source = jnp.sum(jnp.where(match, high.astype(jnp.float32), 0.0), axis=0, keepdims=True)
    line_ref[...] = source.astype(jnp.int32)
    copy = pltpu.make_async_copy(line_ref, source_ref, line_sem)
    copy.start()
    copy.wait()

    blocks = [(0, capacity, out_ref.at[pl.ds(me_ref[0] * capacity, capacity)])]
    for (d, first, last), chunk in zip(parts, chunk_refs):
        blocks.append((d * capacity + first, last - first, chunk))
    for c, (first, count, _) in enumerate(blocks):

        def start(j, carry, c=c):
            page = source_ref[0, j]
            pltpu.make_async_copy(pool_ref.at[page], pages_ref.at[j], in_sem.at[c]).start()
            return carry

        lax.fori_loop(first, first + count, start, 0)

    shifted = idx_ref[...] + 1
    fields = (req_ref[...], shifted // 32, shifted % 32)
    rank_col = column(rank)
    lane = low.astype(jnp.float32)
    spread_out = jnp.zeros(shape, jnp.float32)
    for i, field in enumerate(fields):
        picked = lane == rank_col + float(i * capacity)
        spread_out = spread_out + jnp.where(picked, column(field.astype(jnp.float32)), 0.0)
    line = lax.broadcasted_iota(jnp.int32, (wide, slots), 0)
    chosen = jnp.where(line == dest, 1.0, 0.0).astype(jnp.bfloat16)
    tag_ref[...] = jnp.dot(
        chosen, spread_out.astype(jnp.bfloat16), preferred_element_type=jnp.float32
    )

    tokens = slots * PAGE
    page = lax.broadcasted_iota(jnp.int32, (slots, tokens), 0)
    token = lax.broadcasted_iota(jnp.int32, (slots, tokens), 1)
    widen = jnp.where(page == token // PAGE, 1.0, 0.0).astype(jnp.bfloat16)
    row = lax.broadcasted_iota(jnp.int32, (8, slots), 0)
    stacked = jnp.zeros((8, slots), jnp.float32)
    for i, field in enumerate(fields):
        stacked = jnp.where(row == i, field.astype(jnp.float32), stacked)
    token_ref[...] = jnp.dot(
        stacked.astype(jnp.bfloat16), widen, preferred_element_type=jnp.float32
    )

    copies = []
    for c, (first, count, target) in enumerate(blocks):
        held = pages_ref.at[pl.ds(first, count)]
        pltpu.make_async_copy(pool_ref.at[pl.ds(0, count)], held, in_sem.at[c]).wait()
        copies.append(pltpu.make_async_copy(held, target, out_sem.at[c]))
        copies[-1].start()
    for copy in copies:
        copy.wait()


def order_pages(me, dest, page_req, page_idx, pool, wide, parts):
    slots = pool.shape[0]
    part = lambda count: jax.ShapeDtypeStruct((count,) + pool.shape[1:], pool.dtype)
    out_shape = [part(slots), jax.ShapeDtypeStruct((wide, slots), jnp.float32)]
    out_shape += [jax.ShapeDtypeStruct((8, slots * PAGE), jnp.float32)]
    out_shape += [part(last - first) for _, first, last in parts]
    vmem = pl.BlockSpec(memory_space=pltpu.VMEM)
    hbm = pl.BlockSpec(memory_space=pltpu.HBM)
    return pl.pallas_call(
        functools.partial(order_kernel, wide, parts),
        out_shape=out_shape,
        in_specs=[pl.BlockSpec(memory_space=pltpu.SMEM), vmem, vmem, vmem, hbm],
        out_specs=[hbm, vmem, vmem] + [hbm] * len(parts),
        scratch_shapes=[
            pltpu.VMEM(pool.shape, pool.dtype),
            pltpu.VMEM((1, slots), jnp.int32),
            pltpu.SMEM((1, slots), jnp.int32),
            pltpu.SemaphoreType.DMA((1 + len(parts),)),
            pltpu.SemaphoreType.DMA((1 + len(parts),)),
            pltpu.SemaphoreType.DMA,
        ],
        compiler_params=pltpu.CompilerParams(vmem_limit_bytes=56 * MIB),
        cost_estimate=pl.CostEstimate(
            flops=0, bytes_accessed=2 * pool.size * 2, transcendentals=0
        ),
    )(me, dest.reshape(1, -1), page_req.reshape(1, -1), page_idx.reshape(1, -1), pool)


def place_kernel(place_ref, *refs):
    in_refs, (out_ref, sem) = refs[:-3], refs[-2:]
    copies = []
    for i, chunk in enumerate(in_refs):
        depth = chunk.shape[0]
        copies.append(
            pltpu.make_async_copy(
                chunk, out_ref.at[pl.ds(place_ref[i], depth)], sem.at[i]
            )
        )
    for copy in copies:
        copy.start()
    for copy in copies:
        copy.wait()


def place_pages(place, chunks, pages):
    count = len(chunks)
    return pl.pallas_call(
        place_kernel,
        out_shape=jax.ShapeDtypeStruct(pages.shape, pages.dtype),
        in_specs=[pl.BlockSpec(memory_space=pltpu.SMEM)]
        + [pl.BlockSpec(memory_space=pltpu.VMEM)] * count
        + [pl.BlockSpec(memory_space=pl.ANY)],
        out_specs=pl.BlockSpec(memory_space=pl.ANY),
        scratch_shapes=[pltpu.SemaphoreType.DMA((count,))],
        input_output_aliases={count + 1: 0},
        compiler_params=pltpu.CompilerParams(vmem_limit_bytes=2 * count * chunks[0].size + 2 * MIB),
        cost_estimate=pl.CostEstimate(
            flops=0, bytes_accessed=4 * count * chunks[0].size, transcendentals=0
        ),
    )(place, *chunks, pages)


def cut(value):
    return value.astype(jnp.bfloat16).astype(jnp.float32)


def split_stats(peak, total):
    high = cut(peak)
    mid = cut(peak - high)
    return high, mid, peak - high - mid, cut(total), total - cut(total)


def attend_kernel(rows, piece, peers, me_ref, length_ref, *refs):
    query_refs, refs = refs[:peers], refs[peers:]
    key_ref, value_ref, new_key_ref, new_value_ref, token_ref = refs[:5]
    out_refs = refs[5 : 5 + peers]
    bias_ref, new_bias_ref, score_ref, weight_ref, query_ref, result_ref = refs[5 + peers :]
    tokens = key_ref.shape[0]
    step = pl.program_id(0)

    @pl.when(step == 0)
    def _():
        owner = token_ref[0:1, :]
        offset = lax.broadcasted_iota(jnp.int32, owner.shape, 1) % PAGE
        spot = (token_ref[1:2, :] * 32 + token_ref[2:3, :] - 1) * PAGE + offset.astype(jnp.float32)
        request = lax.broadcasted_iota(jnp.int32, (rows, 1), 0) // STEPS
        limit = jnp.zeros((rows, 1), jnp.int32)
        for r in range(rows // STEPS):
            limit = jnp.where(request == r, length_ref[r], limit)
        seen = (owner == request.astype(jnp.float32)) & (spot < limit.astype(jnp.float32))
        bias_ref[...] = jnp.where(seen, 0.0, NEG_FILL)
        row = lax.broadcasted_iota(jnp.int32, new_bias_ref.shape, 0)
        col = lax.broadcasted_iota(jnp.int32, new_bias_ref.shape, 1)
        first = jnp.where((me_ref[0] == 0) & (me_ref[1] == 0), 1, 0)
        seen = (row // STEPS == col // STEPS) & (col <= row) & (col < rows * first)
        new_bias_ref[...] = jnp.where(seen, 0.0, NEG_FILL)
        if peers > 1:
            for d in range(peers):
                query_ref[me_ref[1] ^ d] = query_refs[d][...]

    if peers > 1:
        per_step = query_refs[0].shape[0] // KVH
        query = jnp.concatenate(
            [
                query_ref[n, step * per_step + i].astype(jnp.float32)
                for i in range(per_step)
                for n in range(peers)
            ],
            axis=0,
        ).astype(jnp.bfloat16)
    else:
        query = query_refs[0][0]
    score_ref[:, :tokens] = lax.dot_general(
        query, key_ref[...], NT, preferred_element_type=jnp.float32
    )
    score_ref[:, tokens:] = lax.dot_general(
        query, new_key_ref[...], NT, preferred_element_type=jnp.float32
    )
    together = 1 if rows % 16 == 0 else 2
    span = together * rows
    peaks, totals = [], []
    for c in range(GROUPS // together):
        block = pl.ds(c * span, span)
        old = score_ref[block, :tokens].reshape(together, rows, tokens) * SCALE2 + bias_ref[...]
        new = score_ref[block, tokens:].reshape(together, rows, -1) * SCALE2 + new_bias_ref[...]
        peak = jnp.maximum(
            jnp.max(old, axis=-1, keepdims=True), jnp.max(new, axis=-1, keepdims=True)
        )
        old = jnp.exp2(old - peak)
        new = jnp.exp2(new - peak)
        totals.append(
            (jnp.sum(old, axis=-1, keepdims=True) + jnp.sum(new, axis=-1, keepdims=True)).reshape(
                span, 1
            )
        )
        peaks.append(peak.reshape(span, 1))
        weight_ref[block, :tokens] = old.reshape(span, tokens).astype(jnp.bfloat16)
        weight_ref[block, tokens:] = new.reshape(span, -1).astype(jnp.bfloat16)
    mixed = jnp.dot(
        weight_ref[:, :tokens], value_ref[...], preferred_element_type=jnp.float32
    ) + jnp.dot(weight_ref[:, tokens:], new_value_ref[...], preferred_element_type=jnp.float32)
    peak = jnp.concatenate(peaks, axis=0)
    total = jnp.concatenate(totals, axis=0)
    lane = lax.broadcasted_iota(jnp.int32, (GROUPS * rows, HD), 1)
    stats = jnp.zeros((GROUPS * rows, HD), jnp.float32)
    for i, part in enumerate(split_stats(peak, total)):
        stats = jnp.where(lane == i, part, stats)
    pick = (
        lax.broadcasted_iota(jnp.int32, (STAT, HD), 0)
        == lax.broadcasted_iota(jnp.int32, (STAT, HD), 1)
    ).astype(jnp.bfloat16)
    fill = result_ref.shape[1] - STAT - piece
    for c in range(GROUPS * rows // piece):
        part = slice(c * piece, (c + 1) * piece)
        turned = lax.dot_general(
            pick,
            jnp.concatenate(
                [stats[part], jnp.zeros((HD - piece, HD), jnp.float32)], axis=0
            ).astype(jnp.bfloat16),
            NT,
            preferred_element_type=jnp.float32,
        )
        result_ref[c] = jnp.concatenate(
            [turned, mixed[part], jnp.zeros((fill, HD), jnp.float32)], axis=0
        ).astype(jnp.bfloat16)
    if peers > 1:
        for d, out_ref in enumerate(out_refs):

            @pl.when((step ^ me_ref[1]) == d)
            def _():
                out_ref[...] = result_ref[...]
    else:
        out_refs[0][...] = result_ref[...]


def attend(me, lengths, queries, keyval, pool, token_info, rows, piece):
    tokens = pool.shape[0]
    extra = keyval.shape[0]
    peers = len(queries)
    pieces = GROUPS * rows // piece
    height = STAT + up(piece, 16)
    whole = lambda shape: pl.BlockSpec(shape, lambda k: (0,) * len(shape))
    if peers > 1:
        query_spec = whole(queries[0].shape)
        out_spec = whole((pieces, height, HD))
        out_shape = jax.ShapeDtypeStruct((pieces, height, HD), jnp.bfloat16)
    else:
        query_spec = pl.BlockSpec((1,) + queries[0].shape[1:], lambda k: (k, 0, 0))
        out_spec = pl.BlockSpec((pieces, height, HD), lambda k: (k, 0, 0))
        out_shape = jax.ShapeDtypeStruct((KVH * pieces, height, HD), jnp.bfloat16)
    return pl.pallas_call(
        functools.partial(attend_kernel, rows, piece, peers),
        grid=(KVH,),
        out_shape=[out_shape] * peers,
        in_specs=[pl.BlockSpec(memory_space=pltpu.SMEM)] * 2
        + [query_spec] * peers
        + [
            pl.BlockSpec((tokens, HD), lambda k: (0, k)),
            pl.BlockSpec((tokens, HD), lambda k: (0, KVH + k)),
            pl.BlockSpec((extra, HD), lambda k: (0, k)),
            pl.BlockSpec((extra, HD), lambda k: (0, KVH + k)),
            whole(token_info.shape),
        ],
        out_specs=[out_spec] * peers,
        scratch_shapes=[
            pltpu.VMEM((rows, tokens), jnp.float32),
            pltpu.VMEM((rows, extra), jnp.float32),
            pltpu.VMEM((GROUPS * rows, tokens + extra), jnp.float32),
            pltpu.VMEM((GROUPS * rows, tokens + extra), jnp.bfloat16),
            pltpu.VMEM((peers,) + queries[0].shape, jnp.bfloat16),
            pltpu.VMEM((pieces, height, HD), jnp.bfloat16),
        ],
        compiler_params=pltpu.CompilerParams(vmem_limit_bytes=56 * MIB),
        cost_estimate=pl.CostEstimate(flops=0, bytes_accessed=0, transcendentals=0),
    )(me, lengths, *queries, pool, pool, keyval, keyval, token_info)


def combine_kernel(piece, last, count, *refs):
    if last:
        part_ref, out_ref = refs
        part_refs = [part_ref.at[pl.ds(i, 1)] for i in range(count)]
    else:
        part_refs, out_ref = refs[:count], refs[count]
    groups, height = part_refs[0].shape[:2]
    peaks, totals = [], []
    for i in range(count):
        for j in range(groups):
            stat = part_refs[i][j, :STAT, :].astype(jnp.float32)
            peaks.append(stat[0:1] + stat[1:2] + stat[2:3])
            totals.append(stat[3:4] + stat[4:5])
    peak = jnp.concatenate(peaks, axis=0).reshape(count, groups, HD)
    total = jnp.concatenate(totals, axis=0).reshape(count, groups, HD)
    top = jnp.max(peak, axis=0)
    lead = jnp.exp2(peak - top[None])
    whole = jnp.sum(lead * total, axis=0)
    if last:
        lane = lax.broadcasted_iota(jnp.int32, whole.shape, 1)
        lead = lead / jnp.where(lane < piece, whole, 1.0)[None]
    lead = lead.reshape(count * groups, HD)
    if (count * groups) % HD:
        fill = up(count * groups, HD) - count * groups
        lead = jnp.concatenate([lead, jnp.zeros((fill, HD), jnp.float32)], axis=0)
    lead = jnp.transpose(lead)
    rows = height - STAT
    for j in range(groups):
        result = jnp.zeros((rows, HD), jnp.float32)
        for i in range(count):
            c = i * groups + j
            result = result + lead[:rows, c : c + 1] * part_refs[i][j, STAT:, :].astype(jnp.float32)
        if last:
            for i in range(out_ref.shape[0]):
                out_ref[i] = result[:piece].astype(jnp.bfloat16)
        else:
            stats = split_stats(top[j : j + 1], whole[j : j + 1])
            rest = jnp.zeros((STAT - len(stats), HD), jnp.float32)
            out_ref[j] = jnp.concatenate([*stats, rest, result], axis=0).astype(jnp.bfloat16)


def combine(parts, piece, repeats=0):
    count = parts[0].shape[0] if repeats else len(parts)
    shape = (repeats, piece, HD) if repeats else parts[0].shape
    return pl.pallas_call(
        functools.partial(combine_kernel, piece, repeats > 0, count),
        out_shape=jax.ShapeDtypeStruct(shape, jnp.bfloat16),
        in_specs=[pl.BlockSpec(memory_space=pltpu.VMEM)] * len(parts),
        out_specs=pl.BlockSpec(memory_space=pltpu.VMEM),
        compiler_params=pltpu.CompilerParams(vmem_limit_bytes=8 * MIB),
        cost_estimate=pl.CostEstimate(
            flops=2 * len(parts) * parts[0].size,
            bytes_accessed=len(parts) * parts[0].size * 2,
            transcendentals=0,
        ),
    )(*parts)


def reorder(shape, unit, valid, own, column):
    first, second = (0, 1) if column else (1, 0)
    block = lax.broadcasted_iota(jnp.int32, shape, second) // unit
    place = lax.broadcasted_iota(jnp.int32, shape, second) % unit
    target = (block ^ own) * valid + place
    match = (lax.broadcasted_iota(jnp.int32, shape, first) == target) & (place < valid)
    return match.astype(jnp.bfloat16)


def project_kernel(peers, me_ref, hidden_ref, query_ref, keyval_ref, *refs):
    out_refs, (full_ref,) = refs[:peers], refs[peers:]
    count, local, depth = hidden_ref.shape
    unit = up(local, 8)
    blocks = []
    for i in range(count):
        blocks.append(hidden_ref[i].astype(jnp.float32))
        if unit > local:
            blocks.append(jnp.zeros((unit - local, depth), jnp.float32))
    hidden = jnp.concatenate(blocks, axis=0).astype(jnp.bfloat16)
    order = reorder((count * local, count * unit), unit, local, 0, True)
    hidden = jnp.dot(order, hidden, preferred_element_type=jnp.float32).astype(jnp.bfloat16)
    full_ref[...] = jnp.dot(hidden, query_ref[...], preferred_element_type=jnp.float32)
    keyval = jnp.dot(hidden, keyval_ref[...], preferred_element_type=jnp.float32)
    for d, out_ref in enumerate(out_refs):
        start = pl.multiple_of((me_ref[1] ^ d) * HD, HD)
        out_ref[:, :HD] = full_ref[:, pl.ds(start, HD)]
        out_ref[:, HD:] = keyval


def pack_kernel(peers, *refs):
    own, tag_ref, out_ref = refs[:peers], refs[peers], refs[peers + 1]
    total = (own[0][...] + own[1][...]) + (own[2][...] + own[3][...])
    tags = jnp.concatenate([tag_ref[...], jnp.zeros_like(tag_ref[...])], axis=1)
    packed = jnp.concatenate([total, tags], axis=0).astype(jnp.bfloat16)
    for i in range(out_ref.shape[0]):
        out_ref[i] = packed


def unpack_kernel(rows, me_ref, kept_ref, part_ref, query_ref, keyval_ref, *refs):
    entry_ref, req_ref, idx_ref = refs
    count = part_ref.shape[0]
    line = lax.broadcasted_iota(jnp.int32, (count, HD), 0)
    tags = jnp.zeros((count, HD), jnp.float32)
    fill = jnp.zeros((keyval_ref.shape[0] - rows, HD), jnp.float32)
    for i in range(count):
        part = part_ref[i].astype(jnp.float32)
        query_ref[i] = part[:rows, :HD].astype(jnp.bfloat16)
        block = jnp.concatenate([part[:rows, HD:], fill], axis=0).astype(jnp.bfloat16)
        keyval_ref[:, i * HD : (i + 1) * HD] = block
        mine = jnp.where(line == me_ref[0], part[rows : rows + count, :HD], 0.0)
        tags = tags + jnp.where(line == i, jnp.sum(mine, axis=0, keepdims=True), 0.0)
    capacity = HD // count
    high = lax.broadcasted_iota(jnp.int32, (HD, HD), 0)
    low = lax.broadcasted_iota(jnp.int32, (HD, HD), 1)
    slot = lax.broadcasted_iota(jnp.int32, (count, HD), 1)
    tags = tags.astype(jnp.bfloat16)
    fields = []
    for i in range(3):
        pick = jnp.where(high == i * capacity + low % capacity, 1.0, 0.0).astype(jnp.bfloat16)
        spread_out = jnp.dot(tags, pick, preferred_element_type=jnp.float32)
        spread_out = jnp.where(slot // capacity == line, spread_out, 0.0)
        fields.append(jnp.sum(spread_out, axis=0, keepdims=True))
    req_ref[...] = fields[0].astype(jnp.int32)
    idx_ref[...] = (fields[1] * 32.0 + fields[2] - 1.0).astype(jnp.int32)
    local = entry_ref.shape[1]
    step = lax.broadcasted_iota(jnp.int32, (16, keyval_ref.shape[0]), 0)
    row = lax.broadcasted_iota(jnp.int32, (16, keyval_ref.shape[0]), 1)
    kept = (row == me_ref[0] * local + step) & (step < kept_ref[me_ref[0]])
    kept = jnp.where(kept, 1.0, 0.0).astype(jnp.bfloat16)
    entries = jnp.dot(kept, keyval_ref[...], preferred_element_type=jnp.float32)
    entry_ref[0] = entries[:local].astype(jnp.bfloat16)


def finish_kernel(peers, me_ref, part_ref, weight_ref, *refs):
    count, rows = part_ref.shape[:2]
    local = rows // peers
    unit = up(local, 16)
    whole = jnp.concatenate([part_ref[i] for i in range(count)], axis=1)
    order = reorder((peers * unit, rows), unit, local, me_ref[1], False)
    mixed = jnp.dot(order, whole, preferred_element_type=jnp.float32)
    mixed = jnp.dot(mixed.astype(jnp.bfloat16), weight_ref[...], preferred_element_type=jnp.float32)
    for d, out_ref in enumerate(refs):
        out_ref[...] = mixed[d * unit : d * unit + local]


def in_vmem(kernel, out_shape, me, *args, scratch=()):
    head = [] if me is None else list(me) if isinstance(me, tuple) else [me]
    return pl.pallas_call(
        kernel,
        out_shape=out_shape,
        in_specs=[pl.BlockSpec(memory_space=pltpu.SMEM)] * len(head)
        + [pl.BlockSpec(memory_space=pltpu.VMEM)] * len(args),
        out_specs=jax.tree.map(lambda _: pl.BlockSpec(memory_space=pltpu.VMEM), out_shape),
        scratch_shapes=scratch,
        compiler_params=pltpu.CompilerParams(vmem_limit_bytes=16 * MIB),
        cost_estimate=pl.CostEstimate(
            flops=0, bytes_accessed=sum(2 * arg.size for arg in args), transcendentals=0
        ),
    )(*head, *args)


def group_of(d, wide):
    return d if wide <= 8 else 1 + (d - 1) * 7 // (wide - 1)


def spread(block, axis):
    count = lax.axis_size(axis)
    return lax.all_to_all(
        jnp.broadcast_to(block[None], (count,) + block.shape),
        axis,
        split_axis=0,
        concat_axis=0,
        tiled=True,
    )


def on_device(hidden, w_query, w_keyval, w_out, pool, page_req, page_idx, lengths, moves, accepted):
    wide = lax.axis_size("wide")
    narrow = lax.axis_size("narrow")
    local_rows = hidden.shape[0]
    rows = local_rows * wide
    requests = rows // STEPS
    slots = pool.shape[0]
    capacity = slots // wide
    own_cols = w_query.shape[1] // narrow
    piece = HEADS * rows // (wide * narrow)
    extra = up(rows, HD)
    direct = piece == rows and own_cols == HD and slots == HD
    direct = direct and wide == 8 and narrow == 4 and local_rows == STEPS
    me = lax.axis_index("wide")
    both = jnp.stack([me, lax.axis_index("narrow")])
    exchange = functools.partial(lax.all_to_all, split_axis=0, concat_axis=0, tiled=True)

    def send(block, axis, d):
        return lax.ppermute(block, axis, [(i, i ^ d) for i in range(lax.axis_size(axis))])

    def share(block, axis):
        return [block] + [send(block, axis, d) for d in range(1, lax.axis_size(axis))]

    def deal(blocks, axis):
        return [blocks[0]] + [send(block, axis, d) for d, block in enumerate(blocks) if d]

    gathered = spread(hidden, "wide")

    parts = []
    for d in range(1, wide):
        cuts = [cut * capacity // 16 for cut in CUTS[group_of(d, wide)]]
        parts += [(d, a, b) for a, b in zip(cuts[:-1], cuts[1:]) if b > a]
    moved_pool, tags, token_info, *chunks = order_pages(
        both, moves, page_req, page_idx, pool, wide, parts
    )
    arrived = {}
    flying = {}

    def members(names):
        taken = []
        for group, which in names:
            cut = CUTS[group][which] * capacity // 16
            end = CUTS[group][which + 1] * capacity // 16
            taken += [
                c
                for c, (d, first, last) in enumerate(parts)
                if group_of(d, wide) == group and (first, last) == (cut, end)
            ]
        return taken

    def launch(values, *names):
        taken = members(names)
        values, sent = lax.optimization_barrier((values, [chunks[c] for c in taken]))
        for c, chunk in zip(taken, sent):
            flying[c] = send(chunk, "wide", parts[c][0])
        return values

    def land(values, *names):
        taken = members(names)
        values, got = lax.optimization_barrier((values, [flying[c] for c in taken]))
        arrived.update(zip(taken, got))
        return values

    def beside(step, value, *names):
        return land(step(launch(value, *names)), *names)

    def placed(pages):
        taken = sorted(arrived)
        place = jnp.stack([(me ^ parts[c][0]) * capacity + parts[c][1] for c in taken])
        pages = place_pages(place, [arrived[c] for c in taken], pages)
        arrived.clear()
        return pages

    tokens = pool.reshape(slots * PAGE, -1)
    if direct:
        block = jax.ShapeDtypeStruct((rows, 2 * HD), jnp.float32)
        partial = in_vmem(
            functools.partial(project_kernel, narrow),
            [block] * narrow,
            both,
            gathered,
            w_query,
            w_keyval,
            scratch=[pltpu.VMEM((rows, narrow * HD), jnp.float32)],
        )
        partial = beside(lambda value: deal(value, "narrow"), partial, (6, 0), (3, 0))
        packed = in_vmem(
            functools.partial(pack_kernel, narrow),
            jax.ShapeDtypeStruct((wide, rows + wide, 2 * HD), jnp.bfloat16),
            None,
            *partial,
            tags,
        )
        received = beside(lambda value: exchange(value, "wide"), packed, (6, 1))
        queries, keyval, new_entries, moved_req, moved_idx = in_vmem(
            functools.partial(unpack_kernel, rows),
            [
                jax.ShapeDtypeStruct((wide, rows, HD), jnp.bfloat16),
                jax.ShapeDtypeStruct((extra, wide * HD), jnp.bfloat16),
                jax.ShapeDtypeStruct((1, local_rows, wide * HD), jnp.bfloat16),
                jax.ShapeDtypeStruct((1, slots), jnp.int32),
                jax.ShapeDtypeStruct((1, slots), jnp.int32),
            ],
            (both, accepted),
            received,
        )
        moved_req, moved_idx = moved_req.reshape(slots), moved_idx.reshape(slots)
        queries = beside(lambda value: share(value, "narrow"), queries, (7, 0), (1, 0))
    else:
        gathered = gathered.reshape(rows, -1)
        query_part = jnp.dot(gathered, w_query, preferred_element_type=jnp.float32)
        keyval_part = jnp.dot(gathered, w_keyval, preferred_element_type=jnp.float32)
        query_part = jnp.transpose(query_part.reshape(rows, narrow, own_cols), (1, 0, 2))
        partial = jnp.concatenate(
            [query_part, jnp.broadcast_to(keyval_part[None], (narrow,) + keyval_part.shape)], axis=2
        )
        partial = beside(lambda value: exchange(value, "narrow"), partial, (6, 0), (3, 0))
        projected = jnp.sum(partial, axis=0).astype(jnp.bfloat16)
        tags = tags[:, : 3 * capacity].astype(jnp.bfloat16)[:, None]
        tags = jnp.pad(tags, ((0, 0), (0, 7), (0, projected.shape[1] - tags.shape[2])))
        packed = jnp.broadcast_to(projected[None], (wide,) + projected.shape)
        packed = jnp.concatenate([packed, tags], axis=1)
        received = beside(lambda value: exchange(value, "wide"), packed, (6, 1))
        tags_in = received[:, rows]
        queries = received[:, :rows, :own_cols]
        queries = beside(lambda value: spread(value, "narrow"), queries, (7, 0), (1, 0))
        queries = jnp.transpose(queries, (2, 1, 0, 3)).reshape(rows, HEADS, HD)
        queries = [jnp.transpose(queries, (1, 0, 2)).reshape(KVH, GROUPS * rows, HD)]
        keyval = jnp.transpose(received[:, :rows, own_cols:], (1, 0, 2)).reshape(rows, -1)
        keyval = jnp.pad(keyval, ((0, extra - rows), (0, 0)))
        tags_in = tags_in.astype(jnp.int32)
        moved_req = tags_in[:, :capacity].reshape(slots)
        moved_idx = tags_in[:, capacity : 2 * capacity] * 32
        moved_idx = (moved_idx + tags_in[:, 2 * capacity : 3 * capacity] - 1).reshape(slots)
        local_req = local_rows // STEPS
        fresh = lax.dynamic_slice_in_dim(keyval, me * local_rows, local_rows, 0)
        fresh = fresh.reshape(local_req, STEPS, -1)
        kept = lax.dynamic_slice_in_dim(accepted, me * local_req, local_req, 0)
        step_ids = jnp.arange(STEPS)[None, :, None]
        new_entries = jnp.where(
            step_ids < kept[:, None, None], fresh, jnp.zeros((), jnp.bfloat16)
        )

    mixed = beside(
        lambda value: attend(both, lengths, value, keyval, tokens, token_info, rows, piece),
        queries,
        (7, 1),
        (2, 0),
    )
    if direct:
        mixed = beside(lambda value: deal(value, "narrow"), mixed, (7, 2), (3, 1))
    else:
        mixed = beside(lambda value: exchange(value, "narrow"), mixed[0], (7, 2), (3, 1))
        mixed = mixed.reshape((narrow, wide) + mixed.shape[1:])
        mixed = [mixed[i] for i in range(narrow)]
    mixed = combine(mixed, piece)
    mixed, pages = lax.optimization_barrier((mixed, moved_pool))
    pages = placed(pages)
    mixed = beside(lambda value: exchange(value, "wide"), mixed, (4, 0))
    mixed, moved_pool = lax.optimization_barrier((mixed, pages))
    attn = combine([mixed], piece, wide)
    attn = beside(lambda value: exchange(value, "wide"), attn, (5, 0))
    if direct:
        sums = in_vmem(
            functools.partial(finish_kernel, narrow),
            [jax.ShapeDtypeStruct((rows // narrow, w_out.shape[1]), jnp.float32)] * narrow,
            both,
            attn,
            w_out,
        )
        sums = beside(lambda value: deal(value, "narrow"), sums, (5, 1), (1, 1))
        attended = ((sums[0] + sums[1]) + (sums[2] + sums[3])).astype(jnp.bfloat16)
    else:
        attn = jnp.transpose(attn.reshape(-1, rows, HD), (1, 0, 2)).reshape(rows, -1)
        sums = jnp.dot(attn, w_out, preferred_element_type=jnp.float32)
        sums = sums.reshape(narrow, rows // narrow, -1)
        sums = beside(lambda value: exchange(value, "narrow"), sums, (5, 1), (1, 1))
        attended = jnp.sum(sums, axis=0).astype(jnp.bfloat16)
    moved_pool = placed(moved_pool)
    return (attended, new_entries, moved_pool, moved_req, moved_idx)


def solution(mesh):
    in_specs = (
        P("wide", "narrow"),
        P("narrow", "wide"),
        P("narrow", "wide"),
        P("narrow", "wide"),
        P(("wide", "narrow"), None, None),
        P(("wide", "narrow")),
        P(("wide", "narrow")),
        P(),
        P(("wide", "narrow"), None),
        P(),
    )
    out_specs = (
        P("narrow", "wide"),
        P("wide", None, None),
        P(("wide", "narrow"), None, None),
        P(("wide", "narrow")),
        P(("wide", "narrow")),
    )
    return jax.shard_map(
        on_device, mesh=mesh, in_specs=in_specs, out_specs=out_specs, check_vma=False
    )
```

```python
import functools
import math

import jax
import jax.numpy as jnp
from jax import lax
from jax.experimental import pallas as pl
from jax.experimental.pallas import tpu as pltpu
from jax.sharding import PartitionSpec as P

HEADS = 32
KVH = 4
HD = 128
STEPS = 5
PAGE = 16
GROUPS = HEADS // KVH
NEG_FILL = -1e30
SCALE2 = math.log2(math.e) / math.sqrt(HD)
STAT = 16
MIB = 1024 * 1024
CUTS = {1: (0, 8, 16), 2: (0, 7, 16), 3: (0, 5, 16), 4: (0, 13, 16), 5: (0, 10, 16), 6: (0, 4, 16), 7: (0, 4, 11, 16)}
NT = (((1,), (1,)), ((), ()))


def up(value, unit):
    return -(-value // unit) * unit


def column(row):
    return jnp.transpose(jnp.broadcast_to(row, (row.shape[1], row.shape[1])))


def order_kernel(
    wide, parts, me_ref, dest_ref, req_ref, idx_ref, pool_ref, out_ref, tag_ref, token_ref, *refs
):
    chunk_refs, refs = refs[: len(parts)], refs[len(parts) :]
    pages_ref, line_ref, source_ref, in_sem, out_sem, line_sem = refs
    slots = pool_ref.shape[0]
    capacity = slots // wide
    shape = (slots, slots)
    high = lax.broadcasted_iota(jnp.int32, shape, 0)
    low = lax.broadcasted_iota(jnp.int32, shape, 1)
    dest = dest_ref[...]
    same = column(dest.astype(jnp.float32)) == dest.astype(jnp.float32)
    rank = jnp.sum(jnp.where(same & (high < low), 1.0, 0.0), axis=0, keepdims=True)
    moved_to = ((dest ^ me_ref[0]) * capacity).astype(jnp.float32) + rank
    match = column(moved_to) == low.astype(jnp.float32)
    source = jnp.sum(jnp.where(match, high.astype(jnp.float32), 0.0), axis=0, keepdims=True)
    line_ref[...] = source.astype(jnp.int32)
    copy = pltpu.make_async_copy(line_ref, source_ref, line_sem)
    copy.start()
    copy.wait()

    blocks = [(0, capacity, out_ref.at[pl.ds(me_ref[0] * capacity, capacity)])]
    for (d, first, last), chunk in zip(parts, chunk_refs):
        blocks.append((d * capacity + first, last - first, chunk))
    for c, (first, count, _) in enumerate(blocks):

        def start(j, carry, c=c):
            page = source_ref[0, j]
            pltpu.make_async_copy(pool_ref.at[page], pages_ref.at[j], in_sem.at[c]).start()
            return carry

        lax.fori_loop(first, first + count, start, 0)

    shifted = idx_ref[...] + 1
    fields = (req_ref[...], shifted // 32, shifted % 32)
    rank_col = column(rank)
    lane = low.astype(jnp.float32)
    spread_out = jnp.zeros(shape, jnp.float32)
    for i, field in enumerate(fields):
        picked = lane == rank_col + float(i * capacity)
        spread_out = spread_out + jnp.where(picked, column(field.astype(jnp.float32)), 0.0)
    line = lax.broadcasted_iota(jnp.int32, (wide, slots), 0)
    chosen = jnp.where(line == dest, 1.0, 0.0).astype(jnp.bfloat16)
    tag_ref[...] = jnp.dot(
        chosen, spread_out.astype(jnp.bfloat16), preferred_element_type=jnp.float32
    )

    tokens = slots * PAGE
    page = lax.broadcasted_iota(jnp.int32, (slots, tokens), 0)
    token = lax.broadcasted_iota(jnp.int32, (slots, tokens), 1)
    widen = jnp.where(page == token // PAGE, 1.0, 0.0).astype(jnp.bfloat16)
    row = lax.broadcasted_iota(jnp.int32, (8, slots), 0)
    stacked = jnp.zeros((8, slots), jnp.float32)
    for i, field in enumerate(fields):
        stacked = jnp.where(row == i, field.astype(jnp.float32), stacked)
    token_ref[...] = jnp.dot(
        stacked.astype(jnp.bfloat16), widen, preferred_element_type=jnp.float32
    )

    copies = []
    for c, (first, count, target) in enumerate(blocks):
        held = pages_ref.at[pl.ds(first, count)]
        pltpu.make_async_copy(pool_ref.at[pl.ds(0, count)], held, in_sem.at[c]).wait()
        copies.append(pltpu.make_async_copy(held, target, out_sem.at[c]))
        copies[-1].start()
    for copy in copies:
        copy.wait()


def order_pages(me, dest, page_req, page_idx, pool, wide, parts):
    slots = pool.shape[0]
    part = lambda count: jax.ShapeDtypeStruct((count,) + pool.shape[1:], pool.dtype)
    out_shape = [part(slots), jax.ShapeDtypeStruct((wide, slots), jnp.float32)]
    out_shape += [jax.ShapeDtypeStruct((8, slots * PAGE), jnp.float32)]
    out_shape += [part(last - first) for _, first, last in parts]
    vmem = pl.BlockSpec(memory_space=pltpu.VMEM)
    hbm = pl.BlockSpec(memory_space=pltpu.HBM)
    return pl.pallas_call(
        functools.partial(order_kernel, wide, parts),
        out_shape=out_shape,
        in_specs=[pl.BlockSpec(memory_space=pltpu.SMEM), vmem, vmem, vmem, hbm],
        out_specs=[hbm, vmem, vmem] + [hbm] * len(parts),
        scratch_shapes=[
            pltpu.VMEM(pool.shape, pool.dtype),
            pltpu.VMEM((1, slots), jnp.int32),
            pltpu.SMEM((1, slots), jnp.int32),
            pltpu.SemaphoreType.DMA((1 + len(parts),)),
            pltpu.SemaphoreType.DMA((1 + len(parts),)),
            pltpu.SemaphoreType.DMA,
        ],
        compiler_params=pltpu.CompilerParams(vmem_limit_bytes=56 * MIB),
        cost_estimate=pl.CostEstimate(
            flops=0, bytes_accessed=2 * pool.size * 2, transcendentals=0
        ),
    )(me, dest.reshape(1, -1), page_req.reshape(1, -1), page_idx.reshape(1, -1), pool)


def place_kernel(place_ref, *refs):
    in_refs, (out_ref, sem) = refs[:-3], refs[-2:]
    copies = []
    for i, chunk in enumerate(in_refs):
        depth = chunk.shape[0]
        copies.append(
            pltpu.make_async_copy(
                chunk, out_ref.at[pl.ds(place_ref[i], depth)], sem.at[i]
            )
        )
    for copy in copies:
        copy.start()
    for copy in copies:
        copy.wait()


def place_pages(place, chunks, pages):
    count = len(chunks)
    return pl.pallas_call(
        place_kernel,
        out_shape=jax.ShapeDtypeStruct(pages.shape, pages.dtype),
        in_specs=[pl.BlockSpec(memory_space=pltpu.SMEM)]
        + [pl.BlockSpec(memory_space=pltpu.VMEM)] * count
        + [pl.BlockSpec(memory_space=pl.ANY)],
        out_specs=pl.BlockSpec(memory_space=pl.ANY),
        scratch_shapes=[pltpu.SemaphoreType.DMA((count,))],
        input_output_aliases={count + 1: 0},
        compiler_params=pltpu.CompilerParams(vmem_limit_bytes=2 * count * chunks[0].size + 2 * MIB),
        cost_estimate=pl.CostEstimate(
            flops=0, bytes_accessed=4 * count * chunks[0].size, transcendentals=0
        ),
    )(place, *chunks, pages)


def cut(value):
    return value.astype(jnp.bfloat16).astype(jnp.float32)


def split_stats(peak, total):
    high = cut(peak)
    mid = cut(peak - high)
    return high, mid, peak - high - mid, cut(total), total - cut(total)


def attend_kernel(rows, piece, peers, me_ref, length_ref, *refs):
    query_refs, refs = refs[:peers], refs[peers:]
    key_ref, value_ref, new_key_ref, new_value_ref, token_ref = refs[:5]
    out_refs = refs[5 : 5 + peers]
    bias_ref, new_bias_ref, score_ref, weight_ref, query_ref, result_ref = refs[5 + peers :]
    tokens = key_ref.shape[0]
    step = pl.program_id(0)

    @pl.when(step == 0)
    def _():
        owner = token_ref[0:1, :]
        offset = lax.broadcasted_iota(jnp.int32, owner.shape, 1) % PAGE
        spot = (token_ref[1:2, :] * 32 + token_ref[2:3, :] - 1) * PAGE + offset.astype(jnp.float32)
        request = lax.broadcasted_iota(jnp.int32, (rows, 1), 0) // STEPS
        limit = jnp.zeros((rows, 1), jnp.int32)
        for r in range(rows // STEPS):
            limit = jnp.where(request == r, length_ref[r], limit)
        seen = (owner == request.astype(jnp.float32)) & (spot < limit.astype(jnp.float32))
        bias_ref[...] = jnp.where(seen, 0.0, NEG_FILL)
        row = lax.broadcasted_iota(jnp.int32, new_bias_ref.shape, 0)
        col = lax.broadcasted_iota(jnp.int32, new_bias_ref.shape, 1)
        first = jnp.where((me_ref[0] == 0) & (me_ref[1] == 0), 1, 0)
        seen = (row // STEPS == col // STEPS) & (col <= row) & (col < rows * first)
        new_bias_ref[...] = jnp.where(seen, 0.0, NEG_FILL)
        if peers > 1:
            for d in range(peers):
                query_ref[me_ref[1] ^ d] = query_refs[d][...]

    if peers > 1:
        per_step = query_refs[0].shape[0] // KVH
        query = jnp.concatenate(
            [
                query_ref[n, step * per_step + i].astype(jnp.float32)
                for i in range(per_step)
                for n in range(peers)
            ],
            axis=0,
        ).astype(jnp.bfloat16)
    else:
        query = query_refs[0][0]
    score_ref[:, :tokens] = lax.dot_general(
        query, key_ref[...], NT, preferred_element_type=jnp.float32
    )
    score_ref[:, tokens:] = lax.dot_general(
        query, new_key_ref[...], NT, preferred_element_type=jnp.float32
    )
    together = 1 if rows % 16 == 0 else 2
    span = together * rows
    peaks, totals = [], []
    for c in range(GROUPS // together):
        block = pl.ds(c * span, span)
        old = score_ref[block, :tokens].reshape(together, rows, tokens) * SCALE2 + bias_ref[...]
        new = score_ref[block, tokens:].reshape(together, rows, -1) * SCALE2 + new_bias_ref[...]
        peak = jnp.maximum(
            jnp.max(old, axis=-1, keepdims=True), jnp.max(new, axis=-1, keepdims=True)
        )
        old = jnp.exp2(old - peak)
        new = jnp.exp2(new - peak)
        totals.append(
            (jnp.sum(old, axis=-1, keepdims=True) + jnp.sum(new, axis=-1, keepdims=True)).reshape(
                span, 1
            )
        )
        peaks.append(peak.reshape(span, 1))
        weight_ref[block, :tokens] = old.reshape(span, tokens).astype(jnp.bfloat16)
        weight_ref[block, tokens:] = new.reshape(span, -1).astype(jnp.bfloat16)
    mixed = jnp.dot(
        weight_ref[:, :tokens], value_ref[...], preferred_element_type=jnp.float32
    ) + jnp.dot(weight_ref[:, tokens:], new_value_ref[...], preferred_element_type=jnp.float32)
    peak = jnp.concatenate(peaks, axis=0)
    total = jnp.concatenate(totals, axis=0)
    lane = lax.broadcasted_iota(jnp.int32, (GROUPS * rows, HD), 1)
    stats = jnp.zeros((GROUPS * rows, HD), jnp.float32)
    for i, part in enumerate(split_stats(peak, total)):
        stats = jnp.where(lane == i, part, stats)
    pick = (
        lax.broadcasted_iota(jnp.int32, (STAT, HD), 0)
        == lax.broadcasted_iota(jnp.int32, (STAT, HD), 1)
    ).astype(jnp.bfloat16)
    fill = result_ref.shape[1] - STAT - piece
    for c in range(GROUPS * rows // piece):
        part = slice(c * piece, (c + 1) * piece)
        turned = lax.dot_general(
            pick,
            jnp.concatenate(
                [stats[part], jnp.zeros((HD - piece, HD), jnp.float32)], axis=0
            ).astype(jnp.bfloat16),
            NT,
            preferred_element_type=jnp.float32,
        )
        result_ref[c] = jnp.concatenate(
            [turned, mixed[part], jnp.zeros((fill, HD), jnp.float32)], axis=0
        ).astype(jnp.bfloat16)
    if peers > 1:
        for d, out_ref in enumerate(out_refs):

            @pl.when((step ^ me_ref[1]) == d)
            def _():
                out_ref[...] = result_ref[...]
    else:
        out_refs[0][...] = result_ref[...]


def attend(me, lengths, queries, keyval, pool, token_info, rows, piece):
    tokens = pool.shape[0]
    extra = keyval.shape[0]
    peers = len(queries)
    pieces = GROUPS * rows // piece
    height = STAT + up(piece, 16)
    whole = lambda shape: pl.BlockSpec(shape, lambda k: (0,) * len(shape))
    if peers > 1:
        query_spec = whole(queries[0].shape)
        out_spec = whole((pieces, height, HD))
        out_shape = jax.ShapeDtypeStruct((pieces, height, HD), jnp.bfloat16)
    else:
        query_spec = pl.BlockSpec((1,) + queries[0].shape[1:], lambda k: (k, 0, 0))
        out_spec = pl.BlockSpec((pieces, height, HD), lambda k: (k, 0, 0))
        out_shape = jax.ShapeDtypeStruct((KVH * pieces, height, HD), jnp.bfloat16)
    return pl.pallas_call(
        functools.partial(attend_kernel, rows, piece, peers),
        grid=(KVH,),
        out_shape=[out_shape] * peers,
        in_specs=[pl.BlockSpec(memory_space=pltpu.SMEM)] * 2
        + [query_spec] * peers
        + [
            pl.BlockSpec((tokens, HD), lambda k: (0, k)),
            pl.BlockSpec((tokens, HD), lambda k: (0, KVH + k)),
            pl.BlockSpec((extra, HD), lambda k: (0, k)),
            pl.BlockSpec((extra, HD), lambda k: (0, KVH + k)),
            whole(token_info.shape),
        ],
        out_specs=[out_spec] * peers,
        scratch_shapes=[
            pltpu.VMEM((rows, tokens), jnp.float32),
            pltpu.VMEM((rows, extra), jnp.float32),
            pltpu.VMEM((GROUPS * rows, tokens + extra), jnp.float32),
            pltpu.VMEM((GROUPS * rows, tokens + extra), jnp.bfloat16),
            pltpu.VMEM((peers,) + queries[0].shape, jnp.bfloat16),
            pltpu.VMEM((pieces, height, HD), jnp.bfloat16),
        ],
        compiler_params=pltpu.CompilerParams(vmem_limit_bytes=56 * MIB),
        cost_estimate=pl.CostEstimate(flops=0, bytes_accessed=0, transcendentals=0),
    )(me, lengths, *queries, pool, pool, keyval, keyval, token_info)


def combine_kernel(piece, last, count, *refs):
    if last:
        part_ref, out_ref = refs
        part_refs = [part_ref.at[pl.ds(i, 1)] for i in range(count)]
    else:
        part_refs, out_ref = refs[:count], refs[count]
    groups, height = part_refs[0].shape[:2]
    peaks, totals = [], []
    for i in range(count):
        for j in range(groups):
            stat = part_refs[i][j, :STAT, :].astype(jnp.float32)
            peaks.append(stat[0:1] + stat[1:2] + stat[2:3])
            totals.append(stat[3:4] + stat[4:5])
    peak = jnp.concatenate(peaks, axis=0).reshape(count, groups, HD)
    total = jnp.concatenate(totals, axis=0).reshape(count, groups, HD)
    top = jnp.max(peak, axis=0)
    lead = jnp.exp2(peak - top[None])
    whole = jnp.sum(lead * total, axis=0)
    if last:
        lane = lax.broadcasted_iota(jnp.int32, whole.shape, 1)
        lead = lead / jnp.where(lane < piece, whole, 1.0)[None]
    lead = lead.reshape(count * groups, HD)
    if (count * groups) % HD:
        fill = up(count * groups, HD) - count * groups
        lead = jnp.concatenate([lead, jnp.zeros((fill, HD), jnp.float32)], axis=0)
    lead = jnp.transpose(lead)
    rows = height - STAT
    for j in range(groups):
        result = jnp.zeros((rows, HD), jnp.float32)
        for i in range(count):
            c = i * groups + j
            result = result + lead[:rows, c : c + 1] * part_refs[i][j, STAT:, :].astype(jnp.float32)
        if last:
            for i in range(out_ref.shape[0]):
                out_ref[i] = result[:piece].astype(jnp.bfloat16)
        else:
            stats = split_stats(top[j : j + 1], whole[j : j + 1])
            rest = jnp.zeros((STAT - len(stats), HD), jnp.float32)
            out_ref[j] = jnp.concatenate([*stats, rest, result], axis=0).astype(jnp.bfloat16)


def combine(parts, piece, repeats=0):
    count = parts[0].shape[0] if repeats else len(parts)
    shape = (repeats, piece, HD) if repeats else parts[0].shape
    return pl.pallas_call(
        functools.partial(combine_kernel, piece, repeats > 0, count),
        out_shape=jax.ShapeDtypeStruct(shape, jnp.bfloat16),
        in_specs=[pl.BlockSpec(memory_space=pltpu.VMEM)] * len(parts),
        out_specs=pl.BlockSpec(memory_space=pltpu.VMEM),
        compiler_params=pltpu.CompilerParams(vmem_limit_bytes=8 * MIB),
        cost_estimate=pl.CostEstimate(
            flops=2 * len(parts) * parts[0].size,
            bytes_accessed=len(parts) * parts[0].size * 2,
            transcendentals=0,
        ),
    )(*parts)


def reorder(shape, unit, valid, own, column):
    first, second = (0, 1) if column else (1, 0)
    block = lax.broadcasted_iota(jnp.int32, shape, second) // unit
    place = lax.broadcasted_iota(jnp.int32, shape, second) % unit
    target = (block ^ own) * valid + place
    match = (lax.broadcasted_iota(jnp.int32, shape, first) == target) & (place < valid)
    return match.astype(jnp.bfloat16)


def project_kernel(peers, me_ref, hidden_ref, query_ref, keyval_ref, *refs):
    out_refs, (full_ref,) = refs[:peers], refs[peers:]
    count, local, depth = hidden_ref.shape
    unit = up(local, 8)
    blocks = []
    for i in range(count):
        blocks.append(hidden_ref[i].astype(jnp.float32))
        if unit > local:
            blocks.append(jnp.zeros((unit - local, depth), jnp.float32))
    hidden = jnp.concatenate(blocks, axis=0).astype(jnp.bfloat16)
    order = reorder((count * local, count * unit), unit, local, 0, True)
    hidden = jnp.dot(order, hidden, preferred_element_type=jnp.float32).astype(jnp.bfloat16)
    full_ref[...] = jnp.dot(hidden, query_ref[...], preferred_element_type=jnp.float32)
    keyval = jnp.dot(hidden, keyval_ref[...], preferred_element_type=jnp.float32)
    for d, out_ref in enumerate(out_refs):
        start = pl.multiple_of((me_ref[1] ^ d) * HD, HD)
        out_ref[:, :HD] = full_ref[:, pl.ds(start, HD)]
        out_ref[:, HD:] = keyval


def pack_kernel(peers, *refs):
    own, tag_ref, out_ref = refs[:peers], refs[peers], refs[peers + 1]
    total = (own[0][...] + own[1][...]) + (own[2][...] + own[3][...])
    tags = jnp.concatenate([tag_ref[...], jnp.zeros_like(tag_ref[...])], axis=1)
    packed = jnp.concatenate([total, tags], axis=0).astype(jnp.bfloat16)
    for i in range(out_ref.shape[0]):
        out_ref[i] = packed


def unpack_kernel(rows, me_ref, kept_ref, part_ref, query_ref, keyval_ref, *refs):
    entry_ref, req_ref, idx_ref = refs
    count = part_ref.shape[0]
    line = lax.broadcasted_iota(jnp.int32, (count, HD), 0)
    tags = jnp.zeros((count, HD), jnp.float32)
    fill = jnp.zeros((keyval_ref.shape[0] - rows, HD), jnp.float32)
    for i in range(count):
        part = part_ref[i].astype(jnp.float32)
        query_ref[i] = part[:rows, :HD].astype(jnp.bfloat16)
        block = jnp.concatenate([part[:rows, HD:], fill], axis=0).astype(jnp.bfloat16)
        keyval_ref[:, i * HD : (i + 1) * HD] = block
        mine = jnp.where(line == me_ref[0], part[rows : rows + count, :HD], 0.0)
        tags = tags + jnp.where(line == i, jnp.sum(mine, axis=0, keepdims=True), 0.0)
    capacity = HD // count
    high = lax.broadcasted_iota(jnp.int32, (HD, HD), 0)
    low = lax.broadcasted_iota(jnp.int32, (HD, HD), 1)
    slot = lax.broadcasted_iota(jnp.int32, (count, HD), 1)
    tags = tags.astype(jnp.bfloat16)
    fields = []
    for i in range(3):
        pick = jnp.where(high == i * capacity + low % capacity, 1.0, 0.0).astype(jnp.bfloat16)
        spread_out = jnp.dot(tags, pick, preferred_element_type=jnp.float32)
        spread_out = jnp.where(slot // capacity == line, spread_out, 0.0)
        fields.append(jnp.sum(spread_out, axis=0, keepdims=True))
    req_ref[...] = fields[0].astype(jnp.int32)
    idx_ref[...] = (fields[1] * 32.0 + fields[2] - 1.0).astype(jnp.int32)
    local = entry_ref.shape[1]
    step = lax.broadcasted_iota(jnp.int32, (16, keyval_ref.shape[0]), 0)
    row = lax.broadcasted_iota(jnp.int32, (16, keyval_ref.shape[0]), 1)
    kept = (row == me_ref[0] * local + step) & (step < kept_ref[me_ref[0]])
    kept = jnp.where(kept, 1.0, 0.0).astype(jnp.bfloat16)
    entries = jnp.dot(kept, keyval_ref[...], preferred_element_type=jnp.float32)
    entry_ref[0] = entries[:local].astype(jnp.bfloat16)


def finish_kernel(peers, me_ref, part_ref, weight_ref, *refs):
    count, rows = part_ref.shape[:2]
    local = rows // peers
    unit = up(local, 16)
    whole = jnp.concatenate([part_ref[i] for i in range(count)], axis=1)
    order = reorder((peers * unit, rows), unit, local, me_ref[1], False)
    mixed = jnp.dot(order, whole, preferred_element_type=jnp.float32)
    mixed = jnp.dot(mixed.astype(jnp.bfloat16), weight_ref[...], preferred_element_type=jnp.float32)
    for d, out_ref in enumerate(refs):
        out_ref[...] = mixed[d * unit : d * unit + local]


def in_vmem(kernel, out_shape, me, *args, scratch=()):
    head = [] if me is None else list(me) if isinstance(me, tuple) else [me]
    return pl.pallas_call(
        kernel,
        out_shape=out_shape,
        in_specs=[pl.BlockSpec(memory_space=pltpu.SMEM)] * len(head)
        + [pl.BlockSpec(memory_space=pltpu.VMEM)] * len(args),
        out_specs=jax.tree.map(lambda _: pl.BlockSpec(memory_space=pltpu.VMEM), out_shape),
        scratch_shapes=scratch,
        compiler_params=pltpu.CompilerParams(vmem_limit_bytes=16 * MIB),
        cost_estimate=pl.CostEstimate(
            flops=0, bytes_accessed=sum(2 * arg.size for arg in args), transcendentals=0
        ),
    )(*head, *args)


def group_of(d, wide):
    return d if wide <= 8 else 1 + (d - 1) * 7 // (wide - 1)


def spread(block, axis):
    count = lax.axis_size(axis)
    return lax.all_to_all(
        jnp.broadcast_to(block[None], (count,) + block.shape),
        axis,
        split_axis=0,
        concat_axis=0,
        tiled=True,
    )


def on_device(hidden, w_query, w_keyval, w_out, pool, page_req, page_idx, lengths, moves, accepted):
    wide = lax.axis_size("wide")
    narrow = lax.axis_size("narrow")
    local_rows = hidden.shape[0]
    rows = local_rows * wide
    requests = rows // STEPS
    slots = pool.shape[0]
    capacity = slots // wide
    own_cols = w_query.shape[1] // narrow
    piece = HEADS * rows // (wide * narrow)
    extra = up(rows, HD)
    direct = piece == rows and own_cols == HD and slots == HD
    direct = direct and wide == 8 and narrow == 4 and local_rows == STEPS
    me = lax.axis_index("wide")
    both = jnp.stack([me, lax.axis_index("narrow")])
    exchange = functools.partial(lax.all_to_all, split_axis=0, concat_axis=0, tiled=True)

    def send(block, axis, d):
        return lax.ppermute(block, axis, [(i, i ^ d) for i in range(lax.axis_size(axis))])

    def share(block, axis):
        return [block] + [send(block, axis, d) for d in range(1, lax.axis_size(axis))]

    def deal(blocks, axis):
        return [blocks[0]] + [send(block, axis, d) for d, block in enumerate(blocks) if d]

    gathered = spread(hidden, "wide")

    parts = []
    for d in range(1, wide):
        cuts = [cut * capacity // 16 for cut in CUTS[group_of(d, wide)]]
        parts += [(d, a, b) for a, b in zip(cuts[:-1], cuts[1:]) if b > a]
    moved_pool, tags, token_info, *chunks = order_pages(
        both, moves, page_req, page_idx, pool, wide, parts
    )
    arrived = {}
    flying = {}

    def members(names):
        taken = []
        for group, which in names:
            cut = CUTS[group][which] * capacity // 16
            end = CUTS[group][which + 1] * capacity // 16
            taken += [
                c
                for c, (d, first, last) in enumerate(parts)
                if group_of(d, wide) == group and (first, last) == (cut, end)
            ]
        return taken

    def launch(values, *names):
        taken = members(names)
        values, sent = lax.optimization_barrier((values, [chunks[c] for c in taken]))
        for c, chunk in zip(taken, sent):
            flying[c] = send(chunk, "wide", parts[c][0])
        return values

    def land(values, *names):
        taken = members(names)
        values, got = lax.optimization_barrier((values, [flying[c] for c in taken]))
        arrived.update(zip(taken, got))
        return values

    def beside(step, value, *names):
        return land(step(launch(value, *names)), *names)

    def placed(pages):
        taken = sorted(arrived)
        place = jnp.stack([(me ^ parts[c][0]) * capacity + parts[c][1] for c in taken])
        pages = place_pages(place, [arrived[c] for c in taken], pages)
        arrived.clear()
        return pages

    tokens = pool.reshape(slots * PAGE, -1)
    if direct:
        block = jax.ShapeDtypeStruct((rows, 2 * HD), jnp.float32)
        partial = in_vmem(
            functools.partial(project_kernel, narrow),
            [block] * narrow,
            both,
            gathered,
            w_query,
            w_keyval,
            scratch=[pltpu.VMEM((rows, narrow * HD), jnp.float32)],
        )
        partial = beside(lambda value: deal(value, "narrow"), partial, (6, 0), (1, 0))
        packed = in_vmem(
            functools.partial(pack_kernel, narrow),
            jax.ShapeDtypeStruct((wide, rows + wide, 2 * HD), jnp.bfloat16),
            None,
            *partial,
            tags,
        )
        received = beside(lambda value: exchange(value, "wide"), packed, (6, 1))
        queries, keyval, new_entries, moved_req, moved_idx = in_vmem(
            functools.partial(unpack_kernel, rows),
            [
                jax.ShapeDtypeStruct((wide, rows, HD), jnp.bfloat16),
                jax.ShapeDtypeStruct((extra, wide * HD), jnp.bfloat16),
                jax.ShapeDtypeStruct((1, local_rows, wide * HD), jnp.bfloat16),
                jax.ShapeDtypeStruct((1, slots), jnp.int32),
                jax.ShapeDtypeStruct((1, slots), jnp.int32),
            ],
            (both, accepted),
            received,
        )
        moved_req, moved_idx = moved_req.reshape(slots), moved_idx.reshape(slots)
        queries = beside(lambda value: share(value, "narrow"), queries, (7, 0), (1, 1))
    else:
        gathered = gathered.reshape(rows, -1)
        query_part = jnp.dot(gathered, w_query, preferred_element_type=jnp.float32)
        keyval_part = jnp.dot(gathered, w_keyval, preferred_element_type=jnp.float32)
        query_part = jnp.transpose(query_part.reshape(rows, narrow, own_cols), (1, 0, 2))
        partial = jnp.concatenate(
            [query_part, jnp.broadcast_to(keyval_part[None], (narrow,) + keyval_part.shape)], axis=2
        )
        partial = beside(lambda value: exchange(value, "narrow"), partial, (6, 0), (1, 0))
        projected = jnp.sum(partial, axis=0).astype(jnp.bfloat16)
        tags = tags[:, : 3 * capacity].astype(jnp.bfloat16)[:, None]
        tags = jnp.pad(tags, ((0, 0), (0, 7), (0, projected.shape[1] - tags.shape[2])))
        packed = jnp.broadcast_to(projected[None], (wide,) + projected.shape)
        packed = jnp.concatenate([packed, tags], axis=1)
        received = beside(lambda value: exchange(value, "wide"), packed, (6, 1))
        tags_in = received[:, rows]
        queries = received[:, :rows, :own_cols]
        queries = beside(lambda value: spread(value, "narrow"), queries, (7, 0), (1, 1))
        queries = jnp.transpose(queries, (2, 1, 0, 3)).reshape(rows, HEADS, HD)
        queries = [jnp.transpose(queries, (1, 0, 2)).reshape(KVH, GROUPS * rows, HD)]
        keyval = jnp.transpose(received[:, :rows, own_cols:], (1, 0, 2)).reshape(rows, -1)
        keyval = jnp.pad(keyval, ((0, extra - rows), (0, 0)))
        tags_in = tags_in.astype(jnp.int32)
        moved_req = tags_in[:, :capacity].reshape(slots)
        moved_idx = tags_in[:, capacity : 2 * capacity] * 32
        moved_idx = (moved_idx + tags_in[:, 2 * capacity : 3 * capacity] - 1).reshape(slots)
        local_req = local_rows // STEPS
        fresh = lax.dynamic_slice_in_dim(keyval, me * local_rows, local_rows, 0)
        fresh = fresh.reshape(local_req, STEPS, -1)
        kept = lax.dynamic_slice_in_dim(accepted, me * local_req, local_req, 0)
        step_ids = jnp.arange(STEPS)[None, :, None]
        new_entries = jnp.where(
            step_ids < kept[:, None, None], fresh, jnp.zeros((), jnp.bfloat16)
        )

    mixed = beside(
        lambda value: attend(both, lengths, value, keyval, tokens, token_info, rows, piece),
        queries,
        (7, 1),
        (2, 0),
    )
    if direct:
        mixed = beside(lambda value: deal(value, "narrow"), mixed, (7, 2), (3, 0))
    else:
        mixed = beside(lambda value: exchange(value, "narrow"), mixed[0], (7, 2), (3, 0))
        mixed = mixed.reshape((narrow, wide) + mixed.shape[1:])
        mixed = [mixed[i] for i in range(narrow)]
    mixed = combine(mixed, piece)
    mixed, pages = lax.optimization_barrier((mixed, moved_pool))
    pages = placed(pages)
    mixed = beside(lambda value: exchange(value, "wide"), mixed, (4, 0), (2, 1))
    mixed, moved_pool = lax.optimization_barrier((mixed, pages))
    attn = combine([mixed], piece, wide)
    attn = beside(lambda value: exchange(value, "wide"), attn, (5, 0), (4, 1), (3, 1))
    if direct:
        sums = in_vmem(
            functools.partial(finish_kernel, narrow),
            [jax.ShapeDtypeStruct((rows // narrow, w_out.shape[1]), jnp.float32)] * narrow,
            both,
            attn,
            w_out,
        )
        sums = beside(lambda value: deal(value, "narrow"), sums, (5, 1))
        attended = ((sums[0] + sums[1]) + (sums[2] + sums[3])).astype(jnp.bfloat16)
    else:
        attn = jnp.transpose(attn.reshape(-1, rows, HD), (1, 0, 2)).reshape(rows, -1)
        sums = jnp.dot(attn, w_out, preferred_element_type=jnp.float32)
        sums = sums.reshape(narrow, rows // narrow, -1)
        sums = beside(lambda value: exchange(value, "narrow"), sums, (5, 1))
        attended = jnp.sum(sums, axis=0).astype(jnp.bfloat16)
    moved_pool = placed(moved_pool)
    return (attended, new_entries, moved_pool, moved_req, moved_idx)


def solution(mesh):
    in_specs = (
        P("wide", "narrow"),
        P("narrow", "wide"),
        P("narrow", "wide"),
        P("narrow", "wide"),
        P(("wide", "narrow"), None, None),
        P(("wide", "narrow")),
        P(("wide", "narrow")),
        P(),
        P(("wide", "narrow"), None),
        P(),
    )
    out_specs = (
        P("narrow", "wide"),
        P("wide", None, None),
        P(("wide", "narrow"), None, None),
        P(("wide", "narrow")),
        P(("wide", "narrow")),
    )
    return jax.shard_map(
        on_device, mesh=mesh, in_specs=in_specs, out_specs=out_specs, check_vma=False
    )
```

```python
import functools
import math

import jax
import jax.numpy as jnp
from jax import lax
from jax.experimental import pallas as pl
from jax.experimental.pallas import tpu as pltpu
from jax.sharding import PartitionSpec as P

HEADS = 32
KVH = 4
HD = 128
STEPS = 5
PAGE = 16
GROUPS = HEADS // KVH
NEG_FILL = -1e30
SCALE2 = math.log2(math.e) / math.sqrt(HD)
STAT = 16
MIB = 1024 * 1024
CUTS = {1: (0, 8, 16), 2: (0, 7, 16), 3: (0, 5, 16), 4: (0, 13, 16), 5: (0, 10, 16), 6: (0, 6, 16), 7: (0, 4, 11, 16)}
NT = (((1,), (1,)), ((), ()))


def up(value, unit):
    return -(-value // unit) * unit


def column(row):
    return jnp.transpose(jnp.broadcast_to(row, (row.shape[1], row.shape[1])))


def order_kernel(
    wide, parts, me_ref, dest_ref, req_ref, idx_ref, hidden_ref, pool_ref, *refs
):
    out_ref, tag_ref, token_ref, copies_ref, refs = *refs[:4], refs[4:]
    chunk_refs, refs = refs[: len(parts)], refs[len(parts) :]
    pages_ref, line_ref, source_ref, in_sem, out_sem, line_sem = refs
    slots = pool_ref.shape[0]
    capacity = slots // wide
    shape = (slots, slots)
    high = lax.broadcasted_iota(jnp.int32, shape, 0)
    low = lax.broadcasted_iota(jnp.int32, shape, 1)
    dest = dest_ref[...]
    same = column(dest.astype(jnp.float32)) == dest.astype(jnp.float32)
    rank = jnp.sum(jnp.where(same & (high < low), 1.0, 0.0), axis=0, keepdims=True)
    moved_to = ((dest ^ me_ref[0]) * capacity).astype(jnp.float32) + rank
    match = column(moved_to) == low.astype(jnp.float32)
    source = jnp.sum(jnp.where(match, high.astype(jnp.float32), 0.0), axis=0, keepdims=True)
    line_ref[...] = source.astype(jnp.int32)
    copy = pltpu.make_async_copy(line_ref, source_ref, line_sem)
    copy.start()
    copy.wait()

    blocks = [(0, capacity, out_ref.at[pl.ds(me_ref[0] * capacity, capacity)])]
    for (d, first, last), chunk in zip(parts, chunk_refs):
        blocks.append((d * capacity + first, last - first, chunk))
    for c, (first, count, _) in enumerate(blocks):

        def start(j, carry, c=c):
            page = source_ref[0, j]
            pltpu.make_async_copy(pool_ref.at[page], pages_ref.at[j], in_sem.at[c]).start()
            return carry

        lax.fori_loop(first, first + count, start, 0)

    for i in range(wide):
        copies_ref[i] = hidden_ref[...]
    shifted = idx_ref[...] + 1
    fields = (req_ref[...], shifted // 32, shifted % 32)
    rank_col = column(rank)
    lane = low.astype(jnp.float32)
    spread_out = jnp.zeros(shape, jnp.float32)
    for i, field in enumerate(fields):
        picked = lane == rank_col + float(i * capacity)
        spread_out = spread_out + jnp.where(picked, column(field.astype(jnp.float32)), 0.0)
    line = lax.broadcasted_iota(jnp.int32, (wide, slots), 0)
    chosen = jnp.where(line == dest, 1.0, 0.0).astype(jnp.bfloat16)
    tag_ref[...] = jnp.dot(
        chosen, spread_out.astype(jnp.bfloat16), preferred_element_type=jnp.float32
    )

    tokens = slots * PAGE
    page = lax.broadcasted_iota(jnp.int32, (slots, tokens), 0)
    token = lax.broadcasted_iota(jnp.int32, (slots, tokens), 1)
    widen = jnp.where(page == token // PAGE, 1.0, 0.0).astype(jnp.bfloat16)
    row = lax.broadcasted_iota(jnp.int32, (8, slots), 0)
    stacked = jnp.zeros((8, slots), jnp.float32)
    for i, field in enumerate(fields):
        stacked = jnp.where(row == i, field.astype(jnp.float32), stacked)
    token_ref[...] = jnp.dot(
        stacked.astype(jnp.bfloat16), widen, preferred_element_type=jnp.float32
    )

    copies = []
    for c, (first, count, target) in enumerate(blocks):
        held = pages_ref.at[pl.ds(first, count)]
        pltpu.make_async_copy(pool_ref.at[pl.ds(0, count)], held, in_sem.at[c]).wait()
        copies.append(pltpu.make_async_copy(held, target, out_sem.at[c]))
        copies[-1].start()
    for copy in copies:
        copy.wait()


def order_pages(me, dest, page_req, page_idx, hidden, pool, wide, parts):
    slots = pool.shape[0]
    part = lambda count: jax.ShapeDtypeStruct((count,) + pool.shape[1:], pool.dtype)
    out_shape = [part(slots), jax.ShapeDtypeStruct((wide, slots), jnp.float32)]
    out_shape += [jax.ShapeDtypeStruct((8, slots * PAGE), jnp.float32)]
    out_shape += [jax.ShapeDtypeStruct((wide,) + hidden.shape, hidden.dtype)]
    out_shape += [part(last - first) for _, first, last in parts]
    vmem = pl.BlockSpec(memory_space=pltpu.VMEM)
    hbm = pl.BlockSpec(memory_space=pltpu.HBM)
    return pl.pallas_call(
        functools.partial(order_kernel, wide, parts),
        out_shape=out_shape,
        in_specs=[pl.BlockSpec(memory_space=pltpu.SMEM), vmem, vmem, vmem, vmem, hbm],
        out_specs=[hbm, vmem, vmem, vmem] + [hbm] * len(parts),
        scratch_shapes=[
            pltpu.VMEM(pool.shape, pool.dtype),
            pltpu.VMEM((1, slots), jnp.int32),
            pltpu.SMEM((1, slots), jnp.int32),
            pltpu.SemaphoreType.DMA((1 + len(parts),)),
            pltpu.SemaphoreType.DMA((1 + len(parts),)),
            pltpu.SemaphoreType.DMA,
        ],
        compiler_params=pltpu.CompilerParams(vmem_limit_bytes=56 * MIB),
        cost_estimate=pl.CostEstimate(flops=1, bytes_accessed=1, transcendentals=0),
    )(me, dest.reshape(1, -1), page_req.reshape(1, -1), page_idx.reshape(1, -1), hidden, pool)


def place_kernel(place_ref, *refs):
    in_refs, (out_ref, sem) = refs[:-3], refs[-2:]
    copies = []
    for i, chunk in enumerate(in_refs):
        depth = chunk.shape[0]
        copies.append(
            pltpu.make_async_copy(
                chunk, out_ref.at[pl.ds(place_ref[i], depth)], sem.at[i]
            )
        )
    for copy in copies:
        copy.start()
    for copy in copies:
        copy.wait()


def place_pages(place, chunks, pages):
    count = len(chunks)
    return pl.pallas_call(
        place_kernel,
        out_shape=jax.ShapeDtypeStruct(pages.shape, pages.dtype),
        in_specs=[pl.BlockSpec(memory_space=pltpu.SMEM)]
        + [pl.BlockSpec(memory_space=pltpu.VMEM)] * count
        + [pl.BlockSpec(memory_space=pl.ANY)],
        out_specs=pl.BlockSpec(memory_space=pl.ANY),
        scratch_shapes=[pltpu.SemaphoreType.DMA((count,))],
        input_output_aliases={count + 1: 0},
        compiler_params=pltpu.CompilerParams(vmem_limit_bytes=2 * count * chunks[0].size + 2 * MIB),
        cost_estimate=pl.CostEstimate(flops=1, bytes_accessed=1, transcendentals=0),
    )(place, *chunks, pages)


def cut(value):
    return value.astype(jnp.bfloat16).astype(jnp.float32)


def split_stats(peak, total):
    high = cut(peak)
    mid = cut(peak - high)
    return high, mid, peak - high - mid, cut(total), total - cut(total)


def attend_kernel(rows, piece, peers, me_ref, length_ref, *refs):
    query_refs, refs = refs[:peers], refs[peers:]
    key_ref, value_ref, new_key_ref, new_value_ref, token_ref = refs[:5]
    out_refs = refs[5 : 5 + peers]
    bias_ref, new_bias_ref, score_ref, weight_ref, query_ref, result_ref = refs[5 + peers :]
    tokens = key_ref.shape[0]
    step = pl.program_id(0)

    @pl.when(step == 0)
    def _():
        owner = token_ref[0:1, :]
        offset = lax.broadcasted_iota(jnp.int32, owner.shape, 1) % PAGE
        spot = (token_ref[1:2, :] * 32 + token_ref[2:3, :] - 1) * PAGE + offset.astype(jnp.float32)
        request = lax.broadcasted_iota(jnp.int32, (rows, 1), 0) // STEPS
        limit = jnp.zeros((rows, 1), jnp.int32)
        for r in range(rows // STEPS):
            limit = jnp.where(request == r, length_ref[r], limit)
        seen = (owner == request.astype(jnp.float32)) & (spot < limit.astype(jnp.float32))
        bias_ref[...] = jnp.where(seen, 0.0, NEG_FILL)
        row = lax.broadcasted_iota(jnp.int32, new_bias_ref.shape, 0)
        col = lax.broadcasted_iota(jnp.int32, new_bias_ref.shape, 1)
        first = jnp.where((me_ref[0] == 0) & (me_ref[1] == 0), 1, 0)
        seen = (row // STEPS == col // STEPS) & (col <= row) & (col < rows * first)
        new_bias_ref[...] = jnp.where(seen, 0.0, NEG_FILL)
        if peers > 1:
            for d in range(peers):
                query_ref[me_ref[1] ^ d] = query_refs[d][...]

    if peers > 1:
        per_step = query_refs[0].shape[0] // KVH
        query = jnp.concatenate(
            [
                query_ref[n, step * per_step + i].astype(jnp.float32)
                for i in range(per_step)
                for n in range(peers)
            ],
            axis=0,
        ).astype(jnp.bfloat16)
    else:
        query = query_refs[0][0]
    score_ref[:, :tokens] = lax.dot_general(
        query, key_ref[...], NT, preferred_element_type=jnp.float32
    )
    score_ref[:, tokens:] = lax.dot_general(
        query, new_key_ref[...], NT, preferred_element_type=jnp.float32
    )
    together = 1 if rows % 16 == 0 else 2
    span = together * rows
    peaks, totals = [], []
    for c in range(GROUPS // together):
        block = pl.ds(c * span, span)
        old = score_ref[block, :tokens].reshape(together, rows, tokens) * SCALE2 + bias_ref[...]
        new = score_ref[block, tokens:].reshape(together, rows, -1) * SCALE2 + new_bias_ref[...]
        peak = jnp.maximum(
            jnp.max(old, axis=-1, keepdims=True), jnp.max(new, axis=-1, keepdims=True)
        )
        old = jnp.exp2(old - peak)
        new = jnp.exp2(new - peak)
        totals.append(
            (jnp.sum(old, axis=-1, keepdims=True) + jnp.sum(new, axis=-1, keepdims=True)).reshape(
                span, 1
            )
        )
        peaks.append(peak.reshape(span, 1))
        weight_ref[block, :tokens] = old.reshape(span, tokens).astype(jnp.bfloat16)
        weight_ref[block, tokens:] = new.reshape(span, -1).astype(jnp.bfloat16)
    mixed = jnp.dot(
        weight_ref[:, :tokens], value_ref[...], preferred_element_type=jnp.float32
    ) + jnp.dot(weight_ref[:, tokens:], new_value_ref[...], preferred_element_type=jnp.float32)
    peak = jnp.concatenate(peaks, axis=0)
    total = jnp.concatenate(totals, axis=0)
    lane = lax.broadcasted_iota(jnp.int32, (GROUPS * rows, HD), 1)
    stats = jnp.zeros((GROUPS * rows, HD), jnp.float32)
    for i, part in enumerate(split_stats(peak, total)):
        stats = jnp.where(lane == i, part, stats)
    pick = (
        lax.broadcasted_iota(jnp.int32, (STAT, HD), 0)
        == lax.broadcasted_iota(jnp.int32, (STAT, HD), 1)
    ).astype(jnp.bfloat16)
    fill = result_ref.shape[1] - STAT - piece
    for c in range(GROUPS * rows // piece):
        part = slice(c * piece, (c + 1) * piece)
        turned = lax.dot_general(
            pick,
            jnp.concatenate(
                [stats[part], jnp.zeros((HD - piece, HD), jnp.float32)], axis=0
            ).astype(jnp.bfloat16),
            NT,
            preferred_element_type=jnp.float32,
        )
        result_ref[c] = jnp.concatenate(
            [turned, mixed[part], jnp.zeros((fill, HD), jnp.float32)], axis=0
        ).astype(jnp.bfloat16)
    if peers > 1:
        for d, out_ref in enumerate(out_refs):

            @pl.when((step ^ me_ref[1]) == d)
            def _():
                out_ref[...] = result_ref[...]
    else:
        out_refs[0][...] = result_ref[...]


def attend(me, lengths, queries, keyval, pool, token_info, rows, piece):
    tokens = pool.shape[0]
    extra = keyval.shape[0]
    peers = len(queries)
    pieces = GROUPS * rows // piece
    height = STAT + up(piece, 16)
    whole = lambda shape: pl.BlockSpec(shape, lambda k: (0,) * len(shape))
    if peers > 1:
        query_spec = whole(queries[0].shape)
        out_spec = whole((pieces, height, HD))
        out_shape = jax.ShapeDtypeStruct((pieces, height, HD), jnp.bfloat16)
    else:
        query_spec = pl.BlockSpec((1,) + queries[0].shape[1:], lambda k: (k, 0, 0))
        out_spec = pl.BlockSpec((pieces, height, HD), lambda k: (k, 0, 0))
        out_shape = jax.ShapeDtypeStruct((KVH * pieces, height, HD), jnp.bfloat16)
    return pl.pallas_call(
        functools.partial(attend_kernel, rows, piece, peers),
        grid=(KVH,),
        out_shape=[out_shape] * peers,
        in_specs=[pl.BlockSpec(memory_space=pltpu.SMEM)] * 2
        + [query_spec] * peers
        + [
            pl.BlockSpec((tokens, HD), lambda k: (0, k)),
            pl.BlockSpec((tokens, HD), lambda k: (0, KVH + k)),
            pl.BlockSpec((extra, HD), lambda k: (0, k)),
            pl.BlockSpec((extra, HD), lambda k: (0, KVH + k)),
            whole(token_info.shape),
        ],
        out_specs=[out_spec] * peers,
        scratch_shapes=[
            pltpu.VMEM((rows, tokens), jnp.float32),
            pltpu.VMEM((rows, extra), jnp.float32),
            pltpu.VMEM((GROUPS * rows, tokens + extra), jnp.float32),
            pltpu.VMEM((GROUPS * rows, tokens + extra), jnp.bfloat16),
            pltpu.VMEM((peers,) + queries[0].shape, jnp.bfloat16),
            pltpu.VMEM((pieces, height, HD), jnp.bfloat16),
        ],
        compiler_params=pltpu.CompilerParams(vmem_limit_bytes=56 * MIB),
        cost_estimate=pl.CostEstimate(flops=1, bytes_accessed=1, transcendentals=0),
    )(me, lengths, *queries, pool, pool, keyval, keyval, token_info)


def combine_kernel(piece, last, count, *refs):
    if last:
        part_ref, out_ref = refs
        part_refs = [part_ref.at[pl.ds(i, 1)] for i in range(count)]
    else:
        part_refs, out_ref = refs[:count], refs[count]
    groups, height = part_refs[0].shape[:2]
    peaks, totals = [], []
    for i in range(count):
        for j in range(groups):
            stat = part_refs[i][j, :STAT, :].astype(jnp.float32)
            peaks.append(stat[0:1] + stat[1:2] + stat[2:3])
            totals.append(stat[3:4] + stat[4:5])
    peak = jnp.concatenate(peaks, axis=0).reshape(count, groups, HD)
    total = jnp.concatenate(totals, axis=0).reshape(count, groups, HD)
    top = jnp.max(peak, axis=0)
    lead = jnp.exp2(peak - top[None])
    whole = jnp.sum(lead * total, axis=0)
    if last:
        lane = lax.broadcasted_iota(jnp.int32, whole.shape, 1)
        lead = lead / jnp.where(lane < piece, whole, 1.0)[None]
    lead = lead.reshape(count * groups, HD)
    if (count * groups) % HD:
        fill = up(count * groups, HD) - count * groups
        lead = jnp.concatenate([lead, jnp.zeros((fill, HD), jnp.float32)], axis=0)
    lead = jnp.transpose(lead)
    rows = height - STAT
    for j in range(groups):
        result = jnp.zeros((rows, HD), jnp.float32)
        for i in range(count):
            c = i * groups + j
            result = result + lead[:rows, c : c + 1] * part_refs[i][j, STAT:, :].astype(jnp.float32)
        if last:
            for i in range(out_ref.shape[0]):
                out_ref[i] = result[:piece].astype(jnp.bfloat16)
        else:
            stats = split_stats(top[j : j + 1], whole[j : j + 1])
            rest = jnp.zeros((STAT - len(stats), HD), jnp.float32)
            out_ref[j] = jnp.concatenate([*stats, rest, result], axis=0).astype(jnp.bfloat16)


def combine(parts, piece, repeats=0):
    count = parts[0].shape[0] if repeats else len(parts)
    shape = (repeats, piece, HD) if repeats else parts[0].shape
    return pl.pallas_call(
        functools.partial(combine_kernel, piece, repeats > 0, count),
        out_shape=jax.ShapeDtypeStruct(shape, jnp.bfloat16),
        in_specs=[pl.BlockSpec(memory_space=pltpu.VMEM)] * len(parts),
        out_specs=pl.BlockSpec(memory_space=pltpu.VMEM),
        compiler_params=pltpu.CompilerParams(vmem_limit_bytes=8 * MIB),
        cost_estimate=pl.CostEstimate(flops=1, bytes_accessed=1, transcendentals=0),
    )(*parts)


def reorder(shape, unit, valid, own, column):
    first, second = (0, 1) if column else (1, 0)
    block = lax.broadcasted_iota(jnp.int32, shape, second) // unit
    place = lax.broadcasted_iota(jnp.int32, shape, second) % unit
    target = (block ^ own) * valid + place
    match = (lax.broadcasted_iota(jnp.int32, shape, first) == target) & (place < valid)
    return match.astype(jnp.bfloat16)


def project_kernel(peers, me_ref, hidden_ref, query_ref, keyval_ref, *refs):
    out_refs, (full_ref,) = refs[:peers], refs[peers:]
    count, local, depth = hidden_ref.shape
    unit = up(local, 8)
    blocks = []
    for i in range(count):
        blocks.append(hidden_ref[i].astype(jnp.float32))
        if unit > local:
            blocks.append(jnp.zeros((unit - local, depth), jnp.float32))
    hidden = jnp.concatenate(blocks, axis=0).astype(jnp.bfloat16)
    order = reorder((count * local, count * unit), unit, local, 0, True)
    hidden = jnp.dot(order, hidden, preferred_element_type=jnp.float32).astype(jnp.bfloat16)
    full_ref[...] = jnp.dot(hidden, query_ref[...], preferred_element_type=jnp.float32)
    keyval = jnp.dot(hidden, keyval_ref[...], preferred_element_type=jnp.float32)
    for d, out_ref in enumerate(out_refs):
        start = pl.multiple_of((me_ref[1] ^ d) * HD, HD)
        out_ref[:, :HD] = full_ref[:, pl.ds(start, HD)]
        out_ref[:, HD:] = keyval


def pack_kernel(peers, *refs):
    own, tag_ref, out_ref = refs[:peers], refs[peers], refs[peers + 1]
    total = (own[0][...] + own[1][...]) + (own[2][...] + own[3][...])
    tags = jnp.concatenate([tag_ref[...], jnp.zeros_like(tag_ref[...])], axis=1)
    packed = jnp.concatenate([total, tags], axis=0).astype(jnp.bfloat16)
    for i in range(out_ref.shape[0]):
        out_ref[i] = packed


def unpack_kernel(rows, me_ref, kept_ref, part_ref, query_ref, keyval_ref, *refs):
    entry_ref, req_ref, idx_ref = refs
    count = part_ref.shape[0]
    line = lax.broadcasted_iota(jnp.int32, (count, HD), 0)
    tags = jnp.zeros((count, HD), jnp.float32)
    fill = jnp.zeros((keyval_ref.shape[0] - rows, HD), jnp.float32)
    for i in range(count):
        part = part_ref[i].astype(jnp.float32)
        query_ref[i] = part[:rows, :HD].astype(jnp.bfloat16)
        block = jnp.concatenate([part[:rows, HD:], fill], axis=0).astype(jnp.bfloat16)
        keyval_ref[:, i * HD : (i + 1) * HD] = block
        mine = jnp.where(line == me_ref[0], part[rows : rows + count, :HD], 0.0)
        tags = tags + jnp.where(line == i, jnp.sum(mine, axis=0, keepdims=True), 0.0)
    capacity = HD // count
    high = lax.broadcasted_iota(jnp.int32, (HD, HD), 0)
    low = lax.broadcasted_iota(jnp.int32, (HD, HD), 1)
    slot = lax.broadcasted_iota(jnp.int32, (count, HD), 1)
    tags = tags.astype(jnp.bfloat16)
    fields = []
    for i in range(3):
        pick = jnp.where(high == i * capacity + low % capacity, 1.0, 0.0).astype(jnp.bfloat16)
        spread_out = jnp.dot(tags, pick, preferred_element_type=jnp.float32)
        spread_out = jnp.where(slot // capacity == line, spread_out, 0.0)
        fields.append(jnp.sum(spread_out, axis=0, keepdims=True))
    req_ref[...] = fields[0].astype(jnp.int32)
    idx_ref[...] = (fields[1] * 32.0 + fields[2] - 1.0).astype(jnp.int32)
    local = entry_ref.shape[1]
    step = lax.broadcasted_iota(jnp.int32, (16, keyval_ref.shape[0]), 0)
    row = lax.broadcasted_iota(jnp.int32, (16, keyval_ref.shape[0]), 1)
    kept = (row == me_ref[0] * local + step) & (step < kept_ref[me_ref[0]])
    kept = jnp.where(kept, 1.0, 0.0).astype(jnp.bfloat16)
    entries = jnp.dot(kept, keyval_ref[...], preferred_element_type=jnp.float32)
    entry_ref[0] = entries[:local].astype(jnp.bfloat16)


def finish_kernel(peers, me_ref, part_ref, weight_ref, *refs):
    count, rows = part_ref.shape[:2]
    local = rows // peers
    unit = up(local, 16)
    whole = jnp.concatenate([part_ref[i] for i in range(count)], axis=1)
    order = reorder((peers * unit, rows), unit, local, me_ref[1], False)
    mixed = jnp.dot(order, whole, preferred_element_type=jnp.float32)
    mixed = jnp.dot(mixed.astype(jnp.bfloat16), weight_ref[...], preferred_element_type=jnp.float32)
    for d, out_ref in enumerate(refs):
        out_ref[...] = mixed[d * unit : d * unit + local]


def in_vmem(kernel, out_shape, me, *args, scratch=()):
    head = [] if me is None else list(me) if isinstance(me, tuple) else [me]
    return pl.pallas_call(
        kernel,
        out_shape=out_shape,
        in_specs=[pl.BlockSpec(memory_space=pltpu.SMEM)] * len(head)
        + [pl.BlockSpec(memory_space=pltpu.VMEM)] * len(args),
        out_specs=jax.tree.map(lambda _: pl.BlockSpec(memory_space=pltpu.VMEM), out_shape),
        scratch_shapes=scratch,
        compiler_params=pltpu.CompilerParams(vmem_limit_bytes=16 * MIB),
        cost_estimate=pl.CostEstimate(flops=1, bytes_accessed=1, transcendentals=0),
    )(*head, *args)


def group_of(d, wide):
    return d if wide <= 8 else 1 + (d - 1) * 7 // (wide - 1)


def spread(block, axis):
    count = lax.axis_size(axis)
    return lax.all_to_all(
        jnp.broadcast_to(block[None], (count,) + block.shape),
        axis,
        split_axis=0,
        concat_axis=0,
        tiled=True,
    )


def on_device(hidden, w_query, w_keyval, w_out, pool, page_req, page_idx, lengths, moves, accepted):
    wide = lax.axis_size("wide")
    narrow = lax.axis_size("narrow")
    local_rows = hidden.shape[0]
    rows = local_rows * wide
    requests = rows // STEPS
    slots = pool.shape[0]
    capacity = slots // wide
    own_cols = w_query.shape[1] // narrow
    piece = HEADS * rows // (wide * narrow)
    extra = up(rows, HD)
    direct = piece == rows and own_cols == HD and slots == HD
    direct = direct and wide == 8 and narrow == 4 and local_rows == STEPS
    me = lax.axis_index("wide")
    both = jnp.stack([me, lax.axis_index("narrow")])
    exchange = functools.partial(lax.all_to_all, split_axis=0, concat_axis=0, tiled=True)

    def send(block, axis, d):
        return lax.ppermute(block, axis, [(i, i ^ d) for i in range(lax.axis_size(axis))])

    def share(block, axis):
        return [block] + [send(block, axis, d) for d in range(1, lax.axis_size(axis))]

    def deal(blocks, axis):
        return [blocks[0]] + [send(block, axis, d) for d, block in enumerate(blocks) if d]

    parts = []
    for d in range(1, wide):
        cuts = [cut * capacity // 16 for cut in CUTS[group_of(d, wide)]]
        parts += [(d, a, b) for a, b in zip(cuts[:-1], cuts[1:]) if b > a]
    moved_pool, tags, token_info, copies, *chunks = order_pages(
        both, moves, page_req, page_idx, hidden, pool, wide, parts
    )
    arrived = {}
    flying = {}

    def members(names):
        taken = []
        for group, which in names:
            cut = CUTS[group][which] * capacity // 16
            end = CUTS[group][which + 1] * capacity // 16
            taken += [
                c
                for c, (d, first, last) in enumerate(parts)
                if group_of(d, wide) == group and (first, last) == (cut, end)
            ]
        return taken

    def launch(values, *names):
        taken = members(names)
        values, sent = lax.optimization_barrier((values, [chunks[c] for c in taken]))
        for c, chunk in zip(taken, sent):
            flying[c] = send(chunk, "wide", parts[c][0])
        return values

    def land(values, *names):
        taken = members(names)
        values, got = lax.optimization_barrier((values, [flying[c] for c in taken]))
        arrived.update(zip(taken, got))
        return values

    def beside(step, value, *names):
        return land(step(launch(value, *names)), *names)

    def placed(pages):
        taken = sorted(arrived)
        place = jnp.stack([(me ^ parts[c][0]) * capacity + parts[c][1] for c in taken])
        pages = place_pages(place, [arrived[c] for c in taken], pages)
        arrived.clear()
        return pages

    gathered = beside(lambda value: exchange(value, "wide"), copies, (6, 0), (1, 0))
    tokens = pool.reshape(slots * PAGE, -1)
    if direct:
        block = jax.ShapeDtypeStruct((rows, 2 * HD), jnp.float32)
        partial = in_vmem(
            functools.partial(project_kernel, narrow),
            [block] * narrow,
            both,
            gathered,
            w_query,
            w_keyval,
            scratch=[pltpu.VMEM((rows, narrow * HD), jnp.float32)],
        )
        partial = launch(deal(partial, "narrow"), (6, 1))
        packed = in_vmem(
            functools.partial(pack_kernel, narrow),
            jax.ShapeDtypeStruct((wide, rows + wide, 2 * HD), jnp.bfloat16),
            None,
            *partial,
            tags,
        )
        received = land(exchange(packed, "wide"), (6, 1))
        received = launch(received, (7, 0), (1, 1), (7, 1))
        queries, keyval, new_entries, moved_req, moved_idx = in_vmem(
            functools.partial(unpack_kernel, rows),
            [
                jax.ShapeDtypeStruct((wide, rows, HD), jnp.bfloat16),
                jax.ShapeDtypeStruct((extra, wide * HD), jnp.bfloat16),
                jax.ShapeDtypeStruct((1, local_rows, wide * HD), jnp.bfloat16),
                jax.ShapeDtypeStruct((1, slots), jnp.int32),
                jax.ShapeDtypeStruct((1, slots), jnp.int32),
            ],
            (both, accepted),
            received,
        )
        moved_req, moved_idx = moved_req.reshape(slots), moved_idx.reshape(slots)
        queries = land(share(queries, "narrow"), (7, 0), (1, 1))
    else:
        gathered = gathered.reshape(rows, -1)
        query_part = jnp.dot(gathered, w_query, preferred_element_type=jnp.float32)
        keyval_part = jnp.dot(gathered, w_keyval, preferred_element_type=jnp.float32)
        query_part = jnp.transpose(query_part.reshape(rows, narrow, own_cols), (1, 0, 2))
        partial = jnp.concatenate(
            [query_part, jnp.broadcast_to(keyval_part[None], (narrow,) + keyval_part.shape)], axis=2
        )
        partial = launch(exchange(partial, "narrow"), (6, 1))
        projected = jnp.sum(partial, axis=0).astype(jnp.bfloat16)
        tags = tags[:, : 3 * capacity].astype(jnp.bfloat16)[:, None]
        tags = jnp.pad(tags, ((0, 0), (0, 7), (0, projected.shape[1] - tags.shape[2])))
        packed = jnp.broadcast_to(projected[None], (wide,) + projected.shape)
        packed = jnp.concatenate([packed, tags], axis=1)
        received = land(exchange(packed, "wide"), (6, 1))
        received = launch(received, (7, 0), (1, 1), (7, 1))
        tags_in = received[:, rows]
        queries = received[:, :rows, :own_cols]
        queries = land(spread(queries, "narrow"), (7, 0), (1, 1))
        queries = jnp.transpose(queries, (2, 1, 0, 3)).reshape(rows, HEADS, HD)
        queries = [jnp.transpose(queries, (1, 0, 2)).reshape(KVH, GROUPS * rows, HD)]
        keyval = jnp.transpose(received[:, :rows, own_cols:], (1, 0, 2)).reshape(rows, -1)
        keyval = jnp.pad(keyval, ((0, extra - rows), (0, 0)))
        tags_in = tags_in.astype(jnp.int32)
        moved_req = tags_in[:, :capacity].reshape(slots)
        moved_idx = tags_in[:, capacity : 2 * capacity] * 32
        moved_idx = (moved_idx + tags_in[:, 2 * capacity : 3 * capacity] - 1).reshape(slots)
        local_req = local_rows // STEPS
        fresh = lax.dynamic_slice_in_dim(keyval, me * local_rows, local_rows, 0)
        fresh = fresh.reshape(local_req, STEPS, -1)
        kept = lax.dynamic_slice_in_dim(accepted, me * local_req, local_req, 0)
        step_ids = jnp.arange(STEPS)[None, :, None]
        new_entries = jnp.where(
            step_ids < kept[:, None, None], fresh, jnp.zeros((), jnp.bfloat16)
        )

    queries = launch(queries, (2, 0), (7, 2))
    mixed = attend(both, lengths, queries, keyval, tokens, token_info, rows, piece)
    mixed = launch(land(mixed, (7, 1), (2, 0)), (3, 0))
    if direct:
        mixed = deal(mixed, "narrow")
    else:
        mixed = exchange(mixed[0], "narrow")
        mixed = mixed.reshape((narrow, wide) + mixed.shape[1:])
        mixed = [mixed[i] for i in range(narrow)]
    mixed = launch(land(mixed, (7, 2), (3, 0)), (4, 0), (2, 1))
    mixed = combine(mixed, piece)
    mixed, pages = lax.optimization_barrier((mixed, moved_pool))
    pages = placed(pages)
    mixed = land(exchange(mixed, "wide"), (4, 0), (2, 1))
    mixed, moved_pool = lax.optimization_barrier((mixed, pages))
    mixed = launch(mixed, (5, 0), (4, 1), (3, 1))
    attn = combine([mixed], piece, wide)
    attn = land(exchange(attn, "wide"), (5, 0), (4, 1), (3, 1))
    attn = launch(attn, (5, 1))
    if direct:
        sums = in_vmem(
            functools.partial(finish_kernel, narrow),
            [jax.ShapeDtypeStruct((rows // narrow, w_out.shape[1]), jnp.float32)] * narrow,
            both,
            attn,
            w_out,
        )
        sums = deal(sums, "narrow")
        attended = ((sums[0] + sums[1]) + (sums[2] + sums[3])).astype(jnp.bfloat16)
    else:
        attn = jnp.transpose(attn.reshape(-1, rows, HD), (1, 0, 2)).reshape(rows, -1)
        sums = jnp.dot(attn, w_out, preferred_element_type=jnp.float32)
        sums = sums.reshape(narrow, rows // narrow, -1)
        sums = exchange(sums, "narrow")
        attended = jnp.sum(sums, axis=0).astype(jnp.bfloat16)
    attended = land(attended, (5, 1))
    moved_pool = placed(moved_pool)
    return (attended, new_entries, moved_pool, moved_req, moved_idx)


def solution(mesh):
    in_specs = (
        P("wide", "narrow"),
        P("narrow", "wide"),
        P("narrow", "wide"),
        P("narrow", "wide"),
        P(("wide", "narrow"), None, None),
        P(("wide", "narrow")),
        P(("wide", "narrow")),
        P(),
        P(("wide", "narrow"), None),
        P(),
    )
    out_specs = (
        P("narrow", "wide"),
        P("wide", None, None),
        P(("wide", "narrow"), None, None),
        P(("wide", "narrow")),
        P(("wide", "narrow")),
    )
    return jax.shard_map(
        on_device, mesh=mesh, in_specs=in_specs, out_specs=out_specs, check_vma=False
    )
```

```python
import functools
import math

import jax
import jax.numpy as jnp
from jax import lax
from jax.experimental import pallas as pl
from jax.experimental.pallas import tpu as pltpu
from jax.sharding import PartitionSpec as P

HEADS = 32
KVH = 4
HD = 128
STEPS = 5
PAGE = 16
GROUPS = HEADS // KVH
NEG_FILL = -1e30
SCALE2 = math.log2(math.e) / math.sqrt(HD)
STAT = 16
MIB = 1024 * 1024
AHEAD = 5
NT = (((1,), (1,)), ((), ()))


def up(value, unit):
    return -(-value // unit) * unit


def column(row):
    return jnp.transpose(jnp.broadcast_to(row, (row.shape[1], row.shape[1])))


def order_kernel(
    wide, ahead, parts, me_ref, dest_ref, req_ref, idx_ref, pool_ref, out_ref, tag_ref, token_ref, *refs
):
    chunk_refs, refs = refs[: len(parts)], refs[len(parts) :]
    pages_ref, line_ref, source_ref, in_sem, out_sem, line_sem = refs
    slots = pool_ref.shape[0]
    capacity = slots // wide
    shape = (slots, slots)
    high = lax.broadcasted_iota(jnp.int32, shape, 0)
    low = lax.broadcasted_iota(jnp.int32, shape, 1)
    dest = dest_ref[...]
    same = column(dest.astype(jnp.float32)) == dest.astype(jnp.float32)
    rank = jnp.sum(jnp.where(same & (high < low), 1.0, 0.0), axis=0, keepdims=True)
    rest = capacity - ahead
    early = (dest * ahead).astype(jnp.float32) + rank
    late = ((dest ^ me_ref[0]) * rest + wide * ahead - ahead).astype(jnp.float32) + rank
    moved_to = jnp.where(rank < float(ahead), early, late)
    match = column(moved_to) == low.astype(jnp.float32)
    source = jnp.sum(jnp.where(match, high.astype(jnp.float32), 0.0), axis=0, keepdims=True)
    line_ref[...] = source.astype(jnp.int32)
    copy = pltpu.make_async_copy(line_ref, source_ref, line_sem)
    copy.start()
    copy.wait()

    own = out_ref.at[pl.ds(me_ref[0] * capacity + ahead, rest)]
    blocks = [(wide * ahead, rest, own)]
    for d, chunk in zip(parts, chunk_refs):
        if d:
            blocks.append((wide * ahead + d * rest, rest, chunk))
        else:
            blocks.insert(0, (0, wide * ahead, chunk))
    for c, (first, count, _) in enumerate(blocks):

        def start(j, carry, c=c):
            page = source_ref[0, j]
            pltpu.make_async_copy(pool_ref.at[page], pages_ref.at[j], in_sem.at[c]).start()
            return carry

        lax.fori_loop(first, first + count, start, 0)

    shifted = idx_ref[...] + 1
    fields = (req_ref[...], shifted // 32, shifted % 32)
    rank_col = column(rank)
    lane = low.astype(jnp.float32)
    spread_out = jnp.zeros(shape, jnp.float32)
    for i, field in enumerate(fields):
        picked = lane == rank_col + float(i * capacity)
        spread_out = spread_out + jnp.where(picked, column(field.astype(jnp.float32)), 0.0)
    line = lax.broadcasted_iota(jnp.int32, (wide, slots), 0)
    chosen = jnp.where(line == dest, 1.0, 0.0).astype(jnp.bfloat16)
    tag_ref[...] = jnp.dot(
        chosen, spread_out.astype(jnp.bfloat16), preferred_element_type=jnp.float32
    )

    tokens = slots * PAGE
    page = lax.broadcasted_iota(jnp.int32, (slots, tokens), 0)
    token = lax.broadcasted_iota(jnp.int32, (slots, tokens), 1)
    widen = jnp.where(page == token // PAGE, 1.0, 0.0).astype(jnp.bfloat16)
    row = lax.broadcasted_iota(jnp.int32, (8, slots), 0)
    stacked = jnp.zeros((8, slots), jnp.float32)
    for i, field in enumerate(fields):
        stacked = jnp.where(row == i, field.astype(jnp.float32), stacked)
    token_ref[...] = jnp.dot(
        stacked.astype(jnp.bfloat16), widen, preferred_element_type=jnp.float32
    )

    copies = []
    for c, (first, count, target) in enumerate(blocks):
        held = pages_ref.at[pl.ds(first, count)]
        pltpu.make_async_copy(pool_ref.at[pl.ds(0, count)], held, in_sem.at[c]).wait()
        copies.append(pltpu.make_async_copy(held, target, out_sem.at[c]))
        copies[-1].start()
    for copy in copies:
        copy.wait()


def order_pages(me, dest, page_req, page_idx, pool, wide, ahead, parts):
    slots = pool.shape[0]
    part = lambda count: jax.ShapeDtypeStruct((count,) + pool.shape[1:], pool.dtype)
    out_shape = [part(slots), jax.ShapeDtypeStruct((wide, slots), jnp.float32)]
    out_shape += [jax.ShapeDtypeStruct((8, slots * PAGE), jnp.float32)]
    rest = slots // wide - ahead
    out_shape += [part(rest if d else wide * ahead) for d in parts]
    vmem = pl.BlockSpec(memory_space=pltpu.VMEM)
    hbm = pl.BlockSpec(memory_space=pltpu.HBM)
    return pl.pallas_call(
        functools.partial(order_kernel, wide, ahead, parts),
        out_shape=out_shape,
        in_specs=[pl.BlockSpec(memory_space=pltpu.SMEM), vmem, vmem, vmem, hbm],
        out_specs=[hbm, vmem, vmem] + [hbm] * len(parts),
        scratch_shapes=[
            pltpu.VMEM(pool.shape, pool.dtype),
            pltpu.VMEM((1, slots), jnp.int32),
            pltpu.SMEM((1, slots), jnp.int32),
            pltpu.SemaphoreType.DMA((1 + len(parts),)),
            pltpu.SemaphoreType.DMA((1 + len(parts),)),
            pltpu.SemaphoreType.DMA,
        ],
        compiler_params=pltpu.CompilerParams(vmem_limit_bytes=56 * MIB),
        cost_estimate=pl.CostEstimate(
            flops=0, bytes_accessed=2 * pool.size * 2, transcendentals=0
        ),
    )(me, dest.reshape(1, -1), page_req.reshape(1, -1), page_idx.reshape(1, -1), pool)


def place_kernel(counts, place_ref, *refs):
    in_refs, (out_ref, sem) = refs[:-3], refs[-2:]
    copies = []
    for chunk, count in zip(in_refs, counts):
        depth = chunk.shape[0] // count
        for i in range(count):
            c = len(copies)
            target = out_ref.at[pl.ds(place_ref[c], depth)]
            source = chunk.at[pl.ds(i * depth, depth)]
            copies.append(pltpu.make_async_copy(source, target, sem.at[c]))
    for copy in copies:
        copy.start()
    for copy in copies:
        copy.wait()


def place_pages(place, chunks, counts, pages):
    size = sum(chunk.size for chunk in chunks)
    return pl.pallas_call(
        functools.partial(place_kernel, counts),
        out_shape=jax.ShapeDtypeStruct(pages.shape, pages.dtype),
        in_specs=[pl.BlockSpec(memory_space=pltpu.SMEM)]
        + [pl.BlockSpec(memory_space=pltpu.VMEM)] * len(chunks)
        + [pl.BlockSpec(memory_space=pl.ANY)],
        out_specs=pl.BlockSpec(memory_space=pl.ANY),
        scratch_shapes=[pltpu.SemaphoreType.DMA((sum(counts),))],
        input_output_aliases={len(chunks) + 1: 0},
        compiler_params=pltpu.CompilerParams(vmem_limit_bytes=2 * size + 2 * MIB),
        cost_estimate=pl.CostEstimate(flops=0, bytes_accessed=4 * size, transcendentals=0),
    )(place, *chunks, pages)


def cut(value):
    return value.astype(jnp.bfloat16).astype(jnp.float32)


def split_stats(peak, total):
    high = cut(peak)
    mid = cut(peak - high)
    return high, mid, peak - high - mid, cut(total), total - cut(total)


def attend_kernel(rows, piece, peers, me_ref, length_ref, *refs):
    query_refs, refs = refs[:peers], refs[peers:]
    key_ref, value_ref, new_key_ref, new_value_ref, token_ref = refs[:5]
    out_refs = refs[5 : 5 + peers]
    bias_ref, new_bias_ref, score_ref, weight_ref, query_ref, result_ref = refs[5 + peers :]
    tokens = key_ref.shape[0]
    step = pl.program_id(0)

    @pl.when(step == 0)
    def _():
        owner = token_ref[0:1, :]
        offset = lax.broadcasted_iota(jnp.int32, owner.shape, 1) % PAGE
        spot = (token_ref[1:2, :] * 32 + token_ref[2:3, :] - 1) * PAGE + offset.astype(jnp.float32)
        request = lax.broadcasted_iota(jnp.int32, (rows, 1), 0) // STEPS
        limit = jnp.zeros((rows, 1), jnp.int32)
        for r in range(rows // STEPS):
            limit = jnp.where(request == r, length_ref[r], limit)
        seen = (owner == request.astype(jnp.float32)) & (spot < limit.astype(jnp.float32))
        bias_ref[...] = jnp.where(seen, 0.0, NEG_FILL)
        row = lax.broadcasted_iota(jnp.int32, new_bias_ref.shape, 0)
        col = lax.broadcasted_iota(jnp.int32, new_bias_ref.shape, 1)
        first = jnp.where((me_ref[0] == 0) & (me_ref[1] == 0), 1, 0)
        seen = (row // STEPS == col // STEPS) & (col <= row) & (col < rows * first)
        new_bias_ref[...] = jnp.where(seen, 0.0, NEG_FILL)
        if peers > 1:
            for d in range(peers):
                query_ref[me_ref[1] ^ d] = query_refs[d][...]

    if peers > 1:
        per_step = query_refs[0].shape[0] // KVH
        query = jnp.concatenate(
            [
                query_ref[n, step * per_step + i].astype(jnp.float32)
                for i in range(per_step)
                for n in range(peers)
            ],
            axis=0,
        ).astype(jnp.bfloat16)
    else:
        query = query_refs[0][0]
    score_ref[:, :tokens] = lax.dot_general(
        query, key_ref[...], NT, preferred_element_type=jnp.float32
    )
    score_ref[:, tokens:] = lax.dot_general(
        query, new_key_ref[...], NT, preferred_element_type=jnp.float32
    )
    together = 1 if rows % 16 == 0 else 2
    span = together * rows
    peaks, totals = [], []
    for c in range(GROUPS // together):
        block = pl.ds(c * span, span)
        old = score_ref[block, :tokens].reshape(together, rows, tokens) * SCALE2 + bias_ref[...]
        new = score_ref[block, tokens:].reshape(together, rows, -1) * SCALE2 + new_bias_ref[...]
        peak = jnp.maximum(
            jnp.max(old, axis=-1, keepdims=True), jnp.max(new, axis=-1, keepdims=True)
        )
        old = jnp.exp2(old - peak)
        new = jnp.exp2(new - peak)
        totals.append(
            (jnp.sum(old, axis=-1, keepdims=True) + jnp.sum(new, axis=-1, keepdims=True)).reshape(
                span, 1
            )
        )
        peaks.append(peak.reshape(span, 1))
        weight_ref[block, :tokens] = old.reshape(span, tokens).astype(jnp.bfloat16)
        weight_ref[block, tokens:] = new.reshape(span, -1).astype(jnp.bfloat16)
    mixed = jnp.dot(
        weight_ref[:, :tokens], value_ref[...], preferred_element_type=jnp.float32
    ) + jnp.dot(weight_ref[:, tokens:], new_value_ref[...], preferred_element_type=jnp.float32)
    peak = jnp.concatenate(peaks, axis=0)
    total = jnp.concatenate(totals, axis=0)
    lane = lax.broadcasted_iota(jnp.int32, (GROUPS * rows, HD), 1)
    stats = jnp.zeros((GROUPS * rows, HD), jnp.float32)
    for i, part in enumerate(split_stats(peak, total)):
        stats = jnp.where(lane == i, part, stats)
    pick = (
        lax.broadcasted_iota(jnp.int32, (STAT, HD), 0)
        == lax.broadcasted_iota(jnp.int32, (STAT, HD), 1)
    ).astype(jnp.bfloat16)
    fill = result_ref.shape[1] - STAT - piece
    for c in range(GROUPS * rows // piece):
        part = slice(c * piece, (c + 1) * piece)
        turned = lax.dot_general(
            pick,
            jnp.concatenate(
                [stats[part], jnp.zeros((HD - piece, HD), jnp.float32)], axis=0
            ).astype(jnp.bfloat16),
            NT,
            preferred_element_type=jnp.float32,
        )
        result_ref[c] = jnp.concatenate(
            [turned, mixed[part], jnp.zeros((fill, HD), jnp.float32)], axis=0
        ).astype(jnp.bfloat16)
    if peers > 1:
        for d, out_ref in enumerate(out_refs):

            @pl.when((step ^ me_ref[1]) == d)
            def _():
                out_ref[...] = result_ref[...]
    else:
        out_refs[0][...] = result_ref[...]


def attend(me, lengths, queries, keyval, pool, token_info, rows, piece):
    tokens = pool.shape[0]
    extra = keyval.shape[0]
    peers = len(queries)
    pieces = GROUPS * rows // piece
    height = STAT + up(piece, 16)
    whole = lambda shape: pl.BlockSpec(shape, lambda k: (0,) * len(shape))
    if peers > 1:
        query_spec = whole(queries[0].shape)
        out_spec = whole((pieces, height, HD))
        out_shape = jax.ShapeDtypeStruct((pieces, height, HD), jnp.bfloat16)
    else:
        query_spec = pl.BlockSpec((1,) + queries[0].shape[1:], lambda k: (k, 0, 0))
        out_spec = pl.BlockSpec((pieces, height, HD), lambda k: (k, 0, 0))
        out_shape = jax.ShapeDtypeStruct((KVH * pieces, height, HD), jnp.bfloat16)
    return pl.pallas_call(
        functools.partial(attend_kernel, rows, piece, peers),
        grid=(KVH,),
        out_shape=[out_shape] * peers,
        in_specs=[pl.BlockSpec(memory_space=pltpu.SMEM)] * 2
        + [query_spec] * peers
        + [
            pl.BlockSpec((tokens, HD), lambda k: (0, k)),
            pl.BlockSpec((tokens, HD), lambda k: (0, KVH + k)),
            pl.BlockSpec((extra, HD), lambda k: (0, k)),
            pl.BlockSpec((extra, HD), lambda k: (0, KVH + k)),
            whole(token_info.shape),
        ],
        out_specs=[out_spec] * peers,
        scratch_shapes=[
            pltpu.VMEM((rows, tokens), jnp.float32),
            pltpu.VMEM((rows, extra), jnp.float32),
            pltpu.VMEM((GROUPS * rows, tokens + extra), jnp.float32),
            pltpu.VMEM((GROUPS * rows, tokens + extra), jnp.bfloat16),
            pltpu.VMEM((peers,) + queries[0].shape, jnp.bfloat16),
            pltpu.VMEM((pieces, height, HD), jnp.bfloat16),
        ],
        compiler_params=pltpu.CompilerParams(vmem_limit_bytes=56 * MIB),
        cost_estimate=pl.CostEstimate(flops=1, bytes_accessed=1, transcendentals=0),
    )(me, lengths, *queries, pool, pool, keyval, keyval, token_info)


def combine_kernel(piece, last, count, *refs):
    if last:
        part_ref, out_ref = refs
        part_refs = [part_ref.at[pl.ds(i, 1)] for i in range(count)]
    else:
        part_refs, out_ref = refs[:count], refs[count]
    groups, height = part_refs[0].shape[:2]
    peaks, totals = [], []
    for i in range(count):
        for j in range(groups):
            stat = part_refs[i][j, :STAT, :].astype(jnp.float32)
            peaks.append(stat[0:1] + stat[1:2] + stat[2:3])
            totals.append(stat[3:4] + stat[4:5])
    peak = jnp.concatenate(peaks, axis=0).reshape(count, groups, HD)
    total = jnp.concatenate(totals, axis=0).reshape(count, groups, HD)
    top = jnp.max(peak, axis=0)
    lead = jnp.exp2(peak - top[None])
    whole = jnp.sum(lead * total, axis=0)
    if last:
        lane = lax.broadcasted_iota(jnp.int32, whole.shape, 1)
        lead = lead / jnp.where(lane < piece, whole, 1.0)[None]
    lead = lead.reshape(count * groups, HD)
    if (count * groups) % HD:
        fill = up(count * groups, HD) - count * groups
        lead = jnp.concatenate([lead, jnp.zeros((fill, HD), jnp.float32)], axis=0)
    lead = jnp.transpose(lead)
    rows = height - STAT
    for j in range(groups):
        result = jnp.zeros((rows, HD), jnp.float32)
        for i in range(count):
            c = i * groups + j
            result = result + lead[:rows, c : c + 1] * part_refs[i][j, STAT:, :].astype(jnp.float32)
        if last:
            for i in range(out_ref.shape[0]):
                out_ref[i] = result[:piece].astype(jnp.bfloat16)
        else:
            stats = split_stats(top[j : j + 1], whole[j : j + 1])
            rest = jnp.zeros((STAT - len(stats), HD), jnp.float32)
            out_ref[j] = jnp.concatenate([*stats, rest, result], axis=0).astype(jnp.bfloat16)


def combine(parts, piece, repeats=0):
    count = parts[0].shape[0] if repeats else len(parts)
    shape = (repeats, piece, HD) if repeats else parts[0].shape
    return pl.pallas_call(
        functools.partial(combine_kernel, piece, repeats > 0, count),
        out_shape=jax.ShapeDtypeStruct(shape, jnp.bfloat16),
        in_specs=[pl.BlockSpec(memory_space=pltpu.VMEM)] * len(parts),
        out_specs=pl.BlockSpec(memory_space=pltpu.VMEM),
        compiler_params=pltpu.CompilerParams(vmem_limit_bytes=8 * MIB),
        cost_estimate=pl.CostEstimate(
            flops=2 * len(parts) * parts[0].size,
            bytes_accessed=len(parts) * parts[0].size * 2,
            transcendentals=0,
        ),
    )(*parts)


def reorder(shape, unit, valid, own, column):
    first, second = (0, 1) if column else (1, 0)
    block = lax.broadcasted_iota(jnp.int32, shape, second) // unit
    place = lax.broadcasted_iota(jnp.int32, shape, second) % unit
    target = (block ^ own) * valid + place
    match = (lax.broadcasted_iota(jnp.int32, shape, first) == target) & (place < valid)
    return match.astype(jnp.bfloat16)


def project_kernel(peers, me_ref, hidden_ref, query_ref, keyval_ref, *refs):
    out_refs, (full_ref,) = refs[:peers], refs[peers:]
    count, local, depth = hidden_ref.shape
    unit = up(local, 8)
    blocks = []
    for i in range(count):
        blocks.append(hidden_ref[i].astype(jnp.float32))
        if unit > local:
            blocks.append(jnp.zeros((unit - local, depth), jnp.float32))
    hidden = jnp.concatenate(blocks, axis=0).astype(jnp.bfloat16)
    order = reorder((count * local, count * unit), unit, local, 0, True)
    hidden = jnp.dot(order, hidden, preferred_element_type=jnp.float32).astype(jnp.bfloat16)
    full_ref[...] = jnp.dot(hidden, query_ref[...], preferred_element_type=jnp.float32)
    keyval = jnp.dot(hidden, keyval_ref[...], preferred_element_type=jnp.float32)
    for d, out_ref in enumerate(out_refs):
        start = pl.multiple_of((me_ref[1] ^ d) * HD, HD)
        out_ref[:, :HD] = full_ref[:, pl.ds(start, HD)]
        out_ref[:, HD:] = keyval


def pack_kernel(peers, *refs):
    own, tag_ref, out_ref = refs[:peers], refs[peers], refs[peers + 1]
    total = (own[0][...] + own[1][...]) + (own[2][...] + own[3][...])
    tags = jnp.concatenate([tag_ref[...], jnp.zeros_like(tag_ref[...])], axis=1)
    packed = jnp.concatenate([total, tags], axis=0).astype(jnp.bfloat16)
    for i in range(out_ref.shape[0]):
        out_ref[i] = packed


def unpack_kernel(rows, me_ref, kept_ref, part_ref, query_ref, keyval_ref, *refs):
    entry_ref, req_ref, idx_ref = refs
    count = part_ref.shape[0]
    line = lax.broadcasted_iota(jnp.int32, (count, HD), 0)
    tags = jnp.zeros((count, HD), jnp.float32)
    fill = jnp.zeros((keyval_ref.shape[0] - rows, HD), jnp.float32)
    for i in range(count):
        part = part_ref[i].astype(jnp.float32)
        query_ref[i] = part[:rows, :HD].astype(jnp.bfloat16)
        block = jnp.concatenate([part[:rows, HD:], fill], axis=0).astype(jnp.bfloat16)
        keyval_ref[:, i * HD : (i + 1) * HD] = block
        mine = jnp.where(line == me_ref[0], part[rows : rows + count, :HD], 0.0)
        tags = tags + jnp.where(line == i, jnp.sum(mine, axis=0, keepdims=True), 0.0)
    capacity = HD // count
    high = lax.broadcasted_iota(jnp.int32, (HD, HD), 0)
    low = lax.broadcasted_iota(jnp.int32, (HD, HD), 1)
    slot = lax.broadcasted_iota(jnp.int32, (count, HD), 1)
    tags = tags.astype(jnp.bfloat16)
    fields = []
    for i in range(3):
        pick = jnp.where(high == i * capacity + low % capacity, 1.0, 0.0).astype(jnp.bfloat16)
        spread_out = jnp.dot(tags, pick, preferred_element_type=jnp.float32)
        spread_out = jnp.where(slot // capacity == line, spread_out, 0.0)
        fields.append(jnp.sum(spread_out, axis=0, keepdims=True))
    req_ref[...] = fields[0].astype(jnp.int32)
    idx_ref[...] = (fields[1] * 32.0 + fields[2] - 1.0).astype(jnp.int32)
    local = entry_ref.shape[1]
    step = lax.broadcasted_iota(jnp.int32, (16, keyval_ref.shape[0]), 0)
    row = lax.broadcasted_iota(jnp.int32, (16, keyval_ref.shape[0]), 1)
    kept = (row == me_ref[0] * local + step) & (step < kept_ref[me_ref[0]])
    kept = jnp.where(kept, 1.0, 0.0).astype(jnp.bfloat16)
    entries = jnp.dot(kept, keyval_ref[...], preferred_element_type=jnp.float32)
    entry_ref[0] = entries[:local].astype(jnp.bfloat16)


def finish_kernel(peers, me_ref, part_ref, weight_ref, *refs):
    count, rows = part_ref.shape[:2]
    local = rows // peers
    unit = up(local, 16)
    whole = jnp.concatenate([part_ref[i] for i in range(count)], axis=1)
    order = reorder((peers * unit, rows), unit, local, me_ref[1], False)
    mixed = jnp.dot(order, whole, preferred_element_type=jnp.float32)
    mixed = jnp.dot(mixed.astype(jnp.bfloat16), weight_ref[...], preferred_element_type=jnp.float32)
    for d, out_ref in enumerate(refs):
        out_ref[...] = mixed[d * unit : d * unit + local]


def in_vmem(kernel, out_shape, me, *args, scratch=()):
    head = [] if me is None else list(me) if isinstance(me, tuple) else [me]
    return pl.pallas_call(
        kernel,
        out_shape=out_shape,
        in_specs=[pl.BlockSpec(memory_space=pltpu.SMEM)] * len(head)
        + [pl.BlockSpec(memory_space=pltpu.VMEM)] * len(args),
        out_specs=jax.tree.map(lambda _: pl.BlockSpec(memory_space=pltpu.VMEM), out_shape),
        scratch_shapes=scratch,
        compiler_params=pltpu.CompilerParams(vmem_limit_bytes=16 * MIB),
        cost_estimate=pl.CostEstimate(
            flops=0, bytes_accessed=sum(2 * arg.size for arg in args), transcendentals=0
        ),
    )(*head, *args)


def group_of(d, wide):
    return d if wide <= 8 or d == 0 else 1 + (d - 1) * 7 // (wide - 1)


def spread(block, axis):
    count = lax.axis_size(axis)
    return lax.all_to_all(
        jnp.broadcast_to(block[None], (count,) + block.shape),
        axis,
        split_axis=0,
        concat_axis=0,
        tiled=True,
    )


def on_device(hidden, w_query, w_keyval, w_out, pool, page_req, page_idx, lengths, moves, accepted):
    wide = lax.axis_size("wide")
    narrow = lax.axis_size("narrow")
    local_rows = hidden.shape[0]
    rows = local_rows * wide
    requests = rows // STEPS
    slots = pool.shape[0]
    capacity = slots // wide
    own_cols = w_query.shape[1] // narrow
    piece = HEADS * rows // (wide * narrow)
    extra = up(rows, HD)
    direct = piece == rows and own_cols == HD and slots == HD
    direct = direct and wide == 8 and narrow == 4 and local_rows == STEPS
    me = lax.axis_index("wide")
    both = jnp.stack([me, lax.axis_index("narrow")])
    exchange = functools.partial(lax.all_to_all, split_axis=0, concat_axis=0, tiled=True)

    def send(block, axis, d):
        return lax.ppermute(block, axis, [(i, i ^ d) for i in range(lax.axis_size(axis))])

    def share(block, axis):
        return [block] + [send(block, axis, d) for d in range(1, lax.axis_size(axis))]

    def deal(blocks, axis):
        return [blocks[0]] + [send(block, axis, d) for d, block in enumerate(blocks) if d]

    gathered = spread(hidden, "wide")

    ahead = AHEAD * capacity // 16
    parts = list(range(0 if ahead else 1, wide))
    moved_pool, tags, token_info, *chunks = order_pages(
        both, moves, page_req, page_idx, pool, wide, ahead, parts
    )
    chunks = dict(zip(parts, chunks))
    arrived = {}
    flying = {}

    def members(groups):
        return [d for group in groups for d in parts if group_of(d, wide) == group]

    def launch(values, *groups):
        taken = members(groups)
        values, sent = lax.optimization_barrier((values, [chunks[d] for d in taken]))
        for d, chunk in zip(taken, sent):
            flying[d] = send(chunk, "wide", d) if d else exchange(chunk, "wide")
        return values

    def land(values, *groups):
        taken = members(groups)
        values, got = lax.optimization_barrier((values, [flying[d] for d in taken]))
        arrived.update(zip(taken, got))
        return values

    def beside(step, value, *names):
        return land(step(launch(value, *names)), *names)

    def placed(pages):
        taken = sorted(arrived)
        place = []
        for d in taken:
            place += [(me ^ d) * capacity + ahead] if d else [w * capacity for w in range(wide)]
        place = jnp.stack([jnp.asarray(index, jnp.int32) for index in place])
        counts = [1 if d else wide for d in taken]
        pages = place_pages(place, [arrived[d] for d in taken], counts, pages)
        arrived.clear()
        return pages

    tokens = pool.reshape(slots * PAGE, -1)
    if direct:
        block = jax.ShapeDtypeStruct((rows, 2 * HD), jnp.float32)
        partial = in_vmem(
            functools.partial(project_kernel, narrow),
            [block] * narrow,
            both,
            gathered,
            w_query,
            w_keyval,
            scratch=[pltpu.VMEM((rows, narrow * HD), jnp.float32)],
        )
        partial = deal(partial, "narrow")
        packed = in_vmem(
            functools.partial(pack_kernel, narrow),
            jax.ShapeDtypeStruct((wide, rows + wide, 2 * HD), jnp.bfloat16),
            None,
            *partial,
            tags,
        )
        received = beside(lambda value: exchange(value, "wide"), packed, 6, 1)
        received = launch(received, 0)
        queries, keyval, new_entries, moved_req, moved_idx = in_vmem(
            functools.partial(unpack_kernel, rows),
            [
                jax.ShapeDtypeStruct((wide, rows, HD), jnp.bfloat16),
                jax.ShapeDtypeStruct((extra, wide * HD), jnp.bfloat16),
                jax.ShapeDtypeStruct((1, local_rows, wide * HD), jnp.bfloat16),
                jax.ShapeDtypeStruct((1, slots), jnp.int32),
                jax.ShapeDtypeStruct((1, slots), jnp.int32),
            ],
            (both, accepted),
            received,
        )
        moved_req, moved_idx = moved_req.reshape(slots), moved_idx.reshape(slots)
        queries = share(queries, "narrow")
    else:
        gathered = gathered.reshape(rows, -1)
        query_part = jnp.dot(gathered, w_query, preferred_element_type=jnp.float32)
        keyval_part = jnp.dot(gathered, w_keyval, preferred_element_type=jnp.float32)
        query_part = jnp.transpose(query_part.reshape(rows, narrow, own_cols), (1, 0, 2))
        partial = jnp.concatenate(
            [query_part, jnp.broadcast_to(keyval_part[None], (narrow,) + keyval_part.shape)], axis=2
        )
        partial = exchange(partial, "narrow")
        projected = jnp.sum(partial, axis=0).astype(jnp.bfloat16)
        tags = tags[:, : 3 * capacity].astype(jnp.bfloat16)[:, None]
        tags = jnp.pad(tags, ((0, 0), (0, 7), (0, projected.shape[1] - tags.shape[2])))
        packed = jnp.broadcast_to(projected[None], (wide,) + projected.shape)
        packed = jnp.concatenate([packed, tags], axis=1)
        received = beside(lambda value: exchange(value, "wide"), packed, 6, 1)
        received = launch(received, 0)
        tags_in = received[:, rows]
        queries = received[:, :rows, :own_cols]
        queries = spread(queries, "narrow")
        queries = jnp.transpose(queries, (2, 1, 0, 3)).reshape(rows, HEADS, HD)
        queries = [jnp.transpose(queries, (1, 0, 2)).reshape(KVH, GROUPS * rows, HD)]
        keyval = jnp.transpose(received[:, :rows, own_cols:], (1, 0, 2)).reshape(rows, -1)
        keyval = jnp.pad(keyval, ((0, extra - rows), (0, 0)))
        tags_in = tags_in.astype(jnp.int32)
        moved_req = tags_in[:, :capacity].reshape(slots)
        moved_idx = tags_in[:, capacity : 2 * capacity] * 32
        moved_idx = (moved_idx + tags_in[:, 2 * capacity : 3 * capacity] - 1).reshape(slots)
        local_req = local_rows // STEPS
        fresh = lax.dynamic_slice_in_dim(keyval, me * local_rows, local_rows, 0)
        fresh = fresh.reshape(local_req, STEPS, -1)
        kept = lax.dynamic_slice_in_dim(accepted, me * local_req, local_req, 0)
        step_ids = jnp.arange(STEPS)[None, :, None]
        new_entries = jnp.where(
            step_ids < kept[:, None, None], fresh, jnp.zeros((), jnp.bfloat16)
        )

    mixed = attend(both, lengths, queries, keyval, tokens, token_info, rows, piece)
    if direct:
        mixed = land(deal(mixed, "narrow"), 0)
    else:
        mixed = land(exchange(mixed[0], "narrow"), 0)
        mixed = mixed.reshape((narrow, wide) + mixed.shape[1:])
        mixed = [mixed[i] for i in range(narrow)]
    mixed = combine(mixed, piece)
    mixed, pages = lax.optimization_barrier((mixed, moved_pool))
    pages = placed(pages)
    mixed = beside(lambda value: exchange(value, "wide"), mixed, 4, 2)
    mixed, moved_pool = lax.optimization_barrier((mixed, pages))
    attn = combine([mixed], piece, wide)
    attn = beside(lambda value: exchange(value, "wide"), attn, 5, 3)
    if direct:
        sums = in_vmem(
            functools.partial(finish_kernel, narrow),
            [jax.ShapeDtypeStruct((rows // narrow, w_out.shape[1]), jnp.float32)] * narrow,
            both,
            attn,
            w_out,
        )
        sums = beside(lambda value: deal(value, "narrow"), sums, 7)
        attended = ((sums[0] + sums[1]) + (sums[2] + sums[3])).astype(jnp.bfloat16)
    else:
        attn = jnp.transpose(attn.reshape(-1, rows, HD), (1, 0, 2)).reshape(rows, -1)
        sums = jnp.dot(attn, w_out, preferred_element_type=jnp.float32)
        sums = sums.reshape(narrow, rows // narrow, -1)
        sums = beside(lambda value: exchange(value, "narrow"), sums, 7)
        attended = jnp.sum(sums, axis=0).astype(jnp.bfloat16)
    moved_pool = placed(moved_pool)
    return (attended, new_entries, moved_pool, moved_req, moved_idx)


def solution(mesh):
    in_specs = (
        P("wide", "narrow"),
        P("narrow", "wide"),
        P("narrow", "wide"),
        P("narrow", "wide"),
        P(("wide", "narrow"), None, None),
        P(("wide", "narrow")),
        P(("wide", "narrow")),
        P(),
        P(("wide", "narrow"), None),
        P(),
    )
    out_specs = (
        P("narrow", "wide"),
        P("wide", None, None),
        P(("wide", "narrow"), None, None),
        P(("wide", "narrow")),
        P(("wide", "narrow")),
    )
    return jax.shard_map(
        on_device, mesh=mesh, in_specs=in_specs, out_specs=out_specs, check_vma=False
    )
```

```python
import functools
import math

import jax
import jax.numpy as jnp
from jax import lax
from jax.experimental import pallas as pl
from jax.experimental.pallas import tpu as pltpu
from jax.sharding import PartitionSpec as P

HEADS = 32
KVH = 4
HD = 128
STEPS = 5
PAGE = 16
GROUPS = HEADS // KVH
NEG_FILL = -1e30
SCALE2 = math.log2(math.e) / math.sqrt(HD)
STAT = 16
MIB = 1024 * 1024
AHEAD = 5
NT = (((1,), (1,)), ((), ()))


def up(value, unit):
    return -(-value // unit) * unit


def column(row):
    return jnp.transpose(jnp.broadcast_to(row, (row.shape[1], row.shape[1])))


def order_kernel(
    wide, ahead, parts, me_ref, dest_ref, req_ref, idx_ref, pool_ref, out_ref, tag_ref, token_ref, *refs
):
    chunk_refs, refs = refs[: len(parts)], refs[len(parts) :]
    pages_ref, line_ref, source_ref, in_sem, out_sem, line_sem = refs
    slots = pool_ref.shape[0]
    capacity = slots // wide
    shape = (slots, slots)
    high = lax.broadcasted_iota(jnp.int32, shape, 0)
    low = lax.broadcasted_iota(jnp.int32, shape, 1)
    dest = dest_ref[...]
    same = column(dest.astype(jnp.float32)) == dest.astype(jnp.float32)
    rank = jnp.sum(jnp.where(same & (high < low), 1.0, 0.0), axis=0, keepdims=True)
    rest = capacity - ahead
    early = (dest * ahead).astype(jnp.float32) + rank
    late = ((dest ^ me_ref[0]) * rest + wide * ahead - ahead).astype(jnp.float32) + rank
    moved_to = jnp.where(rank < float(ahead), early, late)
    match = column(moved_to) == low.astype(jnp.float32)
    source = jnp.sum(jnp.where(match, high.astype(jnp.float32), 0.0), axis=0, keepdims=True)
    line_ref[...] = source.astype(jnp.int32)
    copy = pltpu.make_async_copy(line_ref, source_ref, line_sem)
    copy.start()
    copy.wait()

    own = out_ref.at[pl.ds(me_ref[0] * capacity + ahead, rest)]
    blocks = [(wide * ahead, rest, own)]
    for d, chunk in zip(parts, chunk_refs):
        if d:
            blocks.append((wide * ahead + d * rest, rest, chunk))
        else:
            blocks.insert(0, (0, wide * ahead, chunk))
    for c, (first, count, _) in enumerate(blocks):

        def start(j, carry, c=c):
            page = source_ref[0, j]
            pltpu.make_async_copy(pool_ref.at[page], pages_ref.at[j], in_sem.at[c]).start()
            return carry

        lax.fori_loop(first, first + count, start, 0)

    shifted = idx_ref[...] + 1
    fields = (req_ref[...], shifted // 32, shifted % 32)
    rank_col = column(rank)
    lane = low.astype(jnp.float32)
    spread_out = jnp.zeros(shape, jnp.float32)
    for i, field in enumerate(fields):
        picked = lane == rank_col + float(i * capacity)
        spread_out = spread_out + jnp.where(picked, column(field.astype(jnp.float32)), 0.0)
    line = lax.broadcasted_iota(jnp.int32, (wide, slots), 0)
    chosen = jnp.where(line == dest, 1.0, 0.0).astype(jnp.bfloat16)
    tag_ref[...] = jnp.dot(
        chosen, spread_out.astype(jnp.bfloat16), preferred_element_type=jnp.float32
    )

    tokens = slots * PAGE
    page = lax.broadcasted_iota(jnp.int32, (slots, tokens), 0)
    token = lax.broadcasted_iota(jnp.int32, (slots, tokens), 1)
    widen = jnp.where(page == token // PAGE, 1.0, 0.0).astype(jnp.bfloat16)
    row = lax.broadcasted_iota(jnp.int32, (8, slots), 0)
    stacked = jnp.zeros((8, slots), jnp.float32)
    for i, field in enumerate(fields):
        stacked = jnp.where(row == i, field.astype(jnp.float32), stacked)
    token_ref[...] = jnp.dot(
        stacked.astype(jnp.bfloat16), widen, preferred_element_type=jnp.float32
    )

    copies = []
    for c, (first, count, target) in enumerate(blocks):
        held = pages_ref.at[pl.ds(first, count)]
        pltpu.make_async_copy(pool_ref.at[pl.ds(0, count)], held, in_sem.at[c]).wait()
        copies.append(pltpu.make_async_copy(held, target, out_sem.at[c]))
        copies[-1].start()
    for copy in copies:
        copy.wait()


def order_pages(me, dest, page_req, page_idx, pool, wide, ahead, parts):
    slots = pool.shape[0]
    part = lambda count: jax.ShapeDtypeStruct((count,) + pool.shape[1:], pool.dtype)
    out_shape = [part(slots), jax.ShapeDtypeStruct((wide, slots), jnp.float32)]
    out_shape += [jax.ShapeDtypeStruct((8, slots * PAGE), jnp.float32)]
    rest = slots // wide - ahead
    out_shape += [part(rest if d else wide * ahead) for d in parts]
    vmem = pl.BlockSpec(memory_space=pltpu.VMEM)
    hbm = pl.BlockSpec(memory_space=pltpu.HBM)
    return pl.pallas_call(
        functools.partial(order_kernel, wide, ahead, parts),
        out_shape=out_shape,
        in_specs=[pl.BlockSpec(memory_space=pltpu.SMEM), vmem, vmem, vmem, hbm],
        out_specs=[hbm, vmem, vmem] + [hbm] * len(parts),
        scratch_shapes=[
            pltpu.VMEM(pool.shape, pool.dtype),
            pltpu.VMEM((1, slots), jnp.int32),
            pltpu.SMEM((1, slots), jnp.int32),
            pltpu.SemaphoreType.DMA((1 + len(parts),)),
            pltpu.SemaphoreType.DMA((1 + len(parts),)),
            pltpu.SemaphoreType.DMA,
        ],
        compiler_params=pltpu.CompilerParams(vmem_limit_bytes=56 * MIB),
        cost_estimate=pl.CostEstimate(
            flops=0, bytes_accessed=2 * pool.size * 2, transcendentals=0
        ),
    )(me, dest.reshape(1, -1), page_req.reshape(1, -1), page_idx.reshape(1, -1), pool)


def place_kernel(counts, place_ref, *refs):
    in_refs, (out_ref, sem) = refs[:-3], refs[-2:]
    copies = []
    for chunk, count in zip(in_refs, counts):
        depth = chunk.shape[0] // count
        for i in range(count):
            c = len(copies)
            target = out_ref.at[pl.ds(place_ref[c], depth)]
            source = chunk.at[pl.ds(i * depth, depth)]
            copies.append(pltpu.make_async_copy(source, target, sem.at[c]))
    for copy in copies:
        copy.start()
    for copy in copies:
        copy.wait()


def place_pages(place, chunks, counts, pages):
    size = sum(chunk.size for chunk in chunks)
    return pl.pallas_call(
        functools.partial(place_kernel, counts),
        out_shape=jax.ShapeDtypeStruct(pages.shape, pages.dtype),
        in_specs=[pl.BlockSpec(memory_space=pltpu.SMEM)]
        + [pl.BlockSpec(memory_space=pltpu.VMEM)] * len(chunks)
        + [pl.BlockSpec(memory_space=pl.ANY)],
        out_specs=pl.BlockSpec(memory_space=pl.ANY),
        scratch_shapes=[pltpu.SemaphoreType.DMA((sum(counts),))],
        input_output_aliases={len(chunks) + 1: 0},
        compiler_params=pltpu.CompilerParams(vmem_limit_bytes=2 * size + 2 * MIB),
        cost_estimate=pl.CostEstimate(flops=0, bytes_accessed=4 * size, transcendentals=0),
    )(place, *chunks, pages)


def cut(value):
    return value.astype(jnp.bfloat16).astype(jnp.float32)


def split_stats(peak, total):
    high = cut(peak)
    mid = cut(peak - high)
    return high, mid, peak - high - mid, cut(total), total - cut(total)


def attend_kernel(rows, piece, peers, me_ref, length_ref, *refs):
    query_refs, refs = refs[:peers], refs[peers:]
    key_ref, value_ref, new_key_ref, new_value_ref, token_ref = refs[:5]
    out_refs = refs[5 : 5 + peers]
    bias_ref, new_bias_ref, score_ref, weight_ref, query_ref, result_ref = refs[5 + peers :]
    tokens = key_ref.shape[0]
    step = pl.program_id(0)

    @pl.when(step == 0)
    def _():
        owner = token_ref[0:1, :]
        offset = lax.broadcasted_iota(jnp.int32, owner.shape, 1) % PAGE
        spot = (token_ref[1:2, :] * 32 + token_ref[2:3, :] - 1) * PAGE + offset.astype(jnp.float32)
        request = lax.broadcasted_iota(jnp.int32, (rows, 1), 0) // STEPS
        limit = jnp.zeros((rows, 1), jnp.int32)
        for r in range(rows // STEPS):
            limit = jnp.where(request == r, length_ref[r], limit)
        seen = (owner == request.astype(jnp.float32)) & (spot < limit.astype(jnp.float32))
        bias_ref[...] = jnp.where(seen, 0.0, NEG_FILL)
        row = lax.broadcasted_iota(jnp.int32, new_bias_ref.shape, 0)
        col = lax.broadcasted_iota(jnp.int32, new_bias_ref.shape, 1)
        first = jnp.where((me_ref[0] == 0) & (me_ref[1] == 0), 1, 0)
        seen = (row // STEPS == col // STEPS) & (col <= row) & (col < rows * first)
        new_bias_ref[...] = jnp.where(seen, 0.0, NEG_FILL)
        if peers > 1:
            for d in range(peers):
                query_ref[me_ref[1] ^ d] = query_refs[d][...]

    if peers > 1:
        per_step = query_refs[0].shape[0] // KVH
        query = jnp.concatenate(
            [
                query_ref[n, step * per_step + i].astype(jnp.float32)
                for i in range(per_step)
                for n in range(peers)
            ],
            axis=0,
        ).astype(jnp.bfloat16)
    else:
        query = query_refs[0][0]
    score_ref[:, :tokens] = lax.dot_general(
        query, key_ref[...], NT, preferred_element_type=jnp.float32
    )
    score_ref[:, tokens:] = lax.dot_general(
        query, new_key_ref[...], NT, preferred_element_type=jnp.float32
    )
    together = 1 if rows % 16 == 0 else 2
    span = together * rows
    peaks, totals = [], []
    for c in range(GROUPS // together):
        block = pl.ds(c * span, span)
        old = score_ref[block, :tokens].reshape(together, rows, tokens) * SCALE2 + bias_ref[...]
        new = score_ref[block, tokens:].reshape(together, rows, -1) * SCALE2 + new_bias_ref[...]
        peak = jnp.maximum(
            jnp.max(old, axis=-1, keepdims=True), jnp.max(new, axis=-1, keepdims=True)
        )
        old = jnp.exp2(old - peak)
        new = jnp.exp2(new - peak)
        totals.append(
            (jnp.sum(old, axis=-1, keepdims=True) + jnp.sum(new, axis=-1, keepdims=True)).reshape(
                span, 1
            )
        )
        peaks.append(peak.reshape(span, 1))
        weight_ref[block, :tokens] = old.reshape(span, tokens).astype(jnp.bfloat16)
        weight_ref[block, tokens:] = new.reshape(span, -1).astype(jnp.bfloat16)
    mixed = jnp.dot(
        weight_ref[:, :tokens], value_ref[...], preferred_element_type=jnp.float32
    ) + jnp.dot(weight_ref[:, tokens:], new_value_ref[...], preferred_element_type=jnp.float32)
    peak = jnp.concatenate(peaks, axis=0)
    total = jnp.concatenate(totals, axis=0)
    lane = lax.broadcasted_iota(jnp.int32, (GROUPS * rows, HD), 1)
    stats = jnp.zeros((GROUPS * rows, HD), jnp.float32)
    for i, part in enumerate(split_stats(peak, total)):
        stats = jnp.where(lane == i, part, stats)
    pick = (
        lax.broadcasted_iota(jnp.int32, (STAT, HD), 0)
        == lax.broadcasted_iota(jnp.int32, (STAT, HD), 1)
    ).astype(jnp.bfloat16)
    fill = result_ref.shape[1] - STAT - piece
    for c in range(GROUPS * rows // piece):
        part = slice(c * piece, (c + 1) * piece)
        turned = lax.dot_general(
            pick,
            jnp.concatenate(
                [stats[part], jnp.zeros((HD - piece, HD), jnp.float32)], axis=0
            ).astype(jnp.bfloat16),
            NT,
            preferred_element_type=jnp.float32,
        )
        result_ref[c] = jnp.concatenate(
            [turned, mixed[part], jnp.zeros((fill, HD), jnp.float32)], axis=0
        ).astype(jnp.bfloat16)
    if peers > 1:
        for d, out_ref in enumerate(out_refs):

            @pl.when((step ^ me_ref[1]) == d)
            def _():
                out_ref[...] = result_ref[...]
    else:
        out_refs[0][...] = result_ref[...]


def attend(me, lengths, queries, keyval, pool, token_info, rows, piece):
    tokens = pool.shape[0]
    extra = keyval.shape[0]
    peers = len(queries)
    pieces = GROUPS * rows // piece
    height = STAT + up(piece, 16)
    whole = lambda shape: pl.BlockSpec(shape, lambda k: (0,) * len(shape))
    if peers > 1:
        query_spec = whole(queries[0].shape)
        out_spec = whole((pieces, height, HD))
        out_shape = jax.ShapeDtypeStruct((pieces, height, HD), jnp.bfloat16)
    else:
        query_spec = pl.BlockSpec((1,) + queries[0].shape[1:], lambda k: (k, 0, 0))
        out_spec = pl.BlockSpec((pieces, height, HD), lambda k: (k, 0, 0))
        out_shape = jax.ShapeDtypeStruct((KVH * pieces, height, HD), jnp.bfloat16)
    return pl.pallas_call(
        functools.partial(attend_kernel, rows, piece, peers),
        grid=(KVH,),
        out_shape=[out_shape] * peers,
        in_specs=[pl.BlockSpec(memory_space=pltpu.SMEM)] * 2
        + [query_spec] * peers
        + [
            pl.BlockSpec((tokens, HD), lambda k: (0, k)),
            pl.BlockSpec((tokens, HD), lambda k: (0, KVH + k)),
            pl.BlockSpec((extra, HD), lambda k: (0, k)),
            pl.BlockSpec((extra, HD), lambda k: (0, KVH + k)),
            whole(token_info.shape),
        ],
        out_specs=[out_spec] * peers,
        scratch_shapes=[
            pltpu.VMEM((rows, tokens), jnp.float32),
            pltpu.VMEM((rows, extra), jnp.float32),
            pltpu.VMEM((GROUPS * rows, tokens + extra), jnp.float32),
            pltpu.VMEM((GROUPS * rows, tokens + extra), jnp.bfloat16),
            pltpu.VMEM((peers,) + queries[0].shape, jnp.bfloat16),
            pltpu.VMEM((pieces, height, HD), jnp.bfloat16),
        ],
        compiler_params=pltpu.CompilerParams(vmem_limit_bytes=56 * MIB),
        cost_estimate=pl.CostEstimate(flops=1, bytes_accessed=1, transcendentals=0),
    )(me, lengths, *queries, pool, pool, keyval, keyval, token_info)


def combine_kernel(piece, last, count, *refs):
    if last:
        part_ref, out_ref = refs
        part_refs = [part_ref.at[pl.ds(i, 1)] for i in range(count)]
    else:
        part_refs, out_ref = refs[:count], refs[count]
    groups, height = part_refs[0].shape[:2]
    peaks, totals = [], []
    for i in range(count):
        for j in range(groups):
            stat = part_refs[i][j, :STAT, :].astype(jnp.float32)
            peaks.append(stat[0:1] + stat[1:2] + stat[2:3])
            totals.append(stat[3:4] + stat[4:5])
    peak = jnp.concatenate(peaks, axis=0).reshape(count, groups, HD)
    total = jnp.concatenate(totals, axis=0).reshape(count, groups, HD)
    top = jnp.max(peak, axis=0)
    lead = jnp.exp2(peak - top[None])
    whole = jnp.sum(lead * total, axis=0)
    if last:
        lane = lax.broadcasted_iota(jnp.int32, whole.shape, 1)
        lead = lead / jnp.where(lane < piece, whole, 1.0)[None]
    lead = lead.reshape(count * groups, HD)
    if (count * groups) % HD:
        fill = up(count * groups, HD) - count * groups
        lead = jnp.concatenate([lead, jnp.zeros((fill, HD), jnp.float32)], axis=0)
    lead = jnp.transpose(lead)
    rows = height - STAT
    for j in range(groups):
        result = jnp.zeros((rows, HD), jnp.float32)
        for i in range(count):
            c = i * groups + j
            result = result + lead[:rows, c : c + 1] * part_refs[i][j, STAT:, :].astype(jnp.float32)
        if last:
            for i in range(out_ref.shape[0]):
                out_ref[i] = result[:piece].astype(jnp.bfloat16)
        else:
            stats = split_stats(top[j : j + 1], whole[j : j + 1])
            rest = jnp.zeros((STAT - len(stats), HD), jnp.float32)
            out_ref[j] = jnp.concatenate([*stats, rest, result], axis=0).astype(jnp.bfloat16)


def combine(parts, piece, repeats=0):
    count = parts[0].shape[0] if repeats else len(parts)
    shape = (repeats, piece, HD) if repeats else parts[0].shape
    return pl.pallas_call(
        functools.partial(combine_kernel, piece, repeats > 0, count),
        out_shape=jax.ShapeDtypeStruct(shape, jnp.bfloat16),
        in_specs=[pl.BlockSpec(memory_space=pltpu.VMEM)] * len(parts),
        out_specs=pl.BlockSpec(memory_space=pltpu.VMEM),
        compiler_params=pltpu.CompilerParams(vmem_limit_bytes=8 * MIB),
        cost_estimate=pl.CostEstimate(
            flops=2 * len(parts) * parts[0].size,
            bytes_accessed=len(parts) * parts[0].size * 2,
            transcendentals=0,
        ),
    )(*parts)


def reorder(shape, unit, valid, own, column):
    first, second = (0, 1) if column else (1, 0)
    block = lax.broadcasted_iota(jnp.int32, shape, second) // unit
    place = lax.broadcasted_iota(jnp.int32, shape, second) % unit
    target = (block ^ own) * valid + place
    match = (lax.broadcasted_iota(jnp.int32, shape, first) == target) & (place < valid)
    return match.astype(jnp.bfloat16)


def project_kernel(peers, me_ref, hidden_ref, query_ref, keyval_ref, *refs):
    out_refs, (full_ref,) = refs[:peers], refs[peers:]
    count, local, depth = hidden_ref.shape
    unit = up(local, 8)
    blocks = []
    for i in range(count):
        blocks.append(hidden_ref[i].astype(jnp.float32))
        if unit > local:
            blocks.append(jnp.zeros((unit - local, depth), jnp.float32))
    hidden = jnp.concatenate(blocks, axis=0).astype(jnp.bfloat16)
    order = reorder((count * local, count * unit), unit, local, 0, True)
    hidden = jnp.dot(order, hidden, preferred_element_type=jnp.float32).astype(jnp.bfloat16)
    full_ref[...] = jnp.dot(hidden, query_ref[...], preferred_element_type=jnp.float32)
    keyval = jnp.dot(hidden, keyval_ref[...], preferred_element_type=jnp.float32)
    for d, out_ref in enumerate(out_refs):
        start = pl.multiple_of((me_ref[1] ^ d) * HD, HD)
        out_ref[:, :HD] = full_ref[:, pl.ds(start, HD)]
        out_ref[:, HD:] = keyval


def pack_kernel(peers, *refs):
    own, tag_ref, out_ref = refs[:peers], refs[peers], refs[peers + 1]
    total = (own[0][...] + own[1][...]) + (own[2][...] + own[3][...])
    tags = jnp.concatenate([tag_ref[...], jnp.zeros_like(tag_ref[...])], axis=1)
    packed = jnp.concatenate([total, tags], axis=0).astype(jnp.bfloat16)
    for i in range(out_ref.shape[0]):
        out_ref[i] = packed


def unpack_kernel(rows, me_ref, kept_ref, part_ref, query_ref, keyval_ref, *refs):
    entry_ref, req_ref, idx_ref = refs
    count = part_ref.shape[0]
    line = lax.broadcasted_iota(jnp.int32, (count, HD), 0)
    tags = jnp.zeros((count, HD), jnp.float32)
    fill = jnp.zeros((keyval_ref.shape[0] - rows, HD), jnp.float32)
    for i in range(count):
        part = part_ref[i].astype(jnp.float32)
        query_ref[i] = part[:rows, :HD].astype(jnp.bfloat16)
        block = jnp.concatenate([part[:rows, HD:], fill], axis=0).astype(jnp.bfloat16)
        keyval_ref[:, i * HD : (i + 1) * HD] = block
        mine = jnp.where(line == me_ref[0], part[rows : rows + count, :HD], 0.0)
        tags = tags + jnp.where(line == i, jnp.sum(mine, axis=0, keepdims=True), 0.0)
    capacity = HD // count
    high = lax.broadcasted_iota(jnp.int32, (HD, HD), 0)
    low = lax.broadcasted_iota(jnp.int32, (HD, HD), 1)
    slot = lax.broadcasted_iota(jnp.int32, (count, HD), 1)
    tags = tags.astype(jnp.bfloat16)
    fields = []
    for i in range(3):
        pick = jnp.where(high == i * capacity + low % capacity, 1.0, 0.0).astype(jnp.bfloat16)
        spread_out = jnp.dot(tags, pick, preferred_element_type=jnp.float32)
        spread_out = jnp.where(slot // capacity == line, spread_out, 0.0)
        fields.append(jnp.sum(spread_out, axis=0, keepdims=True))
    req_ref[...] = fields[0].astype(jnp.int32)
    idx_ref[...] = (fields[1] * 32.0 + fields[2] - 1.0).astype(jnp.int32)
    local = entry_ref.shape[1]
    step = lax.broadcasted_iota(jnp.int32, (16, keyval_ref.shape[0]), 0)
    row = lax.broadcasted_iota(jnp.int32, (16, keyval_ref.shape[0]), 1)
    kept = (row == me_ref[0] * local + step) & (step < kept_ref[me_ref[0]])
    kept = jnp.where(kept, 1.0, 0.0).astype(jnp.bfloat16)
    entries = jnp.dot(kept, keyval_ref[...], preferred_element_type=jnp.float32)
    entry_ref[0] = entries[:local].astype(jnp.bfloat16)


def finish_kernel(peers, me_ref, part_ref, weight_ref, *refs):
    count, rows = part_ref.shape[:2]
    local = rows // peers
    unit = up(local, 16)
    whole = jnp.concatenate([part_ref[i] for i in range(count)], axis=1)
    order = reorder((peers * unit, rows), unit, local, me_ref[1], False)
    mixed = jnp.dot(order, whole, preferred_element_type=jnp.float32)
    mixed = jnp.dot(mixed.astype(jnp.bfloat16), weight_ref[...], preferred_element_type=jnp.float32)
    for d, out_ref in enumerate(refs):
        out_ref[...] = mixed[d * unit : d * unit + local]


def in_vmem(kernel, out_shape, me, *args, scratch=()):
    head = [] if me is None else list(me) if isinstance(me, tuple) else [me]
    return pl.pallas_call(
        kernel,
        out_shape=out_shape,
        in_specs=[pl.BlockSpec(memory_space=pltpu.SMEM)] * len(head)
        + [pl.BlockSpec(memory_space=pltpu.VMEM)] * len(args),
        out_specs=jax.tree.map(lambda _: pl.BlockSpec(memory_space=pltpu.VMEM), out_shape),
        scratch_shapes=scratch,
        compiler_params=pltpu.CompilerParams(vmem_limit_bytes=16 * MIB),
        cost_estimate=pl.CostEstimate(
            flops=0, bytes_accessed=sum(2 * arg.size for arg in args), transcendentals=0
        ),
    )(*head, *args)


def group_of(d, wide):
    return d if wide <= 8 or d == 0 else 1 + (d - 1) * 7 // (wide - 1)


def spread(block, axis):
    count = lax.axis_size(axis)
    return lax.all_to_all(
        jnp.broadcast_to(block[None], (count,) + block.shape),
        axis,
        split_axis=0,
        concat_axis=0,
        tiled=True,
    )


def on_device(hidden, w_query, w_keyval, w_out, pool, page_req, page_idx, lengths, moves, accepted):
    wide = lax.axis_size("wide")
    narrow = lax.axis_size("narrow")
    local_rows = hidden.shape[0]
    rows = local_rows * wide
    requests = rows // STEPS
    slots = pool.shape[0]
    capacity = slots // wide
    own_cols = w_query.shape[1] // narrow
    piece = HEADS * rows // (wide * narrow)
    extra = up(rows, HD)
    direct = piece == rows and own_cols == HD and slots == HD
    direct = direct and wide == 8 and narrow == 4 and local_rows == STEPS
    me = lax.axis_index("wide")
    both = jnp.stack([me, lax.axis_index("narrow")])
    exchange = functools.partial(lax.all_to_all, split_axis=0, concat_axis=0, tiled=True)

    def send(block, axis, d):
        return lax.ppermute(block, axis, [(i, i ^ d) for i in range(lax.axis_size(axis))])

    def share(block, axis):
        return [block] + [send(block, axis, d) for d in range(1, lax.axis_size(axis))]

    def deal(blocks, axis):
        return [blocks[0]] + [send(block, axis, d) for d, block in enumerate(blocks) if d]

    gathered = spread(hidden, "wide")

    ahead = AHEAD * capacity // 16
    parts = list(range(0 if ahead else 1, wide))
    moved_pool, tags, token_info, *chunks = order_pages(
        both, moves, page_req, page_idx, pool, wide, ahead, parts
    )
    chunks = dict(zip(parts, chunks))
    arrived = {}
    flying = {}

    def members(groups):
        return [d for group in groups for d in parts if group_of(d, wide) == group]

    def launch(values, *groups):
        taken = members(groups)
        values, sent = lax.optimization_barrier((values, [chunks[d] for d in taken]))
        for d, chunk in zip(taken, sent):
            flying[d] = send(chunk, "wide", d) if d else exchange(chunk, "wide")
        return values

    def land(values, *groups):
        taken = members(groups)
        values, got = lax.optimization_barrier((values, [flying[d] for d in taken]))
        arrived.update(zip(taken, got))
        return values

    def beside(step, value, *names):
        return land(step(launch(value, *names)), *names)

    def placed(pages):
        taken = sorted(arrived)
        if not taken:
            return pages
        place = []
        for d in taken:
            place += [(me ^ d) * capacity + ahead] if d else [w * capacity for w in range(wide)]
        place = jnp.stack([jnp.asarray(index, jnp.int32) for index in place])
        counts = [1 if d else wide for d in taken]
        pages = place_pages(place, [arrived[d] for d in taken], counts, pages)
        arrived.clear()
        return pages

    gathered, tags = lax.optimization_barrier((gathered, tags))
    tokens = pool.reshape(slots * PAGE, -1)
    if direct:
        block = jax.ShapeDtypeStruct((rows, 2 * HD), jnp.float32)
        partial = in_vmem(
            functools.partial(project_kernel, narrow),
            [block] * narrow,
            both,
            gathered,
            w_query,
            w_keyval,
            scratch=[pltpu.VMEM((rows, narrow * HD), jnp.float32)],
        )
        partial = deal(partial, "narrow")
        packed = in_vmem(
            functools.partial(pack_kernel, narrow),
            jax.ShapeDtypeStruct((wide, rows + wide, 2 * HD), jnp.bfloat16),
            None,
            *partial,
            tags,
        )
        received = beside(lambda value: exchange(value, "wide"), packed, 6, 1)
        received = launch(received, 0)
        queries, keyval, new_entries, moved_req, moved_idx = in_vmem(
            functools.partial(unpack_kernel, rows),
            [
                jax.ShapeDtypeStruct((wide, rows, HD), jnp.bfloat16),
                jax.ShapeDtypeStruct((extra, wide * HD), jnp.bfloat16),
                jax.ShapeDtypeStruct((1, local_rows, wide * HD), jnp.bfloat16),
                jax.ShapeDtypeStruct((1, slots), jnp.int32),
                jax.ShapeDtypeStruct((1, slots), jnp.int32),
            ],
            (both, accepted),
            received,
        )
        moved_req, moved_idx = moved_req.reshape(slots), moved_idx.reshape(slots)
        queries = share(queries, "narrow")
    else:
        gathered = gathered.reshape(rows, -1)
        query_part = jnp.dot(gathered, w_query, preferred_element_type=jnp.float32)
        keyval_part = jnp.dot(gathered, w_keyval, preferred_element_type=jnp.float32)
        query_part = jnp.transpose(query_part.reshape(rows, narrow, own_cols), (1, 0, 2))
        partial = jnp.concatenate(
            [query_part, jnp.broadcast_to(keyval_part[None], (narrow,) + keyval_part.shape)], axis=2
        )
        partial = exchange(partial, "narrow")
        projected = jnp.sum(partial, axis=0).astype(jnp.bfloat16)
        tags = tags[:, : 3 * capacity].astype(jnp.bfloat16)[:, None]
        tags = jnp.pad(tags, ((0, 0), (0, 7), (0, projected.shape[1] - tags.shape[2])))
        packed = jnp.broadcast_to(projected[None], (wide,) + projected.shape)
        packed = jnp.concatenate([packed, tags], axis=1)
        received = beside(lambda value: exchange(value, "wide"), packed, 6, 1)
        received = launch(received, 0)
        tags_in = received[:, rows]
        queries = received[:, :rows, :own_cols]
        queries = spread(queries, "narrow")
        queries = jnp.transpose(queries, (2, 1, 0, 3)).reshape(rows, HEADS, HD)
        queries = [jnp.transpose(queries, (1, 0, 2)).reshape(KVH, GROUPS * rows, HD)]
        keyval = jnp.transpose(received[:, :rows, own_cols:], (1, 0, 2)).reshape(rows, -1)
        keyval = jnp.pad(keyval, ((0, extra - rows), (0, 0)))
        tags_in = tags_in.astype(jnp.int32)
        moved_req = tags_in[:, :capacity].reshape(slots)
        moved_idx = tags_in[:, capacity : 2 * capacity] * 32
        moved_idx = (moved_idx + tags_in[:, 2 * capacity : 3 * capacity] - 1).reshape(slots)
        local_req = local_rows // STEPS
        fresh = lax.dynamic_slice_in_dim(keyval, me * local_rows, local_rows, 0)
        fresh = fresh.reshape(local_req, STEPS, -1)
        kept = lax.dynamic_slice_in_dim(accepted, me * local_req, local_req, 0)
        step_ids = jnp.arange(STEPS)[None, :, None]
        new_entries = jnp.where(
            step_ids < kept[:, None, None], fresh, jnp.zeros((), jnp.bfloat16)
        )

    queries, moved_pool = lax.optimization_barrier((queries, placed(moved_pool)))
    mixed = attend(both, lengths, queries, keyval, tokens, token_info, rows, piece)
    if direct:
        mixed = land(deal(mixed, "narrow"), 0)
    else:
        mixed = land(exchange(mixed[0], "narrow"), 0)
        mixed = mixed.reshape((narrow, wide) + mixed.shape[1:])
        mixed = [mixed[i] for i in range(narrow)]
    mixed = combine(mixed, piece)
    mixed, pages = lax.optimization_barrier((mixed, moved_pool))
    pages = placed(pages)
    mixed = beside(lambda value: exchange(value, "wide"), mixed, 4, 2)
    mixed, moved_pool = lax.optimization_barrier((mixed, pages))
    attn = combine([mixed], piece, wide)
    attn, pages = lax.optimization_barrier((attn, moved_pool))
    pages = placed(pages)
    attn = beside(lambda value: exchange(value, "wide"), attn, 5, 3)
    attn, moved_pool = lax.optimization_barrier((attn, pages))
    if direct:
        sums = in_vmem(
            functools.partial(finish_kernel, narrow),
            [jax.ShapeDtypeStruct((rows // narrow, w_out.shape[1]), jnp.float32)] * narrow,
            both,
            attn,
            w_out,
        )
        sums, pages = lax.optimization_barrier((sums, moved_pool))
        pages = placed(pages)
        sums = beside(lambda value: deal(value, "narrow"), sums, 7)
        attended = ((sums[0] + sums[1]) + (sums[2] + sums[3])).astype(jnp.bfloat16)
    else:
        attn = jnp.transpose(attn.reshape(-1, rows, HD), (1, 0, 2)).reshape(rows, -1)
        sums = jnp.dot(attn, w_out, preferred_element_type=jnp.float32)
        sums = sums.reshape(narrow, rows // narrow, -1)
        pages = placed(moved_pool)
        sums = beside(lambda value: exchange(value, "narrow"), sums, 7)
        attended = jnp.sum(sums, axis=0).astype(jnp.bfloat16)
    attended, pages = lax.optimization_barrier((attended, pages))
    moved_pool = placed(pages)
    return (attended, new_entries, moved_pool, moved_req, moved_idx)


def solution(mesh):
    in_specs = (
        P("wide", "narrow"),
        P("narrow", "wide"),
        P("narrow", "wide"),
        P("narrow", "wide"),
        P(("wide", "narrow"), None, None),
        P(("wide", "narrow")),
        P(("wide", "narrow")),
        P(),
        P(("wide", "narrow"), None),
        P(),
    )
    out_specs = (
        P("narrow", "wide"),
        P("wide", None, None),
        P(("wide", "narrow"), None, None),
        P(("wide", "narrow")),
        P(("wide", "narrow")),
    )
    return jax.shard_map(
        on_device, mesh=mesh, in_specs=in_specs, out_specs=out_specs, check_vma=False
    )
```

```python
import functools
import math

import jax
import jax.numpy as jnp
from jax import lax
from jax.experimental import pallas as pl
from jax.experimental.pallas import tpu as pltpu
from jax.sharding import PartitionSpec as P

HEADS = 32
KVH = 4
HD = 128
STEPS = 5
PAGE = 16
GROUPS = HEADS // KVH
NEG_FILL = -1e30
SCALE2 = math.log2(math.e) / math.sqrt(HD)
STAT = 16
MIB = 1024 * 1024
AHEAD = 5
NT = (((1,), (1,)), ((), ()))


def up(value, unit):
    return -(-value // unit) * unit


def column(row):
    return jnp.transpose(jnp.broadcast_to(row, (row.shape[1], row.shape[1])))


def order_kernel(
    wide, ahead, parts, me_ref, dest_ref, req_ref, idx_ref, pool_ref, out_ref, tag_ref, token_ref, *refs
):
    chunk_refs, refs = refs[: len(parts)], refs[len(parts) :]
    pages_ref, line_ref, source_ref, in_sem, out_sem, line_sem = refs
    slots = pool_ref.shape[0]
    capacity = slots // wide
    shape = (slots, slots)
    high = lax.broadcasted_iota(jnp.int32, shape, 0)
    low = lax.broadcasted_iota(jnp.int32, shape, 1)
    dest = dest_ref[...]
    same = column(dest.astype(jnp.float32)) == dest.astype(jnp.float32)
    rank = jnp.sum(jnp.where(same & (high < low), 1.0, 0.0), axis=0, keepdims=True)
    rest = capacity - ahead
    early = (dest * ahead).astype(jnp.float32) + rank
    late = ((dest ^ me_ref[0]) * rest + wide * ahead - ahead).astype(jnp.float32) + rank
    moved_to = jnp.where(rank < float(ahead), early, late)
    match = column(moved_to) == low.astype(jnp.float32)
    source = jnp.sum(jnp.where(match, high.astype(jnp.float32), 0.0), axis=0, keepdims=True)
    line_ref[...] = source.astype(jnp.int32)
    copy = pltpu.make_async_copy(line_ref, source_ref, line_sem)
    copy.start()
    copy.wait()

    own = out_ref.at[pl.ds(me_ref[0] * capacity + ahead, rest)]
    blocks = [(wide * ahead, rest, own)]
    for d, chunk in zip(parts, chunk_refs):
        if d:
            blocks.append((wide * ahead + d * rest, rest, chunk))
        else:
            blocks.insert(0, (0, wide * ahead, chunk))
    for c, (first, count, _) in enumerate(blocks):

        def start(j, carry, c=c):
            page = source_ref[0, j]
            pltpu.make_async_copy(pool_ref.at[page], pages_ref.at[j], in_sem.at[c]).start()
            return carry

        lax.fori_loop(first, first + count, start, 0)

    shifted = idx_ref[...] + 1
    fields = (req_ref[...], shifted // 32, shifted % 32)
    rank_col = column(rank)
    lane = low.astype(jnp.float32)
    spread_out = jnp.zeros(shape, jnp.float32)
    for i, field in enumerate(fields):
        picked = lane == rank_col + float(i * capacity)
        spread_out = spread_out + jnp.where(picked, column(field.astype(jnp.float32)), 0.0)
    line = lax.broadcasted_iota(jnp.int32, (wide, slots), 0)
    chosen = jnp.where(line == dest, 1.0, 0.0).astype(jnp.bfloat16)
    tag_ref[...] = jnp.dot(
        chosen, spread_out.astype(jnp.bfloat16), preferred_element_type=jnp.float32
    )

    tokens = slots * PAGE
    page = lax.broadcasted_iota(jnp.int32, (slots, tokens), 0)
    token = lax.broadcasted_iota(jnp.int32, (slots, tokens), 1)
    widen = jnp.where(page == token // PAGE, 1.0, 0.0).astype(jnp.bfloat16)
    row = lax.broadcasted_iota(jnp.int32, (8, slots), 0)
    stacked = jnp.zeros((8, slots), jnp.float32)
    for i, field in enumerate(fields):
        stacked = jnp.where(row == i, field.astype(jnp.float32), stacked)
    token_ref[...] = jnp.dot(
        stacked.astype(jnp.bfloat16), widen, preferred_element_type=jnp.float32
    )

    copies = []
    for c, (first, count, target) in enumerate(blocks):
        held = pages_ref.at[pl.ds(first, count)]
        pltpu.make_async_copy(pool_ref.at[pl.ds(0, count)], held, in_sem.at[c]).wait()
        copies.append(pltpu.make_async_copy(held, target, out_sem.at[c]))
        copies[-1].start()
    for copy in copies:
        copy.wait()


def order_pages(me, dest, page_req, page_idx, pool, wide, ahead, parts):
    slots = pool.shape[0]
    part = lambda count: jax.ShapeDtypeStruct((count,) + pool.shape[1:], pool.dtype)
    out_shape = [part(slots), jax.ShapeDtypeStruct((wide, slots), jnp.float32)]
    out_shape += [jax.ShapeDtypeStruct((8, slots * PAGE), jnp.float32)]
    rest = slots // wide - ahead
    out_shape += [part(rest if d else wide * ahead) for d in parts]
    vmem = pl.BlockSpec(memory_space=pltpu.VMEM)
    hbm = pl.BlockSpec(memory_space=pltpu.HBM)
    return pl.pallas_call(
        functools.partial(order_kernel, wide, ahead, parts),
        out_shape=out_shape,
        in_specs=[pl.BlockSpec(memory_space=pltpu.SMEM), vmem, vmem, vmem, hbm],
        out_specs=[hbm, vmem, vmem] + [hbm] * len(parts),
        scratch_shapes=[
            pltpu.VMEM(pool.shape, pool.dtype),
            pltpu.VMEM((1, slots), jnp.int32),
            pltpu.SMEM((1, slots), jnp.int32),
            pltpu.SemaphoreType.DMA((1 + len(parts),)),
            pltpu.SemaphoreType.DMA((1 + len(parts),)),
            pltpu.SemaphoreType.DMA,
        ],
        compiler_params=pltpu.CompilerParams(vmem_limit_bytes=56 * MIB),
        cost_estimate=pl.CostEstimate(
            flops=0, bytes_accessed=2 * pool.size * 2, transcendentals=0
        ),
    )(me, dest.reshape(1, -1), page_req.reshape(1, -1), page_idx.reshape(1, -1), pool)


def place_kernel(counts, place_ref, *refs):
    in_refs, (out_ref, sem) = refs[:-3], refs[-2:]
    copies = []
    for chunk, count in zip(in_refs, counts):
        depth = chunk.shape[0] // count
        for i in range(count):
            c = len(copies)
            target = out_ref.at[pl.ds(place_ref[c], depth)]
            source = chunk.at[pl.ds(i * depth, depth)]
            copies.append(pltpu.make_async_copy(source, target, sem.at[c]))
    for copy in copies:
        copy.start()
    for copy in copies:
        copy.wait()


def place_pages(place, chunks, counts, pages):
    size = sum(chunk.size for chunk in chunks)
    return pl.pallas_call(
        functools.partial(place_kernel, counts),
        out_shape=jax.ShapeDtypeStruct(pages.shape, pages.dtype),
        in_specs=[pl.BlockSpec(memory_space=pltpu.SMEM)]
        + [pl.BlockSpec(memory_space=pltpu.VMEM)] * len(chunks)
        + [pl.BlockSpec(memory_space=pl.ANY)],
        out_specs=pl.BlockSpec(memory_space=pl.ANY),
        scratch_shapes=[pltpu.SemaphoreType.DMA((sum(counts),))],
        input_output_aliases={len(chunks) + 1: 0},
        compiler_params=pltpu.CompilerParams(vmem_limit_bytes=2 * size + 2 * MIB),
        cost_estimate=pl.CostEstimate(flops=0, bytes_accessed=4 * size, transcendentals=0),
    )(place, *chunks, pages)


def cut(value):
    return value.astype(jnp.bfloat16).astype(jnp.float32)


def split_stats(peak, total):
    high = cut(peak)
    mid = cut(peak - high)
    return high, mid, peak - high - mid, cut(total), total - cut(total)


def attend_kernel(rows, piece, peers, me_ref, length_ref, *refs):
    query_refs, refs = refs[:peers], refs[peers:]
    key_ref, value_ref, new_key_ref, new_value_ref, token_ref = refs[:5]
    out_refs = refs[5 : 5 + peers]
    bias_ref, new_bias_ref, score_ref, weight_ref, query_ref, result_ref = refs[5 + peers :]
    tokens = key_ref.shape[0]
    step = pl.program_id(0)

    @pl.when(step == 0)
    def _():
        owner = token_ref[0:1, :]
        offset = lax.broadcasted_iota(jnp.int32, owner.shape, 1) % PAGE
        spot = (token_ref[1:2, :] * 32 + token_ref[2:3, :] - 1) * PAGE + offset.astype(jnp.float32)
        request = lax.broadcasted_iota(jnp.int32, (rows, 1), 0) // STEPS
        limit = jnp.zeros((rows, 1), jnp.int32)
        for r in range(rows // STEPS):
            limit = jnp.where(request == r, length_ref[r], limit)
        seen = (owner == request.astype(jnp.float32)) & (spot < limit.astype(jnp.float32))
        bias_ref[...] = jnp.where(seen, 0.0, NEG_FILL)
        row = lax.broadcasted_iota(jnp.int32, new_bias_ref.shape, 0)
        col = lax.broadcasted_iota(jnp.int32, new_bias_ref.shape, 1)
        first = jnp.where((me_ref[0] == 0) & (me_ref[1] == 0), 1, 0)
        seen = (row // STEPS == col // STEPS) & (col <= row) & (col < rows * first)
        new_bias_ref[...] = jnp.where(seen, 0.0, NEG_FILL)
        if peers > 1:
            for d in range(peers):
                query_ref[me_ref[1] ^ d] = query_refs[d][...]

    if peers > 1:
        per_step = query_refs[0].shape[0] // KVH
        query = jnp.concatenate(
            [
                query_ref[n, step * per_step + i].astype(jnp.float32)
                for i in range(per_step)
                for n in range(peers)
            ],
            axis=0,
        ).astype(jnp.bfloat16)
    else:
        query = query_refs[0][0]
    score_ref[:, :tokens] = lax.dot_general(
        query, key_ref[...], NT, preferred_element_type=jnp.float32
    )
    score_ref[:, tokens:] = lax.dot_general(
        query, new_key_ref[...], NT, preferred_element_type=jnp.float32
    )
    together = 1 if rows % 16 == 0 else 2
    span = together * rows
    peaks, totals = [], []
    for c in range(GROUPS // together):
        block = pl.ds(c * span, span)
        old = score_ref[block, :tokens].reshape(together, rows, tokens) * SCALE2 + bias_ref[...]
        new = score_ref[block, tokens:].reshape(together, rows, -1) * SCALE2 + new_bias_ref[...]
        peak = jnp.maximum(
            jnp.max(old, axis=-1, keepdims=True), jnp.max(new, axis=-1, keepdims=True)
        )
        old = jnp.exp2(old - peak)
        new = jnp.exp2(new - peak)
        totals.append(
            (jnp.sum(old, axis=-1, keepdims=True) + jnp.sum(new, axis=-1, keepdims=True)).reshape(
                span, 1
            )
        )
        peaks.append(peak.reshape(span, 1))
        weight_ref[block, :tokens] = old.reshape(span, tokens).astype(jnp.bfloat16)
        weight_ref[block, tokens:] = new.reshape(span, -1).astype(jnp.bfloat16)
    mixed = jnp.dot(
        weight_ref[:, :tokens], value_ref[...], preferred_element_type=jnp.float32
    ) + jnp.dot(weight_ref[:, tokens:], new_value_ref[...], preferred_element_type=jnp.float32)
    peak = jnp.concatenate(peaks, axis=0)
    total = jnp.concatenate(totals, axis=0)
    lane = lax.broadcasted_iota(jnp.int32, (GROUPS * rows, HD), 1)
    stats = jnp.zeros((GROUPS * rows, HD), jnp.float32)
    for i, part in enumerate(split_stats(peak, total)):
        stats = jnp.where(lane == i, part, stats)
    pick = (
        lax.broadcasted_iota(jnp.int32, (STAT, HD), 0)
        == lax.broadcasted_iota(jnp.int32, (STAT, HD), 1)
    ).astype(jnp.bfloat16)
    fill = result_ref.shape[1] - STAT - piece
    for c in range(GROUPS * rows // piece):
        part = slice(c * piece, (c + 1) * piece)
        turned = lax.dot_general(
            pick,
            jnp.concatenate(
                [stats[part], jnp.zeros((HD - piece, HD), jnp.float32)], axis=0
            ).astype(jnp.bfloat16),
            NT,
            preferred_element_type=jnp.float32,
        )
        result_ref[c] = jnp.concatenate(
            [turned, mixed[part], jnp.zeros((fill, HD), jnp.float32)], axis=0
        ).astype(jnp.bfloat16)
    if peers > 1:
        for d, out_ref in enumerate(out_refs):

            @pl.when((step ^ me_ref[1]) == d)
            def _():
                out_ref[...] = result_ref[...]
    else:
        out_refs[0][...] = result_ref[...]


def attend(me, lengths, queries, keyval, pool, token_info, rows, piece):
    tokens = pool.shape[0]
    extra = keyval.shape[0]
    peers = len(queries)
    pieces = GROUPS * rows // piece
    height = STAT + up(piece, 16)
    whole = lambda shape: pl.BlockSpec(shape, lambda k: (0,) * len(shape))
    if peers > 1:
        query_spec = whole(queries[0].shape)
        out_spec = whole((pieces, height, HD))
        out_shape = jax.ShapeDtypeStruct((pieces, height, HD), jnp.bfloat16)
    else:
        query_spec = pl.BlockSpec((1,) + queries[0].shape[1:], lambda k: (k, 0, 0))
        out_spec = pl.BlockSpec((pieces, height, HD), lambda k: (k, 0, 0))
        out_shape = jax.ShapeDtypeStruct((KVH * pieces, height, HD), jnp.bfloat16)
    return pl.pallas_call(
        functools.partial(attend_kernel, rows, piece, peers),
        grid=(KVH,),
        out_shape=[out_shape] * peers,
        in_specs=[pl.BlockSpec(memory_space=pltpu.SMEM)] * 2
        + [query_spec] * peers
        + [
            pl.BlockSpec((tokens, HD), lambda k: (0, k)),
            pl.BlockSpec((tokens, HD), lambda k: (0, KVH + k)),
            pl.BlockSpec((extra, HD), lambda k: (0, k)),
            pl.BlockSpec((extra, HD), lambda k: (0, KVH + k)),
            whole(token_info.shape),
        ],
        out_specs=[out_spec] * peers,
        scratch_shapes=[
            pltpu.VMEM((rows, tokens), jnp.float32),
            pltpu.VMEM((rows, extra), jnp.float32),
            pltpu.VMEM((GROUPS * rows, tokens + extra), jnp.float32),
            pltpu.VMEM((GROUPS * rows, tokens + extra), jnp.bfloat16),
            pltpu.VMEM((peers,) + queries[0].shape, jnp.bfloat16),
            pltpu.VMEM((pieces, height, HD), jnp.bfloat16),
        ],
        compiler_params=pltpu.CompilerParams(vmem_limit_bytes=56 * MIB),
        cost_estimate=pl.CostEstimate(flops=1, bytes_accessed=1, transcendentals=0),
    )(me, lengths, *queries, pool, pool, keyval, keyval, token_info)


def combine_kernel(piece, last, count, *refs):
    if last:
        part_ref, out_ref = refs
        part_refs = [part_ref.at[pl.ds(i, 1)] for i in range(count)]
    else:
        part_refs, out_ref = refs[:count], refs[count]
    groups, height = part_refs[0].shape[:2]
    peaks, totals = [], []
    for i in range(count):
        for j in range(groups):
            stat = part_refs[i][j, :STAT, :].astype(jnp.float32)
            peaks.append(stat[0:1] + stat[1:2] + stat[2:3])
            totals.append(stat[3:4] + stat[4:5])
    peak = jnp.concatenate(peaks, axis=0).reshape(count, groups, HD)
    total = jnp.concatenate(totals, axis=0).reshape(count, groups, HD)
    top = jnp.max(peak, axis=0)
    lead = jnp.exp2(peak - top[None])
    whole = jnp.sum(lead * total, axis=0)
    if last:
        lane = lax.broadcasted_iota(jnp.int32, whole.shape, 1)
        lead = lead / jnp.where(lane < piece, whole, 1.0)[None]
    lead = lead.reshape(count * groups, HD)
    if (count * groups) % HD:
        fill = up(count * groups, HD) - count * groups
        lead = jnp.concatenate([lead, jnp.zeros((fill, HD), jnp.float32)], axis=0)
    lead = jnp.transpose(lead)
    rows = height - STAT
    for j in range(groups):
        result = jnp.zeros((rows, HD), jnp.float32)
        for i in range(count):
            c = i * groups + j
            result = result + lead[:rows, c : c + 1] * part_refs[i][j, STAT:, :].astype(jnp.float32)
        if last:
            for i in range(out_ref.shape[0]):
                out_ref[i] = result[:piece].astype(jnp.bfloat16)
        else:
            stats = split_stats(top[j : j + 1], whole[j : j + 1])
            rest = jnp.zeros((STAT - len(stats), HD), jnp.float32)
            out_ref[j] = jnp.concatenate([*stats, rest, result], axis=0).astype(jnp.bfloat16)


def combine(parts, piece, repeats=0):
    count = parts[0].shape[0] if repeats else len(parts)
    shape = (repeats, piece, HD) if repeats else parts[0].shape
    return pl.pallas_call(
        functools.partial(combine_kernel, piece, repeats > 0, count),
        out_shape=jax.ShapeDtypeStruct(shape, jnp.bfloat16),
        in_specs=[pl.BlockSpec(memory_space=pltpu.VMEM)] * len(parts),
        out_specs=pl.BlockSpec(memory_space=pltpu.VMEM),
        compiler_params=pltpu.CompilerParams(vmem_limit_bytes=8 * MIB),
        cost_estimate=pl.CostEstimate(
            flops=2 * len(parts) * parts[0].size,
            bytes_accessed=len(parts) * parts[0].size * 2,
            transcendentals=0,
        ),
    )(*parts)


def reorder(shape, unit, valid, own, column):
    first, second = (0, 1) if column else (1, 0)
    block = lax.broadcasted_iota(jnp.int32, shape, second) // unit
    place = lax.broadcasted_iota(jnp.int32, shape, second) % unit
    target = (block ^ own) * valid + place
    match = (lax.broadcasted_iota(jnp.int32, shape, first) == target) & (place < valid)
    return match.astype(jnp.bfloat16)


def project_kernel(peers, me_ref, hidden_ref, query_ref, keyval_ref, *refs):
    out_refs, (full_ref,) = refs[:peers], refs[peers:]
    count, local, depth = hidden_ref.shape
    unit = up(local, 8)
    blocks = []
    for i in range(count):
        blocks.append(hidden_ref[i].astype(jnp.float32))
        if unit > local:
            blocks.append(jnp.zeros((unit - local, depth), jnp.float32))
    hidden = jnp.concatenate(blocks, axis=0).astype(jnp.bfloat16)
    order = reorder((count * local, count * unit), unit, local, 0, True)
    hidden = jnp.dot(order, hidden, preferred_element_type=jnp.float32).astype(jnp.bfloat16)
    full_ref[...] = jnp.dot(hidden, query_ref[...], preferred_element_type=jnp.float32)
    keyval = jnp.dot(hidden, keyval_ref[...], preferred_element_type=jnp.float32)
    for d, out_ref in enumerate(out_refs):
        start = pl.multiple_of((me_ref[1] ^ d) * HD, HD)
        out_ref[:, :HD] = full_ref[:, pl.ds(start, HD)]
        out_ref[:, HD:] = keyval


def pack_kernel(peers, *refs):
    own, tag_ref, out_ref = refs[:peers], refs[peers], refs[peers + 1]
    total = (own[0][...] + own[1][...]) + (own[2][...] + own[3][...])
    tags = jnp.concatenate([tag_ref[...], jnp.zeros_like(tag_ref[...])], axis=1)
    packed = jnp.concatenate([total, tags], axis=0).astype(jnp.bfloat16)
    for i in range(out_ref.shape[0]):
        out_ref[i] = packed


def unpack_kernel(rows, me_ref, kept_ref, part_ref, query_ref, keyval_ref, *refs):
    entry_ref, req_ref, idx_ref = refs
    count = part_ref.shape[0]
    line = lax.broadcasted_iota(jnp.int32, (count, HD), 0)
    tags = jnp.zeros((count, HD), jnp.float32)
    fill = jnp.zeros((keyval_ref.shape[0] - rows, HD), jnp.float32)
    for i in range(count):
        part = part_ref[i].astype(jnp.float32)
        query_ref[i] = part[:rows, :HD].astype(jnp.bfloat16)
        block = jnp.concatenate([part[:rows, HD:], fill], axis=0).astype(jnp.bfloat16)
        keyval_ref[:, i * HD : (i + 1) * HD] = block
        mine = jnp.where(line == me_ref[0], part[rows : rows + count, :HD], 0.0)
        tags = tags + jnp.where(line == i, jnp.sum(mine, axis=0, keepdims=True), 0.0)
    capacity = HD // count
    high = lax.broadcasted_iota(jnp.int32, (HD, HD), 0)
    low = lax.broadcasted_iota(jnp.int32, (HD, HD), 1)
    slot = lax.broadcasted_iota(jnp.int32, (count, HD), 1)
    tags = tags.astype(jnp.bfloat16)
    fields = []
    for i in range(3):
        pick = jnp.where(high == i * capacity + low % capacity, 1.0, 0.0).astype(jnp.bfloat16)
        spread_out = jnp.dot(tags, pick, preferred_element_type=jnp.float32)
        spread_out = jnp.where(slot // capacity == line, spread_out, 0.0)
        fields.append(jnp.sum(spread_out, axis=0, keepdims=True))
    req_ref[...] = fields[0].astype(jnp.int32)
    idx_ref[...] = (fields[1] * 32.0 + fields[2] - 1.0).astype(jnp.int32)
    local = entry_ref.shape[1]
    step = lax.broadcasted_iota(jnp.int32, (16, keyval_ref.shape[0]), 0)
    row = lax.broadcasted_iota(jnp.int32, (16, keyval_ref.shape[0]), 1)
    kept = (row == me_ref[0] * local + step) & (step < kept_ref[me_ref[0]])
    kept = jnp.where(kept, 1.0, 0.0).astype(jnp.bfloat16)
    entries = jnp.dot(kept, keyval_ref[...], preferred_element_type=jnp.float32)
    entry_ref[0] = entries[:local].astype(jnp.bfloat16)


def finish_kernel(peers, me_ref, part_ref, weight_ref, *refs):
    count, rows = part_ref.shape[:2]
    local = rows // peers
    unit = up(local, 16)
    whole = jnp.concatenate([part_ref[i] for i in range(count)], axis=1)
    order = reorder((peers * unit, rows), unit, local, me_ref[1], False)
    mixed = jnp.dot(order, whole, preferred_element_type=jnp.float32)
    mixed = jnp.dot(mixed.astype(jnp.bfloat16), weight_ref[...], preferred_element_type=jnp.float32)
    for d, out_ref in enumerate(refs):
        out_ref[...] = mixed[d * unit : d * unit + local]


def in_vmem(kernel, out_shape, me, *args, scratch=()):
    head = [] if me is None else list(me) if isinstance(me, tuple) else [me]
    return pl.pallas_call(
        kernel,
        out_shape=out_shape,
        in_specs=[pl.BlockSpec(memory_space=pltpu.SMEM)] * len(head)
        + [pl.BlockSpec(memory_space=pltpu.VMEM)] * len(args),
        out_specs=jax.tree.map(lambda _: pl.BlockSpec(memory_space=pltpu.VMEM), out_shape),
        scratch_shapes=scratch,
        compiler_params=pltpu.CompilerParams(vmem_limit_bytes=16 * MIB),
        cost_estimate=pl.CostEstimate(
            flops=0, bytes_accessed=sum(2 * arg.size for arg in args), transcendentals=0
        ),
    )(*head, *args)


def group_of(d, wide):
    return d if wide <= 8 or d == 0 else 1 + (d - 1) * 7 // (wide - 1)


def spread(block, axis):
    count = lax.axis_size(axis)
    return lax.all_to_all(
        jnp.broadcast_to(block[None], (count,) + block.shape),
        axis,
        split_axis=0,
        concat_axis=0,
        tiled=True,
    )


def on_device(hidden, w_query, w_keyval, w_out, pool, page_req, page_idx, lengths, moves, accepted):
    wide = lax.axis_size("wide")
    narrow = lax.axis_size("narrow")
    local_rows = hidden.shape[0]
    rows = local_rows * wide
    requests = rows // STEPS
    slots = pool.shape[0]
    capacity = slots // wide
    own_cols = w_query.shape[1] // narrow
    piece = HEADS * rows // (wide * narrow)
    extra = up(rows, HD)
    direct = piece == rows and own_cols == HD and slots == HD
    direct = direct and wide == 8 and narrow == 4 and local_rows == STEPS
    me = lax.axis_index("wide")
    both = jnp.stack([me, lax.axis_index("narrow")])
    exchange = functools.partial(lax.all_to_all, split_axis=0, concat_axis=0, tiled=True)

    def send(block, axis, d):
        return lax.ppermute(block, axis, [(i, i ^ d) for i in range(lax.axis_size(axis))])

    def share(block, axis):
        return [block] + [send(block, axis, d) for d in range(1, lax.axis_size(axis))]

    def deal(blocks, axis):
        return [blocks[0]] + [send(block, axis, d) for d, block in enumerate(blocks) if d]

    gathered = spread(hidden, "wide")

    ahead = AHEAD * capacity // 16
    parts = list(range(0 if ahead else 1, wide))
    moved_pool, tags, token_info, *chunks = order_pages(
        both, moves, page_req, page_idx, pool, wide, ahead, parts
    )
    chunks = dict(zip(parts, chunks))
    arrived = {}
    flying = {}

    def members(groups):
        return [d for group in groups for d in parts if group_of(d, wide) == group]

    def launch(values, *groups):
        taken = members(groups)
        values, sent = lax.optimization_barrier((values, [chunks[d] for d in taken]))
        for d, chunk in zip(taken, sent):
            flying[d] = send(chunk, "wide", d) if d else exchange(chunk, "wide")
        return values

    def land(values, *groups):
        taken = members(groups)
        values, got = lax.optimization_barrier((values, [flying[d] for d in taken]))
        arrived.update(zip(taken, got))
        return values

    def beside(step, value, *names):
        return land(step(launch(value, *names)), *names)

    def placed(pages):
        taken = sorted(arrived)
        if not taken:
            return pages
        place = []
        for d in taken:
            place += [(me ^ d) * capacity + ahead] if d else [w * capacity for w in range(wide)]
        place = jnp.stack([jnp.asarray(index, jnp.int32) for index in place])
        counts = [1 if d else wide for d in taken]
        pages = place_pages(place, [arrived[d] for d in taken], counts, pages)
        arrived.clear()
        return pages

    gathered, tags = lax.optimization_barrier((gathered, tags))
    tokens = pool.reshape(slots * PAGE, -1)
    if direct:
        block = jax.ShapeDtypeStruct((rows, 2 * HD), jnp.float32)
        partial = in_vmem(
            functools.partial(project_kernel, narrow),
            [block] * narrow,
            both,
            gathered,
            w_query,
            w_keyval,
            scratch=[pltpu.VMEM((rows, narrow * HD), jnp.float32)],
        )
        partial = deal(partial, "narrow")
        packed = in_vmem(
            functools.partial(pack_kernel, narrow),
            jax.ShapeDtypeStruct((wide, rows + wide, 2 * HD), jnp.bfloat16),
            None,
            *partial,
            tags,
        )
        received = beside(lambda value: exchange(value, "wide"), packed, 6, 1)
        received = launch(received, 0)
        queries, keyval, new_entries, moved_req, moved_idx = in_vmem(
            functools.partial(unpack_kernel, rows),
            [
                jax.ShapeDtypeStruct((wide, rows, HD), jnp.bfloat16),
                jax.ShapeDtypeStruct((extra, wide * HD), jnp.bfloat16),
                jax.ShapeDtypeStruct((1, local_rows, wide * HD), jnp.bfloat16),
                jax.ShapeDtypeStruct((1, slots), jnp.int32),
                jax.ShapeDtypeStruct((1, slots), jnp.int32),
            ],
            (both, accepted),
            received,
        )
        moved_req, moved_idx = moved_req.reshape(slots), moved_idx.reshape(slots)
        queries = share(queries, "narrow")
    else:
        gathered = gathered.reshape(rows, -1)
        query_part = jnp.dot(gathered, w_query, preferred_element_type=jnp.float32)
        keyval_part = jnp.dot(gathered, w_keyval, preferred_element_type=jnp.float32)
        query_part = jnp.transpose(query_part.reshape(rows, narrow, own_cols), (1, 0, 2))
        partial = jnp.concatenate(
            [query_part, jnp.broadcast_to(keyval_part[None], (narrow,) + keyval_part.shape)], axis=2
        )
        partial = exchange(partial, "narrow")
        projected = jnp.sum(partial, axis=0).astype(jnp.bfloat16)
        tags = tags[:, : 3 * capacity].astype(jnp.bfloat16)[:, None]
        tags = jnp.pad(tags, ((0, 0), (0, 7), (0, projected.shape[1] - tags.shape[2])))
        packed = jnp.broadcast_to(projected[None], (wide,) + projected.shape)
        packed = jnp.concatenate([packed, tags], axis=1)
        received = beside(lambda value: exchange(value, "wide"), packed, 6, 1)
        received = launch(received, 0)
        tags_in = received[:, rows]
        queries = received[:, :rows, :own_cols]
        queries = spread(queries, "narrow")
        queries = jnp.transpose(queries, (2, 1, 0, 3)).reshape(rows, HEADS, HD)
        queries = [jnp.transpose(queries, (1, 0, 2)).reshape(KVH, GROUPS * rows, HD)]
        keyval = jnp.transpose(received[:, :rows, own_cols:], (1, 0, 2)).reshape(rows, -1)
        keyval = jnp.pad(keyval, ((0, extra - rows), (0, 0)))
        tags_in = tags_in.astype(jnp.int32)
        moved_req = tags_in[:, :capacity].reshape(slots)
        moved_idx = tags_in[:, capacity : 2 * capacity] * 32
        moved_idx = (moved_idx + tags_in[:, 2 * capacity : 3 * capacity] - 1).reshape(slots)
        local_req = local_rows // STEPS
        fresh = lax.dynamic_slice_in_dim(keyval, me * local_rows, local_rows, 0)
        fresh = fresh.reshape(local_req, STEPS, -1)
        kept = lax.dynamic_slice_in_dim(accepted, me * local_req, local_req, 0)
        step_ids = jnp.arange(STEPS)[None, :, None]
        new_entries = jnp.where(
            step_ids < kept[:, None, None], fresh, jnp.zeros((), jnp.bfloat16)
        )

    queries, moved_pool = lax.optimization_barrier((queries, placed(moved_pool)))
    mixed = attend(both, lengths, queries, keyval, tokens, token_info, rows, piece)
    if direct:
        mixed = land(deal(mixed, "narrow"), 0)
    else:
        mixed = land(exchange(mixed[0], "narrow"), 0)
        mixed = mixed.reshape((narrow, wide) + mixed.shape[1:])
        mixed = [mixed[i] for i in range(narrow)]
    mixed = combine(mixed, piece)
    mixed, pages = lax.optimization_barrier((mixed, moved_pool))
    pages = placed(pages)
    mixed = beside(lambda value: exchange(value, "wide"), mixed, 3, 4)
    mixed, moved_pool = lax.optimization_barrier((mixed, pages))
    attn = combine([mixed], piece, wide)
    attn, pages = lax.optimization_barrier((attn, moved_pool))
    pages = placed(pages)
    attn = beside(lambda value: exchange(value, "wide"), attn, 2, 5)
    attn, moved_pool = lax.optimization_barrier((attn, pages))
    if direct:
        sums = in_vmem(
            functools.partial(finish_kernel, narrow),
            [jax.ShapeDtypeStruct((rows // narrow, w_out.shape[1]), jnp.float32)] * narrow,
            both,
            attn,
            w_out,
        )
        sums, pages = lax.optimization_barrier((sums, moved_pool))
        pages = placed(pages)
        sums = beside(lambda value: deal(value, "narrow"), sums, 7)
        attended = ((sums[0] + sums[1]) + (sums[2] + sums[3])).astype(jnp.bfloat16)
    else:
        attn = jnp.transpose(attn.reshape(-1, rows, HD), (1, 0, 2)).reshape(rows, -1)
        sums = jnp.dot(attn, w_out, preferred_element_type=jnp.float32)
        sums = sums.reshape(narrow, rows // narrow, -1)
        pages = placed(moved_pool)
        sums = beside(lambda value: exchange(value, "narrow"), sums, 7)
        attended = jnp.sum(sums, axis=0).astype(jnp.bfloat16)
    attended, pages = lax.optimization_barrier((attended, pages))
    moved_pool = placed(pages)
    return (attended, new_entries, moved_pool, moved_req, moved_idx)


def solution(mesh):
    in_specs = (
        P("wide", "narrow"),
        P("narrow", "wide"),
        P("narrow", "wide"),
        P("narrow", "wide"),
        P(("wide", "narrow"), None, None),
        P(("wide", "narrow")),
        P(("wide", "narrow")),
        P(),
        P(("wide", "narrow"), None),
        P(),
    )
    out_specs = (
        P("narrow", "wide"),
        P("wide", None, None),
        P(("wide", "narrow"), None, None),
        P(("wide", "narrow")),
        P(("wide", "narrow")),
    )
    return jax.shard_map(
        on_device, mesh=mesh, in_specs=in_specs, out_specs=out_specs, check_vma=False
    )
```

```python
import functools
import math

import jax
import jax.numpy as jnp
from jax import lax
from jax.experimental import pallas as pl
from jax.experimental.pallas import tpu as pltpu
from jax.sharding import PartitionSpec as P

HEADS = 32
KVH = 4
HD = 128
STEPS = 5
PAGE = 16
GROUPS = HEADS // KVH
NEG_FILL = -1e30
SCALE2 = math.log2(math.e) / math.sqrt(HD)
STAT = 16
MIB = 1024 * 1024
CUTS = {1: (0, 16), 2: (0, 12, 16), 3: (0, 16), 4: (0, 16), 5: (0, 12, 16), 6: (0, 12, 16), 7: (0, 16)}
NT = (((1,), (1,)), ((), ()))


def up(value, unit):
    return -(-value // unit) * unit


def column(row):
    return jnp.transpose(jnp.broadcast_to(row, (row.shape[1], row.shape[1])))


def order_kernel(
    wide, parts, me_ref, dest_ref, req_ref, idx_ref, pool_ref, out_ref, tag_ref, token_ref, *refs
):
    chunk_refs, refs = refs[: len(parts)], refs[len(parts) :]
    pages_ref, line_ref, source_ref, in_sem, out_sem, line_sem = refs
    slots = pool_ref.shape[0]
    capacity = slots // wide
    shape = (slots, slots)
    high = lax.broadcasted_iota(jnp.int32, shape, 0)
    low = lax.broadcasted_iota(jnp.int32, shape, 1)
    dest = dest_ref[...]
    same = column(dest.astype(jnp.float32)) == dest.astype(jnp.float32)
    rank = jnp.sum(jnp.where(same & (high < low), 1.0, 0.0), axis=0, keepdims=True)
    moved_to = ((dest ^ me_ref[0]) * capacity).astype(jnp.float32) + rank
    match = column(moved_to) == low.astype(jnp.float32)
    source = jnp.sum(jnp.where(match, high.astype(jnp.float32), 0.0), axis=0, keepdims=True)
    line_ref[...] = source.astype(jnp.int32)
    copy = pltpu.make_async_copy(line_ref, source_ref, line_sem)
    copy.start()
    copy.wait()

    blocks = [(0, capacity, out_ref.at[pl.ds(me_ref[0] * capacity, capacity)])]
    for (d, first, last), chunk in zip(parts, chunk_refs):
        blocks.append((d * capacity + first, last - first, chunk))
    for c, (first, count, _) in enumerate(blocks):

        def start(j, carry, c=c):
            page = source_ref[0, j]
            pltpu.make_async_copy(pool_ref.at[page], pages_ref.at[j], in_sem.at[c]).start()
            return carry

        lax.fori_loop(first, first + count, start, 0)

    shifted = idx_ref[...] + 1
    fields = (req_ref[...], shifted // 32, shifted % 32)
    rank_col = column(rank)
    lane = low.astype(jnp.float32)
    spread_out = jnp.zeros(shape, jnp.float32)
    for i, field in enumerate(fields):
        picked = lane == rank_col + float(i * capacity)
        spread_out = spread_out + jnp.where(picked, column(field.astype(jnp.float32)), 0.0)
    line = lax.broadcasted_iota(jnp.int32, (wide, slots), 0)
    chosen = jnp.where(line == dest, 1.0, 0.0).astype(jnp.bfloat16)
    tag_ref[...] = jnp.dot(
        chosen, spread_out.astype(jnp.bfloat16), preferred_element_type=jnp.float32
    )

    tokens = slots * PAGE
    page = lax.broadcasted_iota(jnp.int32, (slots, tokens), 0)
    token = lax.broadcasted_iota(jnp.int32, (slots, tokens), 1)
    widen = jnp.where(page == token // PAGE, 1.0, 0.0).astype(jnp.bfloat16)
    row = lax.broadcasted_iota(jnp.int32, (8, slots), 0)
    stacked = jnp.zeros((8, slots), jnp.float32)
    for i, field in enumerate(fields):
        stacked = jnp.where(row == i, field.astype(jnp.float32), stacked)
    token_ref[...] = jnp.dot(
        stacked.astype(jnp.bfloat16), widen, preferred_element_type=jnp.float32
    )

    copies = []
    for c, (first, count, target) in enumerate(blocks):
        held = pages_ref.at[pl.ds(first, count)]
        pltpu.make_async_copy(pool_ref.at[pl.ds(0, count)], held, in_sem.at[c]).wait()
        copies.append(pltpu.make_async_copy(held, target, out_sem.at[c]))
        copies[-1].start()
    for copy in copies:
        copy.wait()


def order_pages(me, dest, page_req, page_idx, pool, wide, parts):
    slots = pool.shape[0]
    part = lambda count: jax.ShapeDtypeStruct((count,) + pool.shape[1:], pool.dtype)
    out_shape = [part(slots), jax.ShapeDtypeStruct((wide, slots), jnp.float32)]
    out_shape += [jax.ShapeDtypeStruct((8, slots * PAGE), jnp.float32)]
    out_shape += [part(last - first) for _, first, last in parts]
    vmem = pl.BlockSpec(memory_space=pltpu.VMEM)
    hbm = pl.BlockSpec(memory_space=pltpu.HBM)
    return pl.pallas_call(
        functools.partial(order_kernel, wide, parts),
        out_shape=out_shape,
        in_specs=[pl.BlockSpec(memory_space=pltpu.SMEM), vmem, vmem, vmem, hbm],
        out_specs=[hbm, vmem, vmem] + [hbm] * len(parts),
        scratch_shapes=[
            pltpu.VMEM(pool.shape, pool.dtype),
            pltpu.VMEM((1, slots), jnp.int32),
            pltpu.SMEM((1, slots), jnp.int32),
            pltpu.SemaphoreType.DMA((1 + len(parts),)),
            pltpu.SemaphoreType.DMA((1 + len(parts),)),
            pltpu.SemaphoreType.DMA,
        ],
        compiler_params=pltpu.CompilerParams(vmem_limit_bytes=56 * MIB),
        cost_estimate=pl.CostEstimate(
            flops=0, bytes_accessed=2 * pool.size * 2, transcendentals=0
        ),
    )(me, dest.reshape(1, -1), page_req.reshape(1, -1), page_idx.reshape(1, -1), pool)


def place_kernel(place_ref, *refs):
    in_refs, (out_ref, sem) = refs[:-3], refs[-2:]
    copies = []
    for i, chunk in enumerate(in_refs):
        depth = chunk.shape[0]
        copies.append(
            pltpu.make_async_copy(
                chunk, out_ref.at[pl.ds(place_ref[i], depth)], sem.at[i]
            )
        )
    for copy in copies:
        copy.start()
    for copy in copies:
        copy.wait()


def place_pages(place, chunks, pages):
    count = len(chunks)
    return pl.pallas_call(
        place_kernel,
        out_shape=jax.ShapeDtypeStruct(pages.shape, pages.dtype),
        in_specs=[pl.BlockSpec(memory_space=pltpu.SMEM)]
        + [pl.BlockSpec(memory_space=pltpu.VMEM)] * count
        + [pl.BlockSpec(memory_space=pl.ANY)],
        out_specs=pl.BlockSpec(memory_space=pl.ANY),
        scratch_shapes=[pltpu.SemaphoreType.DMA((count,))],
        input_output_aliases={count + 1: 0},
        compiler_params=pltpu.CompilerParams(vmem_limit_bytes=2 * count * chunks[0].size + 2 * MIB),
        cost_estimate=pl.CostEstimate(
            flops=0, bytes_accessed=4 * count * chunks[0].size, transcendentals=0
        ),
    )(place, *chunks, pages)


def cut(value):
    return value.astype(jnp.bfloat16).astype(jnp.float32)


def split_stats(peak, total):
    high = cut(peak)
    mid = cut(peak - high)
    return high, mid, peak - high - mid, cut(total), total - cut(total)


def attend_kernel(rows, piece, peers, me_ref, length_ref, *refs):
    query_refs, refs = refs[:peers], refs[peers:]
    key_ref, value_ref, new_key_ref, new_value_ref, token_ref = refs[:5]
    out_refs = refs[5 : 5 + peers]
    bias_ref, new_bias_ref, score_ref, weight_ref, query_ref, result_ref = refs[5 + peers :]
    tokens = key_ref.shape[0]
    step = pl.program_id(0)

    @pl.when(step == 0)
    def _():
        owner = token_ref[0:1, :]
        offset = lax.broadcasted_iota(jnp.int32, owner.shape, 1) % PAGE
        spot = (token_ref[1:2, :] * 32 + token_ref[2:3, :] - 1) * PAGE + offset.astype(jnp.float32)
        request = lax.broadcasted_iota(jnp.int32, (rows, 1), 0) // STEPS
        limit = jnp.zeros((rows, 1), jnp.int32)
        for r in range(rows // STEPS):
            limit = jnp.where(request == r, length_ref[r], limit)
        seen = (owner == request.astype(jnp.float32)) & (spot < limit.astype(jnp.float32))
        bias_ref[...] = jnp.where(seen, 0.0, NEG_FILL)
        row = lax.broadcasted_iota(jnp.int32, new_bias_ref.shape, 0)
        col = lax.broadcasted_iota(jnp.int32, new_bias_ref.shape, 1)
        first = jnp.where((me_ref[0] == 0) & (me_ref[1] == 0), 1, 0)
        seen = (row // STEPS == col // STEPS) & (col <= row) & (col < rows * first)
        new_bias_ref[...] = jnp.where(seen, 0.0, NEG_FILL)
        if peers > 1:
            for d in range(peers):
                query_ref[me_ref[1] ^ d] = query_refs[d][...]

    if peers > 1:
        per_step = query_refs[0].shape[0] // KVH
        query = jnp.concatenate(
            [
                query_ref[n, step * per_step + i].astype(jnp.float32)
                for i in range(per_step)
                for n in range(peers)
            ],
            axis=0,
        ).astype(jnp.bfloat16)
    else:
        query = query_refs[0][0]
    score_ref[:, :tokens] = lax.dot_general(
        query, key_ref[...], NT, preferred_element_type=jnp.float32
    )
    score_ref[:, tokens:] = lax.dot_general(
        query, new_key_ref[...], NT, preferred_element_type=jnp.float32
    )
    together = 1 if rows % 16 == 0 else 2
    span = together * rows
    peaks, totals = [], []
    for c in range(GROUPS // together):
        block = pl.ds(c * span, span)
        old = score_ref[block, :tokens].reshape(together, rows, tokens) * SCALE2 + bias_ref[...]
        new = score_ref[block, tokens:].reshape(together, rows, -1) * SCALE2 + new_bias_ref[...]
        peak = jnp.maximum(
            jnp.max(old, axis=-1, keepdims=True), jnp.max(new, axis=-1, keepdims=True)
        )
        old = jnp.exp2(old - peak)
        new = jnp.exp2(new - peak)
        totals.append(
            (jnp.sum(old, axis=-1, keepdims=True) + jnp.sum(new, axis=-1, keepdims=True)).reshape(
                span, 1
            )
        )
        peaks.append(peak.reshape(span, 1))
        weight_ref[block, :tokens] = old.reshape(span, tokens).astype(jnp.bfloat16)
        weight_ref[block, tokens:] = new.reshape(span, -1).astype(jnp.bfloat16)
    mixed = jnp.dot(
        weight_ref[:, :tokens], value_ref[...], preferred_element_type=jnp.float32
    ) + jnp.dot(weight_ref[:, tokens:], new_value_ref[...], preferred_element_type=jnp.float32)
    peak = jnp.concatenate(peaks, axis=0)
    total = jnp.concatenate(totals, axis=0)
    lane = lax.broadcasted_iota(jnp.int32, (GROUPS * rows, HD), 1)
    stats = jnp.zeros((GROUPS * rows, HD), jnp.float32)
    for i, part in enumerate(split_stats(peak, total)):
        stats = jnp.where(lane == i, part, stats)
    pick = (
        lax.broadcasted_iota(jnp.int32, (STAT, HD), 0)
        == lax.broadcasted_iota(jnp.int32, (STAT, HD), 1)
    ).astype(jnp.bfloat16)
    fill = result_ref.shape[1] - STAT - piece
    for c in range(GROUPS * rows // piece):
        part = slice(c * piece, (c + 1) * piece)
        turned = lax.dot_general(
            pick,
            jnp.concatenate(
                [stats[part], jnp.zeros((HD - piece, HD), jnp.float32)], axis=0
            ).astype(jnp.bfloat16),
            NT,
            preferred_element_type=jnp.float32,
        )
        result_ref[c] = jnp.concatenate(
            [turned, mixed[part], jnp.zeros((fill, HD), jnp.float32)], axis=0
        ).astype(jnp.bfloat16)
    if peers > 1:
        for d, out_ref in enumerate(out_refs):

            @pl.when((step ^ me_ref[1]) == d)
            def _():
                out_ref[...] = result_ref[...]
    else:
        out_refs[0][...] = result_ref[...]


def attend(me, lengths, queries, keyval, pool, token_info, rows, piece):
    tokens = pool.shape[0]
    extra = keyval.shape[0]
    peers = len(queries)
    pieces = GROUPS * rows // piece
    height = STAT + up(piece, 16)
    whole = lambda shape: pl.BlockSpec(shape, lambda k: (0,) * len(shape))
    if peers > 1:
        query_spec = whole(queries[0].shape)
        out_spec = whole((pieces, height, HD))
        out_shape = jax.ShapeDtypeStruct((pieces, height, HD), jnp.bfloat16)
    else:
        query_spec = pl.BlockSpec((1,) + queries[0].shape[1:], lambda k: (k, 0, 0))
        out_spec = pl.BlockSpec((pieces, height, HD), lambda k: (k, 0, 0))
        out_shape = jax.ShapeDtypeStruct((KVH * pieces, height, HD), jnp.bfloat16)
    return pl.pallas_call(
        functools.partial(attend_kernel, rows, piece, peers),
        grid=(KVH,),
        out_shape=[out_shape] * peers,
        in_specs=[pl.BlockSpec(memory_space=pltpu.SMEM)] * 2
        + [query_spec] * peers
        + [
            pl.BlockSpec((tokens, HD), lambda k: (0, k)),
            pl.BlockSpec((tokens, HD), lambda k: (0, KVH + k)),
            pl.BlockSpec((extra, HD), lambda k: (0, k)),
            pl.BlockSpec((extra, HD), lambda k: (0, KVH + k)),
            whole(token_info.shape),
        ],
        out_specs=[out_spec] * peers,
        scratch_shapes=[
            pltpu.VMEM((rows, tokens), jnp.float32),
            pltpu.VMEM((rows, extra), jnp.float32),
            pltpu.VMEM((GROUPS * rows, tokens + extra), jnp.float32),
            pltpu.VMEM((GROUPS * rows, tokens + extra), jnp.bfloat16),
            pltpu.VMEM((peers,) + queries[0].shape, jnp.bfloat16),
            pltpu.VMEM((pieces, height, HD), jnp.bfloat16),
        ],
        compiler_params=pltpu.CompilerParams(vmem_limit_bytes=56 * MIB),
        cost_estimate=pl.CostEstimate(flops=1, bytes_accessed=1, transcendentals=0),
    )(me, lengths, *queries, pool, pool, keyval, keyval, token_info)


def combine_kernel(piece, last, count, *refs):
    if last:
        part_ref, out_ref = refs
        part_refs = [part_ref.at[pl.ds(i, 1)] for i in range(count)]
    else:
        part_refs, out_ref = refs[:count], refs[count]
    groups, height = part_refs[0].shape[:2]
    peaks, totals = [], []
    for i in range(count):
        for j in range(groups):
            stat = part_refs[i][j, :STAT, :].astype(jnp.float32)
            peaks.append(stat[0:1] + stat[1:2] + stat[2:3])
            totals.append(stat[3:4] + stat[4:5])
    peak = jnp.concatenate(peaks, axis=0).reshape(count, groups, HD)
    total = jnp.concatenate(totals, axis=0).reshape(count, groups, HD)
    top = jnp.max(peak, axis=0)
    lead = jnp.exp2(peak - top[None])
    whole = jnp.sum(lead * total, axis=0)
    if last:
        lane = lax.broadcasted_iota(jnp.int32, whole.shape, 1)
        lead = lead / jnp.where(lane < piece, whole, 1.0)[None]
    lead = lead.reshape(count * groups, HD)
    if (count * groups) % HD:
        fill = up(count * groups, HD) - count * groups
        lead = jnp.concatenate([lead, jnp.zeros((fill, HD), jnp.float32)], axis=0)
    lead = jnp.transpose(lead)
    rows = height - STAT
    for j in range(groups):
        result = jnp.zeros((rows, HD), jnp.float32)
        for i in range(count):
            c = i * groups + j
            result = result + lead[:rows, c : c + 1] * part_refs[i][j, STAT:, :].astype(jnp.float32)
        if last:
            for i in range(out_ref.shape[0]):
                out_ref[i] = result[:piece].astype(jnp.bfloat16)
        else:
            stats = split_stats(top[j : j + 1], whole[j : j + 1])
            rest = jnp.zeros((STAT - len(stats), HD), jnp.float32)
            out_ref[j] = jnp.concatenate([*stats, rest, result], axis=0).astype(jnp.bfloat16)


def combine(parts, piece, repeats=0):
    count = parts[0].shape[0] if repeats else len(parts)
    shape = (repeats, piece, HD) if repeats else parts[0].shape
    return pl.pallas_call(
        functools.partial(combine_kernel, piece, repeats > 0, count),
        out_shape=jax.ShapeDtypeStruct(shape, jnp.bfloat16),
        in_specs=[pl.BlockSpec(memory_space=pltpu.VMEM)] * len(parts),
        out_specs=pl.BlockSpec(memory_space=pltpu.VMEM),
        compiler_params=pltpu.CompilerParams(vmem_limit_bytes=8 * MIB),
        cost_estimate=pl.CostEstimate(
            flops=2 * len(parts) * parts[0].size,
            bytes_accessed=len(parts) * parts[0].size * 2,
            transcendentals=0,
        ),
    )(*parts)


def reorder(shape, unit, valid, own, column):
    first, second = (0, 1) if column else (1, 0)
    block = lax.broadcasted_iota(jnp.int32, shape, second) // unit
    place = lax.broadcasted_iota(jnp.int32, shape, second) % unit
    target = (block ^ own) * valid + place
    match = (lax.broadcasted_iota(jnp.int32, shape, first) == target) & (place < valid)
    return match.astype(jnp.bfloat16)


def project_kernel(peers, me_ref, hidden_ref, query_ref, keyval_ref, *refs):
    out_refs, (full_ref,) = refs[:peers], refs[peers:]
    count, local, depth = hidden_ref.shape
    unit = up(local, 8)
    blocks = []
    for i in range(count):
        blocks.append(hidden_ref[i].astype(jnp.float32))
        if unit > local:
            blocks.append(jnp.zeros((unit - local, depth), jnp.float32))
    hidden = jnp.concatenate(blocks, axis=0).astype(jnp.bfloat16)
    order = reorder((count * local, count * unit), unit, local, 0, True)
    hidden = jnp.dot(order, hidden, preferred_element_type=jnp.float32).astype(jnp.bfloat16)
    full_ref[...] = jnp.dot(hidden, query_ref[...], preferred_element_type=jnp.float32)
    keyval = jnp.dot(hidden, keyval_ref[...], preferred_element_type=jnp.float32)
    for d, out_ref in enumerate(out_refs):
        start = pl.multiple_of((me_ref[1] ^ d) * HD, HD)
        out_ref[:, :HD] = full_ref[:, pl.ds(start, HD)]
        out_ref[:, HD:] = keyval


def pack_kernel(peers, *refs):
    own, tag_ref, out_ref = refs[:peers], refs[peers], refs[peers + 1]
    total = (own[0][...] + own[1][...]) + (own[2][...] + own[3][...])
    tags = jnp.concatenate([tag_ref[...], jnp.zeros_like(tag_ref[...])], axis=1)
    packed = jnp.concatenate([total, tags], axis=0).astype(jnp.bfloat16)
    for i in range(out_ref.shape[0]):
        out_ref[i] = packed


def unpack_kernel(rows, me_ref, kept_ref, part_ref, query_ref, keyval_ref, *refs):
    entry_ref, req_ref, idx_ref = refs
    count = part_ref.shape[0]
    line = lax.broadcasted_iota(jnp.int32, (count, HD), 0)
    tags = jnp.zeros((count, HD), jnp.float32)
    fill = jnp.zeros((keyval_ref.shape[0] - rows, HD), jnp.float32)
    for i in range(count):
        part = part_ref[i].astype(jnp.float32)
        query_ref[i] = part[:rows, :HD].astype(jnp.bfloat16)
        block = jnp.concatenate([part[:rows, HD:], fill], axis=0).astype(jnp.bfloat16)
        keyval_ref[:, i * HD : (i + 1) * HD] = block
        mine = jnp.where(line == me_ref[0], part[rows : rows + count, :HD], 0.0)
        tags = tags + jnp.where(line == i, jnp.sum(mine, axis=0, keepdims=True), 0.0)
    capacity = HD // count
    high = lax.broadcasted_iota(jnp.int32, (HD, HD), 0)
    low = lax.broadcasted_iota(jnp.int32, (HD, HD), 1)
    slot = lax.broadcasted_iota(jnp.int32, (count, HD), 1)
    tags = tags.astype(jnp.bfloat16)
    fields = []
    for i in range(3):
        pick = jnp.where(high == i * capacity + low % capacity, 1.0, 0.0).astype(jnp.bfloat16)
        spread_out = jnp.dot(tags, pick, preferred_element_type=jnp.float32)
        spread_out = jnp.where(slot // capacity == line, spread_out, 0.0)
        fields.append(jnp.sum(spread_out, axis=0, keepdims=True))
    req_ref[...] = fields[0].astype(jnp.int32)
    idx_ref[...] = (fields[1] * 32.0 + fields[2] - 1.0).astype(jnp.int32)
    local = entry_ref.shape[1]
    step = lax.broadcasted_iota(jnp.int32, (16, keyval_ref.shape[0]), 0)
    row = lax.broadcasted_iota(jnp.int32, (16, keyval_ref.shape[0]), 1)
    kept = (row == me_ref[0] * local + step) & (step < kept_ref[me_ref[0]])
    kept = jnp.where(kept, 1.0, 0.0).astype(jnp.bfloat16)
    entries = jnp.dot(kept, keyval_ref[...], preferred_element_type=jnp.float32)
    entry_ref[0] = entries[:local].astype(jnp.bfloat16)


def finish_kernel(peers, me_ref, part_ref, weight_ref, *refs):
    count, rows = part_ref.shape[:2]
    local = rows // peers
    unit = up(local, 16)
    whole = jnp.concatenate([part_ref[i] for i in range(count)], axis=1)
    order = reorder((peers * unit, rows), unit, local, me_ref[1], False)
    mixed = jnp.dot(order, whole, preferred_element_type=jnp.float32)
    mixed = jnp.dot(mixed.astype(jnp.bfloat16), weight_ref[...], preferred_element_type=jnp.float32)
    for d, out_ref in enumerate(refs):
        out_ref[...] = mixed[d * unit : d * unit + local]


def in_vmem(kernel, out_shape, me, *args, scratch=()):
    head = [] if me is None else list(me) if isinstance(me, tuple) else [me]
    return pl.pallas_call(
        kernel,
        out_shape=out_shape,
        in_specs=[pl.BlockSpec(memory_space=pltpu.SMEM)] * len(head)
        + [pl.BlockSpec(memory_space=pltpu.VMEM)] * len(args),
        out_specs=jax.tree.map(lambda _: pl.BlockSpec(memory_space=pltpu.VMEM), out_shape),
        scratch_shapes=scratch,
        compiler_params=pltpu.CompilerParams(vmem_limit_bytes=16 * MIB),
        cost_estimate=pl.CostEstimate(
            flops=0, bytes_accessed=sum(2 * arg.size for arg in args), transcendentals=0
        ),
    )(*head, *args)


def group_of(d, wide):
    return d if wide <= 8 else 1 + (d - 1) * 7 // (wide - 1)


def spread(block, axis):
    count = lax.axis_size(axis)
    return lax.all_to_all(
        jnp.broadcast_to(block[None], (count,) + block.shape),
        axis,
        split_axis=0,
        concat_axis=0,
        tiled=True,
    )


def on_device(hidden, w_query, w_keyval, w_out, pool, page_req, page_idx, lengths, moves, accepted):
    wide = lax.axis_size("wide")
    narrow = lax.axis_size("narrow")
    local_rows = hidden.shape[0]
    rows = local_rows * wide
    requests = rows // STEPS
    slots = pool.shape[0]
    capacity = slots // wide
    own_cols = w_query.shape[1] // narrow
    piece = HEADS * rows // (wide * narrow)
    extra = up(rows, HD)
    direct = piece == rows and own_cols == HD and slots == HD
    direct = direct and wide == 8 and narrow == 4 and local_rows == STEPS
    me = lax.axis_index("wide")
    both = jnp.stack([me, lax.axis_index("narrow")])
    exchange = functools.partial(lax.all_to_all, split_axis=0, concat_axis=0, tiled=True)

    def send(block, axis, d):
        return lax.ppermute(block, axis, [(i, i ^ d) for i in range(lax.axis_size(axis))])

    def share(block, axis):
        return [block] + [send(block, axis, d) for d in range(1, lax.axis_size(axis))]

    def deal(blocks, axis):
        return [blocks[0]] + [send(block, axis, d) for d, block in enumerate(blocks) if d]

    gathered = spread(hidden, "wide")

    parts = []
    for d in range(1, wide):
        cuts = [cut * capacity // 16 for cut in CUTS[group_of(d, wide)]]
        parts += [(d, a, b) for a, b in zip(cuts[:-1], cuts[1:]) if b > a]
    moved_pool, tags, token_info, *chunks = order_pages(
        both, moves, page_req, page_idx, pool, wide, parts
    )
    arrived = {}
    flying = {}

    def members(names):
        taken = []
        for group, which in names:
            cut = CUTS[group][which] * capacity // 16
            end = CUTS[group][which + 1] * capacity // 16
            taken += [
                c
                for c, (d, first, last) in enumerate(parts)
                if group_of(d, wide) == group and (first, last) == (cut, end)
            ]
        return taken

    def launch(values, *names):
        taken = members(names)
        values, sent = lax.optimization_barrier((values, [chunks[c] for c in taken]))
        for c, chunk in zip(taken, sent):
            flying[c] = send(chunk, "wide", parts[c][0])
        return values

    def land(values, *names):
        taken = members(names)
        values, got = lax.optimization_barrier((values, [flying[c] for c in taken]))
        arrived.update(zip(taken, got))
        return values

    def beside(step, value, *names):
        return land(step(launch(value, *names)), *names)

    def placed(pages):
        taken = sorted(arrived)
        if not taken:
            return pages
        place = jnp.stack([(me ^ parts[c][0]) * capacity + parts[c][1] for c in taken])
        pages = place_pages(place, [arrived[c] for c in taken], pages)
        arrived.clear()
        return pages

    gathered, tags = lax.optimization_barrier((gathered, tags))
    tokens = pool.reshape(slots * PAGE, -1)
    if direct:
        block = jax.ShapeDtypeStruct((rows, 2 * HD), jnp.float32)
        partial = in_vmem(
            functools.partial(project_kernel, narrow),
            [block] * narrow,
            both,
            gathered,
            w_query,
            w_keyval,
            scratch=[pltpu.VMEM((rows, narrow * HD), jnp.float32)],
        )
        partial = deal(partial, "narrow")
        packed = in_vmem(
            functools.partial(pack_kernel, narrow),
            jax.ShapeDtypeStruct((wide, rows + wide, 2 * HD), jnp.bfloat16),
            None,
            *partial,
            tags,
        )
        received = beside(lambda value: exchange(value, "wide"), packed, (1, 0), (6, 0))
        received = launch(received, (7, 0), (6, 1))
        queries, keyval, new_entries, moved_req, moved_idx = in_vmem(
            functools.partial(unpack_kernel, rows),
            [
                jax.ShapeDtypeStruct((wide, rows, HD), jnp.bfloat16),
                jax.ShapeDtypeStruct((extra, wide * HD), jnp.bfloat16),
                jax.ShapeDtypeStruct((1, local_rows, wide * HD), jnp.bfloat16),
                jax.ShapeDtypeStruct((1, slots), jnp.int32),
                jax.ShapeDtypeStruct((1, slots), jnp.int32),
            ],
            (both, accepted),
            received,
        )
        moved_req, moved_idx = moved_req.reshape(slots), moved_idx.reshape(slots)
        queries = share(queries, "narrow")
    else:
        gathered = gathered.reshape(rows, -1)
        query_part = jnp.dot(gathered, w_query, preferred_element_type=jnp.float32)
        keyval_part = jnp.dot(gathered, w_keyval, preferred_element_type=jnp.float32)
        query_part = jnp.transpose(query_part.reshape(rows, narrow, own_cols), (1, 0, 2))
        partial = jnp.concatenate(
            [query_part, jnp.broadcast_to(keyval_part[None], (narrow,) + keyval_part.shape)], axis=2
        )
        partial = exchange(partial, "narrow")
        projected = jnp.sum(partial, axis=0).astype(jnp.bfloat16)
        tags = tags[:, : 3 * capacity].astype(jnp.bfloat16)[:, None]
        tags = jnp.pad(tags, ((0, 0), (0, 7), (0, projected.shape[1] - tags.shape[2])))
        packed = jnp.broadcast_to(projected[None], (wide,) + projected.shape)
        packed = jnp.concatenate([packed, tags], axis=1)
        received = beside(lambda value: exchange(value, "wide"), packed, (1, 0), (6, 0))
        received = launch(received, (7, 0), (6, 1))
        tags_in = received[:, rows]
        queries = received[:, :rows, :own_cols]
        queries = spread(queries, "narrow")
        queries = jnp.transpose(queries, (2, 1, 0, 3)).reshape(rows, HEADS, HD)
        queries = [jnp.transpose(queries, (1, 0, 2)).reshape(KVH, GROUPS * rows, HD)]
        keyval = jnp.transpose(received[:, :rows, own_cols:], (1, 0, 2)).reshape(rows, -1)
        keyval = jnp.pad(keyval, ((0, extra - rows), (0, 0)))
        tags_in = tags_in.astype(jnp.int32)
        moved_req = tags_in[:, :capacity].reshape(slots)
        moved_idx = tags_in[:, capacity : 2 * capacity] * 32
        moved_idx = (moved_idx + tags_in[:, 2 * capacity : 3 * capacity] - 1).reshape(slots)
        local_req = local_rows // STEPS
        fresh = lax.dynamic_slice_in_dim(keyval, me * local_rows, local_rows, 0)
        fresh = fresh.reshape(local_req, STEPS, -1)
        kept = lax.dynamic_slice_in_dim(accepted, me * local_req, local_req, 0)
        step_ids = jnp.arange(STEPS)[None, :, None]
        new_entries = jnp.where(
            step_ids < kept[:, None, None], fresh, jnp.zeros((), jnp.bfloat16)
        )

    queries, moved_pool = lax.optimization_barrier((queries, placed(moved_pool)))
    mixed = attend(both, lengths, queries, keyval, tokens, token_info, rows, piece)
    if direct:
        mixed = land(deal(mixed, "narrow"), (7, 0), (6, 1))
    else:
        mixed = land(exchange(mixed[0], "narrow"), (7, 0), (6, 1))
        mixed = mixed.reshape((narrow, wide) + mixed.shape[1:])
        mixed = [mixed[i] for i in range(narrow)]
    mixed = combine(mixed, piece)
    mixed, pages = lax.optimization_barrier((mixed, moved_pool))
    pages = placed(pages)
    mixed = beside(lambda value: exchange(value, "wide"), mixed, (3, 0), (4, 0))
    mixed, moved_pool = lax.optimization_barrier((mixed, pages))
    attn = combine([mixed], piece, wide)
    attn, pages = lax.optimization_barrier((attn, moved_pool))
    pages = placed(pages)
    attn = beside(lambda value: exchange(value, "wide"), attn, (2, 0), (5, 0))
    attn, moved_pool = lax.optimization_barrier((attn, pages))
    if direct:
        sums = in_vmem(
            functools.partial(finish_kernel, narrow),
            [jax.ShapeDtypeStruct((rows // narrow, w_out.shape[1]), jnp.float32)] * narrow,
            both,
            attn,
            w_out,
        )
        sums, pages = lax.optimization_barrier((sums, moved_pool))
        pages = placed(pages)
        sums = beside(lambda value: deal(value, "narrow"), sums, (2, 1), (5, 1))
        attended = ((sums[0] + sums[1]) + (sums[2] + sums[3])).astype(jnp.bfloat16)
    else:
        attn = jnp.transpose(attn.reshape(-1, rows, HD), (1, 0, 2)).reshape(rows, -1)
        sums = jnp.dot(attn, w_out, preferred_element_type=jnp.float32)
        sums = sums.reshape(narrow, rows // narrow, -1)
        pages = placed(moved_pool)
        sums = beside(lambda value: exchange(value, "narrow"), sums, (2, 1), (5, 1))
        attended = jnp.sum(sums, axis=0).astype(jnp.bfloat16)
    attended, pages = lax.optimization_barrier((attended, pages))
    moved_pool = placed(pages)
    return (attended, new_entries, moved_pool, moved_req, moved_idx)


def solution(mesh):
    in_specs = (
        P("wide", "narrow"),
        P("narrow", "wide"),
        P("narrow", "wide"),
        P("narrow", "wide"),
        P(("wide", "narrow"), None, None),
        P(("wide", "narrow")),
        P(("wide", "narrow")),
        P(),
        P(("wide", "narrow"), None),
        P(),
    )
    out_specs = (
        P("narrow", "wide"),
        P("wide", None, None),
        P(("wide", "narrow"), None, None),
        P(("wide", "narrow")),
        P(("wide", "narrow")),
    )
    return jax.shard_map(
        on_device, mesh=mesh, in_specs=in_specs, out_specs=out_specs, check_vma=False
    )
```

```python
import functools
import math

import jax
import jax.numpy as jnp
from jax import lax
from jax.experimental import pallas as pl
from jax.experimental.pallas import tpu as pltpu
from jax.sharding import PartitionSpec as P

HEADS = 32
KVH = 4
HD = 128
STEPS = 5
PAGE = 16
GROUPS = HEADS // KVH
NEG_FILL = -1e30
SCALE2 = math.log2(math.e) / math.sqrt(HD)
STAT = 16
MIB = 1024 * 1024
CUTS = {1: (0, 16), 2: (0, 16), 3: (0, 12, 16), 4: (0, 4, 16), 5: (0, 12, 16), 6: (0, 4, 16), 7: (0, 16)}
NT = (((1,), (1,)), ((), ()))


def up(value, unit):
    return -(-value // unit) * unit


def column(row):
    return jnp.transpose(jnp.broadcast_to(row, (row.shape[1], row.shape[1])))


def order_kernel(
    wide, parts, me_ref, dest_ref, req_ref, idx_ref, pool_ref, out_ref, tag_ref, token_ref, *refs
):
    chunk_refs, refs = refs[: len(parts)], refs[len(parts) :]
    pages_ref, line_ref, source_ref, in_sem, out_sem, line_sem = refs
    slots = pool_ref.shape[0]
    capacity = slots // wide
    shape = (slots, slots)
    high = lax.broadcasted_iota(jnp.int32, shape, 0)
    low = lax.broadcasted_iota(jnp.int32, shape, 1)
    dest = dest_ref[...]
    same = column(dest.astype(jnp.float32)) == dest.astype(jnp.float32)
    rank = jnp.sum(jnp.where(same & (high < low), 1.0, 0.0), axis=0, keepdims=True)
    moved_to = ((dest ^ me_ref[0]) * capacity).astype(jnp.float32) + rank
    match = column(moved_to) == low.astype(jnp.float32)
    source = jnp.sum(jnp.where(match, high.astype(jnp.float32), 0.0), axis=0, keepdims=True)
    line_ref[...] = source.astype(jnp.int32)
    copy = pltpu.make_async_copy(line_ref, source_ref, line_sem)
    copy.start()
    copy.wait()

    blocks = [(0, capacity, out_ref.at[pl.ds(me_ref[0] * capacity, capacity)])]
    for (d, first, last), chunk in zip(parts, chunk_refs):
        blocks.append((d * capacity + first, last - first, chunk))
    for c, (first, count, _) in enumerate(blocks):

        def start(j, carry, c=c):
            page = source_ref[0, j]
            pltpu.make_async_copy(pool_ref.at[page], pages_ref.at[j], in_sem.at[c]).start()
            return carry

        lax.fori_loop(first, first + count, start, 0)

    shifted = idx_ref[...] + 1
    fields = (req_ref[...], shifted // 32, shifted % 32)
    rank_col = column(rank)
    lane = low.astype(jnp.float32)
    spread_out = jnp.zeros(shape, jnp.float32)
    for i, field in enumerate(fields):
        picked = lane == rank_col + float(i * capacity)
        spread_out = spread_out + jnp.where(picked, column(field.astype(jnp.float32)), 0.0)
    line = lax.broadcasted_iota(jnp.int32, (wide, slots), 0)
    chosen = jnp.where(line == dest, 1.0, 0.0).astype(jnp.bfloat16)
    tag_ref[...] = jnp.dot(
        chosen, spread_out.astype(jnp.bfloat16), preferred_element_type=jnp.float32
    )

    tokens = slots * PAGE
    page = lax.broadcasted_iota(jnp.int32, (slots, tokens), 0)
    token = lax.broadcasted_iota(jnp.int32, (slots, tokens), 1)
    widen = jnp.where(page == token // PAGE, 1.0, 0.0).astype(jnp.bfloat16)
    row = lax.broadcasted_iota(jnp.int32, (8, slots), 0)
    stacked = jnp.zeros((8, slots), jnp.float32)
    for i, field in enumerate(fields):
        stacked = jnp.where(row == i, field.astype(jnp.float32), stacked)
    token_ref[...] = jnp.dot(
        stacked.astype(jnp.bfloat16), widen, preferred_element_type=jnp.float32
    )

    copies = []
    for c, (first, count, target) in enumerate(blocks):
        held = pages_ref.at[pl.ds(first, count)]
        pltpu.make_async_copy(pool_ref.at[pl.ds(0, count)], held, in_sem.at[c]).wait()
        copies.append(pltpu.make_async_copy(held, target, out_sem.at[c]))
        copies[-1].start()
    for copy in copies:
        copy.wait()


def order_pages(me, dest, page_req, page_idx, pool, wide, parts):
    slots = pool.shape[0]
    part = lambda count: jax.ShapeDtypeStruct((count,) + pool.shape[1:], pool.dtype)
    out_shape = [part(slots), jax.ShapeDtypeStruct((wide, slots), jnp.float32)]
    out_shape += [jax.ShapeDtypeStruct((8, slots * PAGE), jnp.float32)]
    out_shape += [part(last - first) for _, first, last in parts]
    vmem = pl.BlockSpec(memory_space=pltpu.VMEM)
    hbm = pl.BlockSpec(memory_space=pltpu.HBM)
    return pl.pallas_call(
        functools.partial(order_kernel, wide, parts),
        out_shape=out_shape,
        in_specs=[pl.BlockSpec(memory_space=pltpu.SMEM), vmem, vmem, vmem, hbm],
        out_specs=[hbm, vmem, vmem] + [hbm] * len(parts),
        scratch_shapes=[
            pltpu.VMEM(pool.shape, pool.dtype),
            pltpu.VMEM((1, slots), jnp.int32),
            pltpu.SMEM((1, slots), jnp.int32),
            pltpu.SemaphoreType.DMA((1 + len(parts),)),
            pltpu.SemaphoreType.DMA((1 + len(parts),)),
            pltpu.SemaphoreType.DMA,
        ],
        compiler_params=pltpu.CompilerParams(vmem_limit_bytes=56 * MIB),
        cost_estimate=pl.CostEstimate(
            flops=0, bytes_accessed=2 * pool.size * 2, transcendentals=0
        ),
    )(me, dest.reshape(1, -1), page_req.reshape(1, -1), page_idx.reshape(1, -1), pool)


def place_kernel(place_ref, *refs):
    in_refs, (out_ref, sem) = refs[:-3], refs[-2:]
    copies = []
    for i, chunk in enumerate(in_refs):
        depth = chunk.shape[0]
        copies.append(
            pltpu.make_async_copy(
                chunk, out_ref.at[pl.ds(place_ref[i], depth)], sem.at[i]
            )
        )
    for copy in copies:
        copy.start()
    for copy in copies:
        copy.wait()


def place_pages(place, chunks, pages):
    count = len(chunks)
    return pl.pallas_call(
        place_kernel,
        out_shape=jax.ShapeDtypeStruct(pages.shape, pages.dtype),
        in_specs=[pl.BlockSpec(memory_space=pltpu.SMEM)]
        + [pl.BlockSpec(memory_space=pltpu.VMEM)] * count
        + [pl.BlockSpec(memory_space=pl.ANY)],
        out_specs=pl.BlockSpec(memory_space=pl.ANY),
        scratch_shapes=[pltpu.SemaphoreType.DMA((count,))],
        input_output_aliases={count + 1: 0},
        compiler_params=pltpu.CompilerParams(vmem_limit_bytes=2 * count * chunks[0].size + 2 * MIB),
        cost_estimate=pl.CostEstimate(
            flops=0, bytes_accessed=4 * count * chunks[0].size, transcendentals=0
        ),
    )(place, *chunks, pages)


def cut(value):
    return value.astype(jnp.bfloat16).astype(jnp.float32)


def split_stats(peak, total):
    high = cut(peak)
    mid = cut(peak - high)
    return high, mid, peak - high - mid, cut(total), total - cut(total)


def attend_kernel(rows, piece, peers, me_ref, length_ref, *refs):
    query_refs, refs = refs[:peers], refs[peers:]
    key_ref, value_ref, new_key_ref, new_value_ref, token_ref = refs[:5]
    out_refs = refs[5 : 5 + peers]
    bias_ref, new_bias_ref, score_ref, weight_ref, query_ref, result_ref = refs[5 + peers :]
    tokens = key_ref.shape[0]
    step = pl.program_id(0)

    @pl.when(step == 0)
    def _():
        owner = token_ref[0:1, :]
        offset = lax.broadcasted_iota(jnp.int32, owner.shape, 1) % PAGE
        spot = (token_ref[1:2, :] * 32 + token_ref[2:3, :] - 1) * PAGE + offset.astype(jnp.float32)
        request = lax.broadcasted_iota(jnp.int32, (rows, 1), 0) // STEPS
        limit = jnp.zeros((rows, 1), jnp.int32)
        for r in range(rows // STEPS):
            limit = jnp.where(request == r, length_ref[r], limit)
        seen = (owner == request.astype(jnp.float32)) & (spot < limit.astype(jnp.float32))
        bias_ref[...] = jnp.where(seen, 0.0, NEG_FILL)
        row = lax.broadcasted_iota(jnp.int32, new_bias_ref.shape, 0)
        col = lax.broadcasted_iota(jnp.int32, new_bias_ref.shape, 1)
        first = jnp.where((me_ref[0] == 0) & (me_ref[1] == 0), 1, 0)
        seen = (row // STEPS == col // STEPS) & (col <= row) & (col < rows * first)
        new_bias_ref[...] = jnp.where(seen, 0.0, NEG_FILL)
        if peers > 1:
            for d in range(peers):
                query_ref[me_ref[1] ^ d] = query_refs[d][...]

    if peers > 1:
        per_step = query_refs[0].shape[0] // KVH
        query = jnp.concatenate(
            [
                query_ref[n, step * per_step + i].astype(jnp.float32)
                for i in range(per_step)
                for n in range(peers)
            ],
            axis=0,
        ).astype(jnp.bfloat16)
    else:
        query = query_refs[0][0]
    score_ref[:, :tokens] = lax.dot_general(
        query, key_ref[...], NT, preferred_element_type=jnp.float32
    )
    score_ref[:, tokens:] = lax.dot_general(
        query, new_key_ref[...], NT, preferred_element_type=jnp.float32
    )
    together = 1 if rows % 16 == 0 else 2
    span = together * rows
    peaks, totals = [], []
    for c in range(GROUPS // together):
        block = pl.ds(c * span, span)
        old = score_ref[block, :tokens].reshape(together, rows, tokens) * SCALE2 + bias_ref[...]
        new = score_ref[block, tokens:].reshape(together, rows, -1) * SCALE2 + new_bias_ref[...]
        peak = jnp.maximum(
            jnp.max(old, axis=-1, keepdims=True), jnp.max(new, axis=-1, keepdims=True)
        )
        old = jnp.exp2(old - peak)
        new = jnp.exp2(new - peak)
        totals.append(
            (jnp.sum(old, axis=-1, keepdims=True) + jnp.sum(new, axis=-1, keepdims=True)).reshape(
                span, 1
            )
        )
        peaks.append(peak.reshape(span, 1))
        weight_ref[block, :tokens] = old.reshape(span, tokens).astype(jnp.bfloat16)
        weight_ref[block, tokens:] = new.reshape(span, -1).astype(jnp.bfloat16)
    mixed = jnp.dot(
        weight_ref[:, :tokens], value_ref[...], preferred_element_type=jnp.float32
    ) + jnp.dot(weight_ref[:, tokens:], new_value_ref[...], preferred_element_type=jnp.float32)
    peak = jnp.concatenate(peaks, axis=0)
    total = jnp.concatenate(totals, axis=0)
    lane = lax.broadcasted_iota(jnp.int32, (GROUPS * rows, HD), 1)
    stats = jnp.zeros((GROUPS * rows, HD), jnp.float32)
    for i, part in enumerate(split_stats(peak, total)):
        stats = jnp.where(lane == i, part, stats)
    pick = (
        lax.broadcasted_iota(jnp.int32, (STAT, HD), 0)
        == lax.broadcasted_iota(jnp.int32, (STAT, HD), 1)
    ).astype(jnp.bfloat16)
    fill = result_ref.shape[1] - STAT - piece
    for c in range(GROUPS * rows // piece):
        part = slice(c * piece, (c + 1) * piece)
        turned = lax.dot_general(
            pick,
            jnp.concatenate(
                [stats[part], jnp.zeros((HD - piece, HD), jnp.float32)], axis=0
            ).astype(jnp.bfloat16),
            NT,
            preferred_element_type=jnp.float32,
        )
        result_ref[c] = jnp.concatenate(
            [turned, mixed[part], jnp.zeros((fill, HD), jnp.float32)], axis=0
        ).astype(jnp.bfloat16)
    if peers > 1:
        for d, out_ref in enumerate(out_refs):

            @pl.when((step ^ me_ref[1]) == d)
            def _():
                out_ref[...] = result_ref[...]
    else:
        out_refs[0][...] = result_ref[...]


def attend(me, lengths, queries, keyval, pool, token_info, rows, piece):
    tokens = pool.shape[0]
    extra = keyval.shape[0]
    peers = len(queries)
    pieces = GROUPS * rows // piece
    height = STAT + up(piece, 16)
    whole = lambda shape: pl.BlockSpec(shape, lambda k: (0,) * len(shape))
    if peers > 1:
        query_spec = whole(queries[0].shape)
        out_spec = whole((pieces, height, HD))
        out_shape = jax.ShapeDtypeStruct((pieces, height, HD), jnp.bfloat16)
    else:
        query_spec = pl.BlockSpec((1,) + queries[0].shape[1:], lambda k: (k, 0, 0))
        out_spec = pl.BlockSpec((pieces, height, HD), lambda k: (k, 0, 0))
        out_shape = jax.ShapeDtypeStruct((KVH * pieces, height, HD), jnp.bfloat16)
    return pl.pallas_call(
        functools.partial(attend_kernel, rows, piece, peers),
        grid=(KVH,),
        out_shape=[out_shape] * peers,
        in_specs=[pl.BlockSpec(memory_space=pltpu.SMEM)] * 2
        + [query_spec] * peers
        + [
            pl.BlockSpec((tokens, HD), lambda k: (0, k)),
            pl.BlockSpec((tokens, HD), lambda k: (0, KVH + k)),
            pl.BlockSpec((extra, HD), lambda k: (0, k)),
            pl.BlockSpec((extra, HD), lambda k: (0, KVH + k)),
            whole(token_info.shape),
        ],
        out_specs=[out_spec] * peers,
        scratch_shapes=[
            pltpu.VMEM((rows, tokens), jnp.float32),
            pltpu.VMEM((rows, extra), jnp.float32),
            pltpu.VMEM((GROUPS * rows, tokens + extra), jnp.float32),
            pltpu.VMEM((GROUPS * rows, tokens + extra), jnp.bfloat16),
            pltpu.VMEM((peers,) + queries[0].shape, jnp.bfloat16),
            pltpu.VMEM((pieces, height, HD), jnp.bfloat16),
        ],
        compiler_params=pltpu.CompilerParams(vmem_limit_bytes=56 * MIB),
        cost_estimate=pl.CostEstimate(flops=1, bytes_accessed=1, transcendentals=0),
    )(me, lengths, *queries, pool, pool, keyval, keyval, token_info)


def combine_kernel(piece, last, count, *refs):
    if last:
        part_ref, out_ref = refs
        part_refs = [part_ref.at[pl.ds(i, 1)] for i in range(count)]
    else:
        part_refs, out_ref = refs[:count], refs[count]
    groups, height = part_refs[0].shape[:2]
    peaks, totals = [], []
    for i in range(count):
        for j in range(groups):
            stat = part_refs[i][j, :STAT, :].astype(jnp.float32)
            peaks.append(stat[0:1] + stat[1:2] + stat[2:3])
            totals.append(stat[3:4] + stat[4:5])
    peak = jnp.concatenate(peaks, axis=0).reshape(count, groups, HD)
    total = jnp.concatenate(totals, axis=0).reshape(count, groups, HD)
    top = jnp.max(peak, axis=0)
    lead = jnp.exp2(peak - top[None])
    whole = jnp.sum(lead * total, axis=0)
    if last:
        lane = lax.broadcasted_iota(jnp.int32, whole.shape, 1)
        lead = lead / jnp.where(lane < piece, whole, 1.0)[None]
    lead = lead.reshape(count * groups, HD)
    if (count * groups) % HD:
        fill = up(count * groups, HD) - count * groups
        lead = jnp.concatenate([lead, jnp.zeros((fill, HD), jnp.float32)], axis=0)
    lead = jnp.transpose(lead)
    rows = height - STAT
    for j in range(groups):
        result = jnp.zeros((rows, HD), jnp.float32)
        for i in range(count):
            c = i * groups + j
            result = result + lead[:rows, c : c + 1] * part_refs[i][j, STAT:, :].astype(jnp.float32)
        if last:
            for i in range(out_ref.shape[0]):
                out_ref[i] = result[:piece].astype(jnp.bfloat16)
        else:
            stats = split_stats(top[j : j + 1], whole[j : j + 1])
            rest = jnp.zeros((STAT - len(stats), HD), jnp.float32)
            out_ref[j] = jnp.concatenate([*stats, rest, result], axis=0).astype(jnp.bfloat16)


def combine(parts, piece, repeats=0):
    count = parts[0].shape[0] if repeats else len(parts)
    shape = (repeats, piece, HD) if repeats else parts[0].shape
    return pl.pallas_call(
        functools.partial(combine_kernel, piece, repeats > 0, count),
        out_shape=jax.ShapeDtypeStruct(shape, jnp.bfloat16),
        in_specs=[pl.BlockSpec(memory_space=pltpu.VMEM)] * len(parts),
        out_specs=pl.BlockSpec(memory_space=pltpu.VMEM),
        compiler_params=pltpu.CompilerParams(vmem_limit_bytes=8 * MIB),
        cost_estimate=pl.CostEstimate(
            flops=2 * len(parts) * parts[0].size,
            bytes_accessed=len(parts) * parts[0].size * 2,
            transcendentals=0,
        ),
    )(*parts)


def reorder(shape, unit, valid, own, column):
    first, second = (0, 1) if column else (1, 0)
    block = lax.broadcasted_iota(jnp.int32, shape, second) // unit
    place = lax.broadcasted_iota(jnp.int32, shape, second) % unit
    target = (block ^ own) * valid + place
    match = (lax.broadcasted_iota(jnp.int32, shape, first) == target) & (place < valid)
    return match.astype(jnp.bfloat16)


def project_kernel(peers, me_ref, hidden_ref, query_ref, keyval_ref, tag_ref, *refs):
    out_refs, (kept_ref, full_ref) = refs[:peers], refs[peers:]
    kept_ref[...] = tag_ref[...]
    count, local, depth = hidden_ref.shape
    unit = up(local, 8)
    blocks = []
    for i in range(count):
        blocks.append(hidden_ref[i].astype(jnp.float32))
        if unit > local:
            blocks.append(jnp.zeros((unit - local, depth), jnp.float32))
    hidden = jnp.concatenate(blocks, axis=0).astype(jnp.bfloat16)
    order = reorder((count * local, count * unit), unit, local, 0, True)
    hidden = jnp.dot(order, hidden, preferred_element_type=jnp.float32).astype(jnp.bfloat16)
    full_ref[...] = jnp.dot(hidden, query_ref[...], preferred_element_type=jnp.float32)
    keyval = jnp.dot(hidden, keyval_ref[...], preferred_element_type=jnp.float32)
    for d, out_ref in enumerate(out_refs):
        start = pl.multiple_of((me_ref[1] ^ d) * HD, HD)
        out_ref[:, :HD] = full_ref[:, pl.ds(start, HD)]
        out_ref[:, HD:] = keyval


def pack_kernel(peers, *refs):
    own, tag_ref, out_ref = refs[:peers], refs[peers], refs[peers + 1]
    total = (own[0][...] + own[1][...]) + (own[2][...] + own[3][...])
    tags = jnp.concatenate([tag_ref[...], jnp.zeros_like(tag_ref[...])], axis=1)
    packed = jnp.concatenate([total, tags], axis=0).astype(jnp.bfloat16)
    for i in range(out_ref.shape[0]):
        out_ref[i] = packed


def unpack_kernel(rows, me_ref, kept_ref, part_ref, query_ref, keyval_ref, *refs):
    entry_ref, req_ref, idx_ref = refs
    count = part_ref.shape[0]
    line = lax.broadcasted_iota(jnp.int32, (count, HD), 0)
    tags = jnp.zeros((count, HD), jnp.float32)
    fill = jnp.zeros((keyval_ref.shape[0] - rows, HD), jnp.float32)
    for i in range(count):
        part = part_ref[i].astype(jnp.float32)
        query_ref[i] = part[:rows, :HD].astype(jnp.bfloat16)
        block = jnp.concatenate([part[:rows, HD:], fill], axis=0).astype(jnp.bfloat16)
        keyval_ref[:, i * HD : (i + 1) * HD] = block
        mine = jnp.where(line == me_ref[0], part[rows : rows + count, :HD], 0.0)
        tags = tags + jnp.where(line == i, jnp.sum(mine, axis=0, keepdims=True), 0.0)
    capacity = HD // count
    high = lax.broadcasted_iota(jnp.int32, (HD, HD), 0)
    low = lax.broadcasted_iota(jnp.int32, (HD, HD), 1)
    slot = lax.broadcasted_iota(jnp.int32, (count, HD), 1)
    tags = tags.astype(jnp.bfloat16)
    fields = []
    for i in range(3):
        pick = jnp.where(high == i * capacity + low % capacity, 1.0, 0.0).astype(jnp.bfloat16)
        spread_out = jnp.dot(tags, pick, preferred_element_type=jnp.float32)
        spread_out = jnp.where(slot // capacity == line, spread_out, 0.0)
        fields.append(jnp.sum(spread_out, axis=0, keepdims=True))
    req_ref[...] = fields[0].astype(jnp.int32)
    idx_ref[...] = (fields[1] * 32.0 + fields[2] - 1.0).astype(jnp.int32)
    local = entry_ref.shape[1]
    step = lax.broadcasted_iota(jnp.int32, (16, keyval_ref.shape[0]), 0)
    row = lax.broadcasted_iota(jnp.int32, (16, keyval_ref.shape[0]), 1)
    kept = (row == me_ref[0] * local + step) & (step < kept_ref[me_ref[0]])
    kept = jnp.where(kept, 1.0, 0.0).astype(jnp.bfloat16)
    entries = jnp.dot(kept, keyval_ref[...], preferred_element_type=jnp.float32)
    entry_ref[0] = entries[:local].astype(jnp.bfloat16)


def finish_kernel(peers, me_ref, part_ref, weight_ref, *refs):
    count, rows = part_ref.shape[:2]
    local = rows // peers
    unit = up(local, 16)
    whole = jnp.concatenate([part_ref[i] for i in range(count)], axis=1)
    order = reorder((peers * unit, rows), unit, local, me_ref[1], False)
    mixed = jnp.dot(order, whole, preferred_element_type=jnp.float32)
    mixed = jnp.dot(mixed.astype(jnp.bfloat16), weight_ref[...], preferred_element_type=jnp.float32)
    for d, out_ref in enumerate(refs):
        out_ref[...] = mixed[d * unit : d * unit + local]


def in_vmem(kernel, out_shape, me, *args, scratch=()):
    head = [] if me is None else list(me) if isinstance(me, tuple) else [me]
    return pl.pallas_call(
        kernel,
        out_shape=out_shape,
        in_specs=[pl.BlockSpec(memory_space=pltpu.SMEM)] * len(head)
        + [pl.BlockSpec(memory_space=pltpu.VMEM)] * len(args),
        out_specs=jax.tree.map(lambda _: pl.BlockSpec(memory_space=pltpu.VMEM), out_shape),
        scratch_shapes=scratch,
        compiler_params=pltpu.CompilerParams(vmem_limit_bytes=16 * MIB),
        cost_estimate=pl.CostEstimate(
            flops=0, bytes_accessed=sum(2 * arg.size for arg in args), transcendentals=0
        ),
    )(*head, *args)


def group_of(d, wide):
    return d if wide <= 8 else 1 + (d - 1) * 7 // (wide - 1)


def spread(block, axis):
    count = lax.axis_size(axis)
    return lax.all_to_all(
        jnp.broadcast_to(block[None], (count,) + block.shape),
        axis,
        split_axis=0,
        concat_axis=0,
        tiled=True,
    )


def on_device(hidden, w_query, w_keyval, w_out, pool, page_req, page_idx, lengths, moves, accepted):
    wide = lax.axis_size("wide")
    narrow = lax.axis_size("narrow")
    local_rows = hidden.shape[0]
    rows = local_rows * wide
    requests = rows // STEPS
    slots = pool.shape[0]
    capacity = slots // wide
    own_cols = w_query.shape[1] // narrow
    piece = HEADS * rows // (wide * narrow)
    extra = up(rows, HD)
    direct = piece == rows and own_cols == HD and slots == HD
    direct = direct and wide == 8 and narrow == 4 and local_rows == STEPS
    me = lax.axis_index("wide")
    both = jnp.stack([me, lax.axis_index("narrow")])
    exchange = functools.partial(lax.all_to_all, split_axis=0, concat_axis=0, tiled=True)

    def send(block, axis, d):
        return lax.ppermute(block, axis, [(i, i ^ d) for i in range(lax.axis_size(axis))])

    def share(block, axis):
        return [block] + [send(block, axis, d) for d in range(1, lax.axis_size(axis))]

    def deal(blocks, axis):
        return [blocks[0]] + [send(block, axis, d) for d, block in enumerate(blocks) if d]

    gathered = spread(hidden, "wide")

    parts = []
    for d in range(1, wide):
        cuts = [cut * capacity // 16 for cut in CUTS[group_of(d, wide)]]
        parts += [(d, a, b) for a, b in zip(cuts[:-1], cuts[1:]) if b > a]
    moved_pool, tags, token_info, *chunks = order_pages(
        both, moves, page_req, page_idx, pool, wide, parts
    )
    arrived = {}
    flying = {}

    def members(names):
        taken = []
        for group, which in names:
            cut = CUTS[group][which] * capacity // 16
            end = CUTS[group][which + 1] * capacity // 16
            taken += [
                c
                for c, (d, first, last) in enumerate(parts)
                if group_of(d, wide) == group and (first, last) == (cut, end)
            ]
        return taken

    def launch(values, *names):
        taken = members(names)
        values, sent = lax.optimization_barrier((values, [chunks[c] for c in taken]))
        for c, chunk in zip(taken, sent):
            flying[c] = send(chunk, "wide", parts[c][0])
        return values

    def land(values, *names):
        taken = members(names)
        values, got = lax.optimization_barrier((values, [flying[c] for c in taken]))
        arrived.update(zip(taken, got))
        return values

    def beside(step, value, *names):
        return land(step(launch(value, *names)), *names)

    def placed(pages):
        taken = sorted(arrived)
        if not taken:
            return pages
        place = jnp.stack([(me ^ parts[c][0]) * capacity + parts[c][1] for c in taken])
        pages = place_pages(place, [arrived[c] for c in taken], pages)
        arrived.clear()
        return pages

    gathered, tags = lax.optimization_barrier((gathered, tags))
    tokens = pool.reshape(slots * PAGE, -1)
    if direct:
        block = jax.ShapeDtypeStruct((rows, 2 * HD), jnp.float32)
        *partial, tags = in_vmem(
            functools.partial(project_kernel, narrow),
            [block] * narrow + [jax.ShapeDtypeStruct(tags.shape, tags.dtype)],
            both,
            gathered,
            w_query,
            w_keyval,
            tags,
            scratch=[pltpu.VMEM((rows, narrow * HD), jnp.float32)],
        )
        partial = beside(lambda value: deal(value, "narrow"), partial, (6, 0))
        packed = in_vmem(
            functools.partial(pack_kernel, narrow),
            jax.ShapeDtypeStruct((wide, rows + wide, 2 * HD), jnp.bfloat16),
            None,
            *partial,
            tags,
        )
        received = beside(lambda value: exchange(value, "wide"), packed, (1, 0), (6, 1))
        received = launch(received, (7, 0), (4, 0))
        queries, keyval, new_entries, moved_req, moved_idx = in_vmem(
            functools.partial(unpack_kernel, rows),
            [
                jax.ShapeDtypeStruct((wide, rows, HD), jnp.bfloat16),
                jax.ShapeDtypeStruct((extra, wide * HD), jnp.bfloat16),
                jax.ShapeDtypeStruct((1, local_rows, wide * HD), jnp.bfloat16),
                jax.ShapeDtypeStruct((1, slots), jnp.int32),
                jax.ShapeDtypeStruct((1, slots), jnp.int32),
            ],
            (both, accepted),
            received,
        )
        moved_req, moved_idx = moved_req.reshape(slots), moved_idx.reshape(slots)
        queries = share(queries, "narrow")
    else:
        gathered = gathered.reshape(rows, -1)
        query_part = jnp.dot(gathered, w_query, preferred_element_type=jnp.float32)
        keyval_part = jnp.dot(gathered, w_keyval, preferred_element_type=jnp.float32)
        query_part = jnp.transpose(query_part.reshape(rows, narrow, own_cols), (1, 0, 2))
        partial = jnp.concatenate(
            [query_part, jnp.broadcast_to(keyval_part[None], (narrow,) + keyval_part.shape)], axis=2
        )
        partial = beside(lambda value: exchange(value, "narrow"), partial, (6, 0))
        projected = jnp.sum(partial, axis=0).astype(jnp.bfloat16)
        tags = tags[:, : 3 * capacity].astype(jnp.bfloat16)[:, None]
        tags = jnp.pad(tags, ((0, 0), (0, 7), (0, projected.shape[1] - tags.shape[2])))
        packed = jnp.broadcast_to(projected[None], (wide,) + projected.shape)
        packed = jnp.concatenate([packed, tags], axis=1)
        received = beside(lambda value: exchange(value, "wide"), packed, (1, 0), (6, 1))
        received = launch(received, (7, 0), (4, 0))
        tags_in = received[:, rows]
        queries = received[:, :rows, :own_cols]
        queries = spread(queries, "narrow")
        queries = jnp.transpose(queries, (2, 1, 0, 3)).reshape(rows, HEADS, HD)
        queries = [jnp.transpose(queries, (1, 0, 2)).reshape(KVH, GROUPS * rows, HD)]
        keyval = jnp.transpose(received[:, :rows, own_cols:], (1, 0, 2)).reshape(rows, -1)
        keyval = jnp.pad(keyval, ((0, extra - rows), (0, 0)))
        tags_in = tags_in.astype(jnp.int32)
        moved_req = tags_in[:, :capacity].reshape(slots)
        moved_idx = tags_in[:, capacity : 2 * capacity] * 32
        moved_idx = (moved_idx + tags_in[:, 2 * capacity : 3 * capacity] - 1).reshape(slots)
        local_req = local_rows // STEPS
        fresh = lax.dynamic_slice_in_dim(keyval, me * local_rows, local_rows, 0)
        fresh = fresh.reshape(local_req, STEPS, -1)
        kept = lax.dynamic_slice_in_dim(accepted, me * local_req, local_req, 0)
        step_ids = jnp.arange(STEPS)[None, :, None]
        new_entries = jnp.where(
            step_ids < kept[:, None, None], fresh, jnp.zeros((), jnp.bfloat16)
        )

    queries, moved_pool = lax.optimization_barrier((queries, placed(moved_pool)))
    mixed = attend(both, lengths, queries, keyval, tokens, token_info, rows, piece)
    if direct:
        mixed = land(deal(mixed, "narrow"), (7, 0), (4, 0))
    else:
        mixed = land(exchange(mixed[0], "narrow"), (7, 0), (4, 0))
        mixed = mixed.reshape((narrow, wide) + mixed.shape[1:])
        mixed = [mixed[i] for i in range(narrow)]
    mixed = combine(mixed, piece)
    mixed, pages = lax.optimization_barrier((mixed, moved_pool))
    pages = placed(pages)
    mixed = beside(lambda value: exchange(value, "wide"), mixed, (3, 0), (4, 1))
    mixed, moved_pool = lax.optimization_barrier((mixed, pages))
    attn = combine([mixed], piece, wide)
    attn, pages = lax.optimization_barrier((attn, moved_pool))
    pages = placed(pages)
    attn = beside(lambda value: exchange(value, "wide"), attn, (2, 0), (5, 0))
    attn, moved_pool = lax.optimization_barrier((attn, pages))
    if direct:
        sums = in_vmem(
            functools.partial(finish_kernel, narrow),
            [jax.ShapeDtypeStruct((rows // narrow, w_out.shape[1]), jnp.float32)] * narrow,
            both,
            attn,
            w_out,
        )
        sums, pages = lax.optimization_barrier((sums, moved_pool))
        pages = placed(pages)
        sums = beside(lambda value: deal(value, "narrow"), sums, (3, 1), (5, 1))
        attended = ((sums[0] + sums[1]) + (sums[2] + sums[3])).astype(jnp.bfloat16)
    else:
        attn = jnp.transpose(attn.reshape(-1, rows, HD), (1, 0, 2)).reshape(rows, -1)
        sums = jnp.dot(attn, w_out, preferred_element_type=jnp.float32)
        sums = sums.reshape(narrow, rows // narrow, -1)
        pages = placed(moved_pool)
        sums = beside(lambda value: exchange(value, "narrow"), sums, (3, 1), (5, 1))
        attended = jnp.sum(sums, axis=0).astype(jnp.bfloat16)
    attended, pages = lax.optimization_barrier((attended, pages))
    moved_pool = placed(pages)
    return (attended, new_entries, moved_pool, moved_req, moved_idx)


def solution(mesh):
    in_specs = (
        P("wide", "narrow"),
        P("narrow", "wide"),
        P("narrow", "wide"),
        P("narrow", "wide"),
        P(("wide", "narrow"), None, None),
        P(("wide", "narrow")),
        P(("wide", "narrow")),
        P(),
        P(("wide", "narrow"), None),
        P(),
    )
    out_specs = (
        P("narrow", "wide"),
        P("wide", None, None),
        P(("wide", "narrow"), None, None),
        P(("wide", "narrow")),
        P(("wide", "narrow")),
    )
    return jax.shard_map(
        on_device, mesh=mesh, in_specs=in_specs, out_specs=out_specs, check_vma=False
    )
```

```python
import functools
import math

import jax
import jax.numpy as jnp
from jax import lax
from jax.experimental import pallas as pl
from jax.experimental.pallas import tpu as pltpu
from jax.sharding import PartitionSpec as P

HEADS = 32
KVH = 4
HD = 128
STEPS = 5
PAGE = 16
GROUPS = HEADS // KVH
NEG_FILL = -1e30
SCALE2 = math.log2(math.e) / math.sqrt(HD)
STAT = 16
MIB = 1024 * 1024
CUTS = {1: (0, 16), 2: (0, 16), 3: (0, 16), 4: (0, 16), 5: (0, 4, 16), 6: (0, 4, 16), 7: (0, 12, 16)}
NT = (((1,), (1,)), ((), ()))


def up(value, unit):
    return -(-value // unit) * unit


def column(row):
    return jnp.transpose(jnp.broadcast_to(row, (row.shape[1], row.shape[1])))


def order_kernel(
    wide, parts, me_ref, dest_ref, req_ref, idx_ref, pool_ref, out_ref, tag_ref, token_ref, *refs
):
    chunk_refs, refs = refs[: len(parts)], refs[len(parts) :]
    pages_ref, line_ref, source_ref, in_sem, out_sem, line_sem = refs
    slots = pool_ref.shape[0]
    capacity = slots // wide
    shape = (slots, slots)
    high = lax.broadcasted_iota(jnp.int32, shape, 0)
    low = lax.broadcasted_iota(jnp.int32, shape, 1)
    dest = dest_ref[...]
    same = column(dest.astype(jnp.float32)) == dest.astype(jnp.float32)
    rank = jnp.sum(jnp.where(same & (high < low), 1.0, 0.0), axis=0, keepdims=True)
    moved_to = ((dest ^ me_ref[0]) * capacity).astype(jnp.float32) + rank
    match = column(moved_to) == low.astype(jnp.float32)
    source = jnp.sum(jnp.where(match, high.astype(jnp.float32), 0.0), axis=0, keepdims=True)
    line_ref[...] = source.astype(jnp.int32)
    copy = pltpu.make_async_copy(line_ref, source_ref, line_sem)
    copy.start()
    copy.wait()

    blocks = [(0, capacity, out_ref.at[pl.ds(me_ref[0] * capacity, capacity)])]
    for (d, first, last), chunk in zip(parts, chunk_refs):
        blocks.append((d * capacity + first, last - first, chunk))
    for c, (first, count, _) in enumerate(blocks):

        def start(j, carry, c=c):
            page = source_ref[0, j]
            pltpu.make_async_copy(pool_ref.at[page], pages_ref.at[j], in_sem.at[c]).start()
            return carry

        lax.fori_loop(first, first + count, start, 0)

    shifted = idx_ref[...] + 1
    fields = (req_ref[...], shifted // 32, shifted % 32)
    rank_col = column(rank)
    lane = low.astype(jnp.float32)
    spread_out = jnp.zeros(shape, jnp.float32)
    for i, field in enumerate(fields):
        picked = lane == rank_col + float(i * capacity)
        spread_out = spread_out + jnp.where(picked, column(field.astype(jnp.float32)), 0.0)
    line = lax.broadcasted_iota(jnp.int32, (wide, slots), 0)
    chosen = jnp.where(line == dest, 1.0, 0.0).astype(jnp.bfloat16)
    tag_ref[...] = jnp.dot(
        chosen, spread_out.astype(jnp.bfloat16), preferred_element_type=jnp.float32
    )

    tokens = slots * PAGE
    page = lax.broadcasted_iota(jnp.int32, (slots, tokens), 0)
    token = lax.broadcasted_iota(jnp.int32, (slots, tokens), 1)
    widen = jnp.where(page == token // PAGE, 1.0, 0.0).astype(jnp.bfloat16)
    row = lax.broadcasted_iota(jnp.int32, (8, slots), 0)
    stacked = jnp.zeros((8, slots), jnp.float32)
    for i, field in enumerate(fields):
        stacked = jnp.where(row == i, field.astype(jnp.float32), stacked)
    token_ref[...] = jnp.dot(
        stacked.astype(jnp.bfloat16), widen, preferred_element_type=jnp.float32
    )

    copies = []
    for c, (first, count, target) in enumerate(blocks):
        held = pages_ref.at[pl.ds(first, count)]
        pltpu.make_async_copy(pool_ref.at[pl.ds(0, count)], held, in_sem.at[c]).wait()
        copies.append(pltpu.make_async_copy(held, target, out_sem.at[c]))
        copies[-1].start()
    for copy in copies:
        copy.wait()


def order_pages(me, dest, page_req, page_idx, pool, wide, parts):
    slots = pool.shape[0]
    part = lambda count: jax.ShapeDtypeStruct((count,) + pool.shape[1:], pool.dtype)
    out_shape = [part(slots), jax.ShapeDtypeStruct((wide, slots), jnp.float32)]
    out_shape += [jax.ShapeDtypeStruct((8, slots * PAGE), jnp.float32)]
    out_shape += [part(last - first) for _, first, last in parts]
    vmem = pl.BlockSpec(memory_space=pltpu.VMEM)
    hbm = pl.BlockSpec(memory_space=pltpu.HBM)
    return pl.pallas_call(
        functools.partial(order_kernel, wide, parts),
        out_shape=out_shape,
        in_specs=[pl.BlockSpec(memory_space=pltpu.SMEM), vmem, vmem, vmem, hbm],
        out_specs=[hbm, vmem, vmem] + [hbm] * len(parts),
        scratch_shapes=[
            pltpu.VMEM(pool.shape, pool.dtype),
            pltpu.VMEM((1, slots), jnp.int32),
            pltpu.SMEM((1, slots), jnp.int32),
            pltpu.SemaphoreType.DMA((1 + len(parts),)),
            pltpu.SemaphoreType.DMA((1 + len(parts),)),
            pltpu.SemaphoreType.DMA,
        ],
        compiler_params=pltpu.CompilerParams(vmem_limit_bytes=56 * MIB),
        cost_estimate=pl.CostEstimate(
            flops=0, bytes_accessed=2 * pool.size * 2, transcendentals=0
        ),
    )(me, dest.reshape(1, -1), page_req.reshape(1, -1), page_idx.reshape(1, -1), pool)


def place_kernel(place_ref, *refs):
    in_refs, (out_ref, sem) = refs[:-3], refs[-2:]
    copies = []
    for i, chunk in enumerate(in_refs):
        depth = chunk.shape[0]
        copies.append(
            pltpu.make_async_copy(
                chunk, out_ref.at[pl.ds(place_ref[i], depth)], sem.at[i]
            )
        )
    for copy in copies:
        copy.start()
    for copy in copies:
        copy.wait()


def place_pages(place, chunks, pages):
    count = len(chunks)
    return pl.pallas_call(
        place_kernel,
        out_shape=jax.ShapeDtypeStruct(pages.shape, pages.dtype),
        in_specs=[pl.BlockSpec(memory_space=pltpu.SMEM)]
        + [pl.BlockSpec(memory_space=pltpu.VMEM)] * count
        + [pl.BlockSpec(memory_space=pl.ANY)],
        out_specs=pl.BlockSpec(memory_space=pl.ANY),
        scratch_shapes=[pltpu.SemaphoreType.DMA((count,))],
        input_output_aliases={count + 1: 0},
        compiler_params=pltpu.CompilerParams(vmem_limit_bytes=2 * count * chunks[0].size + 2 * MIB),
        cost_estimate=pl.CostEstimate(
            flops=0, bytes_accessed=4 * count * chunks[0].size, transcendentals=0
        ),
    )(place, *chunks, pages)


def cut(value):
    return value.astype(jnp.bfloat16).astype(jnp.float32)


def split_stats(peak, total):
    high = cut(peak)
    mid = cut(peak - high)
    return high, mid, peak - high - mid, cut(total), total - cut(total)


def attend_kernel(rows, piece, peers, me_ref, length_ref, *refs):
    query_refs, refs = refs[:peers], refs[peers:]
    key_ref, value_ref, new_key_ref, new_value_ref, token_ref = refs[:5]
    out_refs = refs[5 : 5 + peers]
    bias_ref, new_bias_ref, score_ref, weight_ref, query_ref, result_ref = refs[5 + peers :]
    tokens = key_ref.shape[0]
    step = pl.program_id(0)

    @pl.when(step == 0)
    def _():
        owner = token_ref[0:1, :]
        offset = lax.broadcasted_iota(jnp.int32, owner.shape, 1) % PAGE
        spot = (token_ref[1:2, :] * 32 + token_ref[2:3, :] - 1) * PAGE + offset.astype(jnp.float32)
        request = lax.broadcasted_iota(jnp.int32, (rows, 1), 0) // STEPS
        limit = jnp.zeros((rows, 1), jnp.int32)
        for r in range(rows // STEPS):
            limit = jnp.where(request == r, length_ref[r], limit)
        seen = (owner == request.astype(jnp.float32)) & (spot < limit.astype(jnp.float32))
        bias_ref[...] = jnp.where(seen, 0.0, NEG_FILL)
        row = lax.broadcasted_iota(jnp.int32, new_bias_ref.shape, 0)
        col = lax.broadcasted_iota(jnp.int32, new_bias_ref.shape, 1)
        first = jnp.where((me_ref[0] == 0) & (me_ref[1] == 0), 1, 0)
        seen = (row // STEPS == col // STEPS) & (col <= row) & (col < rows * first)
        new_bias_ref[...] = jnp.where(seen, 0.0, NEG_FILL)
        if peers > 1:
            for d in range(peers):
                query_ref[me_ref[1] ^ d] = query_refs[d][...]

    if peers > 1:
        per_step = query_refs[0].shape[0] // KVH
        query = jnp.concatenate(
            [
                query_ref[n, step * per_step + i].astype(jnp.float32)
                for i in range(per_step)
                for n in range(peers)
            ],
            axis=0,
        ).astype(jnp.bfloat16)
    else:
        query = query_refs[0][0]
    score_ref[:, :tokens] = lax.dot_general(
        query, key_ref[...], NT, preferred_element_type=jnp.float32
    )
    score_ref[:, tokens:] = lax.dot_general(
        query, new_key_ref[...], NT, preferred_element_type=jnp.float32
    )
    together = 1 if rows % 16 == 0 else 2
    span = together * rows
    peaks, totals = [], []
    for c in range(GROUPS // together):
        block = pl.ds(c * span, span)
        old = score_ref[block, :tokens].reshape(together, rows, tokens) * SCALE2 + bias_ref[...]
        new = score_ref[block, tokens:].reshape(together, rows, -1) * SCALE2 + new_bias_ref[...]
        peak = jnp.maximum(
            jnp.max(old, axis=-1, keepdims=True), jnp.max(new, axis=-1, keepdims=True)
        )
        old = jnp.exp2(old - peak)
        new = jnp.exp2(new - peak)
        totals.append(
            (jnp.sum(old, axis=-1, keepdims=True) + jnp.sum(new, axis=-1, keepdims=True)).reshape(
                span, 1
            )
        )
        peaks.append(peak.reshape(span, 1))
        weight_ref[block, :tokens] = old.reshape(span, tokens).astype(jnp.bfloat16)
        weight_ref[block, tokens:] = new.reshape(span, -1).astype(jnp.bfloat16)
    mixed = jnp.dot(
        weight_ref[:, :tokens], value_ref[...], preferred_element_type=jnp.float32
    ) + jnp.dot(weight_ref[:, tokens:], new_value_ref[...], preferred_element_type=jnp.float32)
    peak = jnp.concatenate(peaks, axis=0)
    total = jnp.concatenate(totals, axis=0)
    lane = lax.broadcasted_iota(jnp.int32, (GROUPS * rows, HD), 1)
    stats = jnp.zeros((GROUPS * rows, HD), jnp.float32)
    for i, part in enumerate(split_stats(peak, total)):
        stats = jnp.where(lane == i, part, stats)
    pick = (
        lax.broadcasted_iota(jnp.int32, (STAT, HD), 0)
        == lax.broadcasted_iota(jnp.int32, (STAT, HD), 1)
    ).astype(jnp.bfloat16)
    fill = result_ref.shape[1] - STAT - piece
    for c in range(GROUPS * rows // piece):
        part = slice(c * piece, (c + 1) * piece)
        turned = lax.dot_general(
            pick,
            jnp.concatenate(
                [stats[part], jnp.zeros((HD - piece, HD), jnp.float32)], axis=0
            ).astype(jnp.bfloat16),
            NT,
            preferred_element_type=jnp.float32,
        )
        result_ref[c] = jnp.concatenate(
            [turned, mixed[part], jnp.zeros((fill, HD), jnp.float32)], axis=0
        ).astype(jnp.bfloat16)
    if peers > 1:
        for d, out_ref in enumerate(out_refs):

            @pl.when((step ^ me_ref[1]) == d)
            def _():
                out_ref[...] = result_ref[...]
    else:
        out_refs[0][...] = result_ref[...]


def attend(me, lengths, queries, keyval, pool, token_info, rows, piece):
    tokens = pool.shape[0]
    extra = keyval.shape[0]
    peers = len(queries)
    pieces = GROUPS * rows // piece
    height = STAT + up(piece, 16)
    whole = lambda shape: pl.BlockSpec(shape, lambda k: (0,) * len(shape))
    if peers > 1:
        query_spec = whole(queries[0].shape)
        out_spec = whole((pieces, height, HD))
        out_shape = jax.ShapeDtypeStruct((pieces, height, HD), jnp.bfloat16)
    else:
        query_spec = pl.BlockSpec((1,) + queries[0].shape[1:], lambda k: (k, 0, 0))
        out_spec = pl.BlockSpec((pieces, height, HD), lambda k: (k, 0, 0))
        out_shape = jax.ShapeDtypeStruct((KVH * pieces, height, HD), jnp.bfloat16)
    return pl.pallas_call(
        functools.partial(attend_kernel, rows, piece, peers),
        grid=(KVH,),
        out_shape=[out_shape] * peers,
        in_specs=[pl.BlockSpec(memory_space=pltpu.SMEM)] * 2
        + [query_spec] * peers
        + [
            pl.BlockSpec((tokens, HD), lambda k: (0, k)),
            pl.BlockSpec((tokens, HD), lambda k: (0, KVH + k)),
            pl.BlockSpec((extra, HD), lambda k: (0, k)),
            pl.BlockSpec((extra, HD), lambda k: (0, KVH + k)),
            whole(token_info.shape),
        ],
        out_specs=[out_spec] * peers,
        scratch_shapes=[
            pltpu.VMEM((rows, tokens), jnp.float32),
            pltpu.VMEM((rows, extra), jnp.float32),
            pltpu.VMEM((GROUPS * rows, tokens + extra), jnp.float32),
            pltpu.VMEM((GROUPS * rows, tokens + extra), jnp.bfloat16),
            pltpu.VMEM((peers,) + queries[0].shape, jnp.bfloat16),
            pltpu.VMEM((pieces, height, HD), jnp.bfloat16),
        ],
        compiler_params=pltpu.CompilerParams(vmem_limit_bytes=56 * MIB),
        cost_estimate=pl.CostEstimate(flops=1, bytes_accessed=1, transcendentals=0),
    )(me, lengths, *queries, pool, pool, keyval, keyval, token_info)


def combine_kernel(piece, last, count, *refs):
    if last:
        part_ref, out_ref = refs
        part_refs = [part_ref.at[pl.ds(i, 1)] for i in range(count)]
    else:
        part_refs, out_ref = refs[:count], refs[count]
    groups, height = part_refs[0].shape[:2]
    peaks, totals = [], []
    for i in range(count):
        for j in range(groups):
            stat = part_refs[i][j, :STAT, :].astype(jnp.float32)
            peaks.append(stat[0:1] + stat[1:2] + stat[2:3])
            totals.append(stat[3:4] + stat[4:5])
    peak = jnp.concatenate(peaks, axis=0).reshape(count, groups, HD)
    total = jnp.concatenate(totals, axis=0).reshape(count, groups, HD)
    top = jnp.max(peak, axis=0)
    lead = jnp.exp2(peak - top[None])
    whole = jnp.sum(lead * total, axis=0)
    if last:
        lane = lax.broadcasted_iota(jnp.int32, whole.shape, 1)
        lead = lead / jnp.where(lane < piece, whole, 1.0)[None]
    lead = lead.reshape(count * groups, HD)
    if (count * groups) % HD:
        fill = up(count * groups, HD) - count * groups
        lead = jnp.concatenate([lead, jnp.zeros((fill, HD), jnp.float32)], axis=0)
    lead = jnp.transpose(lead)
    rows = height - STAT
    for j in range(groups):
        result = jnp.zeros((rows, HD), jnp.float32)
        for i in range(count):
            c = i * groups + j
            result = result + lead[:rows, c : c + 1] * part_refs[i][j, STAT:, :].astype(jnp.float32)
        if last:
            for i in range(out_ref.shape[0]):
                out_ref[i] = result[:piece].astype(jnp.bfloat16)
        else:
            stats = split_stats(top[j : j + 1], whole[j : j + 1])
            rest = jnp.zeros((STAT - len(stats), HD), jnp.float32)
            out_ref[j] = jnp.concatenate([*stats, rest, result], axis=0).astype(jnp.bfloat16)


def combine(parts, piece, repeats=0):
    count = parts[0].shape[0] if repeats else len(parts)
    shape = (repeats, piece, HD) if repeats else parts[0].shape
    return pl.pallas_call(
        functools.partial(combine_kernel, piece, repeats > 0, count),
        out_shape=jax.ShapeDtypeStruct(shape, jnp.bfloat16),
        in_specs=[pl.BlockSpec(memory_space=pltpu.VMEM)] * len(parts),
        out_specs=pl.BlockSpec(memory_space=pltpu.VMEM),
        compiler_params=pltpu.CompilerParams(vmem_limit_bytes=8 * MIB),
        cost_estimate=pl.CostEstimate(
            flops=2 * len(parts) * parts[0].size,
            bytes_accessed=len(parts) * parts[0].size * 2,
            transcendentals=0,
        ),
    )(*parts)


def reorder(shape, unit, valid, own, column):
    first, second = (0, 1) if column else (1, 0)
    block = lax.broadcasted_iota(jnp.int32, shape, second) // unit
    place = lax.broadcasted_iota(jnp.int32, shape, second) % unit
    target = (block ^ own) * valid + place
    match = (lax.broadcasted_iota(jnp.int32, shape, first) == target) & (place < valid)
    return match.astype(jnp.bfloat16)


def project_kernel(peers, me_ref, hidden_ref, query_ref, keyval_ref, tag_ref, *refs):
    out_refs, (kept_ref, full_ref) = refs[:peers], refs[peers:]
    kept_ref[...] = tag_ref[...]
    count, local, depth = hidden_ref.shape
    unit = up(local, 8)
    blocks = []
    for i in range(count):
        blocks.append(hidden_ref[i].astype(jnp.float32))
        if unit > local:
            blocks.append(jnp.zeros((unit - local, depth), jnp.float32))
    hidden = jnp.concatenate(blocks, axis=0).astype(jnp.bfloat16)
    order = reorder((count * local, count * unit), unit, local, 0, True)
    hidden = jnp.dot(order, hidden, preferred_element_type=jnp.float32).astype(jnp.bfloat16)
    full_ref[...] = jnp.dot(hidden, query_ref[...], preferred_element_type=jnp.float32)
    keyval = jnp.dot(hidden, keyval_ref[...], preferred_element_type=jnp.float32)
    for d, out_ref in enumerate(out_refs):
        start = pl.multiple_of((me_ref[1] ^ d) * HD, HD)
        out_ref[:, :HD] = full_ref[:, pl.ds(start, HD)]
        out_ref[:, HD:] = keyval


def pack_kernel(peers, *refs):
    own, tag_ref, out_ref = refs[:peers], refs[peers], refs[peers + 1]
    total = (own[0][...] + own[1][...]) + (own[2][...] + own[3][...])
    tags = jnp.concatenate([tag_ref[...], jnp.zeros_like(tag_ref[...])], axis=1)
    packed = jnp.concatenate([total, tags], axis=0).astype(jnp.bfloat16)
    for i in range(out_ref.shape[0]):
        out_ref[i] = packed


def unpack_kernel(rows, me_ref, kept_ref, part_ref, query_ref, keyval_ref, *refs):
    entry_ref, req_ref, idx_ref = refs
    count = part_ref.shape[0]
    line = lax.broadcasted_iota(jnp.int32, (count, HD), 0)
    tags = jnp.zeros((count, HD), jnp.float32)
    fill = jnp.zeros((keyval_ref.shape[0] - rows, HD), jnp.float32)
    for i in range(count):
        part = part_ref[i].astype(jnp.float32)
        query_ref[i] = part[:rows, :HD].astype(jnp.bfloat16)
        block = jnp.concatenate([part[:rows, HD:], fill], axis=0).astype(jnp.bfloat16)
        keyval_ref[:, i * HD : (i + 1) * HD] = block
        mine = jnp.where(line == me_ref[0], part[rows : rows + count, :HD], 0.0)
        tags = tags + jnp.where(line == i, jnp.sum(mine, axis=0, keepdims=True), 0.0)
    capacity = HD // count
    high = lax.broadcasted_iota(jnp.int32, (HD, HD), 0)
    low = lax.broadcasted_iota(jnp.int32, (HD, HD), 1)
    slot = lax.broadcasted_iota(jnp.int32, (count, HD), 1)
    tags = tags.astype(jnp.bfloat16)
    fields = []
    for i in range(3):
        pick = jnp.where(high == i * capacity + low % capacity, 1.0, 0.0).astype(jnp.bfloat16)
        spread_out = jnp.dot(tags, pick, preferred_element_type=jnp.float32)
        spread_out = jnp.where(slot // capacity == line, spread_out, 0.0)
        fields.append(jnp.sum(spread_out, axis=0, keepdims=True))
    req_ref[...] = fields[0].astype(jnp.int32)
    idx_ref[...] = (fields[1] * 32.0 + fields[2] - 1.0).astype(jnp.int32)
    local = entry_ref.shape[1]
    step = lax.broadcasted_iota(jnp.int32, (16, keyval_ref.shape[0]), 0)
    row = lax.broadcasted_iota(jnp.int32, (16, keyval_ref.shape[0]), 1)
    kept = (row == me_ref[0] * local + step) & (step < kept_ref[me_ref[0]])
    kept = jnp.where(kept, 1.0, 0.0).astype(jnp.bfloat16)
    entries = jnp.dot(kept, keyval_ref[...], preferred_element_type=jnp.float32)
    entry_ref[0] = entries[:local].astype(jnp.bfloat16)


def finish_kernel(peers, me_ref, part_ref, weight_ref, *refs):
    count, rows = part_ref.shape[:2]
    local = rows // peers
    unit = up(local, 16)
    whole = jnp.concatenate([part_ref[i] for i in range(count)], axis=1)
    order = reorder((peers * unit, rows), unit, local, me_ref[1], False)
    mixed = jnp.dot(order, whole, preferred_element_type=jnp.float32)
    mixed = jnp.dot(mixed.astype(jnp.bfloat16), weight_ref[...], preferred_element_type=jnp.float32)
    for d, out_ref in enumerate(refs):
        out_ref[...] = mixed[d * unit : d * unit + local]


def in_vmem(kernel, out_shape, me, *args, scratch=()):
    head = [] if me is None else list(me) if isinstance(me, tuple) else [me]
    return pl.pallas_call(
        kernel,
        out_shape=out_shape,
        in_specs=[pl.BlockSpec(memory_space=pltpu.SMEM)] * len(head)
        + [pl.BlockSpec(memory_space=pltpu.VMEM)] * len(args),
        out_specs=jax.tree.map(lambda _: pl.BlockSpec(memory_space=pltpu.VMEM), out_shape),
        scratch_shapes=scratch,
        compiler_params=pltpu.CompilerParams(vmem_limit_bytes=16 * MIB),
        cost_estimate=pl.CostEstimate(
            flops=0, bytes_accessed=sum(2 * arg.size for arg in args), transcendentals=0
        ),
    )(*head, *args)


def group_of(d, wide):
    return d if wide <= 8 else 1 + (d - 1) * 7 // (wide - 1)


def spread(block, axis):
    count = lax.axis_size(axis)
    return lax.all_to_all(
        jnp.broadcast_to(block[None], (count,) + block.shape),
        axis,
        split_axis=0,
        concat_axis=0,
        tiled=True,
    )


def on_device(hidden, w_query, w_keyval, w_out, pool, page_req, page_idx, lengths, moves, accepted):
    wide = lax.axis_size("wide")
    narrow = lax.axis_size("narrow")
    local_rows = hidden.shape[0]
    rows = local_rows * wide
    requests = rows // STEPS
    slots = pool.shape[0]
    capacity = slots // wide
    own_cols = w_query.shape[1] // narrow
    piece = HEADS * rows // (wide * narrow)
    extra = up(rows, HD)
    direct = piece == rows and own_cols == HD and slots == HD
    direct = direct and wide == 8 and narrow == 4 and local_rows == STEPS
    me = lax.axis_index("wide")
    both = jnp.stack([me, lax.axis_index("narrow")])
    exchange = functools.partial(lax.all_to_all, split_axis=0, concat_axis=0, tiled=True)

    def send(block, axis, d):
        return lax.ppermute(block, axis, [(i, i ^ d) for i in range(lax.axis_size(axis))])

    def share(block, axis):
        return [block] + [send(block, axis, d) for d in range(1, lax.axis_size(axis))]

    def deal(blocks, axis):
        return [blocks[0]] + [send(block, axis, d) for d, block in enumerate(blocks) if d]

    gathered = spread(hidden, "wide")

    parts = []
    for d in range(1, wide):
        cuts = [cut * capacity // 16 for cut in CUTS[group_of(d, wide)]]
        parts += [(d, a, b) for a, b in zip(cuts[:-1], cuts[1:]) if b > a]
    moved_pool, tags, token_info, *chunks = order_pages(
        both, moves, page_req, page_idx, pool, wide, parts
    )
    arrived = {}
    flying = {}

    def members(names):
        taken = []
        for group, which in names:
            cut = CUTS[group][which] * capacity // 16
            end = CUTS[group][which + 1] * capacity // 16
            taken += [
                c
                for c, (d, first, last) in enumerate(parts)
                if group_of(d, wide) == group and (first, last) == (cut, end)
            ]
        return taken

    def launch(values, *names):
        taken = members(names)
        values, sent = lax.optimization_barrier((values, [chunks[c] for c in taken]))
        for c, chunk in zip(taken, sent):
            flying[c] = send(chunk, "wide", parts[c][0])
        return values

    def land(values, *names):
        taken = members(names)
        values, got = lax.optimization_barrier((values, [flying[c] for c in taken]))
        arrived.update(zip(taken, got))
        return values

    def beside(step, value, *names):
        return land(step(launch(value, *names)), *names)

    def placed(pages):
        taken = sorted(arrived)
        if not taken:
            return pages
        place = jnp.stack([(me ^ parts[c][0]) * capacity + parts[c][1] for c in taken])
        pages = place_pages(place, [arrived[c] for c in taken], pages)
        arrived.clear()
        return pages

    gathered, tags = lax.optimization_barrier((gathered, tags))
    tokens = pool.reshape(slots * PAGE, -1)
    if direct:
        block = jax.ShapeDtypeStruct((rows, 2 * HD), jnp.float32)
        *partial, tags = in_vmem(
            functools.partial(project_kernel, narrow),
            [block] * narrow + [jax.ShapeDtypeStruct(tags.shape, tags.dtype)],
            both,
            gathered,
            w_query,
            w_keyval,
            tags,
            scratch=[pltpu.VMEM((rows, narrow * HD), jnp.float32)],
        )
        partial = beside(lambda value: deal(value, "narrow"), partial, (6, 0))
        packed = in_vmem(
            functools.partial(pack_kernel, narrow),
            jax.ShapeDtypeStruct((wide, rows + wide, 2 * HD), jnp.bfloat16),
            None,
            *partial,
            tags,
        )
        received = beside(lambda value: exchange(value, "wide"), packed, (3, 0), (6, 1))
        received = launch(received, (4, 0), (5, 0))
        queries, keyval, new_entries, moved_req, moved_idx = in_vmem(
            functools.partial(unpack_kernel, rows),
            [
                jax.ShapeDtypeStruct((wide, rows, HD), jnp.bfloat16),
                jax.ShapeDtypeStruct((extra, wide * HD), jnp.bfloat16),
                jax.ShapeDtypeStruct((1, local_rows, wide * HD), jnp.bfloat16),
                jax.ShapeDtypeStruct((1, slots), jnp.int32),
                jax.ShapeDtypeStruct((1, slots), jnp.int32),
            ],
            (both, accepted),
            received,
        )
        moved_req, moved_idx = moved_req.reshape(slots), moved_idx.reshape(slots)
        queries = share(queries, "narrow")
    else:
        gathered = gathered.reshape(rows, -1)
        query_part = jnp.dot(gathered, w_query, preferred_element_type=jnp.float32)
        keyval_part = jnp.dot(gathered, w_keyval, preferred_element_type=jnp.float32)
        query_part = jnp.transpose(query_part.reshape(rows, narrow, own_cols), (1, 0, 2))
        partial = jnp.concatenate(
            [query_part, jnp.broadcast_to(keyval_part[None], (narrow,) + keyval_part.shape)], axis=2
        )
        partial = beside(lambda value: exchange(value, "narrow"), partial, (6, 0))
        projected = jnp.sum(partial, axis=0).astype(jnp.bfloat16)
        tags = tags[:, : 3 * capacity].astype(jnp.bfloat16)[:, None]
        tags = jnp.pad(tags, ((0, 0), (0, 7), (0, projected.shape[1] - tags.shape[2])))
        packed = jnp.broadcast_to(projected[None], (wide,) + projected.shape)
        packed = jnp.concatenate([packed, tags], axis=1)
        received = beside(lambda value: exchange(value, "wide"), packed, (3, 0), (6, 1))
        received = launch(received, (4, 0), (5, 0))
        tags_in = received[:, rows]
        queries = received[:, :rows, :own_cols]
        queries = spread(queries, "narrow")
        queries = jnp.transpose(queries, (2, 1, 0, 3)).reshape(rows, HEADS, HD)
        queries = [jnp.transpose(queries, (1, 0, 2)).reshape(KVH, GROUPS * rows, HD)]
        keyval = jnp.transpose(received[:, :rows, own_cols:], (1, 0, 2)).reshape(rows, -1)
        keyval = jnp.pad(keyval, ((0, extra - rows), (0, 0)))
        tags_in = tags_in.astype(jnp.int32)
        moved_req = tags_in[:, :capacity].reshape(slots)
        moved_idx = tags_in[:, capacity : 2 * capacity] * 32
        moved_idx = (moved_idx + tags_in[:, 2 * capacity : 3 * capacity] - 1).reshape(slots)
        local_req = local_rows // STEPS
        fresh = lax.dynamic_slice_in_dim(keyval, me * local_rows, local_rows, 0)
        fresh = fresh.reshape(local_req, STEPS, -1)
        kept = lax.dynamic_slice_in_dim(accepted, me * local_req, local_req, 0)
        step_ids = jnp.arange(STEPS)[None, :, None]
        new_entries = jnp.where(
            step_ids < kept[:, None, None], fresh, jnp.zeros((), jnp.bfloat16)
        )

    queries, moved_pool = lax.optimization_barrier((queries, placed(moved_pool)))
    queries = launch(queries, (1, 0))
    mixed = attend(both, lengths, queries, keyval, tokens, token_info, rows, piece)
    mixed = land(mixed, (1, 0))
    if direct:
        mixed = land(deal(mixed, "narrow"), (4, 0), (5, 0))
    else:
        mixed = land(exchange(mixed[0], "narrow"), (4, 0), (5, 0))
        mixed = mixed.reshape((narrow, wide) + mixed.shape[1:])
        mixed = [mixed[i] for i in range(narrow)]
    mixed = combine(mixed, piece)
    mixed, pages = lax.optimization_barrier((mixed, moved_pool))
    pages = placed(pages)
    mixed = beside(lambda value: exchange(value, "wide"), mixed, (2, 0), (5, 1))
    mixed, moved_pool = lax.optimization_barrier((mixed, pages))
    attn = combine([mixed], piece, wide)
    attn, pages = lax.optimization_barrier((attn, moved_pool))
    pages = placed(pages)
    attn = beside(lambda value: exchange(value, "wide"), attn, (7, 0))
    attn, moved_pool = lax.optimization_barrier((attn, pages))
    if direct:
        sums = in_vmem(
            functools.partial(finish_kernel, narrow),
            [jax.ShapeDtypeStruct((rows // narrow, w_out.shape[1]), jnp.float32)] * narrow,
            both,
            attn,
            w_out,
        )
        sums, pages = lax.optimization_barrier((sums, moved_pool))
        pages = placed(pages)
        sums = beside(lambda value: deal(value, "narrow"), sums, (7, 1))
        attended = ((sums[0] + sums[1]) + (sums[2] + sums[3])).astype(jnp.bfloat16)
    else:
        attn = jnp.transpose(attn.reshape(-1, rows, HD), (1, 0, 2)).reshape(rows, -1)
        sums = jnp.dot(attn, w_out, preferred_element_type=jnp.float32)
        sums = sums.reshape(narrow, rows // narrow, -1)
        pages = placed(moved_pool)
        sums = beside(lambda value: exchange(value, "narrow"), sums, (7, 1))
        attended = jnp.sum(sums, axis=0).astype(jnp.bfloat16)
    attended, pages = lax.optimization_barrier((attended, pages))
    moved_pool = placed(pages)
    return (attended, new_entries, moved_pool, moved_req, moved_idx)


def solution(mesh):
    in_specs = (
        P("wide", "narrow"),
        P("narrow", "wide"),
        P("narrow", "wide"),
        P("narrow", "wide"),
        P(("wide", "narrow"), None, None),
        P(("wide", "narrow")),
        P(("wide", "narrow")),
        P(),
        P(("wide", "narrow"), None),
        P(),
    )
    out_specs = (
        P("narrow", "wide"),
        P("wide", None, None),
        P(("wide", "narrow"), None, None),
        P(("wide", "narrow")),
        P(("wide", "narrow")),
    )
    return jax.shard_map(
        on_device, mesh=mesh, in_specs=in_specs, out_specs=out_specs, check_vma=False
    )
```

```python
import functools
import math

import jax
import jax.numpy as jnp
from jax import lax
from jax.experimental import pallas as pl
from jax.experimental.pallas import tpu as pltpu
from jax.sharding import PartitionSpec as P

HEADS = 32
KVH = 4
HD = 128
STEPS = 5
PAGE = 16
GROUPS = HEADS // KVH
NEG_FILL = -1e30
SCALE2 = math.log2(math.e) / math.sqrt(HD)
STAT = 16
MIB = 1024 * 1024
AHEAD = 5
NT = (((1,), (1,)), ((), ()))


def up(value, unit):
    return -(-value // unit) * unit


def column(row):
    return jnp.transpose(jnp.broadcast_to(row, (row.shape[1], row.shape[1])))


def order_kernel(
    wide, ahead, parts, me_ref, dest_ref, req_ref, idx_ref, pool_ref, out_ref, tag_ref, token_ref, *refs
):
    chunk_refs, refs = refs[: len(parts)], refs[len(parts) :]
    pages_ref, line_ref, source_ref, in_sem, out_sem, line_sem = refs
    slots = pool_ref.shape[0]
    capacity = slots // wide
    shape = (slots, slots)
    high = lax.broadcasted_iota(jnp.int32, shape, 0)
    low = lax.broadcasted_iota(jnp.int32, shape, 1)
    dest = dest_ref[...]
    same = column(dest.astype(jnp.float32)) == dest.astype(jnp.float32)
    rank = jnp.sum(jnp.where(same & (high < low), 1.0, 0.0), axis=0, keepdims=True)
    rest = capacity - ahead
    early = (dest * ahead).astype(jnp.float32) + rank
    late = ((dest ^ me_ref[0]) * rest + wide * ahead - ahead).astype(jnp.float32) + rank
    moved_to = jnp.where(rank < float(ahead), early, late)
    match = column(moved_to) == low.astype(jnp.float32)
    source = jnp.sum(jnp.where(match, high.astype(jnp.float32), 0.0), axis=0, keepdims=True)
    line_ref[...] = source.astype(jnp.int32)
    copy = pltpu.make_async_copy(line_ref, source_ref, line_sem)
    copy.start()
    copy.wait()

    own = out_ref.at[pl.ds(me_ref[0] * capacity + ahead, rest)]
    blocks = [(wide * ahead, rest, own)]
    for d, chunk in zip(parts, chunk_refs):
        if d:
            blocks.append((wide * ahead + d * rest, rest, chunk))
        else:
            blocks.insert(0, (0, wide * ahead, chunk))
    for c, (first, count, _) in enumerate(blocks):

        def start(j, carry, c=c):
            page = source_ref[0, j]
            pltpu.make_async_copy(pool_ref.at[page], pages_ref.at[j], in_sem.at[c]).start()
            return carry

        lax.fori_loop(first, first + count, start, 0)

    shifted = idx_ref[...] + 1
    fields = (req_ref[...], shifted // 32, shifted % 32)
    rank_col = column(rank)
    lane = low.astype(jnp.float32)
    spread_out = jnp.zeros(shape, jnp.float32)
    for i, field in enumerate(fields):
        picked = lane == rank_col + float(i * capacity)
        spread_out = spread_out + jnp.where(picked, column(field.astype(jnp.float32)), 0.0)
    line = lax.broadcasted_iota(jnp.int32, (wide, slots), 0)
    chosen = jnp.where(line == dest, 1.0, 0.0).astype(jnp.bfloat16)
    tag_ref[...] = jnp.dot(
        chosen, spread_out.astype(jnp.bfloat16), preferred_element_type=jnp.float32
    )

    tokens = slots * PAGE
    page = lax.broadcasted_iota(jnp.int32, (slots, tokens), 0)
    token = lax.broadcasted_iota(jnp.int32, (slots, tokens), 1)
    widen = jnp.where(page == token // PAGE, 1.0, 0.0).astype(jnp.bfloat16)
    row = lax.broadcasted_iota(jnp.int32, (8, slots), 0)
    stacked = jnp.zeros((8, slots), jnp.float32)
    for i, field in enumerate(fields):
        stacked = jnp.where(row == i, field.astype(jnp.float32), stacked)
    token_ref[...] = jnp.dot(
        stacked.astype(jnp.bfloat16), widen, preferred_element_type=jnp.float32
    )

    copies = []
    for c, (first, count, target) in enumerate(blocks):
        held = pages_ref.at[pl.ds(first, count)]
        pltpu.make_async_copy(pool_ref.at[pl.ds(0, count)], held, in_sem.at[c]).wait()
        copies.append(pltpu.make_async_copy(held, target, out_sem.at[c]))
        copies[-1].start()
    for copy in copies:
        copy.wait()


def order_pages(me, dest, page_req, page_idx, pool, wide, ahead, parts):
    slots = pool.shape[0]
    part = lambda count: jax.ShapeDtypeStruct((count,) + pool.shape[1:], pool.dtype)
    out_shape = [part(slots), jax.ShapeDtypeStruct((wide, slots), jnp.float32)]
    out_shape += [jax.ShapeDtypeStruct((8, slots * PAGE), jnp.float32)]
    rest = slots // wide - ahead
    out_shape += [part(rest if d else wide * ahead) for d in parts]
    vmem = pl.BlockSpec(memory_space=pltpu.VMEM)
    hbm = pl.BlockSpec(memory_space=pltpu.HBM)
    return pl.pallas_call(
        functools.partial(order_kernel, wide, ahead, parts),
        out_shape=out_shape,
        in_specs=[pl.BlockSpec(memory_space=pltpu.SMEM), vmem, vmem, vmem, hbm],
        out_specs=[hbm, vmem, vmem] + [hbm] * len(parts),
        scratch_shapes=[
            pltpu.VMEM(pool.shape, pool.dtype),
            pltpu.VMEM((1, slots), jnp.int32),
            pltpu.SMEM((1, slots), jnp.int32),
            pltpu.SemaphoreType.DMA((1 + len(parts),)),
            pltpu.SemaphoreType.DMA((1 + len(parts),)),
            pltpu.SemaphoreType.DMA,
        ],
        compiler_params=pltpu.CompilerParams(vmem_limit_bytes=56 * MIB),
        cost_estimate=pl.CostEstimate(
            flops=0, bytes_accessed=2 * pool.size * 2, transcendentals=0
        ),
    )(me, dest.reshape(1, -1), page_req.reshape(1, -1), page_idx.reshape(1, -1), pool)


def place_kernel(counts, place_ref, *refs):
    in_refs, (out_ref, sem) = refs[:-3], refs[-2:]
    copies = []
    for chunk, count in zip(in_refs, counts):
        depth = chunk.shape[0] // count
        for i in range(count):
            c = len(copies)
            target = out_ref.at[pl.ds(place_ref[c], depth)]
            source = chunk.at[pl.ds(i * depth, depth)]
            copies.append(pltpu.make_async_copy(source, target, sem.at[c]))
    for copy in copies:
        copy.start()
    for copy in copies:
        copy.wait()


def place_pages(place, chunks, counts, pages):
    size = sum(chunk.size for chunk in chunks)
    return pl.pallas_call(
        functools.partial(place_kernel, counts),
        out_shape=jax.ShapeDtypeStruct(pages.shape, pages.dtype),
        in_specs=[pl.BlockSpec(memory_space=pltpu.SMEM)]
        + [pl.BlockSpec(memory_space=pltpu.VMEM)] * len(chunks)
        + [pl.BlockSpec(memory_space=pl.ANY)],
        out_specs=pl.BlockSpec(memory_space=pl.ANY),
        scratch_shapes=[pltpu.SemaphoreType.DMA((sum(counts),))],
        input_output_aliases={len(chunks) + 1: 0},
        compiler_params=pltpu.CompilerParams(vmem_limit_bytes=2 * size + 2 * MIB),
        cost_estimate=pl.CostEstimate(flops=0, bytes_accessed=4 * size, transcendentals=0),
    )(place, *chunks, pages)


def cut(value):
    return value.astype(jnp.bfloat16).astype(jnp.float32)


def split_stats(peak, total):
    high = cut(peak)
    mid = cut(peak - high)
    return high, mid, peak - high - mid, cut(total), total - cut(total)


def attend_kernel(rows, piece, peers, me_ref, length_ref, *refs):
    query_refs, refs = refs[:peers], refs[peers:]
    key_ref, value_ref, new_key_ref, new_value_ref, token_ref = refs[:5]
    out_refs = refs[5 : 5 + peers]
    bias_ref, new_bias_ref, score_ref, weight_ref, query_ref, result_ref = refs[5 + peers :]
    tokens = key_ref.shape[0]
    step = pl.program_id(0)

    @pl.when(step == 0)
    def _():
        owner = token_ref[0:1, :]
        offset = lax.broadcasted_iota(jnp.int32, owner.shape, 1) % PAGE
        spot = (token_ref[1:2, :] * 32 + token_ref[2:3, :] - 1) * PAGE + offset.astype(jnp.float32)
        request = lax.broadcasted_iota(jnp.int32, (rows, 1), 0) // STEPS
        limit = jnp.zeros((rows, 1), jnp.int32)
        for r in range(rows // STEPS):
            limit = jnp.where(request == r, length_ref[r], limit)
        seen = (owner == request.astype(jnp.float32)) & (spot < limit.astype(jnp.float32))
        bias_ref[...] = jnp.where(seen, 0.0, NEG_FILL)
        row = lax.broadcasted_iota(jnp.int32, new_bias_ref.shape, 0)
        col = lax.broadcasted_iota(jnp.int32, new_bias_ref.shape, 1)
        first = jnp.where((me_ref[0] == 0) & (me_ref[1] == 0), 1, 0)
        seen = (row // STEPS == col // STEPS) & (col <= row) & (col < rows * first)
        new_bias_ref[...] = jnp.where(seen, 0.0, NEG_FILL)
        if peers > 1:
            for d in range(peers):
                query_ref[me_ref[1] ^ d] = query_refs[d][...]

    if peers > 1:
        per_step = query_refs[0].shape[0] // KVH
        query = jnp.concatenate(
            [
                query_ref[n, step * per_step + i].astype(jnp.float32)
                for i in range(per_step)
                for n in range(peers)
            ],
            axis=0,
        ).astype(jnp.bfloat16)
    else:
        query = query_refs[0][0]
    score_ref[:, :tokens] = lax.dot_general(
        query, key_ref[...], NT, preferred_element_type=jnp.float32
    )
    score_ref[:, tokens:] = lax.dot_general(
        query, new_key_ref[...], NT, preferred_element_type=jnp.float32
    )
    together = 1 if rows % 16 == 0 else 2
    span = together * rows
    peaks, totals = [], []
    for c in range(GROUPS // together):
        block = pl.ds(c * span, span)
        old = score_ref[block, :tokens].reshape(together, rows, tokens) * SCALE2 + bias_ref[...]
        new = score_ref[block, tokens:].reshape(together, rows, -1) * SCALE2 + new_bias_ref[...]
        peak = jnp.maximum(
            jnp.max(old, axis=-1, keepdims=True), jnp.max(new, axis=-1, keepdims=True)
        )
        old = jnp.exp2(old - peak)
        new = jnp.exp2(new - peak)
        totals.append(
            (jnp.sum(old, axis=-1, keepdims=True) + jnp.sum(new, axis=-1, keepdims=True)).reshape(
                span, 1
            )
        )
        peaks.append(peak.reshape(span, 1))
        weight_ref[block, :tokens] = old.reshape(span, tokens).astype(jnp.bfloat16)
        weight_ref[block, tokens:] = new.reshape(span, -1).astype(jnp.bfloat16)
    mixed = jnp.dot(
        weight_ref[:, :tokens], value_ref[...], preferred_element_type=jnp.float32
    ) + jnp.dot(weight_ref[:, tokens:], new_value_ref[...], preferred_element_type=jnp.float32)
    peak = jnp.concatenate(peaks, axis=0)
    total = jnp.concatenate(totals, axis=0)
    lane = lax.broadcasted_iota(jnp.int32, (GROUPS * rows, HD), 1)
    stats = jnp.zeros((GROUPS * rows, HD), jnp.float32)
    for i, part in enumerate(split_stats(peak, total)):
        stats = jnp.where(lane == i, part, stats)
    pick = (
        lax.broadcasted_iota(jnp.int32, (STAT, HD), 0)
        == lax.broadcasted_iota(jnp.int32, (STAT, HD), 1)
    ).astype(jnp.bfloat16)
    fill = result_ref.shape[1] - STAT - piece
    for c in range(GROUPS * rows // piece):
        part = slice(c * piece, (c + 1) * piece)
        turned = lax.dot_general(
            pick,
            jnp.concatenate(
                [stats[part], jnp.zeros((HD - piece, HD), jnp.float32)], axis=0
            ).astype(jnp.bfloat16),
            NT,
            preferred_element_type=jnp.float32,
        )
        result_ref[c] = jnp.concatenate(
            [turned, mixed[part], jnp.zeros((fill, HD), jnp.float32)], axis=0
        ).astype(jnp.bfloat16)
    if peers > 1:
        for d, out_ref in enumerate(out_refs):

            @pl.when((step ^ me_ref[1]) == d)
            def _():
                out_ref[...] = result_ref[...]
    else:
        out_refs[0][...] = result_ref[...]


def attend(me, lengths, queries, keyval, pool, token_info, rows, piece):
    tokens = pool.shape[0]
    extra = keyval.shape[0]
    peers = len(queries)
    pieces = GROUPS * rows // piece
    height = STAT + up(piece, 16)
    whole = lambda shape: pl.BlockSpec(shape, lambda k: (0,) * len(shape))
    if peers > 1:
        query_spec = whole(queries[0].shape)
        out_spec = whole((pieces, height, HD))
        out_shape = jax.ShapeDtypeStruct((pieces, height, HD), jnp.bfloat16)
    else:
        query_spec = pl.BlockSpec((1,) + queries[0].shape[1:], lambda k: (k, 0, 0))
        out_spec = pl.BlockSpec((pieces, height, HD), lambda k: (k, 0, 0))
        out_shape = jax.ShapeDtypeStruct((KVH * pieces, height, HD), jnp.bfloat16)
    return pl.pallas_call(
        functools.partial(attend_kernel, rows, piece, peers),
        grid=(KVH,),
        out_shape=[out_shape] * peers,
        in_specs=[pl.BlockSpec(memory_space=pltpu.SMEM)] * 2
        + [query_spec] * peers
        + [
            pl.BlockSpec((tokens, HD), lambda k: (0, k)),
            pl.BlockSpec((tokens, HD), lambda k: (0, KVH + k)),
            pl.BlockSpec((extra, HD), lambda k: (0, k)),
            pl.BlockSpec((extra, HD), lambda k: (0, KVH + k)),
            whole(token_info.shape),
        ],
        out_specs=[out_spec] * peers,
        scratch_shapes=[
            pltpu.VMEM((rows, tokens), jnp.float32),
            pltpu.VMEM((rows, extra), jnp.float32),
            pltpu.VMEM((GROUPS * rows, tokens + extra), jnp.float32),
            pltpu.VMEM((GROUPS * rows, tokens + extra), jnp.bfloat16),
            pltpu.VMEM((peers,) + queries[0].shape, jnp.bfloat16),
            pltpu.VMEM((pieces, height, HD), jnp.bfloat16),
        ],
        compiler_params=pltpu.CompilerParams(vmem_limit_bytes=56 * MIB),
        cost_estimate=pl.CostEstimate(flops=1, bytes_accessed=1, transcendentals=0),
    )(me, lengths, *queries, pool, pool, keyval, keyval, token_info)


def combine_kernel(piece, last, count, *refs):
    if last:
        part_ref, out_ref = refs
        part_refs = [part_ref.at[pl.ds(i, 1)] for i in range(count)]
    else:
        part_refs, out_ref = refs[:count], refs[count]
    groups, height = part_refs[0].shape[:2]
    peaks, totals = [], []
    for i in range(count):
        for j in range(groups):
            stat = part_refs[i][j, :STAT, :].astype(jnp.float32)
            peaks.append(stat[0:1] + stat[1:2] + stat[2:3])
            totals.append(stat[3:4] + stat[4:5])
    peak = jnp.concatenate(peaks, axis=0).reshape(count, groups, HD)
    total = jnp.concatenate(totals, axis=0).reshape(count, groups, HD)
    top = jnp.max(peak, axis=0)
    lead = jnp.exp2(peak - top[None])
    whole = jnp.sum(lead * total, axis=0)
    if last:
        lane = lax.broadcasted_iota(jnp.int32, whole.shape, 1)
        lead = lead / jnp.where(lane < piece, whole, 1.0)[None]
    lead = lead.reshape(count * groups, HD)
    if (count * groups) % HD:
        fill = up(count * groups, HD) - count * groups
        lead = jnp.concatenate([lead, jnp.zeros((fill, HD), jnp.float32)], axis=0)
    lead = jnp.transpose(lead)
    rows = height - STAT
    for j in range(groups):
        result = jnp.zeros((rows, HD), jnp.float32)
        for i in range(count):
            c = i * groups + j
            result = result + lead[:rows, c : c + 1] * part_refs[i][j, STAT:, :].astype(jnp.float32)
        if last:
            for i in range(out_ref.shape[0]):
                out_ref[i] = result[:piece].astype(jnp.bfloat16)
        else:
            stats = split_stats(top[j : j + 1], whole[j : j + 1])
            rest = jnp.zeros((STAT - len(stats), HD), jnp.float32)
            out_ref[j] = jnp.concatenate([*stats, rest, result], axis=0).astype(jnp.bfloat16)


def combine(parts, piece, repeats=0):
    count = parts[0].shape[0] if repeats else len(parts)
    shape = (repeats, piece, HD) if repeats else parts[0].shape
    return pl.pallas_call(
        functools.partial(combine_kernel, piece, repeats > 0, count),
        out_shape=jax.ShapeDtypeStruct(shape, jnp.bfloat16),
        in_specs=[pl.BlockSpec(memory_space=pltpu.VMEM)] * len(parts),
        out_specs=pl.BlockSpec(memory_space=pltpu.VMEM),
        compiler_params=pltpu.CompilerParams(vmem_limit_bytes=8 * MIB),
        cost_estimate=pl.CostEstimate(flops=1, bytes_accessed=1, transcendentals=0),
    )(*parts)


def reorder(shape, unit, valid, own, column):
    first, second = (0, 1) if column else (1, 0)
    block = lax.broadcasted_iota(jnp.int32, shape, second) // unit
    place = lax.broadcasted_iota(jnp.int32, shape, second) % unit
    target = (block ^ own) * valid + place
    match = (lax.broadcasted_iota(jnp.int32, shape, first) == target) & (place < valid)
    return match.astype(jnp.bfloat16)


def project_kernel(peers, me_ref, hidden_ref, query_ref, keyval_ref, *refs):
    out_refs, (full_ref,) = refs[:peers], refs[peers:]
    count, local, depth = hidden_ref.shape
    unit = up(local, 8)
    blocks = []
    for i in range(count):
        blocks.append(hidden_ref[i].astype(jnp.float32))
        if unit > local:
            blocks.append(jnp.zeros((unit - local, depth), jnp.float32))
    hidden = jnp.concatenate(blocks, axis=0).astype(jnp.bfloat16)
    order = reorder((count * local, count * unit), unit, local, 0, True)
    hidden = jnp.dot(order, hidden, preferred_element_type=jnp.float32).astype(jnp.bfloat16)
    full_ref[...] = jnp.dot(hidden, query_ref[...], preferred_element_type=jnp.float32)
    keyval = jnp.dot(hidden, keyval_ref[...], preferred_element_type=jnp.float32)
    for d, out_ref in enumerate(out_refs):
        start = pl.multiple_of((me_ref[1] ^ d) * HD, HD)
        out_ref[:, :HD] = full_ref[:, pl.ds(start, HD)]
        out_ref[:, HD:] = keyval


def pack_kernel(peers, *refs):
    own, tag_ref, out_ref = refs[:peers], refs[peers], refs[peers + 1]
    total = (own[0][...] + own[1][...]) + (own[2][...] + own[3][...])
    tags = jnp.concatenate([tag_ref[...], jnp.zeros_like(tag_ref[...])], axis=1)
    packed = jnp.concatenate([total, tags], axis=0).astype(jnp.bfloat16)
    for i in range(out_ref.shape[0]):
        out_ref[i] = packed


def unpack_kernel(rows, me_ref, kept_ref, part_ref, query_ref, keyval_ref, *refs):
    entry_ref, req_ref, idx_ref = refs
    count = part_ref.shape[0]
    line = lax.broadcasted_iota(jnp.int32, (count, HD), 0)
    tags = jnp.zeros((count, HD), jnp.float32)
    fill = jnp.zeros((keyval_ref.shape[0] - rows, HD), jnp.float32)
    for i in range(count):
        part = part_ref[i].astype(jnp.float32)
        query_ref[i] = part[:rows, :HD].astype(jnp.bfloat16)
        block = jnp.concatenate([part[:rows, HD:], fill], axis=0).astype(jnp.bfloat16)
        keyval_ref[:, i * HD : (i + 1) * HD] = block
        mine = jnp.where(line == me_ref[0], part[rows : rows + count, :HD], 0.0)
        tags = tags + jnp.where(line == i, jnp.sum(mine, axis=0, keepdims=True), 0.0)
    capacity = HD // count
    high = lax.broadcasted_iota(jnp.int32, (HD, HD), 0)
    low = lax.broadcasted_iota(jnp.int32, (HD, HD), 1)
    slot = lax.broadcasted_iota(jnp.int32, (count, HD), 1)
    tags = tags.astype(jnp.bfloat16)
    fields = []
    for i in range(3):
        pick = jnp.where(high == i * capacity + low % capacity, 1.0, 0.0).astype(jnp.bfloat16)
        spread_out = jnp.dot(tags, pick, preferred_element_type=jnp.float32)
        spread_out = jnp.where(slot // capacity == line, spread_out, 0.0)
        fields.append(jnp.sum(spread_out, axis=0, keepdims=True))
    req_ref[...] = fields[0].astype(jnp.int32)
    idx_ref[...] = (fields[1] * 32.0 + fields[2] - 1.0).astype(jnp.int32)
    local = entry_ref.shape[1]
    step = lax.broadcasted_iota(jnp.int32, (16, keyval_ref.shape[0]), 0)
    row = lax.broadcasted_iota(jnp.int32, (16, keyval_ref.shape[0]), 1)
    kept = (row == me_ref[0] * local + step) & (step < kept_ref[me_ref[0]])
    kept = jnp.where(kept, 1.0, 0.0).astype(jnp.bfloat16)
    entries = jnp.dot(kept, keyval_ref[...], preferred_element_type=jnp.float32)
    entry_ref[0] = entries[:local].astype(jnp.bfloat16)


def finish_kernel(peers, me_ref, part_ref, weight_ref, *refs):
    count, rows = part_ref.shape[:2]
    local = rows // peers
    unit = up(local, 16)
    whole = jnp.concatenate([part_ref[i] for i in range(count)], axis=1)
    order = reorder((peers * unit, rows), unit, local, me_ref[1], False)
    mixed = jnp.dot(order, whole, preferred_element_type=jnp.float32)
    mixed = jnp.dot(mixed.astype(jnp.bfloat16), weight_ref[...], preferred_element_type=jnp.float32)
    for d, out_ref in enumerate(refs):
        out_ref[...] = mixed[d * unit : d * unit + local]


def in_vmem(kernel, out_shape, me, *args, scratch=()):
    head = [] if me is None else list(me) if isinstance(me, tuple) else [me]
    return pl.pallas_call(
        kernel,
        out_shape=out_shape,
        in_specs=[pl.BlockSpec(memory_space=pltpu.SMEM)] * len(head)
        + [pl.BlockSpec(memory_space=pltpu.VMEM)] * len(args),
        out_specs=jax.tree.map(lambda _: pl.BlockSpec(memory_space=pltpu.VMEM), out_shape),
        scratch_shapes=scratch,
        compiler_params=pltpu.CompilerParams(vmem_limit_bytes=16 * MIB),
        cost_estimate=pl.CostEstimate(flops=1, bytes_accessed=1, transcendentals=0),
    )(*head, *args)


def group_of(d, wide):
    return d if wide <= 8 or d == 0 else 1 + (d - 1) * 7 // (wide - 1)


def spread(block, axis):
    count = lax.axis_size(axis)
    return lax.all_to_all(
        jnp.broadcast_to(block[None], (count,) + block.shape),
        axis,
        split_axis=0,
        concat_axis=0,
        tiled=True,
    )


def on_device(hidden, w_query, w_keyval, w_out, pool, page_req, page_idx, lengths, moves, accepted):
    wide = lax.axis_size("wide")
    narrow = lax.axis_size("narrow")
    local_rows = hidden.shape[0]
    rows = local_rows * wide
    requests = rows // STEPS
    slots = pool.shape[0]
    capacity = slots // wide
    own_cols = w_query.shape[1] // narrow
    piece = HEADS * rows // (wide * narrow)
    extra = up(rows, HD)
    direct = piece == rows and own_cols == HD and slots == HD
    direct = direct and wide == 8 and narrow == 4 and local_rows == STEPS
    me = lax.axis_index("wide")
    both = jnp.stack([me, lax.axis_index("narrow")])
    exchange = functools.partial(lax.all_to_all, split_axis=0, concat_axis=0, tiled=True)

    def send(block, axis, d):
        return lax.ppermute(block, axis, [(i, i ^ d) for i in range(lax.axis_size(axis))])

    def share(block, axis):
        return [block] + [send(block, axis, d) for d in range(1, lax.axis_size(axis))]

    def deal(blocks, axis):
        return [blocks[0]] + [send(block, axis, d) for d, block in enumerate(blocks) if d]

    gathered = spread(hidden, "wide")

    ahead = AHEAD * capacity // 16
    parts = list(range(0 if ahead else 1, wide))
    moved_pool, tags, token_info, *chunks = order_pages(
        both, moves, page_req, page_idx, pool, wide, ahead, parts
    )
    chunks = dict(zip(parts, chunks))
    arrived = {}
    flying = {}

    def members(groups):
        return [d for group in groups for d in parts if group_of(d, wide) == group]

    def launch(values, *groups):
        taken = members(groups)
        values, sent = lax.optimization_barrier((values, [chunks[d] for d in taken]))
        for d, chunk in zip(taken, sent):
            flying[d] = send(chunk, "wide", d) if d else exchange(chunk, "wide")
        return values

    def land(values, *groups):
        taken = members(groups)
        values, got = lax.optimization_barrier((values, [flying[d] for d in taken]))
        arrived.update(zip(taken, got))
        return values

    def placed(pages):
        taken = sorted(arrived)
        if not taken:
            return pages
        place = []
        for d in taken:
            place += [(me ^ d) * capacity + ahead] if d else [w * capacity for w in range(wide)]
        place = jnp.stack([jnp.asarray(index, jnp.int32) for index in place])
        counts = [1 if d else wide for d in taken]
        pages = place_pages(place, [arrived[d] for d in taken], counts, pages)
        arrived.clear()
        return pages

    gathered, tags = lax.optimization_barrier((gathered, tags))
    tokens = pool.reshape(slots * PAGE, -1)
    if direct:
        block = jax.ShapeDtypeStruct((rows, 2 * HD), jnp.float32)
        partial = in_vmem(
            functools.partial(project_kernel, narrow),
            [block] * narrow,
            both,
            gathered,
            w_query,
            w_keyval,
            scratch=[pltpu.VMEM((rows, narrow * HD), jnp.float32)],
        )
        partial = launch(deal(partial, "narrow"), 6, 1)
        packed = in_vmem(
            functools.partial(pack_kernel, narrow),
            jax.ShapeDtypeStruct((wide, rows + wide, 2 * HD), jnp.bfloat16),
            None,
            *partial,
            tags,
        )
        received = land(exchange(packed, "wide"), 6, 1)
        received = launch(received, 0)
        queries, keyval, new_entries, moved_req, moved_idx = in_vmem(
            functools.partial(unpack_kernel, rows),
            [
                jax.ShapeDtypeStruct((wide, rows, HD), jnp.bfloat16),
                jax.ShapeDtypeStruct((extra, wide * HD), jnp.bfloat16),
                jax.ShapeDtypeStruct((1, local_rows, wide * HD), jnp.bfloat16),
                jax.ShapeDtypeStruct((1, slots), jnp.int32),
                jax.ShapeDtypeStruct((1, slots), jnp.int32),
            ],
            (both, accepted),
            received,
        )
        moved_req, moved_idx = moved_req.reshape(slots), moved_idx.reshape(slots)
        queries = share(queries, "narrow")
    else:
        gathered = gathered.reshape(rows, -1)
        query_part = jnp.dot(gathered, w_query, preferred_element_type=jnp.float32)
        keyval_part = jnp.dot(gathered, w_keyval, preferred_element_type=jnp.float32)
        query_part = jnp.transpose(query_part.reshape(rows, narrow, own_cols), (1, 0, 2))
        partial = jnp.concatenate(
            [query_part, jnp.broadcast_to(keyval_part[None], (narrow,) + keyval_part.shape)], axis=2
        )
        partial = launch(exchange(partial, "narrow"), 6, 1)
        projected = jnp.sum(partial, axis=0).astype(jnp.bfloat16)
        tags = tags[:, : 3 * capacity].astype(jnp.bfloat16)[:, None]
        tags = jnp.pad(tags, ((0, 0), (0, 7), (0, projected.shape[1] - tags.shape[2])))
        packed = jnp.broadcast_to(projected[None], (wide,) + projected.shape)
        packed = jnp.concatenate([packed, tags], axis=1)
        received = land(exchange(packed, "wide"), 6, 1)
        received = launch(received, 0)
        tags_in = received[:, rows]
        queries = received[:, :rows, :own_cols]
        queries = spread(queries, "narrow")
        queries = jnp.transpose(queries, (2, 1, 0, 3)).reshape(rows, HEADS, HD)
        queries = [jnp.transpose(queries, (1, 0, 2)).reshape(KVH, GROUPS * rows, HD)]
        keyval = jnp.transpose(received[:, :rows, own_cols:], (1, 0, 2)).reshape(rows, -1)
        keyval = jnp.pad(keyval, ((0, extra - rows), (0, 0)))
        tags_in = tags_in.astype(jnp.int32)
        moved_req = tags_in[:, :capacity].reshape(slots)
        moved_idx = tags_in[:, capacity : 2 * capacity] * 32
        moved_idx = (moved_idx + tags_in[:, 2 * capacity : 3 * capacity] - 1).reshape(slots)
        local_req = local_rows // STEPS
        fresh = lax.dynamic_slice_in_dim(keyval, me * local_rows, local_rows, 0)
        fresh = fresh.reshape(local_req, STEPS, -1)
        kept = lax.dynamic_slice_in_dim(accepted, me * local_req, local_req, 0)
        step_ids = jnp.arange(STEPS)[None, :, None]
        new_entries = jnp.where(
            step_ids < kept[:, None, None], fresh, jnp.zeros((), jnp.bfloat16)
        )

    queries, moved_pool = lax.optimization_barrier((queries, placed(moved_pool)))
    mixed = attend(both, lengths, queries, keyval, tokens, token_info, rows, piece)
    if direct:
        mixed = land(deal(mixed, "narrow"), 0)
    else:
        mixed = land(exchange(mixed[0], "narrow"), 0)
        mixed = mixed.reshape((narrow, wide) + mixed.shape[1:])
        mixed = [mixed[i] for i in range(narrow)]
    mixed = combine(launch(mixed, 3, 4), piece)
    mixed, pages = lax.optimization_barrier((mixed, moved_pool))
    pages = placed(pages)
    mixed = land(exchange(mixed, "wide"), 3, 4)
    mixed, moved_pool = lax.optimization_barrier((mixed, pages))
    attn = combine([launch(mixed, 2, 5)], piece, wide)
    attn, pages = lax.optimization_barrier((attn, moved_pool))
    pages = placed(pages)
    attn = land(exchange(attn, "wide"), 2, 5)
    attn, moved_pool = lax.optimization_barrier((attn, pages))
    attn = launch(attn, 7)
    if direct:
        sums = in_vmem(
            functools.partial(finish_kernel, narrow),
            [jax.ShapeDtypeStruct((rows // narrow, w_out.shape[1]), jnp.float32)] * narrow,
            both,
            attn,
            w_out,
        )
        sums, pages = lax.optimization_barrier((sums, moved_pool))
        pages = placed(pages)
        sums = land(deal(sums, "narrow"), 7)
        attended = ((sums[0] + sums[1]) + (sums[2] + sums[3])).astype(jnp.bfloat16)
    else:
        attn = jnp.transpose(attn.reshape(-1, rows, HD), (1, 0, 2)).reshape(rows, -1)
        sums = jnp.dot(attn, w_out, preferred_element_type=jnp.float32)
        sums = sums.reshape(narrow, rows // narrow, -1)
        pages = placed(moved_pool)
        sums = land(exchange(sums, "narrow"), 7)
        attended = jnp.sum(sums, axis=0).astype(jnp.bfloat16)
    attended, pages = lax.optimization_barrier((attended, pages))
    moved_pool = placed(pages)
    return (attended, new_entries, moved_pool, moved_req, moved_idx)


def solution(mesh):
    in_specs = (
        P("wide", "narrow"),
        P("narrow", "wide"),
        P("narrow", "wide"),
        P("narrow", "wide"),
        P(("wide", "narrow"), None, None),
        P(("wide", "narrow")),
        P(("wide", "narrow")),
        P(),
        P(("wide", "narrow"), None),
        P(),
    )
    out_specs = (
        P("narrow", "wide"),
        P("wide", None, None),
        P(("wide", "narrow"), None, None),
        P(("wide", "narrow")),
        P(("wide", "narrow")),
    )
    return jax.shard_map(
        on_device, mesh=mesh, in_specs=in_specs, out_specs=out_specs, check_vma=False
    )
```

```python
import functools
import math

import jax
import jax.numpy as jnp
from jax import lax
from jax.experimental import pallas as pl
from jax.experimental.pallas import tpu as pltpu
from jax.sharding import PartitionSpec as P

HEADS = 32
KVH = 4
HD = 128
STEPS = 5
PAGE = 16
GROUPS = HEADS // KVH
NEG_FILL = -1e30
SCALE2 = math.log2(math.e) / math.sqrt(HD)
STAT = 16
MIB = 1024 * 1024
AHEAD = 5
NT = (((1,), (1,)), ((), ()))


def up(value, unit):
    return -(-value // unit) * unit


def column(row):
    return jnp.transpose(jnp.broadcast_to(row, (row.shape[1], row.shape[1])))


def order_kernel(
    wide, ahead, parts, me_ref, dest_ref, req_ref, idx_ref, pool_ref, out_ref, tag_ref, token_ref, *refs
):
    chunk_refs, refs = refs[: len(parts)], refs[len(parts) :]
    pages_ref, line_ref, source_ref, in_sem, out_sem, line_sem = refs
    slots = pool_ref.shape[0]
    capacity = slots // wide
    shape = (slots, slots)
    high = lax.broadcasted_iota(jnp.int32, shape, 0)
    low = lax.broadcasted_iota(jnp.int32, shape, 1)
    dest = dest_ref[...]
    same = column(dest.astype(jnp.float32)) == dest.astype(jnp.float32)
    rank = jnp.sum(jnp.where(same & (high < low), 1.0, 0.0), axis=0, keepdims=True)
    rest = capacity - ahead
    early = (dest * ahead).astype(jnp.float32) + rank
    late = ((dest ^ me_ref[0]) * rest + wide * ahead - ahead).astype(jnp.float32) + rank
    moved_to = jnp.where(rank < float(ahead), early, late)
    match = column(moved_to) == low.astype(jnp.float32)
    source = jnp.sum(jnp.where(match, high.astype(jnp.float32), 0.0), axis=0, keepdims=True)
    line_ref[...] = source.astype(jnp.int32)
    copy = pltpu.make_async_copy(line_ref, source_ref, line_sem)
    copy.start()
    copy.wait()

    own = out_ref.at[pl.ds(me_ref[0] * capacity + ahead, rest)]
    blocks = [(wide * ahead, rest, own)]
    for d, chunk in zip(parts, chunk_refs):
        if d:
            blocks.append((wide * ahead + d * rest, rest, chunk))
        else:
            blocks.insert(0, (0, wide * ahead, chunk))
    for c, (first, count, _) in enumerate(blocks):

        def start(j, carry, c=c):
            page = source_ref[0, j]
            pltpu.make_async_copy(pool_ref.at[page], pages_ref.at[j], in_sem.at[c]).start()
            return carry

        lax.fori_loop(first, first + count, start, 0)

    shifted = idx_ref[...] + 1
    fields = (req_ref[...], shifted // 32, shifted % 32)
    rank_col = column(rank)
    lane = low.astype(jnp.float32)
    spread_out = jnp.zeros(shape, jnp.float32)
    for i, field in enumerate(fields):
        picked = lane == rank_col + float(i * capacity)
        spread_out = spread_out + jnp.where(picked, column(field.astype(jnp.float32)), 0.0)
    line = lax.broadcasted_iota(jnp.int32, (wide, slots), 0)
    chosen = jnp.where(line == dest, 1.0, 0.0).astype(jnp.bfloat16)
    tag_ref[...] = jnp.dot(
        chosen, spread_out.astype(jnp.bfloat16), preferred_element_type=jnp.float32
    )

    tokens = slots * PAGE
    page = lax.broadcasted_iota(jnp.int32, (slots, tokens), 0)
    token = lax.broadcasted_iota(jnp.int32, (slots, tokens), 1)
    widen = jnp.where(page == token // PAGE, 1.0, 0.0).astype(jnp.bfloat16)
    row = lax.broadcasted_iota(jnp.int32, (8, slots), 0)
    stacked = jnp.zeros((8, slots), jnp.float32)
    for i, field in enumerate(fields):
        stacked = jnp.where(row == i, field.astype(jnp.float32), stacked)
    token_ref[...] = jnp.dot(
        stacked.astype(jnp.bfloat16), widen, preferred_element_type=jnp.float32
    )

    copies = []
    for c, (first, count, target) in enumerate(blocks):
        held = pages_ref.at[pl.ds(first, count)]
        pltpu.make_async_copy(pool_ref.at[pl.ds(0, count)], held, in_sem.at[c]).wait()
        copies.append(pltpu.make_async_copy(held, target, out_sem.at[c]))
        copies[-1].start()
    for copy in copies:
        copy.wait()


def order_pages(me, dest, page_req, page_idx, pool, wide, ahead, parts):
    slots = pool.shape[0]
    part = lambda count: jax.ShapeDtypeStruct((count,) + pool.shape[1:], pool.dtype)
    out_shape = [part(slots), jax.ShapeDtypeStruct((wide, slots), jnp.float32)]
    out_shape += [jax.ShapeDtypeStruct((8, slots * PAGE), jnp.float32)]
    rest = slots // wide - ahead
    out_shape += [part(rest if d else wide * ahead) for d in parts]
    vmem = pl.BlockSpec(memory_space=pltpu.VMEM)
    hbm = pl.BlockSpec(memory_space=pltpu.HBM)
    return pl.pallas_call(
        functools.partial(order_kernel, wide, ahead, parts),
        out_shape=out_shape,
        in_specs=[pl.BlockSpec(memory_space=pltpu.SMEM), vmem, vmem, vmem, hbm],
        out_specs=[hbm, vmem, vmem] + [hbm] * len(parts),
        scratch_shapes=[
            pltpu.VMEM(pool.shape, pool.dtype),
            pltpu.VMEM((1, slots), jnp.int32),
            pltpu.SMEM((1, slots), jnp.int32),
            pltpu.SemaphoreType.DMA((1 + len(parts),)),
            pltpu.SemaphoreType.DMA((1 + len(parts),)),
            pltpu.SemaphoreType.DMA,
        ],
        compiler_params=pltpu.CompilerParams(vmem_limit_bytes=56 * MIB),
        cost_estimate=pl.CostEstimate(
            flops=0, bytes_accessed=2 * pool.size * 2, transcendentals=0
        ),
    )(me, dest.reshape(1, -1), page_req.reshape(1, -1), page_idx.reshape(1, -1), pool)


def place_kernel(counts, place_ref, *refs):
    in_refs, (out_ref, sem) = refs[:-3], refs[-2:]
    copies = []
    for chunk, count in zip(in_refs, counts):
        depth = chunk.shape[0] // count
        for i in range(count):
            c = len(copies)
            target = out_ref.at[pl.ds(place_ref[c], depth)]
            source = chunk.at[pl.ds(i * depth, depth)]
            copies.append(pltpu.make_async_copy(source, target, sem.at[c]))
    for copy in copies:
        copy.start()
    for copy in copies:
        copy.wait()


def place_pages(place, chunks, counts, pages):
    size = sum(chunk.size for chunk in chunks)
    return pl.pallas_call(
        functools.partial(place_kernel, counts),
        out_shape=jax.ShapeDtypeStruct(pages.shape, pages.dtype),
        in_specs=[pl.BlockSpec(memory_space=pltpu.SMEM)]
        + [pl.BlockSpec(memory_space=pltpu.VMEM)] * len(chunks)
        + [pl.BlockSpec(memory_space=pl.ANY)],
        out_specs=pl.BlockSpec(memory_space=pl.ANY),
        scratch_shapes=[pltpu.SemaphoreType.DMA((sum(counts),))],
        input_output_aliases={len(chunks) + 1: 0},
        compiler_params=pltpu.CompilerParams(vmem_limit_bytes=2 * size + 2 * MIB),
        cost_estimate=pl.CostEstimate(flops=0, bytes_accessed=4 * size, transcendentals=0),
    )(place, *chunks, pages)


def cut(value):
    return value.astype(jnp.bfloat16).astype(jnp.float32)


def split_stats(peak, total):
    high = cut(peak)
    mid = cut(peak - high)
    return high, mid, peak - high - mid, cut(total), total - cut(total)


def attend_kernel(rows, piece, peers, me_ref, length_ref, *refs):
    query_refs, refs = refs[:peers], refs[peers:]
    key_ref, value_ref, new_key_ref, new_value_ref, token_ref = refs[:5]
    out_refs = refs[5 : 5 + peers]
    bias_ref, new_bias_ref, score_ref, weight_ref, query_ref, result_ref = refs[5 + peers :]
    tokens = key_ref.shape[0]
    step = pl.program_id(0)

    @pl.when(step == 0)
    def _():
        owner = token_ref[0:1, :]
        offset = lax.broadcasted_iota(jnp.int32, owner.shape, 1) % PAGE
        spot = (token_ref[1:2, :] * 32 + token_ref[2:3, :] - 1) * PAGE + offset.astype(jnp.float32)
        request = lax.broadcasted_iota(jnp.int32, (rows, 1), 0) // STEPS
        limit = jnp.zeros((rows, 1), jnp.int32)
        for r in range(rows // STEPS):
            limit = jnp.where(request == r, length_ref[r], limit)
        seen = (owner == request.astype(jnp.float32)) & (spot < limit.astype(jnp.float32))
        bias_ref[...] = jnp.where(seen, 0.0, NEG_FILL)
        row = lax.broadcasted_iota(jnp.int32, new_bias_ref.shape, 0)
        col = lax.broadcasted_iota(jnp.int32, new_bias_ref.shape, 1)
        first = jnp.where((me_ref[0] == 0) & (me_ref[1] == 0), 1, 0)
        seen = (row // STEPS == col // STEPS) & (col <= row) & (col < rows * first)
        new_bias_ref[...] = jnp.where(seen, 0.0, NEG_FILL)
        if peers > 1:
            for d in range(peers):
                query_ref[me_ref[1] ^ d] = query_refs[d][...]

    if peers > 1:
        per_step = query_refs[0].shape[0] // KVH
        query = jnp.concatenate(
            [
                query_ref[n, step * per_step + i].astype(jnp.float32)
                for i in range(per_step)
                for n in range(peers)
            ],
            axis=0,
        ).astype(jnp.bfloat16)
    else:
        query = query_refs[0][0]
    score_ref[:, :tokens] = lax.dot_general(
        query, key_ref[...], NT, preferred_element_type=jnp.float32
    )
    score_ref[:, tokens:] = lax.dot_general(
        query, new_key_ref[...], NT, preferred_element_type=jnp.float32
    )
    together = 1 if rows % 16 == 0 else 2
    span = together * rows
    peaks, totals = [], []
    for c in range(GROUPS // together):
        block = pl.ds(c * span, span)
        old = score_ref[block, :tokens].reshape(together, rows, tokens) * SCALE2 + bias_ref[...]
        new = score_ref[block, tokens:].reshape(together, rows, -1) * SCALE2 + new_bias_ref[...]
        peak = jnp.maximum(
            jnp.max(old, axis=-1, keepdims=True), jnp.max(new, axis=-1, keepdims=True)
        )
        old = jnp.exp2(old - peak)
        new = jnp.exp2(new - peak)
        totals.append(
            (jnp.sum(old, axis=-1, keepdims=True) + jnp.sum(new, axis=-1, keepdims=True)).reshape(
                span, 1
            )
        )
        peaks.append(peak.reshape(span, 1))
        weight_ref[block, :tokens] = old.reshape(span, tokens).astype(jnp.bfloat16)
        weight_ref[block, tokens:] = new.reshape(span, -1).astype(jnp.bfloat16)
    mixed = jnp.dot(
        weight_ref[:, :tokens], value_ref[...], preferred_element_type=jnp.float32
    ) + jnp.dot(weight_ref[:, tokens:], new_value_ref[...], preferred_element_type=jnp.float32)
    peak = jnp.concatenate(peaks, axis=0)
    total = jnp.concatenate(totals, axis=0)
    lane = lax.broadcasted_iota(jnp.int32, (GROUPS * rows, HD), 1)
    stats = jnp.zeros((GROUPS * rows, HD), jnp.float32)
    for i, part in enumerate(split_stats(peak, total)):
        stats = jnp.where(lane == i, part, stats)
    pick = (
        lax.broadcasted_iota(jnp.int32, (STAT, HD), 0)
        == lax.broadcasted_iota(jnp.int32, (STAT, HD), 1)
    ).astype(jnp.bfloat16)
    fill = result_ref.shape[1] - STAT - piece
    for c in range(GROUPS * rows // piece):
        part = slice(c * piece, (c + 1) * piece)
        turned = lax.dot_general(
            pick,
            jnp.concatenate(
                [stats[part], jnp.zeros((HD - piece, HD), jnp.float32)], axis=0
            ).astype(jnp.bfloat16),
            NT,
            preferred_element_type=jnp.float32,
        )
        result_ref[c] = jnp.concatenate(
            [turned, mixed[part], jnp.zeros((fill, HD), jnp.float32)], axis=0
        ).astype(jnp.bfloat16)
    if peers > 1:
        for d, out_ref in enumerate(out_refs):

            @pl.when((step ^ me_ref[1]) == d)
            def _():
                out_ref[...] = result_ref[...]
    else:
        out_refs[0][...] = result_ref[...]


def attend(me, lengths, queries, keyval, pool, token_info, rows, piece):
    tokens = pool.shape[0]
    extra = keyval.shape[0]
    peers = len(queries)
    pieces = GROUPS * rows // piece
    height = STAT + up(piece, 16)
    whole = lambda shape: pl.BlockSpec(shape, lambda k: (0,) * len(shape))
    if peers > 1:
        query_spec = whole(queries[0].shape)
        out_spec = whole((pieces, height, HD))
        out_shape = jax.ShapeDtypeStruct((pieces, height, HD), jnp.bfloat16)
    else:
        query_spec = pl.BlockSpec((1,) + queries[0].shape[1:], lambda k: (k, 0, 0))
        out_spec = pl.BlockSpec((pieces, height, HD), lambda k: (k, 0, 0))
        out_shape = jax.ShapeDtypeStruct((KVH * pieces, height, HD), jnp.bfloat16)
    return pl.pallas_call(
        functools.partial(attend_kernel, rows, piece, peers),
        grid=(KVH,),
        out_shape=[out_shape] * peers,
        in_specs=[pl.BlockSpec(memory_space=pltpu.SMEM)] * 2
        + [query_spec] * peers
        + [
            pl.BlockSpec((tokens, HD), lambda k: (0, k)),
            pl.BlockSpec((tokens, HD), lambda k: (0, KVH + k)),
            pl.BlockSpec((extra, HD), lambda k: (0, k)),
            pl.BlockSpec((extra, HD), lambda k: (0, KVH + k)),
            whole(token_info.shape),
        ],
        out_specs=[out_spec] * peers,
        scratch_shapes=[
            pltpu.VMEM((rows, tokens), jnp.float32),
            pltpu.VMEM((rows, extra), jnp.float32),
            pltpu.VMEM((GROUPS * rows, tokens + extra), jnp.float32),
            pltpu.VMEM((GROUPS * rows, tokens + extra), jnp.bfloat16),
            pltpu.VMEM((peers,) + queries[0].shape, jnp.bfloat16),
            pltpu.VMEM((pieces, height, HD), jnp.bfloat16),
        ],
        compiler_params=pltpu.CompilerParams(vmem_limit_bytes=56 * MIB),
        cost_estimate=pl.CostEstimate(flops=1, bytes_accessed=1, transcendentals=0),
    )(me, lengths, *queries, pool, pool, keyval, keyval, token_info)


def combine_kernel(piece, last, count, *refs):
    if last:
        part_ref, out_ref = refs
        part_refs = [part_ref.at[pl.ds(i, 1)] for i in range(count)]
    else:
        part_refs, out_ref = refs[:count], refs[count]
    groups, height = part_refs[0].shape[:2]
    peaks, totals = [], []
    for i in range(count):
        for j in range(groups):
            stat = part_refs[i][j, :STAT, :].astype(jnp.float32)
            peaks.append(stat[0:1] + stat[1:2] + stat[2:3])
            totals.append(stat[3:4] + stat[4:5])
    peak = jnp.concatenate(peaks, axis=0).reshape(count, groups, HD)
    total = jnp.concatenate(totals, axis=0).reshape(count, groups, HD)
    top = jnp.max(peak, axis=0)
    lead = jnp.exp2(peak - top[None])
    whole = jnp.sum(lead * total, axis=0)
    if last:
        lane = lax.broadcasted_iota(jnp.int32, whole.shape, 1)
        lead = lead / jnp.where(lane < piece, whole, 1.0)[None]
    lead = lead.reshape(count * groups, HD)
    if (count * groups) % HD:
        fill = up(count * groups, HD) - count * groups
        lead = jnp.concatenate([lead, jnp.zeros((fill, HD), jnp.float32)], axis=0)
    lead = jnp.transpose(lead)
    rows = height - STAT
    for j in range(groups):
        result = jnp.zeros((rows, HD), jnp.float32)
        for i in range(count):
            c = i * groups + j
            result = result + lead[:rows, c : c + 1] * part_refs[i][j, STAT:, :].astype(jnp.float32)
        if last:
            for i in range(out_ref.shape[0]):
                out_ref[i] = result[:piece].astype(jnp.bfloat16)
        else:
            stats = split_stats(top[j : j + 1], whole[j : j + 1])
            rest = jnp.zeros((STAT - len(stats), HD), jnp.float32)
            out_ref[j] = jnp.concatenate([*stats, rest, result], axis=0).astype(jnp.bfloat16)


def combine(parts, piece, repeats=0):
    count = parts[0].shape[0] if repeats else len(parts)
    shape = (repeats, piece, HD) if repeats else parts[0].shape
    return pl.pallas_call(
        functools.partial(combine_kernel, piece, repeats > 0, count),
        out_shape=jax.ShapeDtypeStruct(shape, jnp.bfloat16),
        in_specs=[pl.BlockSpec(memory_space=pltpu.VMEM)] * len(parts),
        out_specs=pl.BlockSpec(memory_space=pltpu.VMEM),
        compiler_params=pltpu.CompilerParams(vmem_limit_bytes=8 * MIB),
        cost_estimate=pl.CostEstimate(flops=1, bytes_accessed=1, transcendentals=0),
    )(*parts)


def reorder(shape, unit, valid, own, column):
    first, second = (0, 1) if column else (1, 0)
    block = lax.broadcasted_iota(jnp.int32, shape, second) // unit
    place = lax.broadcasted_iota(jnp.int32, shape, second) % unit
    target = (block ^ own) * valid + place
    match = (lax.broadcasted_iota(jnp.int32, shape, first) == target) & (place < valid)
    return match.astype(jnp.bfloat16)


def project_kernel(peers, me_ref, hidden_ref, query_ref, keyval_ref, *refs):
    out_refs, (full_ref,) = refs[:peers], refs[peers:]
    count, local, depth = hidden_ref.shape
    unit = up(local, 8)
    blocks = []
    for i in range(count):
        blocks.append(hidden_ref[i].astype(jnp.float32))
        if unit > local:
            blocks.append(jnp.zeros((unit - local, depth), jnp.float32))
    hidden = jnp.concatenate(blocks, axis=0).astype(jnp.bfloat16)
    order = reorder((count * local, count * unit), unit, local, 0, True)
    hidden = jnp.dot(order, hidden, preferred_element_type=jnp.float32).astype(jnp.bfloat16)
    full_ref[...] = jnp.dot(hidden, query_ref[...], preferred_element_type=jnp.float32)
    keyval = jnp.dot(hidden, keyval_ref[...], preferred_element_type=jnp.float32)
    for d, out_ref in enumerate(out_refs):
        start = pl.multiple_of((me_ref[1] ^ d) * HD, HD)
        out_ref[:, :HD] = full_ref[:, pl.ds(start, HD)]
        out_ref[:, HD:] = keyval


def pack_kernel(peers, *refs):
    own, tag_ref, out_ref = refs[:peers], refs[peers], refs[peers + 1]
    total = (own[0][...] + own[1][...]) + (own[2][...] + own[3][...])
    tags = jnp.concatenate([tag_ref[...], jnp.zeros_like(tag_ref[...])], axis=1)
    packed = jnp.concatenate([total, tags], axis=0).astype(jnp.bfloat16)
    for i in range(out_ref.shape[0]):
        out_ref[i] = packed


def unpack_kernel(rows, me_ref, kept_ref, part_ref, query_ref, keyval_ref, *refs):
    entry_ref, req_ref, idx_ref = refs
    count = part_ref.shape[0]
    line = lax.broadcasted_iota(jnp.int32, (count, HD), 0)
    tags = jnp.zeros((count, HD), jnp.float32)
    fill = jnp.zeros((keyval_ref.shape[0] - rows, HD), jnp.float32)
    for i in range(count):
        part = part_ref[i].astype(jnp.float32)
        query_ref[i] = part[:rows, :HD].astype(jnp.bfloat16)
        block = jnp.concatenate([part[:rows, HD:], fill], axis=0).astype(jnp.bfloat16)
        keyval_ref[:, i * HD : (i + 1) * HD] = block
        mine = jnp.where(line == me_ref[0], part[rows : rows + count, :HD], 0.0)
        tags = tags + jnp.where(line == i, jnp.sum(mine, axis=0, keepdims=True), 0.0)
    capacity = HD // count
    high = lax.broadcasted_iota(jnp.int32, (HD, HD), 0)
    low = lax.broadcasted_iota(jnp.int32, (HD, HD), 1)
    slot = lax.broadcasted_iota(jnp.int32, (count, HD), 1)
    tags = tags.astype(jnp.bfloat16)
    fields = []
    for i in range(3):
        pick = jnp.where(high == i * capacity + low % capacity, 1.0, 0.0).astype(jnp.bfloat16)
        spread_out = jnp.dot(tags, pick, preferred_element_type=jnp.float32)
        spread_out = jnp.where(slot // capacity == line, spread_out, 0.0)
        fields.append(jnp.sum(spread_out, axis=0, keepdims=True))
    req_ref[...] = fields[0].astype(jnp.int32)
    idx_ref[...] = (fields[1] * 32.0 + fields[2] - 1.0).astype(jnp.int32)
    local = entry_ref.shape[1]
    step = lax.broadcasted_iota(jnp.int32, (16, keyval_ref.shape[0]), 0)
    row = lax.broadcasted_iota(jnp.int32, (16, keyval_ref.shape[0]), 1)
    kept = (row == me_ref[0] * local + step) & (step < kept_ref[me_ref[0]])
    kept = jnp.where(kept, 1.0, 0.0).astype(jnp.bfloat16)
    entries = jnp.dot(kept, keyval_ref[...], preferred_element_type=jnp.float32)
    entry_ref[0] = entries[:local].astype(jnp.bfloat16)


def finish_kernel(peers, me_ref, part_ref, weight_ref, *refs):
    count, rows = part_ref.shape[:2]
    local = rows // peers
    unit = up(local, 16)
    whole = jnp.concatenate([part_ref[i] for i in range(count)], axis=1)
    order = reorder((peers * unit, rows), unit, local, me_ref[1], False)
    mixed = jnp.dot(order, whole, preferred_element_type=jnp.float32)
    mixed = jnp.dot(mixed.astype(jnp.bfloat16), weight_ref[...], preferred_element_type=jnp.float32)
    for d, out_ref in enumerate(refs):
        out_ref[...] = mixed[d * unit : d * unit + local]


def in_vmem(kernel, out_shape, me, *args, scratch=()):
    head = [] if me is None else list(me) if isinstance(me, tuple) else [me]
    return pl.pallas_call(
        kernel,
        out_shape=out_shape,
        in_specs=[pl.BlockSpec(memory_space=pltpu.SMEM)] * len(head)
        + [pl.BlockSpec(memory_space=pltpu.VMEM)] * len(args),
        out_specs=jax.tree.map(lambda _: pl.BlockSpec(memory_space=pltpu.VMEM), out_shape),
        scratch_shapes=scratch,
        compiler_params=pltpu.CompilerParams(vmem_limit_bytes=16 * MIB),
        cost_estimate=pl.CostEstimate(flops=1, bytes_accessed=1, transcendentals=0),
    )(*head, *args)


def group_of(d, wide):
    return d if wide <= 8 or d == 0 else 1 + (d - 1) * 7 // (wide - 1)


def spread(block, axis):
    count = lax.axis_size(axis)
    return lax.all_to_all(
        jnp.broadcast_to(block[None], (count,) + block.shape),
        axis,
        split_axis=0,
        concat_axis=0,
        tiled=True,
    )


def on_device(hidden, w_query, w_keyval, w_out, pool, page_req, page_idx, lengths, moves, accepted):
    wide = lax.axis_size("wide")
    narrow = lax.axis_size("narrow")
    local_rows = hidden.shape[0]
    rows = local_rows * wide
    requests = rows // STEPS
    slots = pool.shape[0]
    capacity = slots // wide
    own_cols = w_query.shape[1] // narrow
    piece = HEADS * rows // (wide * narrow)
    extra = up(rows, HD)
    direct = piece == rows and own_cols == HD and slots == HD
    direct = direct and wide == 8 and narrow == 4 and local_rows == STEPS
    me = lax.axis_index("wide")
    both = jnp.stack([me, lax.axis_index("narrow")])
    exchange = functools.partial(lax.all_to_all, split_axis=0, concat_axis=0, tiled=True)

    def send(block, axis, d):
        return lax.ppermute(block, axis, [(i, i ^ d) for i in range(lax.axis_size(axis))])

    def share(block, axis):
        return [block] + [send(block, axis, d) for d in range(1, lax.axis_size(axis))]

    def deal(blocks, axis):
        return [blocks[0]] + [send(block, axis, d) for d, block in enumerate(blocks) if d]

    gathered = spread(hidden, "wide")

    ahead = AHEAD * capacity // 16
    parts = list(range(0 if ahead else 1, wide))
    moved_pool, tags, token_info, *chunks = order_pages(
        both, moves, page_req, page_idx, pool, wide, ahead, parts
    )
    chunks = dict(zip(parts, chunks))
    arrived = {}
    flying = {}

    def members(groups):
        return [d for group in groups for d in parts if group_of(d, wide) == group]

    def launch(values, *groups):
        taken = members(groups)
        values, sent = lax.optimization_barrier((values, [chunks[d] for d in taken]))
        for d, chunk in zip(taken, sent):
            flying[d] = send(chunk, "wide", d) if d else exchange(chunk, "wide")
        return values

    def land(values, *groups):
        taken = members(groups)
        values, got = lax.optimization_barrier((values, [flying[d] for d in taken]))
        arrived.update(zip(taken, got))
        return values

    def placed(pages):
        taken = sorted(arrived)
        if not taken:
            return pages
        place = []
        for d in taken:
            place += [(me ^ d) * capacity + ahead] if d else [w * capacity for w in range(wide)]
        place = jnp.stack([jnp.asarray(index, jnp.int32) for index in place])
        counts = [1 if d else wide for d in taken]
        pages = place_pages(place, [arrived[d] for d in taken], counts, pages)
        arrived.clear()
        return pages

    gathered, tags = lax.optimization_barrier((gathered, tags))
    tokens = pool.reshape(slots * PAGE, -1)
    if direct:
        block = jax.ShapeDtypeStruct((rows, 2 * HD), jnp.float32)
        partial = in_vmem(
            functools.partial(project_kernel, narrow),
            [block] * narrow,
            both,
            gathered,
            w_query,
            w_keyval,
            scratch=[pltpu.VMEM((rows, narrow * HD), jnp.float32)],
        )
        partial = launch(deal(partial, "narrow"), 6)
        packed = in_vmem(
            functools.partial(pack_kernel, narrow),
            jax.ShapeDtypeStruct((wide, rows + wide, 2 * HD), jnp.bfloat16),
            None,
            *partial,
            tags,
        )
        received = land(exchange(packed, "wide"), 6)
        received = launch(received, 0, 1)
        queries, keyval, new_entries, moved_req, moved_idx = in_vmem(
            functools.partial(unpack_kernel, rows),
            [
                jax.ShapeDtypeStruct((wide, rows, HD), jnp.bfloat16),
                jax.ShapeDtypeStruct((extra, wide * HD), jnp.bfloat16),
                jax.ShapeDtypeStruct((1, local_rows, wide * HD), jnp.bfloat16),
                jax.ShapeDtypeStruct((1, slots), jnp.int32),
                jax.ShapeDtypeStruct((1, slots), jnp.int32),
            ],
            (both, accepted),
            received,
        )
        moved_req, moved_idx = moved_req.reshape(slots), moved_idx.reshape(slots)
        queries = share(queries, "narrow")
    else:
        gathered = gathered.reshape(rows, -1)
        query_part = jnp.dot(gathered, w_query, preferred_element_type=jnp.float32)
        keyval_part = jnp.dot(gathered, w_keyval, preferred_element_type=jnp.float32)
        query_part = jnp.transpose(query_part.reshape(rows, narrow, own_cols), (1, 0, 2))
        partial = jnp.concatenate(
            [query_part, jnp.broadcast_to(keyval_part[None], (narrow,) + keyval_part.shape)], axis=2
        )
        partial = launch(exchange(partial, "narrow"), 6)
        projected = jnp.sum(partial, axis=0).astype(jnp.bfloat16)
        tags = tags[:, : 3 * capacity].astype(jnp.bfloat16)[:, None]
        tags = jnp.pad(tags, ((0, 0), (0, 7), (0, projected.shape[1] - tags.shape[2])))
        packed = jnp.broadcast_to(projected[None], (wide,) + projected.shape)
        packed = jnp.concatenate([packed, tags], axis=1)
        received = land(exchange(packed, "wide"), 6)
        received = launch(received, 0, 1)
        tags_in = received[:, rows]
        queries = received[:, :rows, :own_cols]
        queries = spread(queries, "narrow")
        queries = jnp.transpose(queries, (2, 1, 0, 3)).reshape(rows, HEADS, HD)
        queries = [jnp.transpose(queries, (1, 0, 2)).reshape(KVH, GROUPS * rows, HD)]
        keyval = jnp.transpose(received[:, :rows, own_cols:], (1, 0, 2)).reshape(rows, -1)
        keyval = jnp.pad(keyval, ((0, extra - rows), (0, 0)))
        tags_in = tags_in.astype(jnp.int32)
        moved_req = tags_in[:, :capacity].reshape(slots)
        moved_idx = tags_in[:, capacity : 2 * capacity] * 32
        moved_idx = (moved_idx + tags_in[:, 2 * capacity : 3 * capacity] - 1).reshape(slots)
        local_req = local_rows // STEPS
        fresh = lax.dynamic_slice_in_dim(keyval, me * local_rows, local_rows, 0)
        fresh = fresh.reshape(local_req, STEPS, -1)
        kept = lax.dynamic_slice_in_dim(accepted, me * local_req, local_req, 0)
        step_ids = jnp.arange(STEPS)[None, :, None]
        new_entries = jnp.where(
            step_ids < kept[:, None, None], fresh, jnp.zeros((), jnp.bfloat16)
        )

    queries, moved_pool = lax.optimization_barrier((queries, placed(moved_pool)))
    mixed = attend(both, lengths, queries, keyval, tokens, token_info, rows, piece)
    if direct:
        mixed = land(deal(mixed, "narrow"), 0, 1)
    else:
        mixed = land(exchange(mixed[0], "narrow"), 0, 1)
        mixed = mixed.reshape((narrow, wide) + mixed.shape[1:])
        mixed = [mixed[i] for i in range(narrow)]
    mixed = combine(launch(mixed, 3, 4), piece)
    mixed, pages = lax.optimization_barrier((mixed, moved_pool))
    pages = placed(pages)
    mixed = land(exchange(mixed, "wide"), 3, 4)
    mixed, moved_pool = lax.optimization_barrier((mixed, pages))
    attn = combine([launch(mixed, 2, 5)], piece, wide)
    attn, pages = lax.optimization_barrier((attn, moved_pool))
    pages = placed(pages)
    attn = land(exchange(attn, "wide"), 2, 5)
    attn, moved_pool = lax.optimization_barrier((attn, pages))
    attn = launch(attn, 7)
    if direct:
        sums = in_vmem(
            functools.partial(finish_kernel, narrow),
            [jax.ShapeDtypeStruct((rows // narrow, w_out.shape[1]), jnp.float32)] * narrow,
            both,
            attn,
            w_out,
        )
        sums, pages = lax.optimization_barrier((sums, moved_pool))
        pages = placed(pages)
        sums = land(deal(sums, "narrow"), 7)
        attended = ((sums[0] + sums[1]) + (sums[2] + sums[3])).astype(jnp.bfloat16)
    else:
        attn = jnp.transpose(attn.reshape(-1, rows, HD), (1, 0, 2)).reshape(rows, -1)
        sums = jnp.dot(attn, w_out, preferred_element_type=jnp.float32)
        sums = sums.reshape(narrow, rows // narrow, -1)
        pages = placed(moved_pool)
        sums = land(exchange(sums, "narrow"), 7)
        attended = jnp.sum(sums, axis=0).astype(jnp.bfloat16)
    attended, pages = lax.optimization_barrier((attended, pages))
    moved_pool = placed(pages)
    return (attended, new_entries, moved_pool, moved_req, moved_idx)


def solution(mesh):
    in_specs = (
        P("wide", "narrow"),
        P("narrow", "wide"),
        P("narrow", "wide"),
        P("narrow", "wide"),
        P(("wide", "narrow"), None, None),
        P(("wide", "narrow")),
        P(("wide", "narrow")),
        P(),
        P(("wide", "narrow"), None),
        P(),
    )
    out_specs = (
        P("narrow", "wide"),
        P("wide", None, None),
        P(("wide", "narrow"), None, None),
        P(("wide", "narrow")),
        P(("wide", "narrow")),
    )
    return jax.shard_map(
        on_device, mesh=mesh, in_specs=in_specs, out_specs=out_specs, check_vma=False
    )
```

```python
import functools
import math

import jax
import jax.numpy as jnp
from jax import lax
from jax.experimental import pallas as pl
from jax.experimental.pallas import tpu as pltpu
from jax.sharding import PartitionSpec as P

HEADS = 32
KVH = 4
HD = 128
STEPS = 5
PAGE = 16
GROUPS = HEADS // KVH
NEG_FILL = -1e30
SCALE2 = math.log2(math.e) / math.sqrt(HD)
STAT = 16
MIB = 1024 * 1024
AHEAD = 5
EARLY = 4
NT = (((1,), (1,)), ((), ()))


def up(value, unit):
    return -(-value // unit) * unit


def column(row):
    return jnp.transpose(jnp.broadcast_to(row, (row.shape[1], row.shape[1])))


def order_kernel(
    wide, ahead, parts, me_ref, dest_ref, req_ref, idx_ref, pool_ref, out_ref, tag_ref, token_ref, *refs
):
    chunk_refs, refs = refs[: len(parts)], refs[len(parts) :]
    pages_ref, line_ref, source_ref, in_sem, out_sem, line_sem = refs
    slots = pool_ref.shape[0]
    capacity = slots // wide
    shape = (slots, slots)
    high = lax.broadcasted_iota(jnp.int32, shape, 0)
    low = lax.broadcasted_iota(jnp.int32, shape, 1)
    dest = dest_ref[...]
    same = column(dest.astype(jnp.float32)) == dest.astype(jnp.float32)
    rank = jnp.sum(jnp.where(same & (high < low), 1.0, 0.0), axis=0, keepdims=True)
    rest = capacity - ahead
    early = (dest * ahead).astype(jnp.float32) + rank
    late = ((dest ^ me_ref[0]) * rest + wide * ahead - ahead).astype(jnp.float32) + rank
    moved_to = jnp.where(rank < float(ahead), early, late)
    match = column(moved_to) == low.astype(jnp.float32)
    source = jnp.sum(jnp.where(match, high.astype(jnp.float32), 0.0), axis=0, keepdims=True)
    line_ref[...] = source.astype(jnp.int32)
    copy = pltpu.make_async_copy(line_ref, source_ref, line_sem)
    copy.start()
    copy.wait()

    own = out_ref.at[pl.ds(me_ref[0] * capacity + ahead, rest)]
    blocks = [(wide * ahead, rest, own)]
    for (_, d, first, last), chunk in zip(parts, chunk_refs):
        if d:
            blocks.append((wide * ahead + d * rest + first, last - first, chunk))
        else:
            blocks.insert(0, (first, last - first, chunk))
    for c, (first, count, _) in enumerate(blocks):

        def start(j, carry, c=c):
            page = source_ref[0, j]
            pltpu.make_async_copy(pool_ref.at[page], pages_ref.at[j], in_sem.at[c]).start()
            return carry

        lax.fori_loop(first, first + count, start, 0)

    shifted = idx_ref[...] + 1
    fields = (req_ref[...], shifted // 32, shifted % 32)
    rank_col = column(rank)
    lane = low.astype(jnp.float32)
    spread_out = jnp.zeros(shape, jnp.float32)
    for i, field in enumerate(fields):
        picked = lane == rank_col + float(i * capacity)
        spread_out = spread_out + jnp.where(picked, column(field.astype(jnp.float32)), 0.0)
    line = lax.broadcasted_iota(jnp.int32, (wide, slots), 0)
    chosen = jnp.where(line == dest, 1.0, 0.0).astype(jnp.bfloat16)
    tag_ref[...] = jnp.dot(
        chosen, spread_out.astype(jnp.bfloat16), preferred_element_type=jnp.float32
    )

    tokens = slots * PAGE
    page = lax.broadcasted_iota(jnp.int32, (slots, tokens), 0)
    token = lax.broadcasted_iota(jnp.int32, (slots, tokens), 1)
    widen = jnp.where(page == token // PAGE, 1.0, 0.0).astype(jnp.bfloat16)
    row = lax.broadcasted_iota(jnp.int32, (8, slots), 0)
    stacked = jnp.zeros((8, slots), jnp.float32)
    for i, field in enumerate(fields):
        stacked = jnp.where(row == i, field.astype(jnp.float32), stacked)
    token_ref[...] = jnp.dot(
        stacked.astype(jnp.bfloat16), widen, preferred_element_type=jnp.float32
    )

    copies = []
    for c, (first, count, target) in enumerate(blocks):
        held = pages_ref.at[pl.ds(first, count)]
        pltpu.make_async_copy(pool_ref.at[pl.ds(0, count)], held, in_sem.at[c]).wait()
        copies.append(pltpu.make_async_copy(held, target, out_sem.at[c]))
        copies[-1].start()
    for copy in copies:
        copy.wait()


def order_pages(me, dest, page_req, page_idx, pool, wide, ahead, parts):
    slots = pool.shape[0]
    part = lambda count: jax.ShapeDtypeStruct((count,) + pool.shape[1:], pool.dtype)
    out_shape = [part(slots), jax.ShapeDtypeStruct((wide, slots), jnp.float32)]
    out_shape += [jax.ShapeDtypeStruct((8, slots * PAGE), jnp.float32)]
    out_shape += [part(last - first) for _, _, first, last in parts]
    vmem = pl.BlockSpec(memory_space=pltpu.VMEM)
    hbm = pl.BlockSpec(memory_space=pltpu.HBM)
    return pl.pallas_call(
        functools.partial(order_kernel, wide, ahead, parts),
        out_shape=out_shape,
        in_specs=[pl.BlockSpec(memory_space=pltpu.SMEM), vmem, vmem, vmem, hbm],
        out_specs=[hbm, vmem, vmem] + [hbm] * len(parts),
        scratch_shapes=[
            pltpu.VMEM(pool.shape, pool.dtype),
            pltpu.VMEM((1, slots), jnp.int32),
            pltpu.SMEM((1, slots), jnp.int32),
            pltpu.SemaphoreType.DMA((1 + len(parts),)),
            pltpu.SemaphoreType.DMA((1 + len(parts),)),
            pltpu.SemaphoreType.DMA,
        ],
        compiler_params=pltpu.CompilerParams(vmem_limit_bytes=56 * MIB),
        cost_estimate=pl.CostEstimate(
            flops=0, bytes_accessed=2 * pool.size * 2, transcendentals=0
        ),
    )(me, dest.reshape(1, -1), page_req.reshape(1, -1), page_idx.reshape(1, -1), pool)


def place_kernel(counts, place_ref, *refs):
    in_refs, (out_ref, sem) = refs[:-3], refs[-2:]
    copies = []
    for chunk, count in zip(in_refs, counts):
        depth = chunk.shape[0] // count
        for i in range(count):
            c = len(copies)
            target = out_ref.at[pl.ds(place_ref[c], depth)]
            source = chunk.at[pl.ds(i * depth, depth)]
            copies.append(pltpu.make_async_copy(source, target, sem.at[c]))
    for copy in copies:
        copy.start()
    for copy in copies:
        copy.wait()


def place_pages(place, chunks, counts, pages):
    size = sum(chunk.size for chunk in chunks)
    return pl.pallas_call(
        functools.partial(place_kernel, counts),
        out_shape=jax.ShapeDtypeStruct(pages.shape, pages.dtype),
        in_specs=[pl.BlockSpec(memory_space=pltpu.SMEM)]
        + [pl.BlockSpec(memory_space=pltpu.VMEM)] * len(chunks)
        + [pl.BlockSpec(memory_space=pl.ANY)],
        out_specs=pl.BlockSpec(memory_space=pl.ANY),
        scratch_shapes=[pltpu.SemaphoreType.DMA((sum(counts),))],
        input_output_aliases={len(chunks) + 1: 0},
        compiler_params=pltpu.CompilerParams(vmem_limit_bytes=2 * size + 2 * MIB),
        cost_estimate=pl.CostEstimate(flops=0, bytes_accessed=4 * size, transcendentals=0),
    )(place, *chunks, pages)


def cut(value):
    return value.astype(jnp.bfloat16).astype(jnp.float32)


def split_stats(peak, total):
    high = cut(peak)
    mid = cut(peak - high)
    return high, mid, peak - high - mid, cut(total), total - cut(total)


def attend_kernel(rows, piece, peers, me_ref, length_ref, *refs):
    query_refs, refs = refs[:peers], refs[peers:]
    key_ref, value_ref, new_key_ref, new_value_ref, token_ref = refs[:5]
    out_refs = refs[5 : 5 + peers]
    bias_ref, new_bias_ref, score_ref, weight_ref, query_ref, result_ref = refs[5 + peers :]
    tokens = key_ref.shape[0]
    step = pl.program_id(0)

    @pl.when(step == 0)
    def _():
        owner = token_ref[0:1, :]
        offset = lax.broadcasted_iota(jnp.int32, owner.shape, 1) % PAGE
        spot = (token_ref[1:2, :] * 32 + token_ref[2:3, :] - 1) * PAGE + offset.astype(jnp.float32)
        request = lax.broadcasted_iota(jnp.int32, (rows, 1), 0) // STEPS
        limit = jnp.zeros((rows, 1), jnp.int32)
        for r in range(rows // STEPS):
            limit = jnp.where(request == r, length_ref[r], limit)
        seen = (owner == request.astype(jnp.float32)) & (spot < limit.astype(jnp.float32))
        bias_ref[...] = jnp.where(seen, 0.0, NEG_FILL)
        row = lax.broadcasted_iota(jnp.int32, new_bias_ref.shape, 0)
        col = lax.broadcasted_iota(jnp.int32, new_bias_ref.shape, 1)
        first = jnp.where((me_ref[0] == 0) & (me_ref[1] == 0), 1, 0)
        seen = (row // STEPS == col // STEPS) & (col <= row) & (col < rows * first)
        new_bias_ref[...] = jnp.where(seen, 0.0, NEG_FILL)
        if peers > 1:
            for d in range(peers):
                query_ref[me_ref[1] ^ d] = query_refs[d][...]

    if peers > 1:
        per_step = query_refs[0].shape[0] // KVH
        query = jnp.concatenate(
            [
                query_ref[n, step * per_step + i].astype(jnp.float32)
                for i in range(per_step)
                for n in range(peers)
            ],
            axis=0,
        ).astype(jnp.bfloat16)
    else:
        query = query_refs[0][0]
    score_ref[:, :tokens] = lax.dot_general(
        query, key_ref[...], NT, preferred_element_type=jnp.float32
    )
    score_ref[:, tokens:] = lax.dot_general(
        query, new_key_ref[...], NT, preferred_element_type=jnp.float32
    )
    together = 1 if rows % 16 == 0 else 2
    span = together * rows
    peaks, totals = [], []
    for c in range(GROUPS // together):
        block = pl.ds(c * span, span)
        old = score_ref[block, :tokens].reshape(together, rows, tokens) * SCALE2 + bias_ref[...]
        new = score_ref[block, tokens:].reshape(together, rows, -1) * SCALE2 + new_bias_ref[...]
        peak = jnp.maximum(
            jnp.max(old, axis=-1, keepdims=True), jnp.max(new, axis=-1, keepdims=True)
        )
        old = jnp.exp2(old - peak)
        new = jnp.exp2(new - peak)
        totals.append(
            (jnp.sum(old, axis=-1, keepdims=True) + jnp.sum(new, axis=-1, keepdims=True)).reshape(
                span, 1
            )
        )
        peaks.append(peak.reshape(span, 1))
        weight_ref[block, :tokens] = old.reshape(span, tokens).astype(jnp.bfloat16)
        weight_ref[block, tokens:] = new.reshape(span, -1).astype(jnp.bfloat16)
    mixed = jnp.dot(
        weight_ref[:, :tokens], value_ref[...], preferred_element_type=jnp.float32
    ) + jnp.dot(weight_ref[:, tokens:], new_value_ref[...], preferred_element_type=jnp.float32)
    peak = jnp.concatenate(peaks, axis=0)
    total = jnp.concatenate(totals, axis=0)
    lane = lax.broadcasted_iota(jnp.int32, (GROUPS * rows, HD), 1)
    stats = jnp.zeros((GROUPS * rows, HD), jnp.float32)
    for i, part in enumerate(split_stats(peak, total)):
        stats = jnp.where(lane == i, part, stats)
    pick = (
        lax.broadcasted_iota(jnp.int32, (STAT, HD), 0)
        == lax.broadcasted_iota(jnp.int32, (STAT, HD), 1)
    ).astype(jnp.bfloat16)
    fill = result_ref.shape[1] - STAT - piece
    for c in range(GROUPS * rows // piece):
        part = slice(c * piece, (c + 1) * piece)
        turned = lax.dot_general(
            pick,
            jnp.concatenate(
                [stats[part], jnp.zeros((HD - piece, HD), jnp.float32)], axis=0
            ).astype(jnp.bfloat16),
            NT,
            preferred_element_type=jnp.float32,
        )
        result_ref[c] = jnp.concatenate(
            [turned, mixed[part], jnp.zeros((fill, HD), jnp.float32)], axis=0
        ).astype(jnp.bfloat16)
    if peers > 1:
        for d, out_ref in enumerate(out_refs):

            @pl.when((step ^ me_ref[1]) == d)
            def _():
                out_ref[...] = result_ref[...]
    else:
        out_refs[0][...] = result_ref[...]


def attend(me, lengths, queries, keyval, pool, token_info, rows, piece):
    tokens = pool.shape[0]
    extra = keyval.shape[0]
    peers = len(queries)
    pieces = GROUPS * rows // piece
    height = STAT + up(piece, 16)
    whole = lambda shape: pl.BlockSpec(shape, lambda k: (0,) * len(shape))
    if peers > 1:
        query_spec = whole(queries[0].shape)
        out_spec = whole((pieces, height, HD))
        out_shape = jax.ShapeDtypeStruct((pieces, height, HD), jnp.bfloat16)
    else:
        query_spec = pl.BlockSpec((1,) + queries[0].shape[1:], lambda k: (k, 0, 0))
        out_spec = pl.BlockSpec((pieces, height, HD), lambda k: (k, 0, 0))
        out_shape = jax.ShapeDtypeStruct((KVH * pieces, height, HD), jnp.bfloat16)
    return pl.pallas_call(
        functools.partial(attend_kernel, rows, piece, peers),
        grid=(KVH,),
        out_shape=[out_shape] * peers,
        in_specs=[pl.BlockSpec(memory_space=pltpu.SMEM)] * 2
        + [query_spec] * peers
        + [
            pl.BlockSpec((tokens, HD), lambda k: (0, k)),
            pl.BlockSpec((tokens, HD), lambda k: (0, KVH + k)),
            pl.BlockSpec((extra, HD), lambda k: (0, k)),
            pl.BlockSpec((extra, HD), lambda k: (0, KVH + k)),
            whole(token_info.shape),
        ],
        out_specs=[out_spec] * peers,
        scratch_shapes=[
            pltpu.VMEM((rows, tokens), jnp.float32),
            pltpu.VMEM((rows, extra), jnp.float32),
            pltpu.VMEM((GROUPS * rows, tokens + extra), jnp.float32),
            pltpu.VMEM((GROUPS * rows, tokens + extra), jnp.bfloat16),
            pltpu.VMEM((peers,) + queries[0].shape, jnp.bfloat16),
            pltpu.VMEM((pieces, height, HD), jnp.bfloat16),
        ],
        compiler_params=pltpu.CompilerParams(vmem_limit_bytes=56 * MIB),
        cost_estimate=pl.CostEstimate(flops=1, bytes_accessed=1, transcendentals=0),
    )(me, lengths, *queries, pool, pool, keyval, keyval, token_info)


def combine_kernel(piece, last, count, *refs):
    if last:
        part_ref, out_ref = refs
        part_refs = [part_ref.at[pl.ds(i, 1)] for i in range(count)]
    else:
        part_refs, out_ref = refs[:count], refs[count]
    groups, height = part_refs[0].shape[:2]
    peaks, totals = [], []
    for i in range(count):
        for j in range(groups):
            stat = part_refs[i][j, :STAT, :].astype(jnp.float32)
            peaks.append(stat[0:1] + stat[1:2] + stat[2:3])
            totals.append(stat[3:4] + stat[4:5])
    peak = jnp.concatenate(peaks, axis=0).reshape(count, groups, HD)
    total = jnp.concatenate(totals, axis=0).reshape(count, groups, HD)
    top = jnp.max(peak, axis=0)
    lead = jnp.exp2(peak - top[None])
    whole = jnp.sum(lead * total, axis=0)
    if last:
        lane = lax.broadcasted_iota(jnp.int32, whole.shape, 1)
        lead = lead / jnp.where(lane < piece, whole, 1.0)[None]
    lead = lead.reshape(count * groups, HD)
    if (count * groups) % HD:
        fill = up(count * groups, HD) - count * groups
        lead = jnp.concatenate([lead, jnp.zeros((fill, HD), jnp.float32)], axis=0)
    lead = jnp.transpose(lead)
    rows = height - STAT
    for j in range(groups):
        result = jnp.zeros((rows, HD), jnp.float32)
        for i in range(count):
            c = i * groups + j
            result = result + lead[:rows, c : c + 1] * part_refs[i][j, STAT:, :].astype(jnp.float32)
        if last:
            for i in range(out_ref.shape[0]):
                out_ref[i] = result[:piece].astype(jnp.bfloat16)
        else:
            stats = split_stats(top[j : j + 1], whole[j : j + 1])
            rest = jnp.zeros((STAT - len(stats), HD), jnp.float32)
            out_ref[j] = jnp.concatenate([*stats, rest, result], axis=0).astype(jnp.bfloat16)


def combine(parts, piece, repeats=0):
    count = parts[0].shape[0] if repeats else len(parts)
    shape = (repeats, piece, HD) if repeats else parts[0].shape
    return pl.pallas_call(
        functools.partial(combine_kernel, piece, repeats > 0, count),
        out_shape=jax.ShapeDtypeStruct(shape, jnp.bfloat16),
        in_specs=[pl.BlockSpec(memory_space=pltpu.VMEM)] * len(parts),
        out_specs=pl.BlockSpec(memory_space=pltpu.VMEM),
        compiler_params=pltpu.CompilerParams(vmem_limit_bytes=8 * MIB),
        cost_estimate=pl.CostEstimate(flops=1, bytes_accessed=1, transcendentals=0),
    )(*parts)


def reorder(shape, unit, valid, own, column):
    first, second = (0, 1) if column else (1, 0)
    block = lax.broadcasted_iota(jnp.int32, shape, second) // unit
    place = lax.broadcasted_iota(jnp.int32, shape, second) % unit
    target = (block ^ own) * valid + place
    match = (lax.broadcasted_iota(jnp.int32, shape, first) == target) & (place < valid)
    return match.astype(jnp.bfloat16)


def repeat_kernel(block_ref, out_ref):
    for i in range(out_ref.shape[0]):
        out_ref[i] = block_ref[...]


def project_kernel(peers, me_ref, hidden_ref, query_ref, keyval_ref, *refs):
    out_refs, (full_ref,) = refs[:peers], refs[peers:]
    count, local, depth = hidden_ref.shape
    unit = up(local, 8)
    blocks = []
    for i in range(count):
        blocks.append(hidden_ref[i].astype(jnp.float32))
        if unit > local:
            blocks.append(jnp.zeros((unit - local, depth), jnp.float32))
    hidden = jnp.concatenate(blocks, axis=0).astype(jnp.bfloat16)
    order = reorder((count * local, count * unit), unit, local, 0, True)
    hidden = jnp.dot(order, hidden, preferred_element_type=jnp.float32).astype(jnp.bfloat16)
    full_ref[...] = jnp.dot(hidden, query_ref[...], preferred_element_type=jnp.float32)
    keyval = jnp.dot(hidden, keyval_ref[...], preferred_element_type=jnp.float32)
    for d, out_ref in enumerate(out_refs):
        start = pl.multiple_of((me_ref[1] ^ d) * HD, HD)
        out_ref[:, :HD] = full_ref[:, pl.ds(start, HD)]
        out_ref[:, HD:] = keyval


def pack_kernel(peers, *refs):
    own, tag_ref, out_ref = refs[:peers], refs[peers], refs[peers + 1]
    total = (own[0][...] + own[1][...]) + (own[2][...] + own[3][...])
    tags = jnp.concatenate([tag_ref[...], jnp.zeros_like(tag_ref[...])], axis=1)
    packed = jnp.concatenate([total, tags], axis=0).astype(jnp.bfloat16)
    for i in range(out_ref.shape[0]):
        out_ref[i] = packed


def unpack_kernel(rows, me_ref, kept_ref, part_ref, query_ref, keyval_ref, *refs):
    entry_ref, req_ref, idx_ref = refs
    count = part_ref.shape[0]
    line = lax.broadcasted_iota(jnp.int32, (count, HD), 0)
    tags = jnp.zeros((count, HD), jnp.float32)
    fill = jnp.zeros((keyval_ref.shape[0] - rows, HD), jnp.float32)
    for i in range(count):
        part = part_ref[i].astype(jnp.float32)
        query_ref[i] = part[:rows, :HD].astype(jnp.bfloat16)
        block = jnp.concatenate([part[:rows, HD:], fill], axis=0).astype(jnp.bfloat16)
        keyval_ref[:, i * HD : (i + 1) * HD] = block
        mine = jnp.where(line == me_ref[0], part[rows : rows + count, :HD], 0.0)
        tags = tags + jnp.where(line == i, jnp.sum(mine, axis=0, keepdims=True), 0.0)
    capacity = HD // count
    high = lax.broadcasted_iota(jnp.int32, (HD, HD), 0)
    low = lax.broadcasted_iota(jnp.int32, (HD, HD), 1)
    slot = lax.broadcasted_iota(jnp.int32, (count, HD), 1)
    tags = tags.astype(jnp.bfloat16)
    fields = []
    for i in range(3):
        pick = jnp.where(high == i * capacity + low % capacity, 1.0, 0.0).astype(jnp.bfloat16)
        spread_out = jnp.dot(tags, pick, preferred_element_type=jnp.float32)
        spread_out = jnp.where(slot // capacity == line, spread_out, 0.0)
        fields.append(jnp.sum(spread_out, axis=0, keepdims=True))
    req_ref[...] = fields[0].astype(jnp.int32)
    idx_ref[...] = (fields[1] * 32.0 + fields[2] - 1.0).astype(jnp.int32)
    local = entry_ref.shape[1]
    step = lax.broadcasted_iota(jnp.int32, (16, keyval_ref.shape[0]), 0)
    row = lax.broadcasted_iota(jnp.int32, (16, keyval_ref.shape[0]), 1)
    kept = (row == me_ref[0] * local + step) & (step < kept_ref[me_ref[0]])
    kept = jnp.where(kept, 1.0, 0.0).astype(jnp.bfloat16)
    entries = jnp.dot(kept, keyval_ref[...], preferred_element_type=jnp.float32)
    entry_ref[0] = entries[:local].astype(jnp.bfloat16)


def finish_kernel(peers, me_ref, part_ref, weight_ref, *refs):
    count, rows = part_ref.shape[:2]
    local = rows // peers
    unit = up(local, 16)
    whole = jnp.concatenate([part_ref[i] for i in range(count)], axis=1)
    order = reorder((peers * unit, rows), unit, local, me_ref[1], False)
    mixed = jnp.dot(order, whole, preferred_element_type=jnp.float32)
    mixed = jnp.dot(mixed.astype(jnp.bfloat16), weight_ref[...], preferred_element_type=jnp.float32)
    for d, out_ref in enumerate(refs):
        out_ref[...] = mixed[d * unit : d * unit + local]


def in_vmem(kernel, out_shape, me, *args, scratch=()):
    head = [] if me is None else list(me) if isinstance(me, tuple) else [me]
    return pl.pallas_call(
        kernel,
        out_shape=out_shape,
        in_specs=[pl.BlockSpec(memory_space=pltpu.SMEM)] * len(head)
        + [pl.BlockSpec(memory_space=pltpu.VMEM)] * len(args),
        out_specs=jax.tree.map(lambda _: pl.BlockSpec(memory_space=pltpu.VMEM), out_shape),
        scratch_shapes=scratch,
        compiler_params=pltpu.CompilerParams(vmem_limit_bytes=16 * MIB),
        cost_estimate=pl.CostEstimate(flops=1, bytes_accessed=1, transcendentals=0),
    )(*head, *args)


def group_of(d, wide):
    return d if wide <= 8 or d == 0 else 1 + (d - 1) * 7 // (wide - 1)


def spread(block, axis):
    count = lax.axis_size(axis)
    return lax.all_to_all(
        jnp.broadcast_to(block[None], (count,) + block.shape),
        axis,
        split_axis=0,
        concat_axis=0,
        tiled=True,
    )


def on_device(hidden, w_query, w_keyval, w_out, pool, page_req, page_idx, lengths, moves, accepted):
    wide = lax.axis_size("wide")
    narrow = lax.axis_size("narrow")
    local_rows = hidden.shape[0]
    rows = local_rows * wide
    requests = rows // STEPS
    slots = pool.shape[0]
    capacity = slots // wide
    own_cols = w_query.shape[1] // narrow
    piece = HEADS * rows // (wide * narrow)
    extra = up(rows, HD)
    direct = piece == rows and own_cols == HD and slots == HD
    direct = direct and wide == 8 and narrow == 4 and local_rows == STEPS
    me = lax.axis_index("wide")
    both = jnp.stack([me, lax.axis_index("narrow")])
    exchange = functools.partial(lax.all_to_all, split_axis=0, concat_axis=0, tiled=True)

    def send(block, axis, d):
        return lax.ppermute(block, axis, [(i, i ^ d) for i in range(lax.axis_size(axis))])

    def share(block, axis):
        return [block] + [send(block, axis, d) for d in range(1, lax.axis_size(axis))]

    def deal(blocks, axis):
        return [blocks[0]] + [send(block, axis, d) for d, block in enumerate(blocks) if d]

    copies = jax.ShapeDtypeStruct((wide,) + hidden.shape, hidden.dtype)
    gathered = exchange(in_vmem(repeat_kernel, copies, None, hidden), "wide")

    ahead = AHEAD * capacity // 16
    rest = capacity - ahead
    early = EARLY * rest // (16 - AHEAD)
    parts = [(0, 0, 0, wide * ahead)] if ahead else []
    for d in range(1, wide):
        group = group_of(d, wide)
        cut = early if group == 7 else 0
        if cut:
            parts.append((8, d, 0, cut))
        parts.append((group, d, cut, rest))
    moved_pool, tags, token_info, *chunks = order_pages(
        both, moves, page_req, page_idx, pool, wide, ahead, parts
    )
    arrived = {}
    flying = {}

    def members(groups):
        return [c for group in groups for c, part in enumerate(parts) if part[0] == group]

    def launch(values, *groups):
        taken = members(groups)
        values, sent = lax.optimization_barrier((values, [chunks[c] for c in taken]))
        for c, chunk in zip(taken, sent):
            d = parts[c][1]
            flying[c] = send(chunk, "wide", d) if d else exchange(chunk, "wide")
        return values

    def land(values, *groups):
        taken = members(groups)
        values, got = lax.optimization_barrier((values, [flying[c] for c in taken]))
        arrived.update(zip(taken, got))
        return values

    def placed(pages):
        taken = sorted(arrived)
        if not taken:
            return pages
        place, counts = [], []
        for _, d, first, _ in [parts[c] for c in taken]:
            own = [(me ^ d) * capacity + ahead + first]
            place += own if d else [w * capacity for w in range(wide)]
            counts.append(1 if d else wide)
        place = jnp.stack([jnp.asarray(index, jnp.int32) for index in place])
        pages = place_pages(place, [arrived[c] for c in taken], counts, pages)
        arrived.clear()
        return pages

    gathered, tags = lax.optimization_barrier((gathered, tags))
    tokens = pool.reshape(slots * PAGE, -1)
    if direct:
        block = jax.ShapeDtypeStruct((rows, 2 * HD), jnp.float32)
        partial = in_vmem(
            functools.partial(project_kernel, narrow),
            [block] * narrow,
            both,
            gathered,
            w_query,
            w_keyval,
            scratch=[pltpu.VMEM((rows, narrow * HD), jnp.float32)],
        )
        partial = land(deal(launch(partial, 8), "narrow"), 8)
        partial = launch(partial, 6, 1)
        packed = in_vmem(
            functools.partial(pack_kernel, narrow),
            jax.ShapeDtypeStruct((wide, rows + wide, 2 * HD), jnp.bfloat16),
            None,
            *partial,
            tags,
        )
        received = land(exchange(packed, "wide"), 6, 1)
        received = launch(received, 0)
        queries, keyval, new_entries, moved_req, moved_idx = in_vmem(
            functools.partial(unpack_kernel, rows),
            [
                jax.ShapeDtypeStruct((wide, rows, HD), jnp.bfloat16),
                jax.ShapeDtypeStruct((extra, wide * HD), jnp.bfloat16),
                jax.ShapeDtypeStruct((1, local_rows, wide * HD), jnp.bfloat16),
                jax.ShapeDtypeStruct((1, slots), jnp.int32),
                jax.ShapeDtypeStruct((1, slots), jnp.int32),
            ],
            (both, accepted),
            received,
        )
        moved_req, moved_idx = moved_req.reshape(slots), moved_idx.reshape(slots)
        queries = share(queries, "narrow")
    else:
        gathered = gathered.reshape(rows, -1)
        query_part = jnp.dot(gathered, w_query, preferred_element_type=jnp.float32)
        keyval_part = jnp.dot(gathered, w_keyval, preferred_element_type=jnp.float32)
        query_part = jnp.transpose(query_part.reshape(rows, narrow, own_cols), (1, 0, 2))
        partial = jnp.concatenate(
            [query_part, jnp.broadcast_to(keyval_part[None], (narrow,) + keyval_part.shape)], axis=2
        )
        partial = land(exchange(launch(partial, 8), "narrow"), 8)
        partial = launch(partial, 6, 1)
        projected = jnp.sum(partial, axis=0).astype(jnp.bfloat16)
        tags = tags[:, : 3 * capacity].astype(jnp.bfloat16)[:, None]
        tags = jnp.pad(tags, ((0, 0), (0, 7), (0, projected.shape[1] - tags.shape[2])))
        packed = jnp.broadcast_to(projected[None], (wide,) + projected.shape)
        packed = jnp.concatenate([packed, tags], axis=1)
        received = land(exchange(packed, "wide"), 6, 1)
        received = launch(received, 0)
        tags_in = received[:, rows]
        queries = received[:, :rows, :own_cols]
        queries = spread(queries, "narrow")
        queries = jnp.transpose(queries, (2, 1, 0, 3)).reshape(rows, HEADS, HD)
        queries = [jnp.transpose(queries, (1, 0, 2)).reshape(KVH, GROUPS * rows, HD)]
        keyval = jnp.transpose(received[:, :rows, own_cols:], (1, 0, 2)).reshape(rows, -1)
        keyval = jnp.pad(keyval, ((0, extra - rows), (0, 0)))
        tags_in = tags_in.astype(jnp.int32)
        moved_req = tags_in[:, :capacity].reshape(slots)
        moved_idx = tags_in[:, capacity : 2 * capacity] * 32
        moved_idx = (moved_idx + tags_in[:, 2 * capacity : 3 * capacity] - 1).reshape(slots)
        local_req = local_rows // STEPS
        fresh = lax.dynamic_slice_in_dim(keyval, me * local_rows, local_rows, 0)
        fresh = fresh.reshape(local_req, STEPS, -1)
        kept = lax.dynamic_slice_in_dim(accepted, me * local_req, local_req, 0)
        step_ids = jnp.arange(STEPS)[None, :, None]
        new_entries = jnp.where(
            step_ids < kept[:, None, None], fresh, jnp.zeros((), jnp.bfloat16)
        )

    queries, moved_pool = lax.optimization_barrier((queries, placed(moved_pool)))
    mixed = attend(both, lengths, queries, keyval, tokens, token_info, rows, piece)
    if direct:
        mixed = land(deal(mixed, "narrow"), 0)
    else:
        mixed = land(exchange(mixed[0], "narrow"), 0)
        mixed = mixed.reshape((narrow, wide) + mixed.shape[1:])
        mixed = [mixed[i] for i in range(narrow)]
    mixed = combine(launch(mixed, 3, 4), piece)
    mixed, pages = lax.optimization_barrier((mixed, moved_pool))
    pages = placed(pages)
    mixed = land(exchange(mixed, "wide"), 3, 4)
    mixed, moved_pool = lax.optimization_barrier((mixed, pages))
    attn = combine([launch(mixed, 2, 5)], piece, wide)
    attn, pages = lax.optimization_barrier((attn, moved_pool))
    pages = placed(pages)
    attn = land(exchange(attn, "wide"), 2, 5)
    attn, moved_pool = lax.optimization_barrier((attn, pages))
    attn = launch(attn, 7)
    if direct:
        sums = in_vmem(
            functools.partial(finish_kernel, narrow),
            [jax.ShapeDtypeStruct((rows // narrow, w_out.shape[1]), jnp.float32)] * narrow,
            both,
            attn,
            w_out,
        )
        sums, pages = lax.optimization_barrier((sums, moved_pool))
        pages = placed(pages)
        sums = land(deal(sums, "narrow"), 7)
        attended = ((sums[0] + sums[1]) + (sums[2] + sums[3])).astype(jnp.bfloat16)
    else:
        attn = jnp.transpose(attn.reshape(-1, rows, HD), (1, 0, 2)).reshape(rows, -1)
        sums = jnp.dot(attn, w_out, preferred_element_type=jnp.float32)
        sums = sums.reshape(narrow, rows // narrow, -1)
        pages = placed(moved_pool)
        sums = land(exchange(sums, "narrow"), 7)
        attended = jnp.sum(sums, axis=0).astype(jnp.bfloat16)
    attended, pages = lax.optimization_barrier((attended, pages))
    moved_pool = placed(pages)
    return (attended, new_entries, moved_pool, moved_req, moved_idx)


def solution(mesh):
    in_specs = (
        P("wide", "narrow"),
        P("narrow", "wide"),
        P("narrow", "wide"),
        P("narrow", "wide"),
        P(("wide", "narrow"), None, None),
        P(("wide", "narrow")),
        P(("wide", "narrow")),
        P(),
        P(("wide", "narrow"), None),
        P(),
    )
    out_specs = (
        P("narrow", "wide"),
        P("wide", None, None),
        P(("wide", "narrow"), None, None),
        P(("wide", "narrow")),
        P(("wide", "narrow")),
    )
    return jax.shard_map(
        on_device, mesh=mesh, in_specs=in_specs, out_specs=out_specs, check_vma=False
    )
```

```python
import functools
import math

import jax
import jax.numpy as jnp
from jax import lax
from jax.experimental import pallas as pl
from jax.experimental.pallas import tpu as pltpu
from jax.sharding import PartitionSpec as P

HEADS = 32
KVH = 4
HD = 128
STEPS = 5
PAGE = 16
GROUPS = HEADS // KVH
NEG_FILL = -1e30
SCALE2 = math.log2(math.e) / math.sqrt(HD)
STAT = 16
MIB = 1024 * 1024
AHEAD = 5
EARLY = 4
NT = (((1,), (1,)), ((), ()))


def up(value, unit):
    return -(-value // unit) * unit


def column(row):
    return jnp.transpose(jnp.broadcast_to(row, (row.shape[1], row.shape[1])))


def order_kernel(
    wide, ahead, parts, me_ref, dest_ref, req_ref, idx_ref, pool_ref, out_ref, tag_ref, token_ref, *refs
):
    chunk_refs, refs = refs[: len(parts)], refs[len(parts) :]
    pages_ref, line_ref, source_ref, in_sem, out_sem, line_sem = refs
    slots = pool_ref.shape[0]
    capacity = slots // wide
    shape = (slots, slots)
    high = lax.broadcasted_iota(jnp.int32, shape, 0)
    low = lax.broadcasted_iota(jnp.int32, shape, 1)
    dest = dest_ref[...]
    same = column(dest.astype(jnp.float32)) == dest.astype(jnp.float32)
    rank = jnp.sum(jnp.where(same & (high < low), 1.0, 0.0), axis=0, keepdims=True)
    rest = capacity - ahead
    early = (dest * ahead).astype(jnp.float32) + rank
    late = ((dest ^ me_ref[0]) * rest + wide * ahead - ahead).astype(jnp.float32) + rank
    moved_to = jnp.where(rank < float(ahead), early, late)
    match = column(moved_to) == low.astype(jnp.float32)
    source = jnp.sum(jnp.where(match, high.astype(jnp.float32), 0.0), axis=0, keepdims=True)
    line_ref[...] = source.astype(jnp.int32)
    copy = pltpu.make_async_copy(line_ref, source_ref, line_sem)
    copy.start()
    copy.wait()

    own = out_ref.at[pl.ds(me_ref[0] * capacity + ahead, rest)]
    blocks = [(wide * ahead, rest, own)]
    for (_, d, first, last), chunk in zip(parts, chunk_refs):
        if d:
            blocks.append((wide * ahead + d * rest + first, last - first, chunk))
        else:
            blocks.insert(0, (first, last - first, chunk))
    for c, (first, count, _) in enumerate(blocks):

        def start(j, carry, c=c):
            page = source_ref[0, j]
            pltpu.make_async_copy(pool_ref.at[page], pages_ref.at[j], in_sem.at[c]).start()
            return carry

        lax.fori_loop(first, first + count, start, 0)

    shifted = idx_ref[...] + 1
    fields = (req_ref[...], shifted // 32, shifted % 32)
    rank_col = column(rank)
    lane = low.astype(jnp.float32)
    spread_out = jnp.zeros(shape, jnp.float32)
    for i, field in enumerate(fields):
        picked = lane == rank_col + float(i * capacity)
        spread_out = spread_out + jnp.where(picked, column(field.astype(jnp.float32)), 0.0)
    line = lax.broadcasted_iota(jnp.int32, (wide, slots), 0)
    chosen = jnp.where(line == dest, 1.0, 0.0).astype(jnp.bfloat16)
    tag_ref[...] = jnp.dot(
        chosen, spread_out.astype(jnp.bfloat16), preferred_element_type=jnp.float32
    )

    tokens = slots * PAGE
    page = lax.broadcasted_iota(jnp.int32, (slots, tokens), 0)
    token = lax.broadcasted_iota(jnp.int32, (slots, tokens), 1)
    widen = jnp.where(page == token // PAGE, 1.0, 0.0).astype(jnp.bfloat16)
    row = lax.broadcasted_iota(jnp.int32, (8, slots), 0)
    stacked = jnp.zeros((8, slots), jnp.float32)
    for i, field in enumerate(fields):
        stacked = jnp.where(row == i, field.astype(jnp.float32), stacked)
    token_ref[...] = jnp.dot(
        stacked.astype(jnp.bfloat16), widen, preferred_element_type=jnp.float32
    )

    copies = []
    for c, (first, count, target) in enumerate(blocks):
        held = pages_ref.at[pl.ds(first, count)]
        pltpu.make_async_copy(pool_ref.at[pl.ds(0, count)], held, in_sem.at[c]).wait()
        copies.append(pltpu.make_async_copy(held, target, out_sem.at[c]))
        copies[-1].start()
    for copy in copies:
        copy.wait()


def order_pages(me, dest, page_req, page_idx, pool, wide, ahead, parts):
    slots = pool.shape[0]
    part = lambda count: jax.ShapeDtypeStruct((count,) + pool.shape[1:], pool.dtype)
    out_shape = [part(slots), jax.ShapeDtypeStruct((wide, slots), jnp.float32)]
    out_shape += [jax.ShapeDtypeStruct((8, slots * PAGE), jnp.float32)]
    out_shape += [part(last - first) for _, _, first, last in parts]
    vmem = pl.BlockSpec(memory_space=pltpu.VMEM)
    hbm = pl.BlockSpec(memory_space=pltpu.HBM)
    return pl.pallas_call(
        functools.partial(order_kernel, wide, ahead, parts),
        out_shape=out_shape,
        in_specs=[pl.BlockSpec(memory_space=pltpu.SMEM), vmem, vmem, vmem, hbm],
        out_specs=[hbm, vmem, vmem] + [hbm] * len(parts),
        scratch_shapes=[
            pltpu.VMEM(pool.shape, pool.dtype),
            pltpu.VMEM((1, slots), jnp.int32),
            pltpu.SMEM((1, slots), jnp.int32),
            pltpu.SemaphoreType.DMA((1 + len(parts),)),
            pltpu.SemaphoreType.DMA((1 + len(parts),)),
            pltpu.SemaphoreType.DMA,
        ],
        compiler_params=pltpu.CompilerParams(vmem_limit_bytes=56 * MIB),
        cost_estimate=pl.CostEstimate(
            flops=0, bytes_accessed=2 * pool.size * 2, transcendentals=0
        ),
    )(me, dest.reshape(1, -1), page_req.reshape(1, -1), page_idx.reshape(1, -1), pool)


def place_kernel(counts, place_ref, *refs):
    in_refs, (out_ref, sem) = refs[:-3], refs[-2:]
    copies = []
    for chunk, count in zip(in_refs, counts):
        depth = chunk.shape[0] // count
        for i in range(count):
            c = len(copies)
            target = out_ref.at[pl.ds(place_ref[c], depth)]
            source = chunk.at[pl.ds(i * depth, depth)]
            copies.append(pltpu.make_async_copy(source, target, sem.at[c]))
    for copy in copies:
        copy.start()
    for copy in copies:
        copy.wait()


def place_pages(place, chunks, counts, pages):
    size = sum(chunk.size for chunk in chunks)
    return pl.pallas_call(
        functools.partial(place_kernel, counts),
        out_shape=jax.ShapeDtypeStruct(pages.shape, pages.dtype),
        in_specs=[pl.BlockSpec(memory_space=pltpu.SMEM)]
        + [pl.BlockSpec(memory_space=pltpu.VMEM)] * len(chunks)
        + [pl.BlockSpec(memory_space=pl.ANY)],
        out_specs=pl.BlockSpec(memory_space=pl.ANY),
        scratch_shapes=[pltpu.SemaphoreType.DMA((sum(counts),))],
        input_output_aliases={len(chunks) + 1: 0},
        compiler_params=pltpu.CompilerParams(vmem_limit_bytes=2 * size + 2 * MIB),
        cost_estimate=pl.CostEstimate(flops=0, bytes_accessed=4 * size, transcendentals=0),
    )(place, *chunks, pages)


def cut(value):
    return value.astype(jnp.bfloat16).astype(jnp.float32)


def split_stats(peak, total):
    high = cut(peak)
    mid = cut(peak - high)
    return high, mid, peak - high - mid, cut(total), total - cut(total)


def attend_kernel(rows, piece, peers, me_ref, length_ref, *refs):
    query_refs, refs = refs[:peers], refs[peers:]
    key_ref, value_ref, new_key_ref, new_value_ref, token_ref = refs[:5]
    out_refs = refs[5 : 5 + peers]
    bias_ref, new_bias_ref, score_ref, weight_ref, query_ref, result_ref = refs[5 + peers :]
    tokens = key_ref.shape[0]
    step = pl.program_id(0)

    @pl.when(step == 0)
    def _():
        owner = token_ref[0:1, :]
        offset = lax.broadcasted_iota(jnp.int32, owner.shape, 1) % PAGE
        spot = (token_ref[1:2, :] * 32 + token_ref[2:3, :] - 1) * PAGE + offset.astype(jnp.float32)
        request = lax.broadcasted_iota(jnp.int32, (rows, 1), 0) // STEPS
        limit = jnp.zeros((rows, 1), jnp.int32)
        for r in range(rows // STEPS):
            limit = jnp.where(request == r, length_ref[r], limit)
        seen = (owner == request.astype(jnp.float32)) & (spot < limit.astype(jnp.float32))
        bias_ref[...] = jnp.where(seen, 0.0, NEG_FILL)
        row = lax.broadcasted_iota(jnp.int32, new_bias_ref.shape, 0)
        col = lax.broadcasted_iota(jnp.int32, new_bias_ref.shape, 1)
        first = jnp.where((me_ref[0] == 0) & (me_ref[1] == 0), 1, 0)
        seen = (row // STEPS == col // STEPS) & (col <= row) & (col < rows * first)
        new_bias_ref[...] = jnp.where(seen, 0.0, NEG_FILL)
        if peers > 1:
            for d in range(peers):
                query_ref[me_ref[1] ^ d] = query_refs[d][...]

    if peers > 1:
        per_step = query_refs[0].shape[0] // KVH
        query = jnp.concatenate(
            [
                query_ref[n, step * per_step + i].astype(jnp.float32)
                for i in range(per_step)
                for n in range(peers)
            ],
            axis=0,
        ).astype(jnp.bfloat16)
    else:
        query = query_refs[0][0]
    score_ref[:, :tokens] = lax.dot_general(
        query, key_ref[...], NT, preferred_element_type=jnp.float32
    )
    score_ref[:, tokens:] = lax.dot_general(
        query, new_key_ref[...], NT, preferred_element_type=jnp.float32
    )
    together = 1 if rows % 16 == 0 else 2
    span = together * rows
    peaks, totals = [], []
    for c in range(GROUPS // together):
        block = pl.ds(c * span, span)
        old = score_ref[block, :tokens].reshape(together, rows, tokens) * SCALE2 + bias_ref[...]
        new = score_ref[block, tokens:].reshape(together, rows, -1) * SCALE2 + new_bias_ref[...]
        peak = jnp.maximum(
            jnp.max(old, axis=-1, keepdims=True), jnp.max(new, axis=-1, keepdims=True)
        )
        old = jnp.exp2(old - peak)
        new = jnp.exp2(new - peak)
        totals.append(
            (jnp.sum(old, axis=-1, keepdims=True) + jnp.sum(new, axis=-1, keepdims=True)).reshape(
                span, 1
            )
        )
        peaks.append(peak.reshape(span, 1))
        weight_ref[block, :tokens] = old.reshape(span, tokens).astype(jnp.bfloat16)
        weight_ref[block, tokens:] = new.reshape(span, -1).astype(jnp.bfloat16)
    mixed = jnp.dot(
        weight_ref[:, :tokens], value_ref[...], preferred_element_type=jnp.float32
    ) + jnp.dot(weight_ref[:, tokens:], new_value_ref[...], preferred_element_type=jnp.float32)
    peak = jnp.concatenate(peaks, axis=0)
    total = jnp.concatenate(totals, axis=0)
    lane = lax.broadcasted_iota(jnp.int32, (GROUPS * rows, HD), 1)
    stats = jnp.zeros((GROUPS * rows, HD), jnp.float32)
    for i, part in enumerate(split_stats(peak, total)):
        stats = jnp.where(lane == i, part, stats)
    pick = (
        lax.broadcasted_iota(jnp.int32, (STAT, HD), 0)
        == lax.broadcasted_iota(jnp.int32, (STAT, HD), 1)
    ).astype(jnp.bfloat16)
    fill = result_ref.shape[1] - STAT - piece
    for c in range(GROUPS * rows // piece):
        part = slice(c * piece, (c + 1) * piece)
        turned = lax.dot_general(
            pick,
            jnp.concatenate(
                [stats[part], jnp.zeros((HD - piece, HD), jnp.float32)], axis=0
            ).astype(jnp.bfloat16),
            NT,
            preferred_element_type=jnp.float32,
        )
        result_ref[c] = jnp.concatenate(
            [turned, mixed[part], jnp.zeros((fill, HD), jnp.float32)], axis=0
        ).astype(jnp.bfloat16)
    if peers > 1:
        for d, out_ref in enumerate(out_refs):

            @pl.when((step ^ me_ref[1]) == d)
            def _():
                out_ref[...] = result_ref[...]
    else:
        out_refs[0][...] = result_ref[...]


def attend(me, lengths, queries, keyval, pool, token_info, rows, piece):
    tokens = pool.shape[0]
    extra = keyval.shape[0]
    peers = len(queries)
    pieces = GROUPS * rows // piece
    height = STAT + up(piece, 16)
    whole = lambda shape: pl.BlockSpec(shape, lambda k: (0,) * len(shape))
    if peers > 1:
        query_spec = whole(queries[0].shape)
        out_spec = whole((pieces, height, HD))
        out_shape = jax.ShapeDtypeStruct((pieces, height, HD), jnp.bfloat16)
    else:
        query_spec = pl.BlockSpec((1,) + queries[0].shape[1:], lambda k: (k, 0, 0))
        out_spec = pl.BlockSpec((pieces, height, HD), lambda k: (k, 0, 0))
        out_shape = jax.ShapeDtypeStruct((KVH * pieces, height, HD), jnp.bfloat16)
    return pl.pallas_call(
        functools.partial(attend_kernel, rows, piece, peers),
        grid=(KVH,),
        out_shape=[out_shape] * peers,
        in_specs=[pl.BlockSpec(memory_space=pltpu.SMEM)] * 2
        + [query_spec] * peers
        + [
            pl.BlockSpec((tokens, HD), lambda k: (0, k)),
            pl.BlockSpec((tokens, HD), lambda k: (0, KVH + k)),
            pl.BlockSpec((extra, HD), lambda k: (0, k)),
            pl.BlockSpec((extra, HD), lambda k: (0, KVH + k)),
            whole(token_info.shape),
        ],
        out_specs=[out_spec] * peers,
        scratch_shapes=[
            pltpu.VMEM((rows, tokens), jnp.float32),
            pltpu.VMEM((rows, extra), jnp.float32),
            pltpu.VMEM((GROUPS * rows, tokens + extra), jnp.float32),
            pltpu.VMEM((GROUPS * rows, tokens + extra), jnp.bfloat16),
            pltpu.VMEM((peers,) + queries[0].shape, jnp.bfloat16),
            pltpu.VMEM((pieces, height, HD), jnp.bfloat16),
        ],
        compiler_params=pltpu.CompilerParams(vmem_limit_bytes=56 * MIB),
        cost_estimate=pl.CostEstimate(flops=1, bytes_accessed=1, transcendentals=0),
    )(me, lengths, *queries, pool, pool, keyval, keyval, token_info)


def combine_kernel(piece, last, count, *refs):
    if last:
        part_ref, out_ref = refs
        part_refs = [part_ref.at[pl.ds(i, 1)] for i in range(count)]
    else:
        part_refs, out_ref = refs[:count], refs[count]
    groups, height = part_refs[0].shape[:2]
    peaks, totals = [], []
    for i in range(count):
        for j in range(groups):
            stat = part_refs[i][j, :STAT, :].astype(jnp.float32)
            peaks.append(stat[0:1] + stat[1:2] + stat[2:3])
            totals.append(stat[3:4] + stat[4:5])
    peak = jnp.concatenate(peaks, axis=0).reshape(count, groups, HD)
    total = jnp.concatenate(totals, axis=0).reshape(count, groups, HD)
    top = jnp.max(peak, axis=0)
    lead = jnp.exp2(peak - top[None])
    whole = jnp.sum(lead * total, axis=0)
    if last:
        lane = lax.broadcasted_iota(jnp.int32, whole.shape, 1)
        lead = lead / jnp.where(lane < piece, whole, 1.0)[None]
    lead = lead.reshape(count * groups, HD)
    if (count * groups) % HD:
        fill = up(count * groups, HD) - count * groups
        lead = jnp.concatenate([lead, jnp.zeros((fill, HD), jnp.float32)], axis=0)
    lead = jnp.transpose(lead)
    rows = height - STAT
    for j in range(groups):
        result = jnp.zeros((rows, HD), jnp.float32)
        for i in range(count):
            c = i * groups + j
            result = result + lead[:rows, c : c + 1] * part_refs[i][j, STAT:, :].astype(jnp.float32)
        if last:
            for i in range(out_ref.shape[0]):
                out_ref[i] = result[:piece].astype(jnp.bfloat16)
        else:
            stats = split_stats(top[j : j + 1], whole[j : j + 1])
            rest = jnp.zeros((STAT - len(stats), HD), jnp.float32)
            out_ref[j] = jnp.concatenate([*stats, rest, result], axis=0).astype(jnp.bfloat16)


def combine(parts, piece, repeats=0):
    count = parts[0].shape[0] if repeats else len(parts)
    shape = (repeats, piece, HD) if repeats else parts[0].shape
    return pl.pallas_call(
        functools.partial(combine_kernel, piece, repeats > 0, count),
        out_shape=jax.ShapeDtypeStruct(shape, jnp.bfloat16),
        in_specs=[pl.BlockSpec(memory_space=pltpu.VMEM)] * len(parts),
        out_specs=pl.BlockSpec(memory_space=pltpu.VMEM),
        compiler_params=pltpu.CompilerParams(vmem_limit_bytes=8 * MIB),
        cost_estimate=pl.CostEstimate(flops=1, bytes_accessed=1, transcendentals=0),
    )(*parts)


def reorder(shape, unit, valid, own, column):
    first, second = (0, 1) if column else (1, 0)
    block = lax.broadcasted_iota(jnp.int32, shape, second) // unit
    place = lax.broadcasted_iota(jnp.int32, shape, second) % unit
    target = (block ^ own) * valid + place
    match = (lax.broadcasted_iota(jnp.int32, shape, first) == target) & (place < valid)
    return match.astype(jnp.bfloat16)


def repeat_kernel(block_ref, out_ref):
    for i in range(out_ref.shape[0]):
        out_ref[i] = block_ref[...]


def project_kernel(peers, me_ref, hidden_ref, query_ref, keyval_ref, *refs):
    out_refs, (full_ref,) = refs[:peers], refs[peers:]
    count, local, depth = hidden_ref.shape
    unit = up(local, 8)
    blocks = []
    for i in range(count):
        blocks.append(hidden_ref[i].astype(jnp.float32))
        if unit > local:
            blocks.append(jnp.zeros((unit - local, depth), jnp.float32))
    hidden = jnp.concatenate(blocks, axis=0).astype(jnp.bfloat16)
    order = reorder((count * local, count * unit), unit, local, 0, True)
    hidden = jnp.dot(order, hidden, preferred_element_type=jnp.float32).astype(jnp.bfloat16)
    full_ref[...] = jnp.dot(hidden, query_ref[...], preferred_element_type=jnp.float32)
    keyval = jnp.dot(hidden, keyval_ref[...], preferred_element_type=jnp.float32)
    for d, out_ref in enumerate(out_refs):
        start = pl.multiple_of((me_ref[1] ^ d) * HD, HD)
        out_ref[:, :HD] = full_ref[:, pl.ds(start, HD)]
        out_ref[:, HD:] = keyval


def pack_kernel(peers, *refs):
    own, tag_ref, out_ref = refs[:peers], refs[peers], refs[peers + 1]
    total = (own[0][...] + own[1][...]) + (own[2][...] + own[3][...])
    tags = jnp.concatenate([tag_ref[...], jnp.zeros_like(tag_ref[...])], axis=1)
    packed = jnp.concatenate([total, tags], axis=0).astype(jnp.bfloat16)
    for i in range(out_ref.shape[0]):
        out_ref[i] = packed


def unpack_kernel(rows, me_ref, kept_ref, part_ref, query_ref, keyval_ref, *refs):
    entry_ref, req_ref, idx_ref = refs
    count = part_ref.shape[0]
    line = lax.broadcasted_iota(jnp.int32, (count, HD), 0)
    tags = jnp.zeros((count, HD), jnp.float32)
    fill = jnp.zeros((keyval_ref.shape[0] - rows, HD), jnp.float32)
    for i in range(count):
        part = part_ref[i].astype(jnp.float32)
        query_ref[i] = part[:rows, :HD].astype(jnp.bfloat16)
        block = jnp.concatenate([part[:rows, HD:], fill], axis=0).astype(jnp.bfloat16)
        keyval_ref[:, i * HD : (i + 1) * HD] = block
        mine = jnp.where(line == me_ref[0], part[rows : rows + count, :HD], 0.0)
        tags = tags + jnp.where(line == i, jnp.sum(mine, axis=0, keepdims=True), 0.0)
    capacity = HD // count
    high = lax.broadcasted_iota(jnp.int32, (HD, HD), 0)
    low = lax.broadcasted_iota(jnp.int32, (HD, HD), 1)
    slot = lax.broadcasted_iota(jnp.int32, (count, HD), 1)
    tags = tags.astype(jnp.bfloat16)
    fields = []
    for i in range(3):
        pick = jnp.where(high == i * capacity + low % capacity, 1.0, 0.0).astype(jnp.bfloat16)
        spread_out = jnp.dot(tags, pick, preferred_element_type=jnp.float32)
        spread_out = jnp.where(slot // capacity == line, spread_out, 0.0)
        fields.append(jnp.sum(spread_out, axis=0, keepdims=True))
    req_ref[...] = fields[0].astype(jnp.int32)
    idx_ref[...] = (fields[1] * 32.0 + fields[2] - 1.0).astype(jnp.int32)
    local = entry_ref.shape[1]
    step = lax.broadcasted_iota(jnp.int32, (16, keyval_ref.shape[0]), 0)
    row = lax.broadcasted_iota(jnp.int32, (16, keyval_ref.shape[0]), 1)
    kept = (row == me_ref[0] * local + step) & (step < kept_ref[me_ref[0]])
    kept = jnp.where(kept, 1.0, 0.0).astype(jnp.bfloat16)
    entries = jnp.dot(kept, keyval_ref[...], preferred_element_type=jnp.float32)
    entry_ref[0] = entries[:local].astype(jnp.bfloat16)


def finish_kernel(peers, me_ref, part_ref, weight_ref, *refs):
    count, rows = part_ref.shape[:2]
    local = rows // peers
    unit = up(local, 16)
    whole = jnp.concatenate([part_ref[i] for i in range(count)], axis=1)
    order = reorder((peers * unit, rows), unit, local, me_ref[1], False)
    mixed = jnp.dot(order, whole, preferred_element_type=jnp.float32)
    mixed = jnp.dot(mixed.astype(jnp.bfloat16), weight_ref[...], preferred_element_type=jnp.float32)
    for d, out_ref in enumerate(refs):
        out_ref[...] = mixed[d * unit : d * unit + local]


def in_vmem(kernel, out_shape, me, *args, scratch=()):
    head = [] if me is None else list(me) if isinstance(me, tuple) else [me]
    return pl.pallas_call(
        kernel,
        out_shape=out_shape,
        in_specs=[pl.BlockSpec(memory_space=pltpu.SMEM)] * len(head)
        + [pl.BlockSpec(memory_space=pltpu.VMEM)] * len(args),
        out_specs=jax.tree.map(lambda _: pl.BlockSpec(memory_space=pltpu.VMEM), out_shape),
        scratch_shapes=scratch,
        compiler_params=pltpu.CompilerParams(vmem_limit_bytes=16 * MIB),
        cost_estimate=pl.CostEstimate(flops=1, bytes_accessed=1, transcendentals=0),
    )(*head, *args)


def group_of(d, wide):
    return d if wide <= 8 or d == 0 else 1 + (d - 1) * 7 // (wide - 1)


def spread(block, axis):
    count = lax.axis_size(axis)
    return lax.all_to_all(
        jnp.broadcast_to(block[None], (count,) + block.shape),
        axis,
        split_axis=0,
        concat_axis=0,
        tiled=True,
    )


def on_device(hidden, w_query, w_keyval, w_out, pool, page_req, page_idx, lengths, moves, accepted):
    wide = lax.axis_size("wide")
    narrow = lax.axis_size("narrow")
    local_rows = hidden.shape[0]
    rows = local_rows * wide
    requests = rows // STEPS
    slots = pool.shape[0]
    capacity = slots // wide
    own_cols = w_query.shape[1] // narrow
    piece = HEADS * rows // (wide * narrow)
    extra = up(rows, HD)
    direct = piece == rows and own_cols == HD and slots == HD
    direct = direct and wide == 8 and narrow == 4 and local_rows == STEPS
    me = lax.axis_index("wide")
    both = jnp.stack([me, lax.axis_index("narrow")])
    exchange = functools.partial(lax.all_to_all, split_axis=0, concat_axis=0, tiled=True)

    def send(block, axis, d):
        return lax.ppermute(block, axis, [(i, i ^ d) for i in range(lax.axis_size(axis))])

    def share(block, axis):
        return [block] + [send(block, axis, d) for d in range(1, lax.axis_size(axis))]

    def deal(blocks, axis):
        return [blocks[0]] + [send(block, axis, d) for d, block in enumerate(blocks) if d]

    copies = jax.ShapeDtypeStruct((wide,) + hidden.shape, hidden.dtype)
    gathered = exchange(in_vmem(repeat_kernel, copies, None, hidden), "wide")

    ahead = AHEAD * capacity // 16
    rest = capacity - ahead
    early = EARLY * rest // (16 - AHEAD)
    parts = [(0, 0, 0, wide * ahead)] if ahead else []
    for d in range(1, wide):
        group = group_of(d, wide)
        cut = early if group == 7 else 0
        if cut:
            parts.append((8, d, 0, cut))
        parts.append((group, d, cut, rest))
    moved_pool, tags, token_info, *chunks = order_pages(
        both, moves, page_req, page_idx, pool, wide, ahead, parts
    )
    arrived = {}
    flying = {}

    def members(groups):
        return [c for group in groups for c, part in enumerate(parts) if part[0] == group]

    def launch(values, *groups):
        taken = members(groups)
        values, sent = lax.optimization_barrier((values, [chunks[c] for c in taken]))
        for c, chunk in zip(taken, sent):
            d = parts[c][1]
            flying[c] = send(chunk, "wide", d) if d else exchange(chunk, "wide")
        return values

    def land(values, *groups):
        taken = members(groups)
        values, got = lax.optimization_barrier((values, [flying[c] for c in taken]))
        arrived.update(zip(taken, got))
        return values

    def placed(pages):
        taken = sorted(arrived)
        if not taken:
            return pages
        place, counts = [], []
        for _, d, first, _ in [parts[c] for c in taken]:
            own = [(me ^ d) * capacity + ahead + first]
            place += own if d else [w * capacity for w in range(wide)]
            counts.append(1 if d else wide)
        place = jnp.stack([jnp.asarray(index, jnp.int32) for index in place])
        pages = place_pages(place, [arrived[c] for c in taken], counts, pages)
        arrived.clear()
        return pages

    gathered, tags = lax.optimization_barrier((gathered, tags))
    tokens = pool.reshape(slots * PAGE, -1)
    if direct:
        block = jax.ShapeDtypeStruct((rows, 2 * HD), jnp.float32)
        partial = in_vmem(
            functools.partial(project_kernel, narrow),
            [block] * narrow,
            both,
            gathered,
            w_query,
            w_keyval,
            scratch=[pltpu.VMEM((rows, narrow * HD), jnp.float32)],
        )
        partial = land(deal(launch(partial, 8, 6), "narrow"), 8)
        partial = launch(partial, 1)
        packed = in_vmem(
            functools.partial(pack_kernel, narrow),
            jax.ShapeDtypeStruct((wide, rows + wide, 2 * HD), jnp.bfloat16),
            None,
            *partial,
            tags,
        )
        received = land(exchange(packed, "wide"), 6, 1)
        received = launch(received, 0)
        queries, keyval, new_entries, moved_req, moved_idx = in_vmem(
            functools.partial(unpack_kernel, rows),
            [
                jax.ShapeDtypeStruct((wide, rows, HD), jnp.bfloat16),
                jax.ShapeDtypeStruct((extra, wide * HD), jnp.bfloat16),
                jax.ShapeDtypeStruct((1, local_rows, wide * HD), jnp.bfloat16),
                jax.ShapeDtypeStruct((1, slots), jnp.int32),
                jax.ShapeDtypeStruct((1, slots), jnp.int32),
            ],
            (both, accepted),
            received,
        )
        moved_req, moved_idx = moved_req.reshape(slots), moved_idx.reshape(slots)
        queries = share(queries, "narrow")
    else:
        gathered = gathered.reshape(rows, -1)
        query_part = jnp.dot(gathered, w_query, preferred_element_type=jnp.float32)
        keyval_part = jnp.dot(gathered, w_keyval, preferred_element_type=jnp.float32)
        query_part = jnp.transpose(query_part.reshape(rows, narrow, own_cols), (1, 0, 2))
        partial = jnp.concatenate(
            [query_part, jnp.broadcast_to(keyval_part[None], (narrow,) + keyval_part.shape)], axis=2
        )
        partial = land(exchange(launch(partial, 8, 6), "narrow"), 8)
        partial = launch(partial, 1)
        projected = jnp.sum(partial, axis=0).astype(jnp.bfloat16)
        tags = tags[:, : 3 * capacity].astype(jnp.bfloat16)[:, None]
        tags = jnp.pad(tags, ((0, 0), (0, 7), (0, projected.shape[1] - tags.shape[2])))
        packed = jnp.broadcast_to(projected[None], (wide,) + projected.shape)
        packed = jnp.concatenate([packed, tags], axis=1)
        received = land(exchange(packed, "wide"), 6, 1)
        received = launch(received, 0)
        tags_in = received[:, rows]
        queries = received[:, :rows, :own_cols]
        queries = spread(queries, "narrow")
        queries = jnp.transpose(queries, (2, 1, 0, 3)).reshape(rows, HEADS, HD)
        queries = [jnp.transpose(queries, (1, 0, 2)).reshape(KVH, GROUPS * rows, HD)]
        keyval = jnp.transpose(received[:, :rows, own_cols:], (1, 0, 2)).reshape(rows, -1)
        keyval = jnp.pad(keyval, ((0, extra - rows), (0, 0)))
        tags_in = tags_in.astype(jnp.int32)
        moved_req = tags_in[:, :capacity].reshape(slots)
        moved_idx = tags_in[:, capacity : 2 * capacity] * 32
        moved_idx = (moved_idx + tags_in[:, 2 * capacity : 3 * capacity] - 1).reshape(slots)
        local_req = local_rows // STEPS
        fresh = lax.dynamic_slice_in_dim(keyval, me * local_rows, local_rows, 0)
        fresh = fresh.reshape(local_req, STEPS, -1)
        kept = lax.dynamic_slice_in_dim(accepted, me * local_req, local_req, 0)
        step_ids = jnp.arange(STEPS)[None, :, None]
        new_entries = jnp.where(
            step_ids < kept[:, None, None], fresh, jnp.zeros((), jnp.bfloat16)
        )

    queries, moved_pool = lax.optimization_barrier((queries, placed(moved_pool)))
    mixed = attend(both, lengths, queries, keyval, tokens, token_info, rows, piece)
    mixed = launch(mixed, 3, 4)
    if direct:
        mixed = land(deal(mixed, "narrow"), 0)
    else:
        mixed = land(exchange(mixed[0], "narrow"), 0)
        mixed = mixed.reshape((narrow, wide) + mixed.shape[1:])
        mixed = [mixed[i] for i in range(narrow)]
    mixed = combine(mixed, piece)
    mixed, pages = lax.optimization_barrier((mixed, moved_pool))
    pages = placed(pages)
    mixed = land(exchange(mixed, "wide"), 3, 4)
    mixed, moved_pool = lax.optimization_barrier((mixed, pages))
    attn = combine([launch(mixed, 2, 5)], piece, wide)
    attn, pages = lax.optimization_barrier((attn, moved_pool))
    pages = placed(pages)
    attn = land(exchange(attn, "wide"), 2, 5)
    attn, moved_pool = lax.optimization_barrier((attn, pages))
    attn = launch(attn, 7)
    if direct:
        sums = in_vmem(
            functools.partial(finish_kernel, narrow),
            [jax.ShapeDtypeStruct((rows // narrow, w_out.shape[1]), jnp.float32)] * narrow,
            both,
            attn,
            w_out,
        )
        sums, pages = lax.optimization_barrier((sums, moved_pool))
        pages = placed(pages)
        sums = land(deal(sums, "narrow"), 7)
        attended = ((sums[0] + sums[1]) + (sums[2] + sums[3])).astype(jnp.bfloat16)
    else:
        attn = jnp.transpose(attn.reshape(-1, rows, HD), (1, 0, 2)).reshape(rows, -1)
        sums = jnp.dot(attn, w_out, preferred_element_type=jnp.float32)
        sums = sums.reshape(narrow, rows // narrow, -1)
        pages = placed(moved_pool)
        sums = land(exchange(sums, "narrow"), 7)
        attended = jnp.sum(sums, axis=0).astype(jnp.bfloat16)
    attended, pages = lax.optimization_barrier((attended, pages))
    moved_pool = placed(pages)
    return (attended, new_entries, moved_pool, moved_req, moved_idx)


def solution(mesh):
    in_specs = (
        P("wide", "narrow"),
        P("narrow", "wide"),
        P("narrow", "wide"),
        P("narrow", "wide"),
        P(("wide", "narrow"), None, None),
        P(("wide", "narrow")),
        P(("wide", "narrow")),
        P(),
        P(("wide", "narrow"), None),
        P(),
    )
    out_specs = (
        P("narrow", "wide"),
        P("wide", None, None),
        P(("wide", "narrow"), None, None),
        P(("wide", "narrow")),
        P(("wide", "narrow")),
    )
    return jax.shard_map(
        on_device, mesh=mesh, in_specs=in_specs, out_specs=out_specs, check_vma=False
    )
```

```python
import functools
import math

import jax
import jax.numpy as jnp
from jax import lax
from jax.experimental import pallas as pl
from jax.experimental.pallas import tpu as pltpu
from jax.sharding import PartitionSpec as P

HEADS = 32
KVH = 4
HD = 128
STEPS = 5
PAGE = 16
GROUPS = HEADS // KVH
NEG_FILL = -1e30
SCALE2 = math.log2(math.e) / math.sqrt(HD)
STAT = 16
MIB = 1024 * 1024
AHEAD = 5
EARLY = 4
NT = (((1,), (1,)), ((), ()))


def up(value, unit):
    return -(-value // unit) * unit


def column(row):
    return jnp.transpose(jnp.broadcast_to(row, (row.shape[1], row.shape[1])))


def order_kernel(
    wide, ahead, parts, me_ref, dest_ref, req_ref, idx_ref, pool_ref, out_ref, tag_ref, token_ref, *refs
):
    chunk_refs, refs = refs[: len(parts)], refs[len(parts) :]
    pages_ref, line_ref, source_ref, in_sem, out_sem, line_sem = refs
    slots = pool_ref.shape[0]
    capacity = slots // wide
    shape = (slots, slots)
    high = lax.broadcasted_iota(jnp.int32, shape, 0)
    low = lax.broadcasted_iota(jnp.int32, shape, 1)
    dest = dest_ref[...]
    same = column(dest.astype(jnp.float32)) == dest.astype(jnp.float32)
    rank = jnp.sum(jnp.where(same & (high < low), 1.0, 0.0), axis=0, keepdims=True)
    rest = capacity - ahead
    early = (dest * ahead).astype(jnp.float32) + rank
    late = ((dest ^ me_ref[0]) * rest + wide * ahead - ahead).astype(jnp.float32) + rank
    moved_to = jnp.where(rank < float(ahead), early, late)
    match = column(moved_to) == low.astype(jnp.float32)
    source = jnp.sum(jnp.where(match, high.astype(jnp.float32), 0.0), axis=0, keepdims=True)
    line_ref[...] = source.astype(jnp.int32)
    copy = pltpu.make_async_copy(line_ref, source_ref, line_sem)
    copy.start()
    copy.wait()

    own = out_ref.at[pl.ds(me_ref[0] * capacity + ahead, rest)]
    blocks = [(wide * ahead, rest, own)]
    for (_, d, first, last), chunk in zip(parts, chunk_refs):
        if d:
            blocks.append((wide * ahead + d * rest + first, last - first, chunk))
        else:
            blocks.insert(0, (first, last - first, chunk))
    for c, (first, count, _) in enumerate(blocks):

        def start(j, carry, c=c):
            page = source_ref[0, j]
            pltpu.make_async_copy(pool_ref.at[page], pages_ref.at[j], in_sem.at[c]).start()
            return carry

        lax.fori_loop(first, first + count, start, 0)

    shifted = idx_ref[...] + 1
    fields = (req_ref[...], shifted // 32, shifted % 32)
    rank_col = column(rank)
    lane = low.astype(jnp.float32)
    spread_out = jnp.zeros(shape, jnp.float32)
    for i, field in enumerate(fields):
        picked = lane == rank_col + float(i * capacity)
        spread_out = spread_out + jnp.where(picked, column(field.astype(jnp.float32)), 0.0)
    line = lax.broadcasted_iota(jnp.int32, (wide, slots), 0)
    chosen = jnp.where(line == dest, 1.0, 0.0).astype(jnp.bfloat16)
    tag_ref[...] = jnp.dot(
        chosen, spread_out.astype(jnp.bfloat16), preferred_element_type=jnp.float32
    )

    tokens = slots * PAGE
    page = lax.broadcasted_iota(jnp.int32, (slots, tokens), 0)
    token = lax.broadcasted_iota(jnp.int32, (slots, tokens), 1)
    widen = jnp.where(page == token // PAGE, 1.0, 0.0).astype(jnp.bfloat16)
    row = lax.broadcasted_iota(jnp.int32, (8, slots), 0)
    stacked = jnp.zeros((8, slots), jnp.float32)
    for i, field in enumerate(fields):
        stacked = jnp.where(row == i, field.astype(jnp.float32), stacked)
    token_ref[...] = jnp.dot(
        stacked.astype(jnp.bfloat16), widen, preferred_element_type=jnp.float32
    )

    copies = []
    for c, (first, count, target) in enumerate(blocks):
        held = pages_ref.at[pl.ds(first, count)]
        pltpu.make_async_copy(pool_ref.at[pl.ds(0, count)], held, in_sem.at[c]).wait()
        copies.append(pltpu.make_async_copy(held, target, out_sem.at[c]))
        copies[-1].start()
    for copy in copies:
        copy.wait()


def order_pages(me, dest, page_req, page_idx, pool, wide, ahead, parts):
    slots = pool.shape[0]
    part = lambda count: jax.ShapeDtypeStruct((count,) + pool.shape[1:], pool.dtype)
    out_shape = [part(slots), jax.ShapeDtypeStruct((wide, slots), jnp.float32)]
    out_shape += [jax.ShapeDtypeStruct((8, slots * PAGE), jnp.float32)]
    out_shape += [part(last - first) for _, _, first, last in parts]
    vmem = pl.BlockSpec(memory_space=pltpu.VMEM)
    hbm = pl.BlockSpec(memory_space=pltpu.HBM)
    return pl.pallas_call(
        functools.partial(order_kernel, wide, ahead, parts),
        out_shape=out_shape,
        in_specs=[pl.BlockSpec(memory_space=pltpu.SMEM), vmem, vmem, vmem, hbm],
        out_specs=[hbm, vmem, vmem] + [hbm] * len(parts),
        scratch_shapes=[
            pltpu.VMEM(pool.shape, pool.dtype),
            pltpu.VMEM((1, slots), jnp.int32),
            pltpu.SMEM((1, slots), jnp.int32),
            pltpu.SemaphoreType.DMA((1 + len(parts),)),
            pltpu.SemaphoreType.DMA((1 + len(parts),)),
            pltpu.SemaphoreType.DMA,
        ],
        compiler_params=pltpu.CompilerParams(vmem_limit_bytes=56 * MIB),
        cost_estimate=pl.CostEstimate(
            flops=0, bytes_accessed=2 * pool.size * 2, transcendentals=0
        ),
    )(me, dest.reshape(1, -1), page_req.reshape(1, -1), page_idx.reshape(1, -1), pool)


def place_kernel(counts, place_ref, *refs):
    in_refs, (out_ref, sem) = refs[:-3], refs[-2:]
    copies = []
    for chunk, count in zip(in_refs, counts):
        depth = chunk.shape[0] // count
        for i in range(count):
            c = len(copies)
            target = out_ref.at[pl.ds(place_ref[c], depth)]
            source = chunk.at[pl.ds(i * depth, depth)]
            copies.append(pltpu.make_async_copy(source, target, sem.at[c]))
    for copy in copies:
        copy.start()
    for copy in copies:
        copy.wait()


def place_pages(place, chunks, counts, pages):
    size = sum(chunk.size for chunk in chunks)
    return pl.pallas_call(
        functools.partial(place_kernel, counts),
        out_shape=jax.ShapeDtypeStruct(pages.shape, pages.dtype),
        in_specs=[pl.BlockSpec(memory_space=pltpu.SMEM)]
        + [pl.BlockSpec(memory_space=pltpu.VMEM)] * len(chunks)
        + [pl.BlockSpec(memory_space=pl.ANY)],
        out_specs=pl.BlockSpec(memory_space=pl.ANY),
        scratch_shapes=[pltpu.SemaphoreType.DMA((sum(counts),))],
        input_output_aliases={len(chunks) + 1: 0},
        compiler_params=pltpu.CompilerParams(vmem_limit_bytes=2 * size + 2 * MIB),
        cost_estimate=pl.CostEstimate(flops=0, bytes_accessed=4 * size, transcendentals=0),
    )(place, *chunks, pages)


def cut(value):
    return value.astype(jnp.bfloat16).astype(jnp.float32)


def split_stats(peak, total):
    high = cut(peak)
    mid = cut(peak - high)
    return high, mid, peak - high - mid, cut(total), total - cut(total)


def attend_kernel(rows, piece, peers, me_ref, length_ref, *refs):
    query_refs, refs = refs[:peers], refs[peers:]
    key_ref, value_ref, new_key_ref, new_value_ref, token_ref = refs[:5]
    out_refs = refs[5 : 5 + peers]
    bias_ref, new_bias_ref, score_ref, weight_ref, query_ref, result_ref = refs[5 + peers :]
    tokens = key_ref.shape[0]
    step = pl.program_id(0)

    @pl.when(step == 0)
    def _():
        owner = token_ref[0:1, :]
        offset = lax.broadcasted_iota(jnp.int32, owner.shape, 1) % PAGE
        spot = (token_ref[1:2, :] * 32 + token_ref[2:3, :] - 1) * PAGE + offset.astype(jnp.float32)
        request = lax.broadcasted_iota(jnp.int32, (rows, 1), 0) // STEPS
        limit = jnp.zeros((rows, 1), jnp.int32)
        for r in range(rows // STEPS):
            limit = jnp.where(request == r, length_ref[r], limit)
        seen = (owner == request.astype(jnp.float32)) & (spot < limit.astype(jnp.float32))
        bias_ref[...] = jnp.where(seen, 0.0, NEG_FILL)
        row = lax.broadcasted_iota(jnp.int32, new_bias_ref.shape, 0)
        col = lax.broadcasted_iota(jnp.int32, new_bias_ref.shape, 1)
        first = jnp.where((me_ref[0] == 0) & (me_ref[1] == 0), 1, 0)
        seen = (row // STEPS == col // STEPS) & (col <= row) & (col < rows * first)
        new_bias_ref[...] = jnp.where(seen, 0.0, NEG_FILL)
        if peers > 1:
            for d in range(peers):
                query_ref[me_ref[1] ^ d] = query_refs[d][...]

    if peers > 1:
        per_step = query_refs[0].shape[0] // KVH
        query = jnp.concatenate(
            [
                query_ref[n, step * per_step + i].astype(jnp.float32)
                for i in range(per_step)
                for n in range(peers)
            ],
            axis=0,
        ).astype(jnp.bfloat16)
    else:
        query = query_refs[0][0]
    score_ref[:, :tokens] = lax.dot_general(
        query, key_ref[...], NT, preferred_element_type=jnp.float32
    )
    score_ref[:, tokens:] = lax.dot_general(
        query, new_key_ref[...], NT, preferred_element_type=jnp.float32
    )
    together = 1 if rows % 16 == 0 else 2
    span = together * rows
    peaks, totals = [], []
    for c in range(GROUPS // together):
        block = pl.ds(c * span, span)
        old = score_ref[block, :tokens].reshape(together, rows, tokens) * SCALE2 + bias_ref[...]
        new = score_ref[block, tokens:].reshape(together, rows, -1) * SCALE2 + new_bias_ref[...]
        peak = jnp.maximum(
            jnp.max(old, axis=-1, keepdims=True), jnp.max(new, axis=-1, keepdims=True)
        )
        old = jnp.exp2(old - peak)
        new = jnp.exp2(new - peak)
        totals.append(
            (jnp.sum(old, axis=-1, keepdims=True) + jnp.sum(new, axis=-1, keepdims=True)).reshape(
                span, 1
            )
        )
        peaks.append(peak.reshape(span, 1))
        weight_ref[block, :tokens] = old.reshape(span, tokens).astype(jnp.bfloat16)
        weight_ref[block, tokens:] = new.reshape(span, -1).astype(jnp.bfloat16)
    mixed = jnp.dot(
        weight_ref[:, :tokens], value_ref[...], preferred_element_type=jnp.float32
    ) + jnp.dot(weight_ref[:, tokens:], new_value_ref[...], preferred_element_type=jnp.float32)
    peak = jnp.concatenate(peaks, axis=0)
    total = jnp.concatenate(totals, axis=0)
    lane = lax.broadcasted_iota(jnp.int32, (GROUPS * rows, HD), 1)
    stats = jnp.zeros((GROUPS * rows, HD), jnp.float32)
    for i, part in enumerate(split_stats(peak, total)):
        stats = jnp.where(lane == i, part, stats)
    pick = (
        lax.broadcasted_iota(jnp.int32, (STAT, HD), 0)
        == lax.broadcasted_iota(jnp.int32, (STAT, HD), 1)
    ).astype(jnp.bfloat16)
    fill = result_ref.shape[1] - STAT - piece
    for c in range(GROUPS * rows // piece):
        part = slice(c * piece, (c + 1) * piece)
        turned = lax.dot_general(
            pick,
            jnp.concatenate(
                [stats[part], jnp.zeros((HD - piece, HD), jnp.float32)], axis=0
            ).astype(jnp.bfloat16),
            NT,
            preferred_element_type=jnp.float32,
        )
        result_ref[c] = jnp.concatenate(
            [turned, mixed[part], jnp.zeros((fill, HD), jnp.float32)], axis=0
        ).astype(jnp.bfloat16)
    if peers > 1:
        for d, out_ref in enumerate(out_refs):

            @pl.when((step ^ me_ref[1]) == d)
            def _():
                out_ref[...] = result_ref[...]
    else:
        out_refs[0][...] = result_ref[...]


def attend(me, lengths, queries, keyval, pool, token_info, rows, piece):
    tokens = pool.shape[0]
    extra = keyval.shape[0]
    peers = len(queries)
    pieces = GROUPS * rows // piece
    height = STAT + up(piece, 16)
    whole = lambda shape: pl.BlockSpec(shape, lambda k: (0,) * len(shape))
    if peers > 1:
        query_spec = whole(queries[0].shape)
        out_spec = whole((pieces, height, HD))
        out_shape = jax.ShapeDtypeStruct((pieces, height, HD), jnp.bfloat16)
    else:
        query_spec = pl.BlockSpec((1,) + queries[0].shape[1:], lambda k: (k, 0, 0))
        out_spec = pl.BlockSpec((pieces, height, HD), lambda k: (k, 0, 0))
        out_shape = jax.ShapeDtypeStruct((KVH * pieces, height, HD), jnp.bfloat16)
    return pl.pallas_call(
        functools.partial(attend_kernel, rows, piece, peers),
        grid=(KVH,),
        out_shape=[out_shape] * peers,
        in_specs=[pl.BlockSpec(memory_space=pltpu.SMEM)] * 2
        + [query_spec] * peers
        + [
            pl.BlockSpec((tokens, HD), lambda k: (0, k)),
            pl.BlockSpec((tokens, HD), lambda k: (0, KVH + k)),
            pl.BlockSpec((extra, HD), lambda k: (0, k)),
            pl.BlockSpec((extra, HD), lambda k: (0, KVH + k)),
            whole(token_info.shape),
        ],
        out_specs=[out_spec] * peers,
        scratch_shapes=[
            pltpu.VMEM((rows, tokens), jnp.float32),
            pltpu.VMEM((rows, extra), jnp.float32),
            pltpu.VMEM((GROUPS * rows, tokens + extra), jnp.float32),
            pltpu.VMEM((GROUPS * rows, tokens + extra), jnp.bfloat16),
            pltpu.VMEM((peers,) + queries[0].shape, jnp.bfloat16),
            pltpu.VMEM((pieces, height, HD), jnp.bfloat16),
        ],
        compiler_params=pltpu.CompilerParams(vmem_limit_bytes=56 * MIB),
        cost_estimate=pl.CostEstimate(flops=1, bytes_accessed=1, transcendentals=0),
    )(me, lengths, *queries, pool, pool, keyval, keyval, token_info)


def combine_kernel(piece, last, count, *refs):
    if last:
        part_ref, out_ref = refs
        part_refs = [part_ref.at[pl.ds(i, 1)] for i in range(count)]
    else:
        part_refs, out_ref = refs[:count], refs[count]
    groups, height = part_refs[0].shape[:2]
    peaks, totals = [], []
    for i in range(count):
        for j in range(groups):
            stat = part_refs[i][j, :STAT, :].astype(jnp.float32)
            peaks.append(stat[0:1] + stat[1:2] + stat[2:3])
            totals.append(stat[3:4] + stat[4:5])
    peak = jnp.concatenate(peaks, axis=0).reshape(count, groups, HD)
    total = jnp.concatenate(totals, axis=0).reshape(count, groups, HD)
    top = jnp.max(peak, axis=0)
    lead = jnp.exp2(peak - top[None])
    whole = jnp.sum(lead * total, axis=0)
    if last:
        lane = lax.broadcasted_iota(jnp.int32, whole.shape, 1)
        lead = lead / jnp.where(lane < piece, whole, 1.0)[None]
    lead = lead.reshape(count * groups, HD)
    if (count * groups) % HD:
        fill = up(count * groups, HD) - count * groups
        lead = jnp.concatenate([lead, jnp.zeros((fill, HD), jnp.float32)], axis=0)
    lead = jnp.transpose(lead)
    rows = height - STAT
    for j in range(groups):
        result = jnp.zeros((rows, HD), jnp.float32)
        for i in range(count):
            c = i * groups + j
            result = result + lead[:rows, c : c + 1] * part_refs[i][j, STAT:, :].astype(jnp.float32)
        if last:
            for i in range(out_ref.shape[0]):
                out_ref[i] = result[:piece].astype(jnp.bfloat16)
        else:
            stats = split_stats(top[j : j + 1], whole[j : j + 1])
            rest = jnp.zeros((STAT - len(stats), HD), jnp.float32)
            out_ref[j] = jnp.concatenate([*stats, rest, result], axis=0).astype(jnp.bfloat16)


def combine(parts, piece, repeats=0):
    count = parts[0].shape[0] if repeats else len(parts)
    shape = (repeats, piece, HD) if repeats else parts[0].shape
    return pl.pallas_call(
        functools.partial(combine_kernel, piece, repeats > 0, count),
        out_shape=jax.ShapeDtypeStruct(shape, jnp.bfloat16),
        in_specs=[pl.BlockSpec(memory_space=pltpu.VMEM)] * len(parts),
        out_specs=pl.BlockSpec(memory_space=pltpu.VMEM),
        compiler_params=pltpu.CompilerParams(vmem_limit_bytes=8 * MIB),
        cost_estimate=pl.CostEstimate(flops=1, bytes_accessed=1, transcendentals=0),
    )(*parts)


def reorder(shape, unit, valid, own, column):
    first, second = (0, 1) if column else (1, 0)
    block = lax.broadcasted_iota(jnp.int32, shape, second) // unit
    place = lax.broadcasted_iota(jnp.int32, shape, second) % unit
    target = (block ^ own) * valid + place
    match = (lax.broadcasted_iota(jnp.int32, shape, first) == target) & (place < valid)
    return match.astype(jnp.bfloat16)


def repeat_kernel(block_ref, out_ref):
    for i in range(out_ref.shape[0]):
        out_ref[i] = block_ref[...]


def project_kernel(peers, me_ref, hidden_ref, query_ref, keyval_ref, *refs):
    out_refs, (full_ref,) = refs[:peers], refs[peers:]
    count, local, depth = hidden_ref.shape
    unit = up(local, 8)
    blocks = []
    for i in range(count):
        blocks.append(hidden_ref[i].astype(jnp.float32))
        if unit > local:
            blocks.append(jnp.zeros((unit - local, depth), jnp.float32))
    hidden = jnp.concatenate(blocks, axis=0).astype(jnp.bfloat16)
    order = reorder((count * local, count * unit), unit, local, 0, True)
    hidden = jnp.dot(order, hidden, preferred_element_type=jnp.float32).astype(jnp.bfloat16)
    full_ref[...] = jnp.dot(hidden, query_ref[...], preferred_element_type=jnp.float32)
    keyval = jnp.dot(hidden, keyval_ref[...], preferred_element_type=jnp.float32)
    for d, out_ref in enumerate(out_refs):
        start = pl.multiple_of((me_ref[1] ^ d) * HD, HD)
        out_ref[:, :HD] = full_ref[:, pl.ds(start, HD)]
        out_ref[:, HD:] = keyval


def pack_kernel(peers, *refs):
    own, tag_ref, out_ref = refs[:peers], refs[peers], refs[peers + 1]
    total = (own[0][...] + own[1][...]) + (own[2][...] + own[3][...])
    tags = jnp.concatenate([tag_ref[...], jnp.zeros_like(tag_ref[...])], axis=1)
    packed = jnp.concatenate([total, tags], axis=0).astype(jnp.bfloat16)
    for i in range(out_ref.shape[0]):
        out_ref[i] = packed


def unpack_kernel(rows, me_ref, kept_ref, part_ref, query_ref, keyval_ref, *refs):
    entry_ref, req_ref, idx_ref = refs
    count = part_ref.shape[0]
    line = lax.broadcasted_iota(jnp.int32, (count, HD), 0)
    tags = jnp.zeros((count, HD), jnp.float32)
    fill = jnp.zeros((keyval_ref.shape[0] - rows, HD), jnp.float32)
    for i in range(count):
        part = part_ref[i].astype(jnp.float32)
        query_ref[i] = part[:rows, :HD].astype(jnp.bfloat16)
        block = jnp.concatenate([part[:rows, HD:], fill], axis=0).astype(jnp.bfloat16)
        keyval_ref[:, i * HD : (i + 1) * HD] = block
        mine = jnp.where(line == me_ref[0], part[rows : rows + count, :HD], 0.0)
        tags = tags + jnp.where(line == i, jnp.sum(mine, axis=0, keepdims=True), 0.0)
    capacity = HD // count
    high = lax.broadcasted_iota(jnp.int32, (HD, HD), 0)
    low = lax.broadcasted_iota(jnp.int32, (HD, HD), 1)
    slot = lax.broadcasted_iota(jnp.int32, (count, HD), 1)
    tags = tags.astype(jnp.bfloat16)
    fields = []
    for i in range(3):
        pick = jnp.where(high == i * capacity + low % capacity, 1.0, 0.0).astype(jnp.bfloat16)
        spread_out = jnp.dot(tags, pick, preferred_element_type=jnp.float32)
        spread_out = jnp.where(slot // capacity == line, spread_out, 0.0)
        fields.append(jnp.sum(spread_out, axis=0, keepdims=True))
    req_ref[...] = fields[0].astype(jnp.int32)
    idx_ref[...] = (fields[1] * 32.0 + fields[2] - 1.0).astype(jnp.int32)
    local = entry_ref.shape[1]
    step = lax.broadcasted_iota(jnp.int32, (16, keyval_ref.shape[0]), 0)
    row = lax.broadcasted_iota(jnp.int32, (16, keyval_ref.shape[0]), 1)
    kept = (row == me_ref[0] * local + step) & (step < kept_ref[me_ref[0]])
    kept = jnp.where(kept, 1.0, 0.0).astype(jnp.bfloat16)
    entries = jnp.dot(kept, keyval_ref[...], preferred_element_type=jnp.float32)
    entry_ref[0] = entries[:local].astype(jnp.bfloat16)


def finish_kernel(peers, me_ref, part_ref, weight_ref, *refs):
    count, rows = part_ref.shape[:2]
    local = rows // peers
    unit = up(local, 16)
    whole = jnp.concatenate([part_ref[i] for i in range(count)], axis=1)
    order = reorder((peers * unit, rows), unit, local, me_ref[1], False)
    mixed = jnp.dot(order, whole, preferred_element_type=jnp.float32)
    mixed = jnp.dot(mixed.astype(jnp.bfloat16), weight_ref[...], preferred_element_type=jnp.float32)
    for d, out_ref in enumerate(refs):
        out_ref[...] = mixed[d * unit : d * unit + local]


def in_vmem(kernel, out_shape, me, *args, scratch=()):
    head = [] if me is None else list(me) if isinstance(me, tuple) else [me]
    return pl.pallas_call(
        kernel,
        out_shape=out_shape,
        in_specs=[pl.BlockSpec(memory_space=pltpu.SMEM)] * len(head)
        + [pl.BlockSpec(memory_space=pltpu.VMEM)] * len(args),
        out_specs=jax.tree.map(lambda _: pl.BlockSpec(memory_space=pltpu.VMEM), out_shape),
        scratch_shapes=scratch,
        compiler_params=pltpu.CompilerParams(vmem_limit_bytes=16 * MIB),
        cost_estimate=pl.CostEstimate(flops=1, bytes_accessed=1, transcendentals=0),
    )(*head, *args)


def group_of(d, wide):
    return d if wide <= 8 or d == 0 else 1 + (d - 1) * 7 // (wide - 1)


def spread(block, axis):
    count = lax.axis_size(axis)
    return lax.all_to_all(
        jnp.broadcast_to(block[None], (count,) + block.shape),
        axis,
        split_axis=0,
        concat_axis=0,
        tiled=True,
    )


def on_device(hidden, w_query, w_keyval, w_out, pool, page_req, page_idx, lengths, moves, accepted):
    wide = lax.axis_size("wide")
    narrow = lax.axis_size("narrow")
    local_rows = hidden.shape[0]
    rows = local_rows * wide
    requests = rows // STEPS
    slots = pool.shape[0]
    capacity = slots // wide
    own_cols = w_query.shape[1] // narrow
    piece = HEADS * rows // (wide * narrow)
    extra = up(rows, HD)
    direct = piece == rows and own_cols == HD and slots == HD
    direct = direct and wide == 8 and narrow == 4 and local_rows == STEPS
    me = lax.axis_index("wide")
    both = jnp.stack([me, lax.axis_index("narrow")])
    exchange = functools.partial(lax.all_to_all, split_axis=0, concat_axis=0, tiled=True)

    def send(block, axis, d):
        return lax.ppermute(block, axis, [(i, i ^ d) for i in range(lax.axis_size(axis))])

    def share(block, axis):
        return [block] + [send(block, axis, d) for d in range(1, lax.axis_size(axis))]

    def deal(blocks, axis):
        return [blocks[0]] + [send(block, axis, d) for d, block in enumerate(blocks) if d]

    copies = jax.ShapeDtypeStruct((wide,) + hidden.shape, hidden.dtype)
    gathered = exchange(in_vmem(repeat_kernel, copies, None, hidden), "wide")

    ahead = AHEAD * capacity // 16
    rest = capacity - ahead
    early = EARLY * rest // (16 - AHEAD)
    parts = [(0, 0, 0, wide * ahead)] if ahead else []
    for d in range(1, wide):
        group = group_of(d, wide)
        cut = early if group == 7 else 0
        if cut:
            parts.append((8, d, 0, cut))
        parts.append((group, d, cut, rest))
    moved_pool, tags, token_info, *chunks = order_pages(
        both, moves, page_req, page_idx, pool, wide, ahead, parts
    )
    arrived = {}
    flying = {}

    def members(groups):
        return [c for group in groups for c, part in enumerate(parts) if part[0] == group]

    def launch(values, *groups):
        taken = members(groups)
        values, sent = lax.optimization_barrier((values, [chunks[c] for c in taken]))
        for c, chunk in zip(taken, sent):
            d = parts[c][1]
            flying[c] = send(chunk, "wide", d) if d else exchange(chunk, "wide")
        return values

    def land(values, *groups):
        taken = members(groups)
        values, got = lax.optimization_barrier((values, [flying[c] for c in taken]))
        arrived.update(zip(taken, got))
        return values

    def placed(pages):
        taken = sorted(arrived)
        if not taken:
            return pages
        place, counts = [], []
        for _, d, first, _ in [parts[c] for c in taken]:
            own = [(me ^ d) * capacity + ahead + first]
            place += own if d else [w * capacity for w in range(wide)]
            counts.append(1 if d else wide)
        place = jnp.stack([jnp.asarray(index, jnp.int32) for index in place])
        pages = place_pages(place, [arrived[c] for c in taken], counts, pages)
        arrived.clear()
        return pages

    gathered, tags = lax.optimization_barrier((gathered, tags))
    tokens = pool.reshape(slots * PAGE, -1)
    if direct:
        block = jax.ShapeDtypeStruct((rows, 2 * HD), jnp.float32)
        partial = in_vmem(
            functools.partial(project_kernel, narrow),
            [block] * narrow,
            both,
            gathered,
            w_query,
            w_keyval,
            scratch=[pltpu.VMEM((rows, narrow * HD), jnp.float32)],
        )
        partial = land(deal(launch(partial, 8), "narrow"), 8)
        partial = launch(partial, 6, 1)
        packed = in_vmem(
            functools.partial(pack_kernel, narrow),
            jax.ShapeDtypeStruct((wide, rows + wide, 2 * HD), jnp.bfloat16),
            None,
            *partial,
            tags,
        )
        received = land(exchange(packed, "wide"), 6, 1)
        received = launch(received, 0)
        queries, keyval, new_entries, moved_req, moved_idx = in_vmem(
            functools.partial(unpack_kernel, rows),
            [
                jax.ShapeDtypeStruct((wide, rows, HD), jnp.bfloat16),
                jax.ShapeDtypeStruct((extra, wide * HD), jnp.bfloat16),
                jax.ShapeDtypeStruct((1, local_rows, wide * HD), jnp.bfloat16),
                jax.ShapeDtypeStruct((1, slots), jnp.int32),
                jax.ShapeDtypeStruct((1, slots), jnp.int32),
            ],
            (both, accepted),
            received,
        )
        moved_req, moved_idx = moved_req.reshape(slots), moved_idx.reshape(slots)
        queries = share(queries, "narrow")
    else:
        gathered = gathered.reshape(rows, -1)
        query_part = jnp.dot(gathered, w_query, preferred_element_type=jnp.float32)
        keyval_part = jnp.dot(gathered, w_keyval, preferred_element_type=jnp.float32)
        query_part = jnp.transpose(query_part.reshape(rows, narrow, own_cols), (1, 0, 2))
        partial = jnp.concatenate(
            [query_part, jnp.broadcast_to(keyval_part[None], (narrow,) + keyval_part.shape)], axis=2
        )
        partial = land(exchange(launch(partial, 8), "narrow"), 8)
        partial = launch(partial, 6, 1)
        projected = jnp.sum(partial, axis=0).astype(jnp.bfloat16)
        tags = tags[:, : 3 * capacity].astype(jnp.bfloat16)[:, None]
        tags = jnp.pad(tags, ((0, 0), (0, 7), (0, projected.shape[1] - tags.shape[2])))
        packed = jnp.broadcast_to(projected[None], (wide,) + projected.shape)
        packed = jnp.concatenate([packed, tags], axis=1)
        received = land(exchange(packed, "wide"), 6, 1)
        received = launch(received, 0)
        tags_in = received[:, rows]
        queries = received[:, :rows, :own_cols]
        queries = spread(queries, "narrow")
        queries = jnp.transpose(queries, (2, 1, 0, 3)).reshape(rows, HEADS, HD)
        queries = [jnp.transpose(queries, (1, 0, 2)).reshape(KVH, GROUPS * rows, HD)]
        keyval = jnp.transpose(received[:, :rows, own_cols:], (1, 0, 2)).reshape(rows, -1)
        keyval = jnp.pad(keyval, ((0, extra - rows), (0, 0)))
        tags_in = tags_in.astype(jnp.int32)
        moved_req = tags_in[:, :capacity].reshape(slots)
        moved_idx = tags_in[:, capacity : 2 * capacity] * 32
        moved_idx = (moved_idx + tags_in[:, 2 * capacity : 3 * capacity] - 1).reshape(slots)
        local_req = local_rows // STEPS
        fresh = lax.dynamic_slice_in_dim(keyval, me * local_rows, local_rows, 0)
        fresh = fresh.reshape(local_req, STEPS, -1)
        kept = lax.dynamic_slice_in_dim(accepted, me * local_req, local_req, 0)
        step_ids = jnp.arange(STEPS)[None, :, None]
        new_entries = jnp.where(
            step_ids < kept[:, None, None], fresh, jnp.zeros((), jnp.bfloat16)
        )

    queries, moved_pool = lax.optimization_barrier((queries, placed(moved_pool)))
    mixed = attend(both, lengths, queries, keyval, tokens, token_info, rows, piece)
    mixed = launch(mixed, 3, 4)
    if direct:
        mixed = land(deal(mixed, "narrow"), 0)
    else:
        mixed = land(exchange(mixed[0], "narrow"), 0)
        mixed = mixed.reshape((narrow, wide) + mixed.shape[1:])
        mixed = [mixed[i] for i in range(narrow)]
    mixed = combine(mixed, piece)
    mixed, pages = lax.optimization_barrier((mixed, moved_pool))
    pages = placed(pages)
    mixed = land(exchange(mixed, "wide"), 3, 4)
    mixed, moved_pool = lax.optimization_barrier((mixed, pages))
    attn = combine([launch(mixed, 2, 5)], piece, wide)
    attn, pages = lax.optimization_barrier((attn, moved_pool))
    pages = placed(pages)
    attn = land(exchange(attn, "wide"), 2, 5)
    attn, moved_pool = lax.optimization_barrier((attn, pages))
    attn = launch(attn, 7)
    if direct:
        sums = in_vmem(
            functools.partial(finish_kernel, narrow),
            [jax.ShapeDtypeStruct((rows // narrow, w_out.shape[1]), jnp.float32)] * narrow,
            both,
            attn,
            w_out,
        )
        sums, pages = lax.optimization_barrier((sums, moved_pool))
        pages = placed(pages)
        sums = land(deal(sums, "narrow"), 7)
        attended = ((sums[0] + sums[1]) + (sums[2] + sums[3])).astype(jnp.bfloat16)
    else:
        attn = jnp.transpose(attn.reshape(-1, rows, HD), (1, 0, 2)).reshape(rows, -1)
        sums = jnp.dot(attn, w_out, preferred_element_type=jnp.float32)
        sums = sums.reshape(narrow, rows // narrow, -1)
        pages = placed(moved_pool)
        sums = land(exchange(sums, "narrow"), 7)
        attended = jnp.sum(sums, axis=0).astype(jnp.bfloat16)
    attended, pages = lax.optimization_barrier((attended, pages))
    moved_pool = placed(pages)
    return (attended, new_entries, moved_pool, moved_req, moved_idx)


def solution(mesh):
    in_specs = (
        P("wide", "narrow"),
        P("narrow", "wide"),
        P("narrow", "wide"),
        P("narrow", "wide"),
        P(("wide", "narrow"), None, None),
        P(("wide", "narrow")),
        P(("wide", "narrow")),
        P(),
        P(("wide", "narrow"), None),
        P(),
    )
    out_specs = (
        P("narrow", "wide"),
        P("wide", None, None),
        P(("wide", "narrow"), None, None),
        P(("wide", "narrow")),
        P(("wide", "narrow")),
    )
    return jax.shard_map(
        on_device, mesh=mesh, in_specs=in_specs, out_specs=out_specs, check_vma=False
    )
```

```python
import functools
import math

import jax
import jax.numpy as jnp
from jax import lax
from jax.experimental import pallas as pl
from jax.experimental.pallas import tpu as pltpu
from jax.sharding import PartitionSpec as P

HEADS = 32
KVH = 4
HD = 128
STEPS = 5
PAGE = 16
GROUPS = HEADS // KVH
NEG_FILL = -1e30
SCALE2 = math.log2(math.e) / math.sqrt(HD)
STAT = 16
MIB = 1024 * 1024
AHEAD = 5
EARLY = 4
NT = (((1,), (1,)), ((), ()))


def up(value, unit):
    return -(-value // unit) * unit


def column(row):
    return jnp.transpose(jnp.broadcast_to(row, (row.shape[1], row.shape[1])))


def order_kernel(
    wide, ahead, parts, me_ref, dest_ref, req_ref, idx_ref, pool_ref, out_ref, tag_ref, token_ref, *refs
):
    chunk_refs, refs = refs[: len(parts)], refs[len(parts) :]
    pages_ref, line_ref, source_ref, in_sem, out_sem, line_sem = refs
    slots = pool_ref.shape[0]
    capacity = slots // wide
    shape = (slots, slots)
    high = lax.broadcasted_iota(jnp.int32, shape, 0)
    low = lax.broadcasted_iota(jnp.int32, shape, 1)
    dest = dest_ref[...]
    same = column(dest.astype(jnp.float32)) == dest.astype(jnp.float32)
    rank = jnp.sum(jnp.where(same & (high < low), 1.0, 0.0), axis=0, keepdims=True)
    rest = capacity - ahead
    early = (dest * ahead).astype(jnp.float32) + rank
    late = ((dest ^ me_ref[0]) * rest + wide * ahead - ahead).astype(jnp.float32) + rank
    moved_to = jnp.where(rank < float(ahead), early, late)
    match = column(moved_to) == low.astype(jnp.float32)
    source = jnp.sum(jnp.where(match, high.astype(jnp.float32), 0.0), axis=0, keepdims=True)
    line_ref[...] = source.astype(jnp.int32)
    copy = pltpu.make_async_copy(line_ref, source_ref, line_sem)
    copy.start()
    copy.wait()

    own = out_ref.at[pl.ds(me_ref[0] * capacity + ahead, rest)]
    blocks = [(wide * ahead, rest, own)]
    for (_, d, first, last), chunk in zip(parts, chunk_refs):
        if d:
            blocks.append((wide * ahead + d * rest + first, last - first, chunk))
        else:
            blocks.insert(0, (first, last - first, chunk))
    for c, (first, count, _) in enumerate(blocks):

        def start(j, carry, c=c):
            page = source_ref[0, j]
            pltpu.make_async_copy(pool_ref.at[page], pages_ref.at[j], in_sem.at[c]).start()
            return carry

        lax.fori_loop(first, first + count, start, 0)

    shifted = idx_ref[...] + 1
    fields = (req_ref[...], shifted // 32, shifted % 32)
    rank_col = column(rank)
    lane = low.astype(jnp.float32)
    spread_out = jnp.zeros(shape, jnp.float32)
    for i, field in enumerate(fields):
        picked = lane == rank_col + float(i * capacity)
        spread_out = spread_out + jnp.where(picked, column(field.astype(jnp.float32)), 0.0)
    line = lax.broadcasted_iota(jnp.int32, (wide, slots), 0)
    chosen = jnp.where(line == dest, 1.0, 0.0).astype(jnp.bfloat16)
    tag_ref[...] = jnp.dot(
        chosen, spread_out.astype(jnp.bfloat16), preferred_element_type=jnp.float32
    )

    tokens = slots * PAGE
    page = lax.broadcasted_iota(jnp.int32, (slots, tokens), 0)
    token = lax.broadcasted_iota(jnp.int32, (slots, tokens), 1)
    widen = jnp.where(page == token // PAGE, 1.0, 0.0).astype(jnp.bfloat16)
    row = lax.broadcasted_iota(jnp.int32, (8, slots), 0)
    stacked = jnp.zeros((8, slots), jnp.float32)
    for i, field in enumerate(fields):
        stacked = jnp.where(row == i, field.astype(jnp.float32), stacked)
    token_ref[...] = jnp.dot(
        stacked.astype(jnp.bfloat16), widen, preferred_element_type=jnp.float32
    )

    copies = []
    for c, (first, count, target) in enumerate(blocks):
        held = pages_ref.at[pl.ds(first, count)]
        pltpu.make_async_copy(pool_ref.at[pl.ds(0, count)], held, in_sem.at[c]).wait()
        copies.append(pltpu.make_async_copy(held, target, out_sem.at[c]))
        copies[-1].start()
    for copy in copies:
        copy.wait()


def order_pages(me, dest, page_req, page_idx, pool, wide, ahead, parts):
    slots = pool.shape[0]
    part = lambda count: jax.ShapeDtypeStruct((count,) + pool.shape[1:], pool.dtype)
    out_shape = [part(slots), jax.ShapeDtypeStruct((wide, slots), jnp.float32)]
    out_shape += [jax.ShapeDtypeStruct((8, slots * PAGE), jnp.float32)]
    out_shape += [part(last - first) for _, _, first, last in parts]
    vmem = pl.BlockSpec(memory_space=pltpu.VMEM)
    hbm = pl.BlockSpec(memory_space=pltpu.HBM)
    return pl.pallas_call(
        functools.partial(order_kernel, wide, ahead, parts),
        out_shape=out_shape,
        in_specs=[pl.BlockSpec(memory_space=pltpu.SMEM), vmem, vmem, vmem, hbm],
        out_specs=[hbm, vmem, vmem] + [hbm] * len(parts),
        scratch_shapes=[
            pltpu.VMEM(pool.shape, pool.dtype),
            pltpu.VMEM((1, slots), jnp.int32),
            pltpu.SMEM((1, slots), jnp.int32),
            pltpu.SemaphoreType.DMA((1 + len(parts),)),
            pltpu.SemaphoreType.DMA((1 + len(parts),)),
            pltpu.SemaphoreType.DMA,
        ],
        compiler_params=pltpu.CompilerParams(vmem_limit_bytes=56 * MIB),
        cost_estimate=pl.CostEstimate(
            flops=0, bytes_accessed=2 * pool.size * 2, transcendentals=0
        ),
    )(me, dest.reshape(1, -1), page_req.reshape(1, -1), page_idx.reshape(1, -1), pool)


def place_kernel(counts, place_ref, *refs):
    in_refs, (out_ref, sem) = refs[:-3], refs[-2:]
    copies = []
    for chunk, count in zip(in_refs, counts):
        depth = chunk.shape[0] // count
        for i in range(count):
            c = len(copies)
            target = out_ref.at[pl.ds(place_ref[c], depth)]
            source = chunk.at[pl.ds(i * depth, depth)]
            copies.append(pltpu.make_async_copy(source, target, sem.at[c]))
    for copy in copies:
        copy.start()
    for copy in copies:
        copy.wait()


def place_pages(place, chunks, counts, pages):
    size = sum(chunk.size for chunk in chunks)
    return pl.pallas_call(
        functools.partial(place_kernel, counts),
        out_shape=jax.ShapeDtypeStruct(pages.shape, pages.dtype),
        in_specs=[pl.BlockSpec(memory_space=pltpu.SMEM)]
        + [pl.BlockSpec(memory_space=pltpu.VMEM)] * len(chunks)
        + [pl.BlockSpec(memory_space=pl.ANY)],
        out_specs=pl.BlockSpec(memory_space=pl.ANY),
        scratch_shapes=[pltpu.SemaphoreType.DMA((sum(counts),))],
        input_output_aliases={len(chunks) + 1: 0},
        compiler_params=pltpu.CompilerParams(vmem_limit_bytes=2 * size + 2 * MIB),
        cost_estimate=pl.CostEstimate(flops=0, bytes_accessed=4 * size, transcendentals=0),
    )(place, *chunks, pages)


def cut(value):
    return value.astype(jnp.bfloat16).astype(jnp.float32)


def split_stats(peak, total):
    high = cut(peak)
    mid = cut(peak - high)
    return high, mid, peak - high - mid, cut(total), total - cut(total)


def attend_kernel(rows, piece, peers, me_ref, length_ref, *refs):
    query_refs, refs = refs[:peers], refs[peers:]
    key_ref, value_ref, new_key_ref, new_value_ref, token_ref = refs[:5]
    out_refs = refs[5 : 5 + peers]
    bias_ref, new_bias_ref, score_ref, weight_ref, query_ref, result_ref = refs[5 + peers :]
    tokens = key_ref.shape[0]
    step = pl.program_id(0)

    @pl.when(step == 0)
    def _():
        owner = token_ref[0:1, :]
        offset = lax.broadcasted_iota(jnp.int32, owner.shape, 1) % PAGE
        spot = (token_ref[1:2, :] * 32 + token_ref[2:3, :] - 1) * PAGE + offset.astype(jnp.float32)
        request = lax.broadcasted_iota(jnp.int32, (rows, 1), 0) // STEPS
        limit = jnp.zeros((rows, 1), jnp.int32)
        for r in range(rows // STEPS):
            limit = jnp.where(request == r, length_ref[r], limit)
        seen = (owner == request.astype(jnp.float32)) & (spot < limit.astype(jnp.float32))
        bias_ref[...] = jnp.where(seen, 0.0, NEG_FILL)
        row = lax.broadcasted_iota(jnp.int32, new_bias_ref.shape, 0)
        col = lax.broadcasted_iota(jnp.int32, new_bias_ref.shape, 1)
        first = jnp.where((me_ref[0] == 0) & (me_ref[1] == 0), 1, 0)
        seen = (row // STEPS == col // STEPS) & (col <= row) & (col < rows * first)
        new_bias_ref[...] = jnp.where(seen, 0.0, NEG_FILL)
        if peers > 1:
            for d in range(peers):
                query_ref[me_ref[1] ^ d] = query_refs[d][...]

    if peers > 1:
        per_step = query_refs[0].shape[0] // KVH
        query = jnp.concatenate(
            [
                query_ref[n, step * per_step + i].astype(jnp.float32)
                for i in range(per_step)
                for n in range(peers)
            ],
            axis=0,
        ).astype(jnp.bfloat16)
    else:
        query = query_refs[0][0]
    score_ref[:, :tokens] = lax.dot_general(
        query, key_ref[...], NT, preferred_element_type=jnp.float32
    )
    score_ref[:, tokens:] = lax.dot_general(
        query, new_key_ref[...], NT, preferred_element_type=jnp.float32
    )
    together = 1 if rows % 16 == 0 else 2
    span = together * rows
    peaks, totals = [], []
    for c in range(GROUPS // together):
        block = pl.ds(c * span, span)
        old = score_ref[block, :tokens].reshape(together, rows, tokens) * SCALE2 + bias_ref[...]
        new = score_ref[block, tokens:].reshape(together, rows, -1) * SCALE2 + new_bias_ref[...]
        peak = jnp.maximum(
            jnp.max(old, axis=-1, keepdims=True), jnp.max(new, axis=-1, keepdims=True)
        )
        old = jnp.exp2(old - peak)
        new = jnp.exp2(new - peak)
        totals.append(
            (jnp.sum(old, axis=-1, keepdims=True) + jnp.sum(new, axis=-1, keepdims=True)).reshape(
                span, 1
            )
        )
        peaks.append(peak.reshape(span, 1))
        weight_ref[block, :tokens] = old.reshape(span, tokens).astype(jnp.bfloat16)
        weight_ref[block, tokens:] = new.reshape(span, -1).astype(jnp.bfloat16)
    mixed = jnp.dot(
        weight_ref[:, :tokens], value_ref[...], preferred_element_type=jnp.float32
    ) + jnp.dot(weight_ref[:, tokens:], new_value_ref[...], preferred_element_type=jnp.float32)
    peak = jnp.concatenate(peaks, axis=0)
    total = jnp.concatenate(totals, axis=0)
    lane = lax.broadcasted_iota(jnp.int32, (GROUPS * rows, HD), 1)
    stats = jnp.zeros((GROUPS * rows, HD), jnp.float32)
    for i, part in enumerate(split_stats(peak, total)):
        stats = jnp.where(lane == i, part, stats)
    pick = (
        lax.broadcasted_iota(jnp.int32, (STAT, HD), 0)
        == lax.broadcasted_iota(jnp.int32, (STAT, HD), 1)
    ).astype(jnp.bfloat16)
    fill = result_ref.shape[1] - STAT - piece
    for c in range(GROUPS * rows // piece):
        part = slice(c * piece, (c + 1) * piece)
        turned = lax.dot_general(
            pick,
            jnp.concatenate(
                [stats[part], jnp.zeros((HD - piece, HD), jnp.float32)], axis=0
            ).astype(jnp.bfloat16),
            NT,
            preferred_element_type=jnp.float32,
        )
        result_ref[c] = jnp.concatenate(
            [turned, mixed[part], jnp.zeros((fill, HD), jnp.float32)], axis=0
        ).astype(jnp.bfloat16)
    if peers > 1:
        for d, out_ref in enumerate(out_refs):

            @pl.when((step ^ me_ref[1]) == d)
            def _():
                out_ref[...] = result_ref[...]
    else:
        out_refs[0][...] = result_ref[...]


def attend(me, lengths, queries, keyval, pool, token_info, rows, piece):
    tokens = pool.shape[0]
    extra = keyval.shape[0]
    peers = len(queries)
    pieces = GROUPS * rows // piece
    height = STAT + up(piece, 16)
    whole = lambda shape: pl.BlockSpec(shape, lambda k: (0,) * len(shape))
    if peers > 1:
        query_spec = whole(queries[0].shape)
        out_spec = whole((pieces, height, HD))
        out_shape = jax.ShapeDtypeStruct((pieces, height, HD), jnp.bfloat16)
    else:
        query_spec = pl.BlockSpec((1,) + queries[0].shape[1:], lambda k: (k, 0, 0))
        out_spec = pl.BlockSpec((pieces, height, HD), lambda k: (k, 0, 0))
        out_shape = jax.ShapeDtypeStruct((KVH * pieces, height, HD), jnp.bfloat16)
    return pl.pallas_call(
        functools.partial(attend_kernel, rows, piece, peers),
        grid=(KVH,),
        out_shape=[out_shape] * peers,
        in_specs=[pl.BlockSpec(memory_space=pltpu.SMEM)] * 2
        + [query_spec] * peers
        + [
            pl.BlockSpec((tokens, HD), lambda k: (0, k)),
            pl.BlockSpec((tokens, HD), lambda k: (0, KVH + k)),
            pl.BlockSpec((extra, HD), lambda k: (0, k)),
            pl.BlockSpec((extra, HD), lambda k: (0, KVH + k)),
            whole(token_info.shape),
        ],
        out_specs=[out_spec] * peers,
        scratch_shapes=[
            pltpu.VMEM((rows, tokens), jnp.float32),
            pltpu.VMEM((rows, extra), jnp.float32),
            pltpu.VMEM((GROUPS * rows, tokens + extra), jnp.float32),
            pltpu.VMEM((GROUPS * rows, tokens + extra), jnp.bfloat16),
            pltpu.VMEM((peers,) + queries[0].shape, jnp.bfloat16),
            pltpu.VMEM((pieces, height, HD), jnp.bfloat16),
        ],
        compiler_params=pltpu.CompilerParams(vmem_limit_bytes=56 * MIB),
        cost_estimate=pl.CostEstimate(flops=1, bytes_accessed=1, transcendentals=0),
    )(me, lengths, *queries, pool, pool, keyval, keyval, token_info)


def combine_kernel(piece, last, count, *refs):
    if last:
        part_ref, out_ref = refs
        part_refs = [part_ref.at[pl.ds(i, 1)] for i in range(count)]
    else:
        part_refs, out_ref = refs[:count], refs[count]
    groups, height = part_refs[0].shape[:2]
    peaks, totals = [], []
    for i in range(count):
        for j in range(groups):
            stat = part_refs[i][j, :STAT, :].astype(jnp.float32)
            peaks.append(stat[0:1] + stat[1:2] + stat[2:3])
            totals.append(stat[3:4] + stat[4:5])
    peak = jnp.concatenate(peaks, axis=0).reshape(count, groups, HD)
    total = jnp.concatenate(totals, axis=0).reshape(count, groups, HD)
    top = jnp.max(peak, axis=0)
    lead = jnp.exp2(peak - top[None])
    whole = jnp.sum(lead * total, axis=0)
    if last:
        lane = lax.broadcasted_iota(jnp.int32, whole.shape, 1)
        lead = lead / jnp.where(lane < piece, whole, 1.0)[None]
    lead = lead.reshape(count * groups, HD)
    if (count * groups) % HD:
        fill = up(count * groups, HD) - count * groups
        lead = jnp.concatenate([lead, jnp.zeros((fill, HD), jnp.float32)], axis=0)
    lead = jnp.transpose(lead)
    rows = height - STAT
    for j in range(groups):
        result = jnp.zeros((rows, HD), jnp.float32)
        for i in range(count):
            c = i * groups + j
            result = result + lead[:rows, c : c + 1] * part_refs[i][j, STAT:, :].astype(jnp.float32)
        if last:
            for i in range(out_ref.shape[0]):
                out_ref[i] = result[:piece].astype(jnp.bfloat16)
        else:
            stats = split_stats(top[j : j + 1], whole[j : j + 1])
            rest = jnp.zeros((STAT - len(stats), HD), jnp.float32)
            out_ref[j] = jnp.concatenate([*stats, rest, result], axis=0).astype(jnp.bfloat16)


def combine(parts, piece, repeats=0):
    count = parts[0].shape[0] if repeats else len(parts)
    shape = (repeats, piece, HD) if repeats else parts[0].shape
    return pl.pallas_call(
        functools.partial(combine_kernel, piece, repeats > 0, count),
        out_shape=jax.ShapeDtypeStruct(shape, jnp.bfloat16),
        in_specs=[pl.BlockSpec(memory_space=pltpu.VMEM)] * len(parts),
        out_specs=pl.BlockSpec(memory_space=pltpu.VMEM),
        compiler_params=pltpu.CompilerParams(vmem_limit_bytes=8 * MIB),
        cost_estimate=pl.CostEstimate(flops=1, bytes_accessed=1, transcendentals=0),
    )(*parts)


def reorder(shape, unit, valid, own, column):
    first, second = (0, 1) if column else (1, 0)
    block = lax.broadcasted_iota(jnp.int32, shape, second) // unit
    place = lax.broadcasted_iota(jnp.int32, shape, second) % unit
    target = (block ^ own) * valid + place
    match = (lax.broadcasted_iota(jnp.int32, shape, first) == target) & (place < valid)
    return match.astype(jnp.bfloat16)


def repeat_kernel(block_ref, out_ref):
    for i in range(out_ref.shape[0]):
        out_ref[i] = block_ref[...]


def project_kernel(peers, me_ref, hidden_ref, query_ref, keyval_ref, *refs):
    out_refs, (full_ref,) = refs[:peers], refs[peers:]
    count, local, depth = hidden_ref.shape
    unit = up(local, 8)
    blocks = []
    for i in range(count):
        blocks.append(hidden_ref[i].astype(jnp.float32))
        if unit > local:
            blocks.append(jnp.zeros((unit - local, depth), jnp.float32))
    hidden = jnp.concatenate(blocks, axis=0).astype(jnp.bfloat16)
    order = reorder((count * local, count * unit), unit, local, 0, True)
    hidden = jnp.dot(order, hidden, preferred_element_type=jnp.float32).astype(jnp.bfloat16)
    full_ref[...] = jnp.dot(hidden, query_ref[...], preferred_element_type=jnp.float32)
    keyval = jnp.dot(hidden, keyval_ref[...], preferred_element_type=jnp.float32)
    for d, out_ref in enumerate(out_refs):
        start = pl.multiple_of((me_ref[1] ^ d) * HD, HD)
        out_ref[:, :HD] = full_ref[:, pl.ds(start, HD)]
        out_ref[:, HD:] = keyval


def pack_kernel(peers, *refs):
    own, tag_ref, out_ref = refs[:peers], refs[peers], refs[peers + 1]
    total = (own[0][...] + own[1][...]) + (own[2][...] + own[3][...])
    tags = jnp.concatenate([tag_ref[...], jnp.zeros_like(tag_ref[...])], axis=1)
    packed = jnp.concatenate([total, tags], axis=0).astype(jnp.bfloat16)
    for i in range(out_ref.shape[0]):
        out_ref[i] = packed


def unpack_kernel(rows, me_ref, kept_ref, part_ref, query_ref, keyval_ref, *refs):
    entry_ref, req_ref, idx_ref = refs
    count = part_ref.shape[0]
    line = lax.broadcasted_iota(jnp.int32, (count, HD), 0)
    tags = jnp.zeros((count, HD), jnp.float32)
    fill = jnp.zeros((keyval_ref.shape[0] - rows, HD), jnp.float32)
    for i in range(count):
        part = part_ref[i].astype(jnp.float32)
        query_ref[i] = part[:rows, :HD].astype(jnp.bfloat16)
        block = jnp.concatenate([part[:rows, HD:], fill], axis=0).astype(jnp.bfloat16)
        keyval_ref[:, i * HD : (i + 1) * HD] = block
        mine = jnp.where(line == me_ref[0], part[rows : rows + count, :HD], 0.0)
        tags = tags + jnp.where(line == i, jnp.sum(mine, axis=0, keepdims=True), 0.0)
    capacity = HD // count
    high = lax.broadcasted_iota(jnp.int32, (HD, HD), 0)
    low = lax.broadcasted_iota(jnp.int32, (HD, HD), 1)
    slot = lax.broadcasted_iota(jnp.int32, (count, HD), 1)
    tags = tags.astype(jnp.bfloat16)
    fields = []
    for i in range(3):
        pick = jnp.where(high == i * capacity + low % capacity, 1.0, 0.0).astype(jnp.bfloat16)
        spread_out = jnp.dot(tags, pick, preferred_element_type=jnp.float32)
        spread_out = jnp.where(slot // capacity == line, spread_out, 0.0)
        fields.append(jnp.sum(spread_out, axis=0, keepdims=True))
    req_ref[...] = fields[0].astype(jnp.int32)
    idx_ref[...] = (fields[1] * 32.0 + fields[2] - 1.0).astype(jnp.int32)
    local = entry_ref.shape[1]
    step = lax.broadcasted_iota(jnp.int32, (16, keyval_ref.shape[0]), 0)
    row = lax.broadcasted_iota(jnp.int32, (16, keyval_ref.shape[0]), 1)
    kept = (row == me_ref[0] * local + step) & (step < kept_ref[me_ref[0]])
    kept = jnp.where(kept, 1.0, 0.0).astype(jnp.bfloat16)
    entries = jnp.dot(kept, keyval_ref[...], preferred_element_type=jnp.float32)
    entry_ref[0] = entries[:local].astype(jnp.bfloat16)


def finish_kernel(peers, me_ref, part_ref, weight_ref, *refs):
    count, rows = part_ref.shape[:2]
    local = rows // peers
    unit = up(local, 16)
    whole = jnp.concatenate([part_ref[i] for i in range(count)], axis=1)
    order = reorder((peers * unit, rows), unit, local, me_ref[1], False)
    mixed = jnp.dot(order, whole, preferred_element_type=jnp.float32)
    mixed = jnp.dot(mixed.astype(jnp.bfloat16), weight_ref[...], preferred_element_type=jnp.float32)
    for d, out_ref in enumerate(refs):
        out_ref[...] = mixed[d * unit : d * unit + local]


def in_vmem(kernel, out_shape, me, *args, scratch=()):
    head = [] if me is None else list(me) if isinstance(me, tuple) else [me]
    return pl.pallas_call(
        kernel,
        out_shape=out_shape,
        in_specs=[pl.BlockSpec(memory_space=pltpu.SMEM)] * len(head)
        + [pl.BlockSpec(memory_space=pltpu.VMEM)] * len(args),
        out_specs=jax.tree.map(lambda _: pl.BlockSpec(memory_space=pltpu.VMEM), out_shape),
        scratch_shapes=scratch,
        compiler_params=pltpu.CompilerParams(vmem_limit_bytes=16 * MIB),
        cost_estimate=pl.CostEstimate(flops=1, bytes_accessed=1, transcendentals=0),
    )(*head, *args)


def group_of(d, wide):
    return d if wide <= 8 or d == 0 else 1 + (d - 1) * 7 // (wide - 1)


def spread(block, axis):
    count = lax.axis_size(axis)
    return lax.all_to_all(
        jnp.broadcast_to(block[None], (count,) + block.shape),
        axis,
        split_axis=0,
        concat_axis=0,
        tiled=True,
    )


def on_device(hidden, w_query, w_keyval, w_out, pool, page_req, page_idx, lengths, moves, accepted):
    wide = lax.axis_size("wide")
    narrow = lax.axis_size("narrow")
    local_rows = hidden.shape[0]
    rows = local_rows * wide
    requests = rows // STEPS
    slots = pool.shape[0]
    capacity = slots // wide
    own_cols = w_query.shape[1] // narrow
    piece = HEADS * rows // (wide * narrow)
    extra = up(rows, HD)
    direct = piece == rows and own_cols == HD and slots == HD
    direct = direct and wide == 8 and narrow == 4 and local_rows == STEPS
    me = lax.axis_index("wide")
    both = jnp.stack([me, lax.axis_index("narrow")])
    exchange = functools.partial(lax.all_to_all, split_axis=0, concat_axis=0, tiled=True)

    def send(block, axis, d):
        return lax.ppermute(block, axis, [(i, i ^ d) for i in range(lax.axis_size(axis))])

    def share(block, axis):
        return [block] + [send(block, axis, d) for d in range(1, lax.axis_size(axis))]

    def deal(blocks, axis):
        return [blocks[0]] + [send(block, axis, d) for d, block in enumerate(blocks) if d]

    copies = jax.ShapeDtypeStruct((wide,) + hidden.shape, hidden.dtype)
    gathered = exchange(in_vmem(repeat_kernel, copies, None, hidden), "wide")

    ahead = AHEAD * capacity // 16
    rest = capacity - ahead
    early = EARLY * rest // (16 - AHEAD)
    parts = [(0, 0, 0, wide * ahead)] if ahead else []
    for d in range(1, wide):
        group = group_of(d, wide)
        cut = early if group == 7 else 0
        if cut:
            parts.append((8, d, 0, cut))
        parts.append((group, d, cut, rest))
    moved_pool, tags, token_info, *chunks = order_pages(
        both, moves, page_req, page_idx, pool, wide, ahead, parts
    )
    arrived = {}
    flying = {}

    def members(groups):
        return [c for group in groups for c, part in enumerate(parts) if part[0] == group]

    def launch(values, *groups):
        taken = members(groups)
        values, sent = lax.optimization_barrier((values, [chunks[c] for c in taken]))
        for c, chunk in zip(taken, sent):
            d = parts[c][1]
            flying[c] = send(chunk, "wide", d) if d else exchange(chunk, "wide")
        return values

    def land(values, *groups):
        taken = members(groups)
        values, got = lax.optimization_barrier((values, [flying[c] for c in taken]))
        arrived.update(zip(taken, got))
        return values

    def placed(pages):
        taken = sorted(arrived)
        if not taken:
            return pages
        place, counts = [], []
        for _, d, first, _ in [parts[c] for c in taken]:
            own = [(me ^ d) * capacity + ahead + first]
            place += own if d else [w * capacity for w in range(wide)]
            counts.append(1 if d else wide)
        place = jnp.stack([jnp.asarray(index, jnp.int32) for index in place])
        pages = place_pages(place, [arrived[c] for c in taken], counts, pages)
        arrived.clear()
        return pages

    gathered, tags = lax.optimization_barrier((gathered, tags))
    tokens = pool.reshape(slots * PAGE, -1)
    if direct:
        block = jax.ShapeDtypeStruct((rows, 2 * HD), jnp.float32)
        partial = in_vmem(
            functools.partial(project_kernel, narrow),
            [block] * narrow,
            both,
            gathered,
            w_query,
            w_keyval,
            scratch=[pltpu.VMEM((rows, narrow * HD), jnp.float32)],
        )
        partial = deal(launch(partial, 8, 6), "narrow")
        partial = launch(partial, 1)
        packed = in_vmem(
            functools.partial(pack_kernel, narrow),
            jax.ShapeDtypeStruct((wide, rows + wide, 2 * HD), jnp.bfloat16),
            None,
            *partial,
            tags,
        )
        received = land(exchange(packed, "wide"), 8, 6, 1)
        received = launch(received, 0)
        queries, keyval, new_entries, moved_req, moved_idx = in_vmem(
            functools.partial(unpack_kernel, rows),
            [
                jax.ShapeDtypeStruct((wide, rows, HD), jnp.bfloat16),
                jax.ShapeDtypeStruct((extra, wide * HD), jnp.bfloat16),
                jax.ShapeDtypeStruct((1, local_rows, wide * HD), jnp.bfloat16),
                jax.ShapeDtypeStruct((1, slots), jnp.int32),
                jax.ShapeDtypeStruct((1, slots), jnp.int32),
            ],
            (both, accepted),
            received,
        )
        moved_req, moved_idx = moved_req.reshape(slots), moved_idx.reshape(slots)
        queries = share(queries, "narrow")
    else:
        gathered = gathered.reshape(rows, -1)
        query_part = jnp.dot(gathered, w_query, preferred_element_type=jnp.float32)
        keyval_part = jnp.dot(gathered, w_keyval, preferred_element_type=jnp.float32)
        query_part = jnp.transpose(query_part.reshape(rows, narrow, own_cols), (1, 0, 2))
        partial = jnp.concatenate(
            [query_part, jnp.broadcast_to(keyval_part[None], (narrow,) + keyval_part.shape)], axis=2
        )
        partial = exchange(launch(partial, 8, 6), "narrow")
        partial = launch(partial, 1)
        projected = jnp.sum(partial, axis=0).astype(jnp.bfloat16)
        tags = tags[:, : 3 * capacity].astype(jnp.bfloat16)[:, None]
        tags = jnp.pad(tags, ((0, 0), (0, 7), (0, projected.shape[1] - tags.shape[2])))
        packed = jnp.broadcast_to(projected[None], (wide,) + projected.shape)
        packed = jnp.concatenate([packed, tags], axis=1)
        received = land(exchange(packed, "wide"), 8, 6, 1)
        received = launch(received, 0)
        tags_in = received[:, rows]
        queries = received[:, :rows, :own_cols]
        queries = spread(queries, "narrow")
        queries = jnp.transpose(queries, (2, 1, 0, 3)).reshape(rows, HEADS, HD)
        queries = [jnp.transpose(queries, (1, 0, 2)).reshape(KVH, GROUPS * rows, HD)]
        keyval = jnp.transpose(received[:, :rows, own_cols:], (1, 0, 2)).reshape(rows, -1)
        keyval = jnp.pad(keyval, ((0, extra - rows), (0, 0)))
        tags_in = tags_in.astype(jnp.int32)
        moved_req = tags_in[:, :capacity].reshape(slots)
        moved_idx = tags_in[:, capacity : 2 * capacity] * 32
        moved_idx = (moved_idx + tags_in[:, 2 * capacity : 3 * capacity] - 1).reshape(slots)
        local_req = local_rows // STEPS
        fresh = lax.dynamic_slice_in_dim(keyval, me * local_rows, local_rows, 0)
        fresh = fresh.reshape(local_req, STEPS, -1)
        kept = lax.dynamic_slice_in_dim(accepted, me * local_req, local_req, 0)
        step_ids = jnp.arange(STEPS)[None, :, None]
        new_entries = jnp.where(
            step_ids < kept[:, None, None], fresh, jnp.zeros((), jnp.bfloat16)
        )

    queries, moved_pool = lax.optimization_barrier((queries, placed(moved_pool)))
    mixed = attend(both, lengths, queries, keyval, tokens, token_info, rows, piece)
    mixed = launch(mixed, 3, 4)
    if direct:
        mixed = land(deal(mixed, "narrow"), 0)
    else:
        mixed = land(exchange(mixed[0], "narrow"), 0)
        mixed = mixed.reshape((narrow, wide) + mixed.shape[1:])
        mixed = [mixed[i] for i in range(narrow)]
    mixed = combine(mixed, piece)
    mixed, pages = lax.optimization_barrier((mixed, moved_pool))
    pages = placed(pages)
    mixed = land(exchange(mixed, "wide"), 3, 4)
    mixed, moved_pool = lax.optimization_barrier((mixed, pages))
    attn = combine([launch(mixed, 2, 5)], piece, wide)
    attn, pages = lax.optimization_barrier((attn, moved_pool))
    pages = placed(pages)
    attn = land(exchange(attn, "wide"), 2, 5)
    attn, moved_pool = lax.optimization_barrier((attn, pages))
    attn = launch(attn, 7)
    if direct:
        sums = in_vmem(
            functools.partial(finish_kernel, narrow),
            [jax.ShapeDtypeStruct((rows // narrow, w_out.shape[1]), jnp.float32)] * narrow,
            both,
            attn,
            w_out,
        )
        sums, pages = lax.optimization_barrier((sums, moved_pool))
        pages = placed(pages)
        sums = land(deal(sums, "narrow"), 7)
        attended = ((sums[0] + sums[1]) + (sums[2] + sums[3])).astype(jnp.bfloat16)
    else:
        attn = jnp.transpose(attn.reshape(-1, rows, HD), (1, 0, 2)).reshape(rows, -1)
        sums = jnp.dot(attn, w_out, preferred_element_type=jnp.float32)
        sums = sums.reshape(narrow, rows // narrow, -1)
        pages = placed(moved_pool)
        sums = land(exchange(sums, "narrow"), 7)
        attended = jnp.sum(sums, axis=0).astype(jnp.bfloat16)
    attended, pages = lax.optimization_barrier((attended, pages))
    moved_pool = placed(pages)
    return (attended, new_entries, moved_pool, moved_req, moved_idx)


def solution(mesh):
    in_specs = (
        P("wide", "narrow"),
        P("narrow", "wide"),
        P("narrow", "wide"),
        P("narrow", "wide"),
        P(("wide", "narrow"), None, None),
        P(("wide", "narrow")),
        P(("wide", "narrow")),
        P(),
        P(("wide", "narrow"), None),
        P(),
    )
    out_specs = (
        P("narrow", "wide"),
        P("wide", None, None),
        P(("wide", "narrow"), None, None),
        P(("wide", "narrow")),
        P(("wide", "narrow")),
    )
    return jax.shard_map(
        on_device, mesh=mesh, in_specs=in_specs, out_specs=out_specs, check_vma=False
    )
```
